32 devices in a mesh: fsdp: 8 (over z, core), mp: 4 (over y, x).
Axes of the slice: x: 2, y: 2, z: 4, core: 2. Of those that a mesh axis runs over, the one named last changes fastest.
Arguments:
- inputs: bfloat16 [2048, 2048], P('fsdp'), may hold values from -6 to 6
- cotangent: bfloat16 [2048, 2048], P('fsdp'), may hold values from -6 to 6
- lengths: int32 [2], replicated, may hold values from 256 to 1024, as said below
- attn_scale: float32 [2048], P('fsdp'), may hold values from 0.5 to 1.5
- w_query: float32 [2048, 2048], P('fsdp', 'mp'), may hold values from -0.015625 to 0.015625
- w_key: float32 [2048, 2048], P('fsdp', 'mp'), may hold values from -0.125 to 0.125
- w_value: float32 [2048, 2048], P('fsdp', 'mp'), may hold values from -0.125 to 0.125
- w_out: float32 [2048, 2048], P('mp', 'fsdp'), may hold values from -3 to 3
- rel_table: float32 [32, 32], P('fsdp', 'mp'), may hold values from -4 to 4
- ffn_scale: float32 [2048], P('fsdp'), may hold values from 0.5 to 1.5
- w_gate: float32 [2048, 5120], P('fsdp', 'mp'), may hold values from -0.125 to 0.125
- w_up: float32 [2048, 5120], P('fsdp', 'mp'), may hold values from -0.125 to 0.125
- w_down: float32 [5120, 2048], P('mp', 'fsdp'), may hold values from -0.078125 to 0.078125
Outputs:
- outputs: bfloat16 [2048, 2048], P('fsdp')
- d_inputs: bfloat16 [2048, 2048], P('fsdp')
- d_attn_scale: float32 [2048], P('fsdp')
- d_w_query: float32 [2048, 2048], P('fsdp', 'mp')
- d_w_key: float32 [2048, 2048], P('fsdp', 'mp')
- d_w_value: float32 [2048, 2048], P('fsdp', 'mp')
- d_w_out: float32 [2048, 2048], P('mp', 'fsdp')
- d_rel_table: float32 [32, 32], P('fsdp', 'mp')
- d_ffn_scale: float32 [2048], P('fsdp')
- d_w_gate: float32 [2048, 5120], P('fsdp', 'mp')
- d_w_up: float32 [2048, 5120], P('fsdp', 'mp')
- d_w_down: float32 [5120, 2048], P('mp', 'fsdp')
The draws below stay inside these ranges and needn't reach their ends.
Inputs may be any that keep to these rules, and one draw needn't show every extreme that they name: lengths[s] slots at the start of sequence s are used, the rest is padding; in every draw some sequence is full.
All inputs are finite; a program needn't handle non-finite values.
Results may differ from the reference program's by a relative error of at most 0.019.
Values may be sent and summed in bfloat16 or wider, within the bound.
No kernel may reach another device: no remote copies, remote signals or barrier semaphores. Data moves between devices by JAX's collectives and lax.ppermute only.
A program may use at most 192 MiB of HBM per device.

```python
import jax
import jax.numpy as jnp
from jax import lax

D = 2048
HEADS = 32
HEAD = 64
FF = 5120
BUCKETS = 32
QBLOCK = 256
SEQ_LEN = 1024
SEQS = 2
TOKENS = 2048
INNER = 2048


def draw_lengths(key, part):
    first_key, second_key = jax.random.split(jax.random.fold_in(key, 17))
    drawn = jax.random.randint(first_key, (SEQS,), SEQ_LEN // 4, SEQ_LEN + 1)
    chosen = jax.random.randint(second_key, (), 0, SEQS)
    return jnp.where(jnp.arange(SEQS) == chosen, SEQ_LEN, drawn).astype(jnp.int32)


def level_of(rng, shape, shards, least, high):
    level = 1.0
    for axis_at, parts in shards:
        heights = jax.random.uniform(jax.random.fold_in(jax.random.fold_in(rng, 6), axis_at), (parts,), jnp.float32, least / len(shards), high / len(shards))
        level = level * jnp.repeat(jnp.exp(heights), shape[axis_at] // parts).reshape((-1,) + (1,) * (len(shape) - 1 - axis_at))
    return level


def bell_draw(stream_key, dims, spread, most, pieces=(), kind=jnp.bfloat16):
    values = jax.random.normal(stream_key, dims, jnp.float32) * spread
    if len(pieces) > 0:
        values = level_of(stream_key, dims, pieces, -0.22, 0.18) * values
    return jnp.clip(values, min=-most, max=most).astype(kind)


def setup_inputs(seed: int = 0) -> dict:
    streams_of = jax.random.split(jax.random.key(seed), 14)
    return {
        "inputs": bell_draw(streams_of[0], (TOKENS, D), 1.0, 6.0, ((0, 8),)),
        "cotangent": bell_draw(streams_of[1], (TOKENS, D), 1.0, 6.0, ((0, 8),)),
        "lengths": draw_lengths(jax.random.fold_in(streams_of[13], 71), 0),
        "attn_scale": jnp.clip(0.5 + 1.0 * jax.random.uniform(streams_of[3], (D,), jnp.float32) ** level_of(streams_of[3], (D,), ((0, 8),), -0.2, 0.2), 0.5, 1.5),
        "w_query": bell_draw(streams_of[4], (D, INNER), (D * HEAD) ** -0.5, 0.015625, ((0, 8), (1, 4)), jnp.float32),
        "w_key": bell_draw(streams_of[5], (D, INNER), D ** -0.5, 0.125, ((0, 8), (1, 4)), jnp.float32),
        "w_value": bell_draw(streams_of[6], (D, INNER), D ** -0.5, 0.125, ((0, 8), (1, 4)), jnp.float32),
        "w_out": bell_draw(streams_of[7], (INNER, D), (max(D // 512, 1)) ** -0.5, 3.0, ((0, 4), (1, 8)), jnp.float32),
        "rel_table": bell_draw(streams_of[8], (BUCKETS, HEADS), 1.0, 4.0, ((0, 8), (1, 4)), jnp.float32),
        "ffn_scale": jnp.clip(0.5 + 1.0 * jax.random.uniform(streams_of[9], (D,), jnp.float32) ** level_of(streams_of[9], (D,), ((0, 8),), -0.2, 0.2), 0.5, 1.5),
        "w_gate": bell_draw(streams_of[10], (D, FF), D ** -0.5, 0.125, ((0, 8), (1, 4)), jnp.float32),
        "w_up": bell_draw(streams_of[11], (D, FF), D ** -0.5, 0.125, ((0, 8), (1, 4)), jnp.float32),
        "w_down": bell_draw(streams_of[12], (FF, D), FF ** -0.5, 0.078125, ((0, 4), (1, 8)), jnp.float32),
    }


@jax.custom_vjp
def low(v):
    return lax.optimization_barrier(v.astype(jnp.bfloat16)).astype(jnp.float32)

@jax.custom_vjp
def low_back(v):
    return v

def low_keep(v):
    return (low(v), None)

def low_pass(kept, grad):
    return (grad,)

def back_keep(v):
    return (v, None)

def back_low(kept, grad):
    return (low(grad),)
low.defvjp(low_keep, low_pass)
low_back.defvjp(back_keep, back_low)
THRESHOLDS = (12, 16, 23, 32, 46, 64, 91)
EPSILON = 1e-06
MASKED = -1e+30

def bucket_of(rel_offset):
    distance = jnp.abs(rel_offset)
    far_bucket = 8 + sum(((distance >= threshold).astype(jnp.int32) for threshold in THRESHOLDS))
    bucket_abs = jnp.where(distance < 8, distance, far_bucket)
    return (bucket_abs + jnp.where(rel_offset > 0, 16, 0)).astype(jnp.int32)

def matmul(left, right):
    return jnp.dot(left, right, precision=lax.Precision.HIGHEST, preferred_element_type=jnp.float32)

def rms_norm(values, norm_gain):
    return values * lax.rsqrt(lax.optimization_barrier(jnp.mean(values * values, axis=-1, keepdims=True)) + EPSILON) * norm_gain

def attention(queries, keys_all, values_all, table, lengths):
    seq_shape = (SEQS, SEQ_LEN, HEADS, HEAD)

    def one_sequence(seq_items):
        q_seq, k_seq, v_seq, length = seq_items
        allowed = jnp.arange(SEQ_LEN, dtype=jnp.int32) < length

        def one_block(block_items):
            q_block, block_start = block_items
            rel_offset = jnp.arange(SEQ_LEN, dtype=jnp.int32)[None, :] - (block_start + jnp.arange(QBLOCK, dtype=jnp.int32))[:, None]
            pos_bias = jnp.transpose(jnp.take(table, bucket_of(rel_offset), axis=0), (2, 0, 1))
            scores = jnp.einsum('qhd,khd->hqk', q_block, k_seq, precision=lax.Precision.HIGHEST) + pos_bias
            scores = jnp.where(allowed[None, None, :], low_back(scores), MASKED)
            row_max = lax.optimization_barrier(jnp.max(scores, axis=-1, keepdims=True))
            exp_scores = jnp.exp(scores - row_max)
            attn_prob = exp_scores / lax.optimization_barrier(jnp.sum(exp_scores, axis=-1, keepdims=True))
            return jnp.einsum('hqk,khd->qhd', low(attn_prob), v_seq, precision=lax.Precision.HIGHEST)
        q_blocks = q_seq.reshape(SEQ_LEN // QBLOCK, QBLOCK, HEADS, HEAD)
        block_starts = jnp.arange(SEQ_LEN // QBLOCK, dtype=jnp.int32) * QBLOCK
        return lax.map(jax.checkpoint(one_block), (q_blocks, block_starts)).reshape(SEQ_LEN, INNER)
    attn_mixed = lax.map(one_sequence, (queries.reshape(seq_shape), keys_all.reshape(seq_shape), values_all.reshape(seq_shape), lengths))
    return low_back(low(attn_mixed.reshape(TOKENS, INNER)))

def reference(inputs, cotangent, lengths, attn_scale, w_query, w_key, w_value, w_out, rel_table, ffn_scale, w_gate, w_up, w_down):
    slot_index = jnp.arange(TOKENS, dtype=jnp.int32)
    valid_slot = slot_index % SEQ_LEN < jnp.repeat(lengths, SEQ_LEN)

    def forward(resid, attn_gain, query_w, key_w, value_w, out_w, table, ffn_gain, gate_w, up_w, down_w):
        normed = low(rms_norm(resid, low(attn_gain)))
        queries = low_back(low(matmul(normed, low(query_w))))
        keys_all = low_back(low(matmul(normed, low(key_w))))
        values_all = low_back(low(matmul(normed, low(value_w))))
        attended = attention(queries, keys_all, values_all, low(table), lengths)
        after_attn = resid + low_back(matmul(attended, low(out_w)))
        normed_two = low(rms_norm(after_attn, low(ffn_gain)))
        gate_pre = low_back(matmul(normed_two, low(gate_w)))
        up_pre = low_back(matmul(normed_two, low(up_w)))
        hidden = low(jax.nn.gelu(gate_pre, approximate=True) * up_pre)
        after_ffn = after_attn + low_back(matmul(hidden, low(down_w)))
        return jnp.where(valid_slot[:, None], after_ffn, 0.0)
    result, pull_back = jax.vjp(forward, inputs.astype(jnp.float32), attn_scale, w_query, w_key, w_value, w_out, rel_table, ffn_scale, w_gate, w_up, w_down)
    gradients = pull_back(cotangent.astype(jnp.float32))
    return (result.astype(jnp.bfloat16), gradients[0].astype(jnp.bfloat16), gradients[1], gradients[2], gradients[3], gradients[4], gradients[5], gradients[6], gradients[7], gradients[8], gradients[9], gradients[10])
```

```python
import functools

import jax
import jax.numpy as jnp
from jax import lax
from jax.experimental import pallas as pl
from jax.experimental.pallas import tpu as pltpu
from jax.sharding import Mesh, PartitionSpec as P

LOW = jnp.bfloat16
F32 = jnp.float32
CORES = 2
THRESHOLDS = (12, 16, 23, 32, 46, 64, 91)
EPSILON = 1e-06
MASKED = -1e30
SKEW = 128


def bucket_of(rel_offset):
    distance = jnp.abs(rel_offset)
    far_bucket = 8 + sum(((distance >= threshold).astype(jnp.int32) for threshold in THRESHOLDS))
    bucket_abs = jnp.where(distance < 8, distance, far_bucket)
    return bucket_abs + jnp.where(rel_offset > 0, 16, 0)


def bucket_onehot(buckets, seq_len):
    offset = lax.broadcasted_iota(jnp.int32, (buckets, 2 * seq_len), 1) - seq_len
    bucket = lax.broadcasted_iota(jnp.int32, (buckets, 2 * seq_len), 0)
    return bucket_of(offset) == bucket


def head_lanes(rows, width, head_width, head):
    lane = lax.broadcasted_iota(jnp.int32, (rows, width), 1)
    return (lane >= head * head_width) & (lane < (head + 1) * head_width)


def only(mask, values):
    return jnp.where(mask, values, jnp.zeros_like(values))


def block_place(block, core, near_count):
    return lax.rem(block, near_count) * CORES + lax.bitwise_xor(lax.div(block, near_count), core)


def bias_places(place_ref, step, blocks, rows, seq_len):
    core, near_count = place_ref[1], blocks // CORES
    query = block_place(step, core, near_count) * rows
    return [
        [
            pl.multiple_of(
                block_place(block, core, near_count) * rows - query - part * SKEW + seq_len - SKEW,
                SKEW,
            )
            for block in range(blocks)
        ]
        for part in range(rows // SKEW)
    ]


def forward_kernel(heads, rows, place_ref, qkv_ref, table_ref, o_ref, p_ref, skew_ref):
    step = pl.program_id(0)
    seq_len = qkv_ref.shape[0]
    width = qkv_ref.shape[1] // 3
    head_width = width // heads
    span = 2 * seq_len
    blocks = seq_len // rows

    @pl.when(step == 0)
    def _():
        one_hot = bucket_onehot(table_ref.shape[1], seq_len).astype(F32).astype(LOW)
        lines = jnp.dot(table_ref[...], one_hot, preferred_element_type=F32)
        for head in range(heads):
            line = jnp.broadcast_to(lines[head : head + 1], (SKEW, span))
            skew_ref[head] = pltpu.roll(line, span - SKEW, 1, stride=1, stride_axis=0)

    row = lax.broadcasted_iota(jnp.int32, (1, rows), 1)
    allowed = jnp.concatenate(
        [
            block_place(block, place_ref[1], blocks // CORES) * rows + row < place_ref[0]
            for block in range(blocks)
        ],
        1,
    )
    queries = qkv_ref[pl.ds(pl.multiple_of(step * rows, rows), rows), :width]
    keys = qkv_ref[:, width : 2 * width]
    values = qkv_ref[:, 2 * width :]
    total = jnp.zeros((rows, width), F32)
    places = bias_places(place_ref, step, blocks, rows, seq_len)
    for head in range(heads):
        scores = lax.dot_general(
            only(head_lanes(rows, width, head_width, head), queries),
            keys,
            (((1,), (1,)), ((), ())),
            preferred_element_type=F32,
        )
        bias = jnp.concatenate(
            [
                jnp.concatenate([skew_ref[head, :, pl.ds(place, rows)] for place in part], 1)
                for part in places
            ],
            0,
        )
        scores = jnp.where(allowed, scores + bias, MASKED)
        grown = jnp.exp(scores - jnp.max(scores, axis=1, keepdims=True))
        prob = (grown * (1.0 / jnp.sum(grown, axis=1, keepdims=True))).astype(LOW)
        p_ref[head] = prob
        total = total + jnp.dot(
            prob,
            only(head_lanes(seq_len, width, head_width, head), values),
            preferred_element_type=F32,
        )
    o_ref[...] = total.astype(LOW)


def attention_forward(qkv, table, place, heads, rows):
    seq_len, width = qkv.shape[0], qkv.shape[1] // 3
    return pl.pallas_call(
        functools.partial(forward_kernel, heads, rows),
        grid=(seq_len // rows,),
        in_specs=[
            pl.BlockSpec(memory_space=pltpu.SMEM),
            pl.BlockSpec(qkv.shape, lambda i: (0, 0)),
            pl.BlockSpec(table.shape, lambda i: (0, 0)),
        ],
        out_specs=[
            pl.BlockSpec((rows, width), lambda i: (i, 0)),
            pl.BlockSpec((heads, rows, seq_len), lambda i: (0, i, 0)),
        ],
        out_shape=[
            jax.ShapeDtypeStruct((seq_len, width), LOW),
            jax.ShapeDtypeStruct((heads, seq_len, seq_len), LOW),
        ],
        scratch_shapes=[pltpu.VMEM((heads, SKEW, 2 * seq_len), F32)],
        compiler_params=pltpu.CompilerParams(vmem_limit_bytes=32 * 2**20),
        cost_estimate=pl.CostEstimate(
            flops=4 * seq_len * seq_len * width * 4,
            bytes_accessed=2 * heads * seq_len * seq_len,
            transcendentals=heads * seq_len * seq_len,
        ),
        name="attention_forward",
    )(place, qkv, table)


def backward_kernel(
    heads, rows, place_ref, p_ref, do_ref, qkv_ref, d_ref, dt_ref, dk_sum, dv_sum, skew_ref
):
    step = pl.program_id(0)
    seq_len = qkv_ref.shape[0]
    width = qkv_ref.shape[1] // 3
    head_width = width // heads
    span = 2 * seq_len
    blocks = seq_len // rows

    @pl.when(step == 0)
    def _():
        dk_sum[...] = jnp.zeros_like(dk_sum)
        dv_sum[...] = jnp.zeros_like(dv_sum)
        skew_ref[...] = jnp.zeros_like(skew_ref)

    here = pl.ds(pl.multiple_of(step * rows, rows), rows)
    queries = qkv_ref[here, :width]
    keys = qkv_ref[:, width : 2 * width]
    values = qkv_ref[:, 2 * width :]
    grads = do_ref[...]
    total = jnp.zeros((rows, width), F32)
    places = bias_places(place_ref, step, blocks, rows, seq_len)
    for head in range(heads):
        own = head_lanes(rows, width, head_width, head)
        own_grads = only(own, grads)
        d_prob = lax.dot_general(
            own_grads, values, (((1,), (1,)), ((), ())), preferred_element_type=F32
        )
        prob_low = p_ref[head]
        prob = prob_low.astype(F32)
        weighed = prob * d_prob
        d_scores = (weighed - prob * jnp.sum(weighed, axis=1, keepdims=True)).astype(LOW)
        total = total + jnp.dot(
            d_scores,
            only(head_lanes(seq_len, width, head_width, head), keys),
            preferred_element_type=F32,
        )
        dk_sum[...] += lax.dot_general(
            d_scores, only(own, queries), (((0,), (0,)), ((), ())), preferred_element_type=F32
        )
        dv_sum[...] += lax.dot_general(
            prob_low, own_grads, (((0,), (0,)), ((), ())), preferred_element_type=F32
        )
        for part in range(rows // SKEW):
            for block in range(blocks):
                skew_ref[head, :, pl.ds(places[part][block], rows)] += d_scores[
                    part * SKEW : (part + 1) * SKEW, block * rows : (block + 1) * rows
                ].astype(F32)
    d_ref[here, :width] = total.astype(LOW)

    @pl.when(step == pl.num_programs(0) - 1)
    def _():
        d_ref[:, width : 2 * width] = dk_sum[...].astype(LOW)
        d_ref[:, 2 * width :] = dv_sum[...].astype(LOW)
        one_hot = bucket_onehot(dt_ref.shape[0], seq_len)
        row = lax.broadcasted_iota(jnp.int32, (SKEW, span), 0)
        column = lax.broadcasted_iota(jnp.int32, dt_ref.shape, 1)
        result = jnp.zeros(dt_ref.shape, F32)
        for head in range(heads):
            level = pltpu.roll(skew_ref[head], SKEW, 1)
            bit = 1
            while bit < SKEW:
                level = jnp.where((row & bit) != 0, pltpu.roll(level, span - bit, 1), level)
                bit *= 2
            line = jnp.sum(level, axis=0, keepdims=True)
            summed = jnp.sum(jnp.where(one_hot, line, 0.0), axis=1, keepdims=True)
            result = jnp.where(column == head, summed, result)
        dt_ref[...] = result


def attention_backward(prob, d_out, qkv, place, heads, rows, buckets):
    seq_len, width = d_out.shape
    return pl.pallas_call(
        functools.partial(backward_kernel, heads, rows),
        grid=(seq_len // rows,),
        in_specs=[
            pl.BlockSpec(memory_space=pltpu.SMEM),
            pl.BlockSpec((heads, rows, seq_len), lambda i: (0, i, 0)),
            pl.BlockSpec((rows, width), lambda i: (i, 0)),
            pl.BlockSpec(qkv.shape, lambda i: (0, 0)),
        ],
        out_specs=[
            pl.BlockSpec(qkv.shape, lambda i: (0, 0)),
            pl.BlockSpec((buckets, 128), lambda i: (0, 0)),
        ],
        out_shape=[
            jax.ShapeDtypeStruct(qkv.shape, LOW),
            jax.ShapeDtypeStruct((buckets, 128), F32),
        ],
        scratch_shapes=[
            pltpu.VMEM((seq_len, width), F32),
            pltpu.VMEM((seq_len, width), F32),
            pltpu.VMEM((heads, SKEW, 2 * seq_len), F32),
        ],
        compiler_params=pltpu.CompilerParams(vmem_limit_bytes=40 * 2**20),
        cost_estimate=pl.CostEstimate(
            flops=8 * seq_len * seq_len * width * 4,
            bytes_accessed=2 * heads * seq_len * seq_len,
            transcendentals=0,
        ),
        name="attention_backward",
    )(place, prob, d_out, qkv)


COLUMN = ("seq", "near", "core")
EXTRA = 8


def exchange(blocks, axes):
    return lax.all_to_all(blocks, axes, split_axis=0, concat_axis=0, tiled=True)


def swap(block, axis):
    return lax.ppermute(block, axis, [(0, 1), (1, 0)])


def after(value, *done):
    return lax.optimization_barrier((value,) + done)[0]


def rows_dot(left, right):
    return jnp.dot(left, right, preferred_element_type=F32)


def contract_cols(left, right):
    return lax.dot_general(left, right, (((1,), (1,)), ((), ())), preferred_element_type=F32)


def contract_rows(left, right):
    return lax.dot_general(left, right, (((0,), (0,)), ((), ())), preferred_element_type=F32)


def rms(values):
    return lax.rsqrt(jnp.mean(values * values, axis=1, keepdims=True) + EPSILON)


def norm_grad(inner, normed, inverse):
    return inverse * (inner - normed * jnp.mean(inner * normed, axis=1, keepdims=True))


def gelu_tanh(values):
    return jax.nn.gelu(values, approximate=True)


def local(
    inputs,
    cotangent,
    lengths,
    attn_scale,
    w_query,
    w_key,
    w_value,
    w_out,
    rel_table,
    ffn_scale,
    w_gate,
    w_up,
    w_down,
):
    seqs = lax.axis_size("seq")
    near_count = lax.axis_size("near")
    mp_count = lax.axis_size("mp")
    members = near_count * CORES
    sources = seqs * members
    tok_rows, model = inputs.shape
    seq_len = tok_rows * members
    own_rows = tok_rows // mp_count
    half_rows = seq_len // CORES
    shard = attn_scale.shape[0]
    table_rows, heads_mp = rel_table.shape
    buckets = table_rows * sources
    heads = heads_mp // members
    width = w_query.shape[1] // members
    hidden_width = w_gate.shape[1] // members

    near_at = lax.axis_index("near")
    core_at = lax.axis_index("core")
    mp_at = lax.axis_index("mp")
    member_at = near_at * CORES + core_at
    length = lax.dynamic_slice_in_dim(lengths, lax.axis_index("seq"), 1, 0)
    place = jnp.concatenate([length, jnp.reshape(core_at, (1,)).astype(jnp.int32)])

    def to_column(parts):
        return exchange(
            jnp.broadcast_to(parts[None], (seqs,) + parts.shape).reshape(
                (sources,) + parts.shape[1:]
            ),
            COLUMN,
        )

    def by_member(weight):
        return weight.reshape(weight.shape[0], members, -1)

    def scaled(weight, gain):
        low = weight.astype(LOW).astype(F32)
        return (low * gain.astype(LOW).astype(F32)[:, None]).astype(LOW)

    def over_mp(own, axis):
        shape = own.shape[:axis] + (mp_count,) + own.shape[axis:]
        blocks = lax.dynamic_update_index_in_dim(jnp.zeros(shape, own.dtype), own, mp_at, axis)
        moved = [(away, shifted(own, away)) for away in reversed(range(1, mp_count))]
        for away, block in moved:
            blocks = lax.dynamic_update_index_in_dim(blocks, block, mp_at ^ away, axis)
        return blocks

    def shifted(block, away):
        return lax.ppermute(block, "mp", [(i, i ^ away) for i in range(mp_count)])

    def in_near_order(own, moved):
        return jnp.stack(
            [jnp.where(near_at == 0, own, moved), jnp.where(near_at == 0, moved, own)], 0
        )

    def near_block_rows(block):
        own = lax.dynamic_slice_in_dim(block, mp_at * own_rows, own_rows, 0)
        moved = over_mp(swap(own, "near"), 0).reshape(tok_rows, model)
        return in_near_order(block, moved).reshape(half_rows, model)

    def gather_rows(own):
        near = in_near_order(own, swap(own, "near"))
        mine = over_mp(near, 1).reshape(half_rows, model)
        return mine, swap(mine, "core")

    def sum_cores(mine, other):
        arrived = swap(other.astype(LOW), "core")
        return (mine + arrived.astype(F32)).astype(LOW)

    def sum_mp(rows):
        pieces = rows.reshape(near_count, mp_count, own_rows, model)
        moved = []
        for away in reversed(range(1, mp_count)):
            piece = lax.dynamic_index_in_dim(pieces, mp_at ^ away, 1, keepdims=False)
            moved.append(shifted(piece, away))
        kept = lax.dynamic_index_in_dim(pieces, mp_at, 1, keepdims=False)
        return sum((piece.astype(F32) for piece in moved), kept.astype(F32))

    def sum_near(pair):
        sent = jnp.where(near_at == 0, pair[1], pair[0]).astype(LOW)
        kept = jnp.where(near_at == 0, pair[0], pair[1])
        return kept + swap(sent, "near").astype(F32)

    attn_parts = jnp.moveaxis(
        jnp.concatenate(
            [
                by_member(scaled(w_query, attn_scale)),
                by_member(scaled(w_key, attn_scale)),
                by_member(scaled(w_value, attn_scale)),
                by_member(w_out.T.astype(LOW)),
            ],
            2,
        ),
        1,
        0,
    )
    table_parts = rel_table.astype(LOW).reshape(table_rows, members, heads)
    table_parts = jnp.moveaxis(table_parts, 1, 0).reshape(members, 1, table_rows * heads)
    table_parts = jnp.pad(
        table_parts, ((0, 0), (0, EXTRA - 1), (0, 4 * width - table_rows * heads))
    )
    gate_up_parts = jnp.moveaxis(
        jnp.concatenate(
            [by_member(scaled(w_gate, ffn_scale)), by_member(scaled(w_up, ffn_scale))], 2
        ),
        1,
        0,
    )
    down_parts = jnp.moveaxis(by_member(w_down.T.astype(LOW)), 1, 0)

    attn_got = to_column(jnp.concatenate([attn_parts, table_parts], 1))
    attn_weights = attn_got[:, :shard].reshape(model, 4 * width)
    qkv_weight = attn_weights[:, : 3 * width]
    out_weight_t = attn_weights[:, 3 * width :]
    table = attn_got[:, shard, : table_rows * heads].reshape(buckets, heads)
    table = jnp.pad(table.T, ((0, 8 - heads), (0, 0)))

    mine_inputs = near_block_rows(inputs)
    mine_values = mine_inputs.astype(F32)
    mine_normed = (mine_values * rms(mine_values)).astype(LOW)
    normed_rows = jnp.concatenate([mine_normed, swap(mine_normed, "core")], 0)
    row_valid = (member_at * tok_rows + lax.iota(jnp.int32, tok_rows) < length)[:, None]
    masked = after(jnp.where(row_valid, cotangent, jnp.zeros_like(cotangent)), mine_inputs)
    mine_grad = near_block_rows(masked)
    other_grad = swap(mine_grad, "core")

    normed_rows = after(normed_rows, gate_up_parts, down_parts)
    gate_up_weight = to_column(gate_up_parts).reshape(model, 2 * hidden_width)
    down_weight_t = to_column(down_parts).reshape(model, hidden_width)

    qkv = rows_dot(normed_rows, qkv_weight).astype(LOW)
    attended, prob = attention_forward(qkv, table, place, heads, tok_rows)
    attended = after(attended, mine_grad, other_grad)
    mixed = sum_near(
        sum_mp(
            sum_cores(
                contract_cols(attended[:half_rows], out_weight_t),
                contract_cols(attended[half_rows:], out_weight_t),
            )
        )
    )

    own_inputs = lax.dynamic_slice_in_dim(inputs, mp_at * own_rows, own_rows, 0).astype(F32)
    own_cotangent = lax.dynamic_slice_in_dim(cotangent, mp_at * own_rows, own_rows, 0)
    own_first = member_at * tok_rows + mp_at * own_rows
    own_valid = (own_first + lax.iota(jnp.int32, own_rows) < length)[:, None]
    after_attn = own_inputs + mixed
    inv_two = rms(after_attn)
    normed_two = after_attn * inv_two
    halves = gather_rows(after(normed_two.astype(LOW), gate_up_weight))

    acts, d_gate_ups, d_norms, ffn_outs = [], [], [], []
    for rows, grad in zip(halves, (mine_grad, other_grad)):
        gate_up = rows_dot(rows, gate_up_weight)
        gate_pre, up_pre = gate_up[:, :hidden_width], gate_up[:, hidden_width:]
        gelu_value, gelu_pull = jax.vjp(gelu_tanh, gate_pre)
        acts.append((gelu_value * up_pre).astype(LOW))
        d_hidden = rows_dot(grad, down_weight_t)
        (d_gate_pre,) = gelu_pull(d_hidden * up_pre)
        d_gate_ups.append(
            jnp.concatenate([d_gate_pre.astype(LOW), (d_hidden * gelu_value).astype(LOW)], 1)
        )
        d_norms.append(contract_cols(d_gate_ups[-1], gate_up_weight))
        ffn_outs.append(contract_cols(acts[-1], down_weight_t))
    inner_two = sum_near(sum_mp(sum_cores(*d_norms)))

    def to_owners(grad):
        return exchange(grad.astype(LOW), COLUMN)

    def of_owner(got):
        parts = got.reshape((seqs, members) + got.shape[1:]).astype(F32)
        return jnp.moveaxis(jnp.sum(parts, axis=0), 0, 1)

    def flat(parts):
        return parts.reshape(shard, -1)

    d_down = to_owners(
        (contract_rows(mine_grad, acts[0]) + contract_rows(other_grad, acts[1])).reshape(
            sources, shard, -1
        )
    )
    d_gate_up = to_owners(
        (
            contract_rows(halves[0], d_gate_ups[0]) + contract_rows(halves[1], d_gate_ups[1])
        ).reshape(sources, shard, -1)
    )

    grad_one = jnp.where(own_valid, own_cotangent.astype(F32), 0.0) + norm_grad(
        inner_two, normed_two, inv_two
    )
    mine_one, other_one = gather_rows(after(grad_one.astype(LOW), d_down))
    d_attended = jnp.concatenate(
        [rows_dot(mine_one, out_weight_t), rows_dot(other_one, out_weight_t)], 0
    ).astype(LOW)
    d_qkv, d_table = attention_backward(prob, d_attended, qkv, place, heads, tok_rows, buckets)
    inner_cores = sum_cores(
        contract_cols(d_qkv[:half_rows], qkv_weight), contract_cols(d_qkv[half_rows:], qkv_weight)
    )
    d_out = to_owners(
        (
            contract_rows(mine_one, attended[:half_rows])
            + contract_rows(other_one, attended[half_rows:])
        ).reshape(sources, shard, -1)
    )
    ffn_cores = after(sum_cores(*ffn_outs), mine_one)
    ffn_pair = sum_mp(ffn_cores)
    inner_one = sum_near(sum_mp(after(inner_cores, d_gate_up)))
    table_sent = d_table[:, :heads].astype(LOW).reshape(sources, 1, table_rows * heads)
    table_sent = jnp.pad(
        table_sent, ((0, 0), (0, EXTRA - 1), (0, 3 * width - table_rows * heads))
    )
    d_qkv_w = contract_rows(normed_rows, d_qkv).astype(LOW).reshape(sources, shard, -1)
    d_qkv_got = to_owners(jnp.concatenate([d_qkv_w, table_sent], 1))

    normed_one = own_inputs * rms(own_inputs)
    grad_input = grad_one + norm_grad(inner_one, normed_one, rms(own_inputs))
    d_inputs = over_mp(grad_input.astype(LOW), 0).reshape(tok_rows, model)
    after_ffn = after_attn + sum_near(ffn_pair)
    own_out = jnp.where(own_valid, after_ffn, 0.0).astype(LOW)
    layer_out = over_mp(own_out, 0).reshape(tok_rows, model)

    g_gate_up = of_owner(d_gate_up)
    g_gate, g_up = flat(g_gate_up[:, :, :hidden_width]), flat(g_gate_up[:, :, hidden_width:])
    got_qkv = of_owner(d_qkv_got)
    g_query, g_key, g_value = (
        flat(got_qkv[:shard, :, i * width : (i + 1) * width]) for i in range(3)
    )
    d_rel_table = got_qkv[shard, :, : table_rows * heads].reshape(members, table_rows, heads)
    d_rel_table = jnp.moveaxis(d_rel_table, 0, 1).reshape(table_rows, heads_mp)

    def gain_grad(pairs):
        return sum(jnp.sum(w.astype(LOW).astype(F32) * g, axis=1) for w, g in pairs)

    gains = jnp.stack(
        [
            gain_grad([(w_query, g_query), (w_key, g_key), (w_value, g_value)]),
            gain_grad([(w_gate, g_gate), (w_up, g_up)]),
        ]
    )
    gains = sum((shifted(gains, away) for away in range(1, mp_count)), gains)
    attn_gain = attn_scale.astype(LOW).astype(F32)[:, None]
    ffn_gain = ffn_scale.astype(LOW).astype(F32)[:, None]
    return (
        layer_out,
        d_inputs,
        gains[0],
        g_query * attn_gain,
        g_key * attn_gain,
        g_value * attn_gain,
        flat(of_owner(d_out)).T,
        d_rel_table,
        gains[1],
        g_gate * ffn_gain,
        g_up * ffn_gain,
        flat(of_owner(d_down)).T,
    )


def solution(mesh):
    fsdp, mp = mesh.shape["fsdp"], mesh.shape["mp"]

    def run(*args):
        seqs = args[2].shape[0]
        members = fsdp // seqs
        inner = Mesh(
            mesh.devices.reshape(seqs, members // CORES, CORES, mp), ("seq", "near", "core", "mp")
        )
        rows, columns, first = P(COLUMN, None), P("mp", COLUMN), P(COLUMN)
        both = P(COLUMN, "mp")
        in_specs = (
            rows, rows, P(), first, both, both, both, columns, both, first, both, both, columns,
        )
        out_specs = (
            rows, rows, first, both, both, both, columns, both, first, both, both, columns,
        )
        return jax.shard_map(
            local, mesh=inner, in_specs=in_specs, out_specs=out_specs, check_vma=False
        )(*args)

    return run
```

```python
import functools

import jax
import jax.numpy as jnp
from jax import lax
from jax.experimental import pallas as pl
from jax.experimental.pallas import tpu as pltpu
from jax.sharding import Mesh, PartitionSpec as P

LOW = jnp.bfloat16
F32 = jnp.float32
CORES = 2
THRESHOLDS = (12, 16, 23, 32, 46, 64, 91)
EPSILON = 1e-06
MASKED = -1e30
SKEW = 128


def bucket_of(rel_offset):
    distance = jnp.abs(rel_offset)
    far_bucket = 8 + sum(((distance >= threshold).astype(jnp.int32) for threshold in THRESHOLDS))
    bucket_abs = jnp.where(distance < 8, distance, far_bucket)
    return bucket_abs + jnp.where(rel_offset > 0, 16, 0)


def bucket_onehot(buckets, seq_len):
    offset = lax.broadcasted_iota(jnp.int32, (buckets, 2 * seq_len), 1) - seq_len
    bucket = lax.broadcasted_iota(jnp.int32, (buckets, 2 * seq_len), 0)
    return bucket_of(offset) == bucket


def head_lanes(rows, width, head_width, head):
    lane = lax.broadcasted_iota(jnp.int32, (rows, width), 1)
    return (lane >= head * head_width) & (lane < (head + 1) * head_width)


def only(mask, values):
    return jnp.where(mask, values, jnp.zeros_like(values))


def block_place(block, core, near_count):
    return lax.rem(block, near_count) * CORES + lax.bitwise_xor(lax.div(block, near_count), core)


def bias_places(place_ref, step, blocks, rows, seq_len):
    core, near_count = place_ref[1], blocks // CORES
    query = block_place(step, core, near_count) * rows
    return [
        [
            pl.multiple_of(
                block_place(block, core, near_count) * rows - query - part * SKEW + seq_len - SKEW,
                SKEW,
            )
            for block in range(blocks)
        ]
        for part in range(rows // SKEW)
    ]


def forward_kernel(heads, rows, place_ref, qkv_ref, table_ref, o_ref, p_ref, skew_ref):
    step = pl.program_id(0)
    seq_len = qkv_ref.shape[0]
    width = qkv_ref.shape[1] // 3
    head_width = width // heads
    span = 2 * seq_len
    blocks = seq_len // rows

    @pl.when(step == 0)
    def _():
        one_hot = bucket_onehot(table_ref.shape[1], seq_len).astype(F32).astype(LOW)
        lines = jnp.dot(table_ref[...], one_hot, preferred_element_type=F32)
        for head in range(heads):
            line = jnp.broadcast_to(lines[head : head + 1], (SKEW, span))
            skew_ref[head] = pltpu.roll(line, span - SKEW, 1, stride=1, stride_axis=0)

    row = lax.broadcasted_iota(jnp.int32, (1, rows), 1)
    allowed = jnp.concatenate(
        [
            block_place(block, place_ref[1], blocks // CORES) * rows + row < place_ref[0]
            for block in range(blocks)
        ],
        1,
    )
    queries = qkv_ref[pl.ds(pl.multiple_of(step * rows, rows), rows), :width]
    keys = qkv_ref[:, width : 2 * width]
    values = qkv_ref[:, 2 * width :]
    total = jnp.zeros((rows, width), F32)
    places = bias_places(place_ref, step, blocks, rows, seq_len)
    for head in range(heads):
        scores = lax.dot_general(
            only(head_lanes(rows, width, head_width, head), queries),
            keys,
            (((1,), (1,)), ((), ())),
            preferred_element_type=F32,
        )
        bias = jnp.concatenate(
            [
                jnp.concatenate([skew_ref[head, :, pl.ds(place, rows)] for place in part], 1)
                for part in places
            ],
            0,
        )
        scores = jnp.where(allowed, scores + bias, MASKED)
        grown = jnp.exp(scores - jnp.max(scores, axis=1, keepdims=True))
        prob = (grown * (1.0 / jnp.sum(grown, axis=1, keepdims=True))).astype(LOW)
        p_ref[head] = prob
        total = total + jnp.dot(
            prob,
            only(head_lanes(seq_len, width, head_width, head), values),
            preferred_element_type=F32,
        )
    o_ref[...] = total.astype(LOW)


def attention_forward(qkv, table, place, heads, rows):
    seq_len, width = qkv.shape[0], qkv.shape[1] // 3
    return pl.pallas_call(
        functools.partial(forward_kernel, heads, rows),
        grid=(seq_len // rows,),
        in_specs=[
            pl.BlockSpec(memory_space=pltpu.SMEM),
            pl.BlockSpec(qkv.shape, lambda i: (0, 0)),
            pl.BlockSpec(table.shape, lambda i: (0, 0)),
        ],
        out_specs=[
            pl.BlockSpec((rows, width), lambda i: (i, 0)),
            pl.BlockSpec((heads, rows, seq_len), lambda i: (0, i, 0)),
        ],
        out_shape=[
            jax.ShapeDtypeStruct((seq_len, width), LOW),
            jax.ShapeDtypeStruct((heads, seq_len, seq_len), LOW),
        ],
        scratch_shapes=[pltpu.VMEM((heads, SKEW, 2 * seq_len), F32)],
        compiler_params=pltpu.CompilerParams(vmem_limit_bytes=32 * 2**20),
        cost_estimate=pl.CostEstimate(
            flops=4 * seq_len * seq_len * width * 4,
            bytes_accessed=2 * heads * seq_len * seq_len,
            transcendentals=heads * seq_len * seq_len,
        ),
        name="attention_forward",
    )(place, qkv, table)


def backward_kernel(
    heads, rows, place_ref, p_ref, do_ref, qkv_ref, d_ref, dt_ref, dk_sum, dv_sum, skew_ref
):
    step = pl.program_id(0)
    seq_len = qkv_ref.shape[0]
    width = qkv_ref.shape[1] // 3
    head_width = width // heads
    span = 2 * seq_len
    blocks = seq_len // rows

    @pl.when(step == 0)
    def _():
        dk_sum[...] = jnp.zeros_like(dk_sum)
        dv_sum[...] = jnp.zeros_like(dv_sum)
        skew_ref[...] = jnp.zeros_like(skew_ref)

    here = pl.ds(pl.multiple_of(step * rows, rows), rows)
    queries = qkv_ref[here, :width]
    keys = qkv_ref[:, width : 2 * width]
    values = qkv_ref[:, 2 * width :]
    grads = do_ref[...]
    total = jnp.zeros((rows, width), F32)
    places = bias_places(place_ref, step, blocks, rows, seq_len)
    for head in range(heads):
        own = head_lanes(rows, width, head_width, head)
        own_grads = only(own, grads)
        d_prob = lax.dot_general(
            own_grads, values, (((1,), (1,)), ((), ())), preferred_element_type=F32
        )
        prob_low = p_ref[head]
        prob = prob_low.astype(F32)
        weighed = prob * d_prob
        d_scores = (weighed - prob * jnp.sum(weighed, axis=1, keepdims=True)).astype(LOW)
        total = total + jnp.dot(
            d_scores,
            only(head_lanes(seq_len, width, head_width, head), keys),
            preferred_element_type=F32,
        )
        dk_sum[...] += lax.dot_general(
            d_scores, only(own, queries), (((0,), (0,)), ((), ())), preferred_element_type=F32
        )
        dv_sum[...] += lax.dot_general(
            prob_low, own_grads, (((0,), (0,)), ((), ())), preferred_element_type=F32
        )
        for part in range(rows // SKEW):
            for block in range(blocks):
                skew_ref[head, :, pl.ds(places[part][block], rows)] += d_scores[
                    part * SKEW : (part + 1) * SKEW, block * rows : (block + 1) * rows
                ].astype(F32)
    d_ref[here, :width] = total.astype(LOW)

    @pl.when(step == pl.num_programs(0) - 1)
    def _():
        d_ref[:, width : 2 * width] = dk_sum[...].astype(LOW)
        d_ref[:, 2 * width :] = dv_sum[...].astype(LOW)
        one_hot = bucket_onehot(dt_ref.shape[0], seq_len)
        row = lax.broadcasted_iota(jnp.int32, (SKEW, span), 0)
        column = lax.broadcasted_iota(jnp.int32, dt_ref.shape, 1)
        result = jnp.zeros(dt_ref.shape, F32)
        for head in range(heads):
            level = pltpu.roll(skew_ref[head], SKEW, 1)
            bit = 1
            while bit < SKEW:
                level = jnp.where((row & bit) != 0, pltpu.roll(level, span - bit, 1), level)
                bit *= 2
            line = jnp.sum(level, axis=0, keepdims=True)
            summed = jnp.sum(jnp.where(one_hot, line, 0.0), axis=1, keepdims=True)
            result = jnp.where(column == head, summed, result)
        dt_ref[...] = result


def attention_backward(prob, d_out, qkv, place, heads, rows, buckets):
    seq_len, width = d_out.shape
    return pl.pallas_call(
        functools.partial(backward_kernel, heads, rows),
        grid=(seq_len // rows,),
        in_specs=[
            pl.BlockSpec(memory_space=pltpu.SMEM),
            pl.BlockSpec((heads, rows, seq_len), lambda i: (0, i, 0)),
            pl.BlockSpec((rows, width), lambda i: (i, 0)),
            pl.BlockSpec(qkv.shape, lambda i: (0, 0)),
        ],
        out_specs=[
            pl.BlockSpec(qkv.shape, lambda i: (0, 0)),
            pl.BlockSpec((buckets, 128), lambda i: (0, 0)),
        ],
        out_shape=[
            jax.ShapeDtypeStruct(qkv.shape, LOW),
            jax.ShapeDtypeStruct((buckets, 128), F32),
        ],
        scratch_shapes=[
            pltpu.VMEM((seq_len, width), F32),
            pltpu.VMEM((seq_len, width), F32),
            pltpu.VMEM((heads, SKEW, 2 * seq_len), F32),
        ],
        compiler_params=pltpu.CompilerParams(vmem_limit_bytes=40 * 2**20),
        cost_estimate=pl.CostEstimate(
            flops=8 * seq_len * seq_len * width * 4,
            bytes_accessed=2 * heads * seq_len * seq_len,
            transcendentals=0,
        ),
        name="attention_backward",
    )(place, prob, d_out, qkv)


COLUMN = ("seq", "near", "core")
EXTRA = 8


def exchange(blocks, axes):
    return lax.all_to_all(blocks, axes, split_axis=0, concat_axis=0, tiled=True)


def swap(block, axis):
    return lax.ppermute(block, axis, [(0, 1), (1, 0)])


def after(value, *done):
    return lax.optimization_barrier((value,) + done)[0]


def rows_dot(left, right):
    return jnp.dot(left, right, preferred_element_type=F32)


def contract_cols(left, right):
    return lax.dot_general(left, right, (((1,), (1,)), ((), ())), preferred_element_type=F32)


def contract_rows(left, right):
    return lax.dot_general(left, right, (((0,), (0,)), ((), ())), preferred_element_type=F32)


def rms(values):
    return lax.rsqrt(jnp.mean(values * values, axis=1, keepdims=True) + EPSILON)


def norm_grad(inner, normed, inverse):
    return inverse * (inner - normed * jnp.mean(inner * normed, axis=1, keepdims=True))


def gelu_tanh(values):
    return jax.nn.gelu(values, approximate=True)


def local(
    inputs,
    cotangent,
    lengths,
    attn_scale,
    w_query,
    w_key,
    w_value,
    w_out,
    rel_table,
    ffn_scale,
    w_gate,
    w_up,
    w_down,
):
    seqs = lax.axis_size("seq")
    near_count = lax.axis_size("near")
    mp_count = lax.axis_size("mp")
    members = near_count * CORES
    sources = seqs * members
    tok_rows, model = inputs.shape
    seq_len = tok_rows * members
    own_rows = tok_rows // mp_count
    half_rows = seq_len // CORES
    shard = attn_scale.shape[0]
    table_rows, heads_mp = rel_table.shape
    buckets = table_rows * sources
    heads = heads_mp // members
    width = w_query.shape[1] // members
    hidden_width = w_gate.shape[1] // members

    near_at = lax.axis_index("near")
    core_at = lax.axis_index("core")
    mp_at = lax.axis_index("mp")
    member_at = near_at * CORES + core_at
    length = lax.dynamic_slice_in_dim(lengths, lax.axis_index("seq"), 1, 0)
    place = jnp.concatenate([length, jnp.reshape(core_at, (1,)).astype(jnp.int32)])

    def for_column(parts):
        return jnp.broadcast_to(parts[None], (seqs,) + parts.shape).reshape(
            (sources,) + parts.shape[1:]
        )

    def by_member(weight):
        return weight.reshape(weight.shape[0], members, -1)

    def scaled(weight, gain):
        low = weight.astype(LOW).astype(F32)
        return (low * gain.astype(LOW).astype(F32)[:, None]).astype(LOW)

    def over_mp(own, axis):
        shape = own.shape[:axis] + (mp_count,) + own.shape[axis:]
        blocks = lax.dynamic_update_index_in_dim(jnp.zeros(shape, own.dtype), own, mp_at, axis)
        moved = [(away, shifted(own, away)) for away in reversed(range(1, mp_count))]
        for away, block in moved:
            blocks = lax.dynamic_update_index_in_dim(blocks, block, mp_at ^ away, axis)
        return blocks

    def shifted(block, away):
        return lax.ppermute(block, "mp", [(i, i ^ away) for i in range(mp_count)])

    def in_near_order(own, moved):
        return jnp.stack(
            [jnp.where(near_at == 0, own, moved), jnp.where(near_at == 0, moved, own)], 0
        )

    def near_block_rows(block):
        own = lax.dynamic_slice_in_dim(block, mp_at * own_rows, own_rows, 0)
        moved = over_mp(swap(own, "near"), 0).reshape(tok_rows, model)
        return in_near_order(block, moved).reshape(half_rows, model)

    def gather_rows(own):
        near = in_near_order(own, swap(own, "near"))
        blocks = [(0, near)] + [(away, shifted(near, away)) for away in range(1, mp_count)]
        shape = (near_count, mp_count, own_rows, model)
        mine, other = jnp.zeros(shape, own.dtype), jnp.zeros(shape, own.dtype)
        for away, block in blocks:
            at = mp_at ^ away
            mine = lax.dynamic_update_index_in_dim(mine, block, at, 1)
            other = lax.dynamic_update_index_in_dim(other, swap(block, "core"), at, 1)
        return mine.reshape(half_rows, model), other.reshape(half_rows, model), near

    def sum_cores(mine, other):
        mine = mine.reshape(near_count, mp_count, own_rows, model)
        other = other.astype(LOW).reshape(near_count, mp_count, own_rows, model)
        sums = []
        for away in reversed(range(mp_count)):
            at = mp_at ^ away
            arrived = swap(lax.dynamic_index_in_dim(other, at, 1, keepdims=False), "core")
            kept = lax.dynamic_index_in_dim(mine, at, 1, keepdims=False)
            sums.append(kept.astype(F32) + arrived.astype(F32))
        return sums

    def send_mp(sums):
        last = len(sums) - 1
        moved = [shifted(rows.astype(LOW), last - i) for i, rows in enumerate(sums[:-1])]
        return moved, sums[-1]

    def sum_mp(sums):
        moved, kept = send_mp(sums)
        return sum((piece.astype(F32) for piece in moved), kept)

    def sum_near(pair):
        sent = jnp.where(near_at == 0, pair[1], pair[0]).astype(LOW)
        kept = jnp.where(near_at == 0, pair[0], pair[1])
        return kept + swap(sent, "near").astype(F32)

    attn_parts = jnp.moveaxis(
        jnp.concatenate(
            [
                by_member(scaled(w_query, attn_scale)),
                by_member(scaled(w_key, attn_scale)),
                by_member(scaled(w_value, attn_scale)),
                by_member(w_out.T.astype(LOW)),
            ],
            2,
        ),
        1,
        0,
    )
    table_parts = rel_table.astype(LOW).reshape(table_rows, members, heads)
    table_parts = jnp.moveaxis(table_parts, 1, 0).reshape(members, 1, table_rows * heads)
    table_parts = jnp.pad(
        table_parts, ((0, 0), (0, EXTRA - 1), (0, 4 * width - table_rows * heads))
    )
    ffn_parts = for_column(
        jnp.moveaxis(
            jnp.concatenate(
                [
                    by_member(scaled(w_gate, ffn_scale)),
                    by_member(scaled(w_up, ffn_scale)),
                    by_member(w_down.T.astype(LOW)),
                ],
                2,
            ),
            1,
            0,
        )
    )

    attn_got = exchange(for_column(jnp.concatenate([attn_parts, table_parts], 1)), COLUMN)
    attn_weights = attn_got[:, :shard].reshape(model, 4 * width)
    qkv_weight = attn_weights[:, : 3 * width]
    out_weight_t = attn_weights[:, 3 * width :]
    table = attn_got[:, shard, : table_rows * heads].reshape(buckets, heads)
    table = jnp.pad(table.T, ((0, 8 - heads), (0, 0)))

    mine_inputs = near_block_rows(inputs)
    mine_values = mine_inputs.astype(F32)
    mine_normed = (mine_values * rms(mine_values)).astype(LOW)
    normed_rows = jnp.concatenate([mine_normed, swap(mine_normed, "core")], 0)
    row_valid = (member_at * tok_rows + lax.iota(jnp.int32, tok_rows) < length)[:, None]
    later_cotangent = after(cotangent, mine_inputs)
    masked = jnp.where(row_valid, later_cotangent, jnp.zeros_like(cotangent))
    mine_grad = near_block_rows(masked)
    other_grad = swap(mine_grad, "core")

    normed_rows = after(normed_rows, ffn_parts)
    ffn_weights = exchange(after(ffn_parts, attn_got), COLUMN).reshape(model, 3 * hidden_width)
    gate_up_weight = ffn_weights[:, : 2 * hidden_width]
    down_weight_t = ffn_weights[:, 2 * hidden_width :]

    qkv = rows_dot(normed_rows, qkv_weight).astype(LOW)
    attended, prob = attention_forward(qkv, table, place, heads, tok_rows)
    attended = after(attended, mine_grad, other_grad)
    mixed = sum_near(
        sum_mp(
            sum_cores(
                contract_cols(attended[:half_rows], out_weight_t),
                contract_cols(attended[half_rows:], out_weight_t),
            )
        )
    )

    later_inputs = after(inputs, normed_rows)
    own_inputs = lax.dynamic_slice_in_dim(later_inputs, mp_at * own_rows, own_rows, 0).astype(F32)
    own_cotangent = lax.dynamic_slice_in_dim(later_cotangent, mp_at * own_rows, own_rows, 0)
    own_first = member_at * tok_rows + mp_at * own_rows
    own_valid = (own_first + lax.iota(jnp.int32, own_rows) < length)[:, None]
    after_attn = own_inputs + mixed
    inv_two = rms(after_attn)
    normed_two = after_attn * inv_two
    halves = gather_rows(normed_two.astype(LOW))[:2]

    acts, d_gate_ups, d_norms = [], [], []
    for rows, grad in zip(halves, (mine_grad, other_grad)):
        gate_up = rows_dot(rows, gate_up_weight)
        gate_pre, up_pre = gate_up[:, :hidden_width], gate_up[:, hidden_width:]
        gelu_value, gelu_pull = jax.vjp(gelu_tanh, gate_pre)
        acts.append((gelu_value * up_pre).astype(LOW))
        d_hidden = rows_dot(grad, down_weight_t)
        (d_gate_pre,) = gelu_pull(d_hidden * up_pre)
        d_gate_ups.append(
            jnp.concatenate([d_gate_pre.astype(LOW), (d_hidden * gelu_value).astype(LOW)], 1)
        )
        d_norms.append(contract_cols(d_gate_ups[-1], gate_up_weight))
    inner_cores = sum_cores(*d_norms)
    inner_two = sum_near(sum_mp(inner_cores))
    ffn_cores = sum_cores(
        *[contract_cols(after(act, *inner_cores), down_weight_t) for act in acts]
    )
    acts = [after(act, *d_norms) for act in acts]
    d_gate_ups = [after(grad, *d_norms) for grad in d_gate_ups]

    def to_owners(grad):
        return exchange(grad.astype(LOW), COLUMN)

    def of_owner(got):
        parts = got.reshape((seqs, members) + got.shape[1:]).astype(F32)
        return jnp.moveaxis(jnp.sum(parts, axis=0), 0, 1)

    def flat(parts):
        return parts.reshape(shard, -1)

    d_down = to_owners(
        (contract_rows(mine_grad, acts[0]) + contract_rows(other_grad, acts[1])).reshape(
            sources, shard, -1
        )
    )
    d_gate_up = to_owners(
        (
            contract_rows(halves[0], d_gate_ups[0]) + contract_rows(halves[1], d_gate_ups[1])
        ).reshape(sources, shard, -1)
    )

    grad_one = jnp.where(own_valid, own_cotangent.astype(F32), 0.0) + norm_grad(
        inner_two, normed_two, inv_two
    )
    mine_one, other_one, _ = gather_rows(after(grad_one.astype(LOW), d_down, *ffn_cores))
    d_attended = jnp.concatenate(
        [rows_dot(mine_one, out_weight_t), rows_dot(other_one, out_weight_t)], 0
    ).astype(LOW)
    d_qkv, d_table = attention_backward(prob, d_attended, qkv, place, heads, tok_rows, buckets)
    inner_cores = sum_cores(
        contract_cols(d_qkv[:half_rows], qkv_weight), contract_cols(d_qkv[half_rows:], qkv_weight)
    )
    ffn_moved, ffn_kept = send_mp([after(rows, mine_one) for rows in ffn_cores])
    ffn_moved = [after(rows, d_qkv) for rows in ffn_moved]
    inner_one = sum_near(sum_mp(inner_cores))
    table_sent = d_table[:, :heads].astype(LOW).reshape(sources, 1, table_rows * heads)
    table_sent = jnp.pad(
        table_sent, ((0, 0), (0, EXTRA - 1), (0, 3 * width - table_rows * heads))
    )
    d_qkv_w = contract_rows(normed_rows, d_qkv).astype(LOW).reshape(sources, shard, -1)
    d_qkv_got = to_owners(jnp.concatenate([d_qkv_w, table_sent], 1))
    later_attended = after(attended, inner_cores[0])
    d_out = contract_rows(mine_one, later_attended[:half_rows]) + contract_rows(
        other_one, later_attended[half_rows:]
    )
    d_out = to_owners(after(d_out.astype(LOW).reshape(sources, shard, -1), d_qkv_got))

    normed_one = own_inputs * rms(own_inputs)
    grad_input = grad_one + norm_grad(inner_one, normed_one, rms(own_inputs))
    d_inputs = over_mp(grad_input.astype(LOW), 0).reshape(tok_rows, model)
    ffn_pair = sum((piece.astype(F32) for piece in ffn_moved), ffn_kept)
    after_ffn = after_attn + sum_near(after(ffn_pair, inner_one))
    own_out = jnp.where(own_valid, after_ffn, 0.0).astype(LOW)
    layer_out = over_mp(own_out, 0).reshape(tok_rows, model)

    g_gate_up = of_owner(after(d_gate_up, inner_cores[0]))
    g_gate, g_up = flat(g_gate_up[:, :, :hidden_width]), flat(g_gate_up[:, :, hidden_width:])
    got_qkv = of_owner(d_qkv_got)
    g_query, g_key, g_value = (
        flat(got_qkv[:shard, :, i * width : (i + 1) * width]) for i in range(3)
    )
    d_rel_table = got_qkv[shard, :, : table_rows * heads].reshape(members, table_rows, heads)
    d_rel_table = jnp.moveaxis(d_rel_table, 0, 1).reshape(table_rows, heads_mp)

    def gain_grad(pairs):
        return sum(jnp.sum(w.astype(LOW).astype(F32) * g, axis=1) for w, g in pairs)

    gains = jnp.stack(
        [
            gain_grad([(w_query, g_query), (w_key, g_key), (w_value, g_value)]),
            gain_grad([(w_gate, g_gate), (w_up, g_up)]),
        ]
    )
    gains = sum((shifted(gains, away) for away in range(1, mp_count)), gains)
    attn_gain = attn_scale.astype(LOW).astype(F32)[:, None]
    ffn_gain = ffn_scale.astype(LOW).astype(F32)[:, None]
    return (
        layer_out,
        d_inputs,
        gains[0],
        g_query * attn_gain,
        g_key * attn_gain,
        g_value * attn_gain,
        flat(of_owner(d_out)).T,
        d_rel_table,
        gains[1],
        g_gate * ffn_gain,
        g_up * ffn_gain,
        flat(of_owner(after(d_down, d_qkv))).T,
    )


def solution(mesh):
    fsdp, mp = mesh.shape["fsdp"], mesh.shape["mp"]

    def run(*args):
        seqs = args[2].shape[0]
        members = fsdp // seqs
        inner = Mesh(
            mesh.devices.reshape(seqs, members // CORES, CORES, mp), ("seq", "near", "core", "mp")
        )
        rows, columns, first = P(COLUMN, None), P("mp", COLUMN), P(COLUMN)
        both = P(COLUMN, "mp")
        in_specs = (
            rows, rows, P(), first, both, both, both, columns, both, first, both, both, columns,
        )
        out_specs = (
            rows, rows, first, both, both, both, columns, both, first, both, both, columns,
        )
        return jax.shard_map(
            local, mesh=inner, in_specs=in_specs, out_specs=out_specs, check_vma=False
        )(*args)

    return run
```

```python
import functools

import jax
import jax.numpy as jnp
from jax import lax
from jax.experimental import pallas as pl
from jax.experimental.pallas import tpu as pltpu
from jax.sharding import Mesh, PartitionSpec as P

LOW = jnp.bfloat16
F32 = jnp.float32
CORES = 2
THRESHOLDS = (12, 16, 23, 32, 46, 64, 91)
EPSILON = 1e-06
MASKED = -1e30
SKEW = 128


def bucket_of(rel_offset):
    distance = jnp.abs(rel_offset)
    far_bucket = 8 + sum(((distance >= threshold).astype(jnp.int32) for threshold in THRESHOLDS))
    bucket_abs = jnp.where(distance < 8, distance, far_bucket)
    return bucket_abs + jnp.where(rel_offset > 0, 16, 0)


def bucket_onehot(buckets, seq_len):
    offset = lax.broadcasted_iota(jnp.int32, (buckets, 2 * seq_len), 1) - seq_len
    bucket = lax.broadcasted_iota(jnp.int32, (buckets, 2 * seq_len), 0)
    return bucket_of(offset) == bucket


def head_lanes(rows, width, head_width, head):
    lane = lax.broadcasted_iota(jnp.int32, (rows, width), 1)
    return (lane >= head * head_width) & (lane < (head + 1) * head_width)


def only(mask, values):
    return jnp.where(mask, values, jnp.zeros_like(values))


def block_place(block, core, near_count):
    return lax.rem(block, near_count) * CORES + lax.bitwise_xor(lax.div(block, near_count), core)


def bias_places(place_ref, step, blocks, rows, seq_len):
    core, near_count = place_ref[1], blocks // CORES
    query = block_place(step, core, near_count) * rows
    return [
        [
            pl.multiple_of(
                block_place(block, core, near_count) * rows - query - part * SKEW + seq_len - SKEW,
                SKEW,
            )
            for block in range(blocks)
        ]
        for part in range(rows // SKEW)
    ]


def forward_kernel(heads, rows, place_ref, qkv_ref, table_ref, o_ref, p_ref, skew_ref):
    step = pl.program_id(0)
    seq_len = qkv_ref.shape[0]
    width = qkv_ref.shape[1] // 3
    head_width = width // heads
    span = 2 * seq_len
    blocks = seq_len // rows

    @pl.when(step == 0)
    def _():
        one_hot = bucket_onehot(table_ref.shape[1], seq_len).astype(F32).astype(LOW)
        lines = jnp.dot(table_ref[...], one_hot, preferred_element_type=F32)
        for head in range(heads):
            line = jnp.broadcast_to(lines[head : head + 1], (SKEW, span))
            skew_ref[head] = pltpu.roll(line, span - SKEW, 1, stride=1, stride_axis=0)

    row = lax.broadcasted_iota(jnp.int32, (1, rows), 1)
    allowed = jnp.concatenate(
        [
            block_place(block, place_ref[1], blocks // CORES) * rows + row < place_ref[0]
            for block in range(blocks)
        ],
        1,
    )
    queries = qkv_ref[pl.ds(pl.multiple_of(step * rows, rows), rows), :width]
    keys = qkv_ref[:, width : 2 * width]
    values = qkv_ref[:, 2 * width :]
    total = jnp.zeros((rows, width), F32)
    places = bias_places(place_ref, step, blocks, rows, seq_len)
    for head in range(heads):
        scores = lax.dot_general(
            only(head_lanes(rows, width, head_width, head), queries),
            keys,
            (((1,), (1,)), ((), ())),
            preferred_element_type=F32,
        )
        bias = jnp.concatenate(
            [
                jnp.concatenate([skew_ref[head, :, pl.ds(place, rows)] for place in part], 1)
                for part in places
            ],
            0,
        )
        scores = jnp.where(allowed, scores + bias, MASKED)
        grown = jnp.exp(scores - jnp.max(scores, axis=1, keepdims=True))
        prob = (grown * (1.0 / jnp.sum(grown, axis=1, keepdims=True))).astype(LOW)
        p_ref[head] = prob
        total = total + jnp.dot(
            prob,
            only(head_lanes(seq_len, width, head_width, head), values),
            preferred_element_type=F32,
        )
    o_ref[...] = total.astype(LOW)


def attention_forward(qkv, table, place, heads, rows):
    seq_len, width = qkv.shape[0], qkv.shape[1] // 3
    return pl.pallas_call(
        functools.partial(forward_kernel, heads, rows),
        grid=(seq_len // rows,),
        in_specs=[
            pl.BlockSpec(memory_space=pltpu.SMEM),
            pl.BlockSpec(qkv.shape, lambda i: (0, 0)),
            pl.BlockSpec(table.shape, lambda i: (0, 0)),
        ],
        out_specs=[
            pl.BlockSpec((rows, width), lambda i: (i, 0)),
            pl.BlockSpec((heads, rows, seq_len), lambda i: (0, i, 0)),
        ],
        out_shape=[
            jax.ShapeDtypeStruct((seq_len, width), LOW),
            jax.ShapeDtypeStruct((heads, seq_len, seq_len), LOW),
        ],
        scratch_shapes=[pltpu.VMEM((heads, SKEW, 2 * seq_len), F32)],
        compiler_params=pltpu.CompilerParams(vmem_limit_bytes=32 * 2**20),
        cost_estimate=pl.CostEstimate(
            flops=4 * seq_len * seq_len * width,
            bytes_accessed=2 * heads * seq_len * seq_len,
            transcendentals=0,
        ),
        name="attention_forward",
    )(place, qkv, table)


def backward_kernel(
    heads, rows, place_ref, p_ref, do_ref, qkv_ref, d_ref, dt_ref, dk_sum, dv_sum, skew_ref
):
    step = pl.program_id(0)
    seq_len = qkv_ref.shape[0]
    width = qkv_ref.shape[1] // 3
    head_width = width // heads
    span = 2 * seq_len
    blocks = seq_len // rows

    @pl.when(step == 0)
    def _():
        dk_sum[...] = jnp.zeros_like(dk_sum)
        dv_sum[...] = jnp.zeros_like(dv_sum)
        skew_ref[...] = jnp.zeros_like(skew_ref)

    here = pl.ds(pl.multiple_of(step * rows, rows), rows)
    queries = qkv_ref[here, :width]
    keys = qkv_ref[:, width : 2 * width]
    values = qkv_ref[:, 2 * width :]
    grads = do_ref[...]
    total = jnp.zeros((rows, width), F32)
    places = bias_places(place_ref, step, blocks, rows, seq_len)
    for head in range(heads):
        own = head_lanes(rows, width, head_width, head)
        own_grads = only(own, grads)
        d_prob = lax.dot_general(
            own_grads, values, (((1,), (1,)), ((), ())), preferred_element_type=F32
        )
        prob_low = p_ref[head]
        prob = prob_low.astype(F32)
        weighed = prob * d_prob
        d_scores = (weighed - prob * jnp.sum(weighed, axis=1, keepdims=True)).astype(LOW)
        total = total + jnp.dot(
            d_scores,
            only(head_lanes(seq_len, width, head_width, head), keys),
            preferred_element_type=F32,
        )
        dk_sum[...] += lax.dot_general(
            d_scores, only(own, queries), (((0,), (0,)), ((), ())), preferred_element_type=F32
        )
        dv_sum[...] += lax.dot_general(
            prob_low, own_grads, (((0,), (0,)), ((), ())), preferred_element_type=F32
        )
        for part in range(rows // SKEW):
            for block in range(blocks):
                skew_ref[head, :, pl.ds(places[part][block], rows)] += d_scores[
                    part * SKEW : (part + 1) * SKEW, block * rows : (block + 1) * rows
                ].astype(F32)
    d_ref[here, :width] = total.astype(LOW)

    @pl.when(step == pl.num_programs(0) - 1)
    def _():
        d_ref[:, width : 2 * width] = dk_sum[...].astype(LOW)
        d_ref[:, 2 * width :] = dv_sum[...].astype(LOW)
        one_hot = bucket_onehot(dt_ref.shape[0], seq_len)
        row = lax.broadcasted_iota(jnp.int32, (SKEW, span), 0)
        column = lax.broadcasted_iota(jnp.int32, dt_ref.shape, 1)
        result = jnp.zeros(dt_ref.shape, F32)
        for head in range(heads):
            level = pltpu.roll(skew_ref[head], SKEW, 1)
            bit = 1
            while bit < SKEW:
                level = jnp.where((row & bit) != 0, pltpu.roll(level, span - bit, 1), level)
                bit *= 2
            line = jnp.sum(level, axis=0, keepdims=True)
            summed = jnp.sum(jnp.where(one_hot, line, 0.0), axis=1, keepdims=True)
            result = jnp.where(column == head, summed, result)
        dt_ref[...] = result


def attention_backward(prob, d_out, qkv, place, heads, rows, buckets):
    seq_len, width = d_out.shape
    return pl.pallas_call(
        functools.partial(backward_kernel, heads, rows),
        grid=(seq_len // rows,),
        in_specs=[
            pl.BlockSpec(memory_space=pltpu.SMEM),
            pl.BlockSpec((heads, rows, seq_len), lambda i: (0, i, 0)),
            pl.BlockSpec((rows, width), lambda i: (i, 0)),
            pl.BlockSpec(qkv.shape, lambda i: (0, 0)),
        ],
        out_specs=[
            pl.BlockSpec(qkv.shape, lambda i: (0, 0)),
            pl.BlockSpec((buckets, 128), lambda i: (0, 0)),
        ],
        out_shape=[
            jax.ShapeDtypeStruct(qkv.shape, LOW),
            jax.ShapeDtypeStruct((buckets, 128), F32),
        ],
        scratch_shapes=[
            pltpu.VMEM((seq_len, width), F32),
            pltpu.VMEM((seq_len, width), F32),
            pltpu.VMEM((heads, SKEW, 2 * seq_len), F32),
        ],
        compiler_params=pltpu.CompilerParams(vmem_limit_bytes=40 * 2**20),
        cost_estimate=pl.CostEstimate(
            flops=8 * seq_len * seq_len * width * 4,
            bytes_accessed=2 * heads * seq_len * seq_len,
            transcendentals=0,
        ),
        name="attention_backward",
    )(place, prob, d_out, qkv)


COLUMN = ("seq", "near", "core")
EXTRA = 8


def exchange(blocks, axes):
    return lax.all_to_all(blocks, axes, split_axis=0, concat_axis=0, tiled=True)


def swap(block, axis):
    return lax.ppermute(block, axis, [(0, 1), (1, 0)])


def after(value, *done):
    return lax.optimization_barrier((value,) + done)[0]


def rows_dot(left, right):
    return jnp.dot(left, right, preferred_element_type=F32)


def contract_cols(left, right):
    return lax.dot_general(left, right, (((1,), (1,)), ((), ())), preferred_element_type=F32)


def contract_rows(left, right):
    return lax.dot_general(left, right, (((0,), (0,)), ((), ())), preferred_element_type=F32)


def rms(values):
    return lax.rsqrt(jnp.mean(values * values, axis=-1, keepdims=True) + EPSILON)


def norm_grad(inner, normed, inverse):
    return inverse * (inner - normed * jnp.mean(inner * normed, axis=-1, keepdims=True))


def gelu_tanh(values):
    return jax.nn.gelu(values, approximate=True)


def local(
    inputs,
    cotangent,
    lengths,
    attn_scale,
    w_query,
    w_key,
    w_value,
    w_out,
    rel_table,
    ffn_scale,
    w_gate,
    w_up,
    w_down,
):
    seqs = lax.axis_size("seq")
    near_count = lax.axis_size("near")
    mp_count = lax.axis_size("mp")
    members = near_count * CORES
    sources = seqs * members
    tok_rows, model = inputs.shape
    seq_len = tok_rows * members
    own_rows = tok_rows // mp_count
    half_rows = seq_len // CORES
    shard = attn_scale.shape[0]
    table_rows, heads_mp = rel_table.shape
    buckets = table_rows * sources
    heads = heads_mp // members
    width = w_query.shape[1] // members
    hidden_width = w_gate.shape[1] // members

    near_at = lax.axis_index("near")
    core_at = lax.axis_index("core")
    mp_at = lax.axis_index("mp")
    member_at = near_at * CORES + core_at
    length = lax.dynamic_slice_in_dim(lengths, lax.axis_index("seq"), 1, 0)
    place = jnp.concatenate([length, jnp.reshape(core_at, (1,)).astype(jnp.int32)])

    def for_column(parts):
        return jnp.broadcast_to(parts[None], (seqs,) + parts.shape).reshape(
            (sources,) + parts.shape[1:]
        )

    def by_member(weight):
        return weight.reshape(weight.shape[0], members, -1)

    def scaled(weight, gain):
        low = weight.astype(LOW).astype(F32)
        return (low * gain.astype(LOW).astype(F32)[:, None]).astype(LOW)

    def over_mp(own, axis):
        shape = own.shape[:axis] + (mp_count,) + own.shape[axis:]
        blocks = lax.dynamic_update_index_in_dim(jnp.zeros(shape, own.dtype), own, mp_at, axis)
        moved = [(away, shifted(own, away)) for away in reversed(range(1, mp_count))]
        for away, block in moved:
            blocks = lax.dynamic_update_index_in_dim(blocks, block, mp_at ^ away, axis)
        return blocks

    def shifted(block, away):
        return lax.ppermute(block, "mp", [(i, i ^ away) for i in range(mp_count)])

    def in_near_order(own, moved):
        return jnp.stack(
            [jnp.where(near_at == 0, own, moved), jnp.where(near_at == 0, moved, own)], 0
        )

    def near_block_rows(block):
        own = lax.dynamic_slice_in_dim(block, mp_at * own_rows, own_rows, 0)
        moved = over_mp(swap(own, "near"), 0).reshape(tok_rows, model)
        return in_near_order(block, moved).reshape(half_rows, model)

    def gather_rows(near):
        blocks = [(0, near)] + [(away, shifted(near, away)) for away in range(1, mp_count)]
        shape = (near_count, mp_count, own_rows, model)
        mine, other = jnp.zeros(shape, near.dtype), jnp.zeros(shape, near.dtype)
        for away, block in blocks:
            at = mp_at ^ away
            mine = lax.dynamic_update_index_in_dim(mine, block, at, 1)
            other = lax.dynamic_update_index_in_dim(other, swap(block, "core"), at, 1)
        return mine.reshape(half_rows, model), other.reshape(half_rows, model)

    def sum_cores(mine, other):
        mine = mine.reshape(near_count, mp_count, own_rows, model)
        other = other.astype(LOW).reshape(near_count, mp_count, own_rows, model)
        sums = []
        for away in reversed(range(mp_count)):
            at = mp_at ^ away
            arrived = swap(lax.dynamic_index_in_dim(other, at, 1, keepdims=False), "core")
            kept = lax.dynamic_index_in_dim(mine, at, 1, keepdims=False)
            sums.append(kept.astype(F32) + arrived.astype(F32))
        return sums

    def send_mp(sums):
        last = len(sums) - 1
        moved = [shifted(rows.astype(LOW), last - i) for i, rows in enumerate(sums[:-1])]
        return moved, sums[-1]

    def sum_mp(sums):
        moved, kept = send_mp(sums)
        return sum((piece.astype(F32) for piece in moved), kept)

    def sum_near(pair):
        sent = jnp.where(near_at == 0, pair[1], pair[0]).astype(LOW)
        kept = jnp.where(near_at == 0, pair[0], pair[1])
        return kept + swap(sent, "near").astype(F32)

    def sum_near_both(pair):
        low = pair.astype(LOW)
        moved = swap(low, "near")
        return low.astype(F32) + moved.astype(F32), moved

    def near_pair(rows):
        blocks = rows.reshape(near_count, mp_count, own_rows, model)
        return lax.dynamic_index_in_dim(blocks, mp_at, 1, keepdims=False)

    def here(pair):
        return lax.dynamic_index_in_dim(pair, near_at, 0, keepdims=False)

    attn_parts = jnp.moveaxis(
        jnp.concatenate(
            [
                by_member(scaled(w_query, attn_scale)),
                by_member(scaled(w_key, attn_scale)),
                by_member(scaled(w_value, attn_scale)),
                by_member(w_out.T.astype(LOW)),
            ],
            2,
        ),
        1,
        0,
    )
    table_parts = rel_table.astype(LOW).reshape(table_rows, members, heads)
    table_parts = jnp.moveaxis(table_parts, 1, 0).reshape(members, 1, table_rows * heads)
    table_parts = jnp.pad(
        table_parts, ((0, 0), (0, EXTRA - 1), (0, 4 * width - table_rows * heads))
    )
    gate_up_parts = for_column(
        jnp.moveaxis(
            jnp.concatenate(
                [by_member(scaled(w_gate, ffn_scale)), by_member(scaled(w_up, ffn_scale))], 2
            ),
            1,
            0,
        )
    )
    down_parts = for_column(w_down.astype(LOW).reshape(members, hidden_width, shard))

    attn_got = exchange(for_column(jnp.concatenate([attn_parts, table_parts], 1)), COLUMN)
    attn_weights = attn_got[:, :shard].reshape(model, 4 * width)
    qkv_weight = attn_weights[:, : 3 * width]
    out_weight_t = attn_weights[:, 3 * width :]
    table = attn_got[:, shard, : table_rows * heads].reshape(buckets, heads)
    table = jnp.pad(table.T, ((0, 8 - heads), (0, 0)))

    mine_inputs = near_block_rows(inputs)
    mine_values = mine_inputs.astype(F32)
    mine_normed = (mine_values * rms(mine_values)).astype(LOW)
    normed_rows = jnp.concatenate([mine_normed, swap(mine_normed, "core")], 0)
    row_valid = (member_at * tok_rows + lax.iota(jnp.int32, tok_rows) < length)[:, None]
    later_cotangent = after(cotangent, mine_inputs)
    masked = jnp.where(row_valid, later_cotangent, jnp.zeros_like(cotangent))
    mine_grad = near_block_rows(masked)
    other_grad = swap(mine_grad, "core")

    normed_rows = after(normed_rows, gate_up_parts, down_parts)
    down_got = exchange(after(down_parts, attn_got), COLUMN)
    down_weight = jnp.moveaxis(down_got, 0, 1).reshape(hidden_width, model)

    qkv = rows_dot(normed_rows, qkv_weight).astype(LOW)
    attended, prob = attention_forward(qkv, table, place, heads, tok_rows)
    attended = after(attended, mine_grad, other_grad)
    mixed, mixed_moved = sum_near_both(
        after(
            sum_mp(
                sum_cores(
                    contract_cols(attended[:half_rows], out_weight_t),
                    contract_cols(attended[half_rows:], out_weight_t),
                )
            ),
            down_got,
        )
    )
    gate_up_weight = exchange(after(gate_up_parts, mixed_moved), COLUMN).reshape(model, 2 * hidden_width)

    pair_inputs = near_pair(after(mine_inputs, normed_rows)).astype(F32)
    pair_cotangent = near_pair(mine_grad).astype(F32)
    after_attn = pair_inputs + mixed
    inv_two = rms(after_attn)
    normed_two = after_attn * inv_two
    halves = gather_rows(normed_two.astype(LOW))

    grads = (mine_grad, other_grad)
    ups, gelus, acts = [], [], []
    for rows in halves:
        gate_up = rows_dot(rows, gate_up_weight)
        gelus.append(jax.vjp(gelu_tanh, gate_up[:, :hidden_width]))
        ups.append(gate_up[:, hidden_width:])
        acts.append((gelus[-1][0] * ups[-1]).astype(LOW))
    d_down_w = (contract_rows(acts[0], grads[0]) + contract_rows(acts[1], grads[1])).astype(LOW)
    d_gate_ups, d_norms = [], []
    for grad, up_pre, (gelu_value, gelu_pull) in zip(grads, ups, gelus):
        d_hidden = contract_cols(after(grad, d_down_w), down_weight)
        (d_gate_pre,) = gelu_pull(d_hidden * up_pre)
        d_gate_ups.append(
            jnp.concatenate([d_gate_pre.astype(LOW), (d_hidden * gelu_value).astype(LOW)], 1)
        )
        d_norms.append(contract_cols(d_gate_ups[-1], gate_up_weight))
    inner_cores = sum_cores(*d_norms)
    ffn_cores = sum_cores(*[rows_dot(after(act, *inner_cores), down_weight) for act in acts])
    d_gate_ups = [after(grad, *d_norms) for grad in d_gate_ups]

    def to_owners(grad):
        return exchange(grad, COLUMN)

    def of_owner(got):
        parts = got.reshape((seqs, members) + got.shape[1:]).astype(F32)
        return jnp.moveaxis(jnp.sum(parts, axis=0), 0, 1)

    def flat(parts):
        return parts.reshape(shard, -1)

    def by_rows(got):
        parts = got.reshape((seqs, members) + got.shape[1:]).astype(F32)
        return jnp.sum(parts, axis=0).reshape(-1, shard)

    d_down = to_owners(jnp.moveaxis(d_down_w.reshape(hidden_width, sources, shard), 1, 0))
    inner_two, inner_moved = sum_near_both(after(sum_mp(inner_cores), d_down, *ffn_cores))
    d_gate_up_w = (
        contract_rows(halves[0], d_gate_ups[0]) + contract_rows(halves[1], d_gate_ups[1])
    ).astype(LOW)
    d_gate_up = to_owners(after(d_gate_up_w, inner_moved).reshape(sources, shard, -1))

    pair_first = (
        lax.broadcasted_iota(jnp.int32, (near_count, own_rows, 1), 0) * (CORES * tok_rows)
        + lax.broadcasted_iota(jnp.int32, (near_count, own_rows, 1), 1)
        + (core_at * tok_rows + mp_at * own_rows)
    )
    pair_valid = pair_first < length
    grad_one = pair_cotangent + norm_grad(inner_two, normed_two, inv_two)
    mine_one, other_one = gather_rows(grad_one.astype(LOW))
    d_attended = jnp.concatenate(
        [rows_dot(mine_one, out_weight_t), rows_dot(other_one, out_weight_t)], 0
    ).astype(LOW)
    d_qkv, d_table = attention_backward(prob, d_attended, qkv, place, heads, tok_rows, buckets)
    inner_cores = sum_cores(
        contract_cols(d_qkv[:half_rows], qkv_weight), contract_cols(d_qkv[half_rows:], qkv_weight)
    )
    ffn_moved, ffn_kept = send_mp([after(rows, mine_one) for rows in ffn_cores])
    ffn_moved = [after(rows, d_qkv) for rows in ffn_moved]
    inner_one = sum_near(after(sum_mp(inner_cores), d_gate_up))
    table_sent = d_table[:, :heads].astype(LOW).reshape(sources, 1, table_rows * heads)
    table_sent = jnp.pad(
        table_sent, ((0, 0), (0, EXTRA - 1), (0, 3 * width - table_rows * heads))
    )
    d_qkv_w = contract_rows(normed_rows, d_qkv).astype(LOW).reshape(sources, shard, -1)
    d_qkv_got = to_owners(after(jnp.concatenate([d_qkv_w, table_sent], 1), d_gate_up))
    later_attended = after(attended, inner_cores[0])
    d_out = contract_rows(later_attended[:half_rows], mine_one) + contract_rows(
        later_attended[half_rows:], other_one
    )
    d_out = jnp.moveaxis(d_out.astype(LOW).reshape(width, sources, shard), 1, 0)
    d_out = to_owners(after(d_out, d_qkv_got))

    own_inputs = here(pair_inputs)
    normed_one = own_inputs * rms(own_inputs)
    grad_input = here(grad_one) + norm_grad(inner_one, normed_one, rms(own_inputs))
    d_inputs = over_mp(grad_input.astype(LOW), 0).reshape(tok_rows, model)
    ffn_pair = sum((piece.astype(F32) for piece in ffn_moved), ffn_kept)
    after_ffn = here(after_attn) + sum_near(after(ffn_pair, inner_one))
    own_out = jnp.where(here(pair_valid), after_ffn, 0.0).astype(LOW)
    layer_out = over_mp(own_out, 0).reshape(tok_rows, model)

    g_gate_up = of_owner(after(d_gate_up, inner_cores[0]))
    g_gate, g_up = flat(g_gate_up[:, :, :hidden_width]), flat(g_gate_up[:, :, hidden_width:])
    got_qkv = of_owner(d_qkv_got)
    g_query, g_key, g_value = (
        flat(got_qkv[:shard, :, i * width : (i + 1) * width]) for i in range(3)
    )
    d_rel_table = got_qkv[shard, :, : table_rows * heads].reshape(members, table_rows, heads)
    d_rel_table = jnp.moveaxis(d_rel_table, 0, 1).reshape(table_rows, heads_mp)

    def gain_grad(pairs):
        return sum(jnp.sum(w.astype(LOW).astype(F32) * g, axis=1) for w, g in pairs)

    gains = jnp.stack(
        [
            gain_grad([(w_query, g_query), (w_key, g_key), (w_value, g_value)]),
            gain_grad([(w_gate, g_gate), (w_up, g_up)]),
        ]
    )
    gains = sum((shifted(gains, away) for away in range(1, mp_count)), gains)
    attn_gain = attn_scale.astype(LOW).astype(F32)[:, None]
    ffn_gain = ffn_scale.astype(LOW).astype(F32)[:, None]
    return (
        layer_out,
        d_inputs,
        gains[0],
        g_query * attn_gain,
        g_key * attn_gain,
        g_value * attn_gain,
        by_rows(d_out),
        d_rel_table,
        gains[1],
        g_gate * ffn_gain,
        g_up * ffn_gain,
        by_rows(after(d_down, d_qkv)),
    )


def solution(mesh):
    fsdp, mp = mesh.shape["fsdp"], mesh.shape["mp"]

    def run(*args):
        seqs = args[2].shape[0]
        members = fsdp // seqs
        inner = Mesh(
            mesh.devices.reshape(seqs, members // CORES, CORES, mp), ("seq", "near", "core", "mp")
        )
        rows, columns, first = P(COLUMN, None), P("mp", COLUMN), P(COLUMN)
        both = P(COLUMN, "mp")
        in_specs = (
            rows, rows, P(), first, both, both, both, columns, both, first, both, both, columns,
        )
        out_specs = (
            rows, rows, first, both, both, both, columns, both, first, both, both, columns,
        )
        return jax.shard_map(
            local, mesh=inner, in_specs=in_specs, out_specs=out_specs, check_vma=False
        )(*args)

    return run
```

```python
import functools

import jax
import jax.numpy as jnp
from jax import lax
from jax.experimental import pallas as pl
from jax.experimental.pallas import tpu as pltpu
from jax.sharding import Mesh, PartitionSpec as P

LOW = jnp.bfloat16
F32 = jnp.float32
CORES = 2
THRESHOLDS = (12, 16, 23, 32, 46, 64, 91)
EPSILON = 1e-06
MASKED = -1e30
SKEW = 128


def bucket_of(rel_offset):
    distance = jnp.abs(rel_offset)
    far_bucket = 8 + sum(((distance >= threshold).astype(jnp.int32) for threshold in THRESHOLDS))
    bucket_abs = jnp.where(distance < 8, distance, far_bucket)
    return bucket_abs + jnp.where(rel_offset > 0, 16, 0)


def bucket_onehot(buckets, seq_len):
    offset = lax.broadcasted_iota(jnp.int32, (buckets, 2 * seq_len), 1) - seq_len
    bucket = lax.broadcasted_iota(jnp.int32, (buckets, 2 * seq_len), 0)
    return bucket_of(offset) == bucket


def head_lanes(rows, width, head_width, head):
    lane = lax.broadcasted_iota(jnp.int32, (rows, width), 1)
    return (lane >= head * head_width) & (lane < (head + 1) * head_width)


def only(mask, values):
    return jnp.where(mask, values, jnp.zeros_like(values))


def block_place(block, core, near_count):
    return lax.rem(block, near_count) * CORES + lax.bitwise_xor(lax.div(block, near_count), core)


def bias_places(place_ref, step, blocks, rows, seq_len):
    core, near_count = place_ref[1], blocks // CORES
    query = block_place(step, core, near_count) * rows
    return [
        [
            pl.multiple_of(
                block_place(block, core, near_count) * rows - query - part * SKEW + seq_len - SKEW,
                SKEW,
            )
            for block in range(blocks)
        ]
        for part in range(rows // SKEW)
    ]


def forward_kernel(heads, rows, place_ref, qkv_ref, table_ref, o_ref, p_ref, skew_ref):
    step = pl.program_id(0)
    seq_len = qkv_ref.shape[0]
    width = qkv_ref.shape[1] // 3
    head_width = width // heads
    span = 2 * seq_len
    blocks = seq_len // rows

    @pl.when(step == 0)
    def _():
        one_hot = bucket_onehot(table_ref.shape[0], seq_len)
        table = table_ref[...].astype(F32)
        column = lax.broadcasted_iota(jnp.int32, table.shape, 1)
        for head in range(heads):
            here = column == place_ref[2] * heads + head
            levels = jnp.sum(jnp.where(here, table, 0.0), axis=1, keepdims=True)
            line = jnp.sum(jnp.where(one_hot, levels, 0.0), axis=0, keepdims=True)
            line = jnp.broadcast_to(line, (SKEW, span))
            skew_ref[head] = pltpu.roll(line, span - SKEW, 1, stride=1, stride_axis=0)

    row = lax.broadcasted_iota(jnp.int32, (1, rows), 1)
    allowed = jnp.concatenate(
        [
            block_place(block, place_ref[1], blocks // CORES) * rows + row < place_ref[0]
            for block in range(blocks)
        ],
        1,
    )
    queries = qkv_ref[pl.ds(pl.multiple_of(step * rows, rows), rows), :width]
    keys = qkv_ref[:, width : 2 * width]
    values = qkv_ref[:, 2 * width :]
    total = jnp.zeros((rows, width), F32)
    places = bias_places(place_ref, step, blocks, rows, seq_len)
    for head in range(heads):
        scores = lax.dot_general(
            only(head_lanes(rows, width, head_width, head), queries),
            keys,
            (((1,), (1,)), ((), ())),
            preferred_element_type=F32,
        )
        bias = jnp.concatenate(
            [
                jnp.concatenate([skew_ref[head, :, pl.ds(place, rows)] for place in part], 1)
                for part in places
            ],
            0,
        )
        scores = jnp.where(allowed, scores + bias, MASKED)
        grown = jnp.exp(scores - jnp.max(scores, axis=1, keepdims=True))
        prob = (grown * (1.0 / jnp.sum(grown, axis=1, keepdims=True))).astype(LOW)
        p_ref[head] = prob
        total = total + jnp.dot(
            prob,
            only(head_lanes(seq_len, width, head_width, head), values),
            preferred_element_type=F32,
        )
    o_ref[...] = total.astype(LOW)


def attention_forward(qkv, table, place, heads, rows):
    seq_len, width = qkv.shape[0], qkv.shape[1] // 3
    return pl.pallas_call(
        functools.partial(forward_kernel, heads, rows),
        grid=(seq_len // rows,),
        in_specs=[
            pl.BlockSpec(memory_space=pltpu.SMEM),
            pl.BlockSpec(qkv.shape, lambda i: (0, 0)),
            pl.BlockSpec(table.shape, lambda i: (0, 0)),
        ],
        out_specs=[
            pl.BlockSpec((rows, width), lambda i: (i, 0)),
            pl.BlockSpec((heads, rows, seq_len), lambda i: (0, i, 0)),
        ],
        out_shape=[
            jax.ShapeDtypeStruct((seq_len, width), LOW),
            jax.ShapeDtypeStruct((heads, seq_len, seq_len), LOW),
        ],
        scratch_shapes=[pltpu.VMEM((heads, SKEW, 2 * seq_len), F32)],
        compiler_params=pltpu.CompilerParams(vmem_limit_bytes=32 * 2**20),
        cost_estimate=pl.CostEstimate(
            flops=4 * seq_len * seq_len * width,
            bytes_accessed=2 * heads * seq_len * seq_len,
            transcendentals=0,
        ),
        name="attention_forward",
    )(place, qkv, table)


def backward_kernel(
    heads, rows, place_ref, p_ref, do_ref, qkv_ref, d_ref, dt_ref, dk_sum, dv_sum, skew_ref
):
    step = pl.program_id(0)
    seq_len = qkv_ref.shape[0]
    width = qkv_ref.shape[1] // 3
    head_width = width // heads
    span = 2 * seq_len
    blocks = seq_len // rows

    @pl.when(step == 0)
    def _():
        dk_sum[...] = jnp.zeros_like(dk_sum)
        dv_sum[...] = jnp.zeros_like(dv_sum)
        skew_ref[...] = jnp.zeros_like(skew_ref)

    here = pl.ds(pl.multiple_of(step * rows, rows), rows)
    queries = qkv_ref[here, :width]
    keys = qkv_ref[:, width : 2 * width]
    values = qkv_ref[:, 2 * width :]
    grads = do_ref[...]
    total = jnp.zeros((rows, width), F32)
    places = bias_places(place_ref, step, blocks, rows, seq_len)
    for head in range(heads):
        own = head_lanes(rows, width, head_width, head)
        own_grads = only(own, grads)
        d_prob = lax.dot_general(
            own_grads, values, (((1,), (1,)), ((), ())), preferred_element_type=F32
        )
        prob_low = p_ref[head]
        prob = prob_low.astype(F32)
        weighed = prob * d_prob
        d_scores = (weighed - prob * jnp.sum(weighed, axis=1, keepdims=True)).astype(LOW)
        total = total + jnp.dot(
            d_scores,
            only(head_lanes(seq_len, width, head_width, head), keys),
            preferred_element_type=F32,
        )
        dk_sum[...] += lax.dot_general(
            d_scores, only(own, queries), (((0,), (0,)), ((), ())), preferred_element_type=F32
        )
        dv_sum[...] += lax.dot_general(
            prob_low, own_grads, (((0,), (0,)), ((), ())), preferred_element_type=F32
        )
        for part in range(rows // SKEW):
            for block in range(blocks):
                skew_ref[head, :, pl.ds(places[part][block], rows)] += d_scores[
                    part * SKEW : (part + 1) * SKEW, block * rows : (block + 1) * rows
                ].astype(F32)
    d_ref[here, :width] = total.astype(LOW)

    @pl.when(step == pl.num_programs(0) - 1)
    def _():
        d_ref[:, width : 2 * width] = dk_sum[...].astype(LOW)
        d_ref[:, 2 * width :] = dv_sum[...].astype(LOW)
        one_hot = bucket_onehot(dt_ref.shape[0], seq_len)
        row = lax.broadcasted_iota(jnp.int32, (SKEW, span), 0)
        column = lax.broadcasted_iota(jnp.int32, dt_ref.shape, 1)
        result = jnp.zeros(dt_ref.shape, F32)
        for head in range(heads):
            level = pltpu.roll(skew_ref[head], SKEW, 1)
            bit = 1
            while bit < SKEW:
                level = jnp.where((row & bit) != 0, pltpu.roll(level, span - bit, 1), level)
                bit *= 2
            line = jnp.sum(level, axis=0, keepdims=True)
            summed = jnp.sum(jnp.where(one_hot, line, 0.0), axis=1, keepdims=True)
            result = jnp.where(column == head, summed, result)
        dt_ref[...] = result


def attention_backward(prob, d_out, qkv, place, heads, rows, buckets):
    seq_len, width = d_out.shape
    return pl.pallas_call(
        functools.partial(backward_kernel, heads, rows),
        grid=(seq_len // rows,),
        in_specs=[
            pl.BlockSpec(memory_space=pltpu.SMEM),
            pl.BlockSpec((heads, rows, seq_len), lambda i: (0, i, 0)),
            pl.BlockSpec((rows, width), lambda i: (i, 0)),
            pl.BlockSpec(qkv.shape, lambda i: (0, 0)),
        ],
        out_specs=[
            pl.BlockSpec(qkv.shape, lambda i: (0, 0)),
            pl.BlockSpec((buckets, 128), lambda i: (0, 0)),
        ],
        out_shape=[
            jax.ShapeDtypeStruct(qkv.shape, LOW),
            jax.ShapeDtypeStruct((buckets, 128), F32),
        ],
        scratch_shapes=[
            pltpu.VMEM((seq_len, width), F32),
            pltpu.VMEM((seq_len, width), F32),
            pltpu.VMEM((heads, SKEW, 2 * seq_len), F32),
        ],
        compiler_params=pltpu.CompilerParams(vmem_limit_bytes=40 * 2**20),
        cost_estimate=pl.CostEstimate(
            flops=8 * seq_len * seq_len * width * 4,
            bytes_accessed=2 * heads * seq_len * seq_len,
            transcendentals=0,
        ),
        name="attention_backward",
    )(place, prob, d_out, qkv)


EXTRA = 8
OWNER_ROWS = 64


def as_column(row, first, count):
    size = row.shape[1]
    here = lax.broadcasted_iota(jnp.int32, (count, size), 1) == first + lax.broadcasted_iota(
        jnp.int32, (count, size), 0
    )
    return jnp.sum(jnp.where(here, row, 0.0), axis=1, keepdims=True)


def blocks_kernel(seqs, members, q_ref, k_ref, v_ref, o_ref, gain_ref, table_ref, sent_ref):
    shard = q_ref.shape[0]
    width = q_ref.shape[1] // members
    gain = as_column(gain_ref[...].astype(LOW).astype(F32), 0, shard)
    parts = [
        (ref[...].astype(LOW).astype(F32) * gain).astype(LOW) for ref in (q_ref, k_ref, v_ref)
    ]
    parts.append(o_ref[...].T.astype(LOW))
    rest = jnp.zeros((EXTRA, sent_ref.shape[2]), LOW)
    table_rows, heads = table_ref.shape
    for seq in range(seqs):
        for member in range(members):
            at = seq * members + member
            for i, part in enumerate(parts):
                sent_ref[at, :shard, i * width : (i + 1) * width] = part[
                    :, member * width : (member + 1) * width
                ]
            sent_ref[at, shard:, :] = rest
            sent_ref[at, shard : shard + table_rows, :heads] = table_ref[...].astype(LOW)


def attention_blocks(weights, w_out, gain, table, seqs, members):
    shard, columns = weights[0].shape
    return pl.pallas_call(
        functools.partial(blocks_kernel, seqs, members),
        out_shape=jax.ShapeDtypeStruct(
            (seqs * members, shard + EXTRA, 4 * columns // members), LOW
        ),
        compiler_params=pltpu.CompilerParams(vmem_limit_bytes=32 * 2**20),
        cost_estimate=pl.CostEstimate(
            flops=0, bytes_accessed=16 * shard * columns, transcendentals=0
        ),
        name="attention_blocks",
    )(*weights, w_out, gain, table)


def owner_kernel(count, members, table_shape, *refs):
    got_ref, extra_ref = refs[:2]
    weight_refs = refs[2 : 2 + count]
    gain_ref = refs[2 + count]
    grad_refs = refs[3 + count : 3 + 2 * count]
    sum_ref = refs[3 + 2 * count]
    step = pl.program_id(0)
    rows = got_ref.shape[1]
    seqs = got_ref.shape[0] // members
    width = got_ref.shape[2] // count
    size = sum_ref.shape[1]
    gain = as_column(gain_ref[...].astype(LOW).astype(F32), step * rows, rows)
    total = jnp.zeros((rows, 1), F32)
    for member in range(members):
        product = sum(got_ref[seq * members + member].astype(F32) for seq in range(seqs))
        for i in range(count):
            part = product[:, i * width : (i + 1) * width]
            here = pl.ds(member * width, width)
            grad_refs[i][:, here] = part * gain
            weight = weight_refs[i][:, here].astype(LOW).astype(F32)
            total = total + jnp.sum(weight * part, axis=1, keepdims=True)

    @pl.when(step == 0)
    def _():
        sum_ref[...] = jnp.zeros_like(sum_ref)

    diagonal = lax.broadcasted_iota(jnp.int32, (rows, size), 1) == step * rows + (
        lax.broadcasted_iota(jnp.int32, (rows, size), 0)
    )
    sum_ref[...] += jnp.sum(jnp.where(diagonal, total, 0.0), axis=0, keepdims=True)
    if table_shape is not None:
        table_rows, heads = table_shape
        each = heads // members
        for member in range(members):
            piece = sum(extra_ref[seq * members + member].astype(F32) for seq in range(seqs))
            refs[-1][:, member * each : (member + 1) * each] = piece[:table_rows, :each]


def owner_grads(got, weights, gain, members, table_shape):
    sources, height, columns = got.shape
    shard, wide = weights[0].shape
    count = len(weights)
    rows = min(OWNER_ROWS, shard)
    step_rows = pl.BlockSpec((rows, wide), lambda i: (i, 0))
    row = pl.BlockSpec((1, shard), lambda i: (0, 0))
    last = height // EXTRA - 1
    out_specs = [step_rows] * count + [row]
    out_shape = [jax.ShapeDtypeStruct((shard, wide), F32)] * count
    out_shape.append(jax.ShapeDtypeStruct((1, shard), F32))
    if table_shape is not None:
        out_specs.append(pl.BlockSpec(table_shape, lambda i: (0, 0)))
        out_shape.append(jax.ShapeDtypeStruct(table_shape, F32))
    outs = pl.pallas_call(
        functools.partial(owner_kernel, count, members, table_shape),
        grid=(shard // rows,),
        in_specs=[
            pl.BlockSpec((sources, rows, columns), lambda i: (0, i, 0)),
            pl.BlockSpec((sources, EXTRA, columns), lambda i: (0, last, 0)),
        ]
        + [step_rows] * count
        + [row],
        out_specs=out_specs,
        out_shape=out_shape,
        compiler_params=pltpu.CompilerParams(vmem_limit_bytes=32 * 2**20),
        cost_estimate=pl.CostEstimate(
            flops=0, bytes_accessed=10 * count * shard * wide, transcendentals=0
        ),
        name="owner_grads",
    )(got, got, *weights, gain)
    return outs[:count], outs[count], outs[-1] if table_shape is not None else None


COLUMN = ("seq", "near", "core")


def exchange(blocks, axes):
    return lax.all_to_all(blocks, axes, split_axis=0, concat_axis=0, tiled=True)


def swap(block, axis):
    return lax.ppermute(block, axis, [(0, 1), (1, 0)])


def after(value, *done):
    return lax.optimization_barrier((value,) + done)[0]


def rows_dot(left, right):
    return jnp.dot(left, right, preferred_element_type=F32)


def contract_cols(left, right):
    return lax.dot_general(left, right, (((1,), (1,)), ((), ())), preferred_element_type=F32)


def contract_rows(left, right):
    return lax.dot_general(left, right, (((0,), (0,)), ((), ())), preferred_element_type=F32)


def rms(values):
    return lax.rsqrt(jnp.mean(values * values, axis=-1, keepdims=True) + EPSILON)


def norm_grad(inner, normed, inverse):
    return inverse * (inner - normed * jnp.mean(inner * normed, axis=-1, keepdims=True))


def gelu_tanh(values):
    return jax.nn.gelu(values, approximate=True)


def local(
    inputs,
    cotangent,
    lengths,
    attn_scale,
    w_query,
    w_key,
    w_value,
    w_out,
    rel_table,
    ffn_scale,
    w_gate,
    w_up,
    w_down,
):
    seqs = lax.axis_size("seq")
    near_count = lax.axis_size("near")
    mp_count = lax.axis_size("mp")
    members = near_count * CORES
    sources = seqs * members
    tok_rows, model = inputs.shape
    seq_len = tok_rows * members
    own_rows = tok_rows // mp_count
    half_rows = seq_len // CORES
    shard = attn_scale.shape[0]
    table_rows, heads_mp = rel_table.shape
    buckets = table_rows * sources
    heads = heads_mp // members
    width = w_query.shape[1] // members
    hidden_width = w_gate.shape[1] // members

    near_at = lax.axis_index("near")
    core_at = lax.axis_index("core")
    mp_at = lax.axis_index("mp")
    member_at = near_at * CORES + core_at
    length = lax.dynamic_slice_in_dim(lengths, lax.axis_index("seq"), 1, 0)
    place = jnp.stack([length[0], core_at.astype(jnp.int32), member_at.astype(jnp.int32)])

    def for_column(parts):
        return jnp.broadcast_to(parts[None], (seqs,) + parts.shape).reshape(
            (sources,) + parts.shape[1:]
        )

    def by_member(weight):
        return weight.reshape(weight.shape[0], members, -1)

    def scaled(weight, gain):
        low = weight.astype(LOW).astype(F32)
        return (low * gain.astype(LOW).astype(F32)[:, None]).astype(LOW)

    def over_mp(own, axis):
        shape = own.shape[:axis] + (mp_count,) + own.shape[axis:]
        blocks = lax.dynamic_update_index_in_dim(jnp.zeros(shape, own.dtype), own, mp_at, axis)
        moved = [(away, shifted(own, away)) for away in reversed(range(1, mp_count))]
        for away, block in moved:
            blocks = lax.dynamic_update_index_in_dim(blocks, block, mp_at ^ away, axis)
        return blocks

    def shifted(block, away):
        return lax.ppermute(block, "mp", [(i, i ^ away) for i in range(mp_count)])

    def in_near_order(own, moved):
        return jnp.stack(
            [jnp.where(near_at == 0, own, moved), jnp.where(near_at == 0, moved, own)], 0
        )

    def near_block_rows(block):
        own = lax.dynamic_slice_in_dim(block, mp_at * own_rows, own_rows, 0)
        moved = over_mp(swap(own, "near"), 0).reshape(tok_rows, model)
        return in_near_order(block, moved).reshape(half_rows, model)

    def gather_rows(near):
        blocks = [(0, near)] + [(away, shifted(near, away)) for away in range(1, mp_count)]
        shape = (near_count, mp_count, own_rows, model)
        mine, other = jnp.zeros(shape, near.dtype), jnp.zeros(shape, near.dtype)
        for away, block in blocks:
            at = mp_at ^ away
            mine = lax.dynamic_update_index_in_dim(mine, block, at, 1)
            other = lax.dynamic_update_index_in_dim(other, swap(block, "core"), at, 1)
        return mine.reshape(half_rows, model), other.reshape(half_rows, model)

    def sum_cores(mine, other):
        mine = mine.reshape(near_count, mp_count, own_rows, model)
        other = other.astype(LOW).reshape(near_count, mp_count, own_rows, model)
        sums = []
        for away in reversed(range(mp_count)):
            at = mp_at ^ away
            arrived = swap(lax.dynamic_index_in_dim(other, at, 1, keepdims=False), "core")
            kept = lax.dynamic_index_in_dim(mine, at, 1, keepdims=False)
            sums.append(kept.astype(F32) + arrived.astype(F32))
        return sums

    def send_mp(sums):
        last = len(sums) - 1
        moved = [shifted(rows.astype(LOW), last - i) for i, rows in enumerate(sums[:-1])]
        return moved, sums[-1]

    def sum_mp(sums):
        moved, kept = send_mp(sums)
        return sum((piece.astype(F32) for piece in moved), kept)

    def sum_near(pair):
        sent = jnp.where(near_at == 0, pair[1], pair[0]).astype(LOW)
        kept = jnp.where(near_at == 0, pair[0], pair[1])
        return kept + swap(sent, "near").astype(F32)

    def sum_near_both(pair):
        low = pair.astype(LOW)
        moved = swap(low, "near")
        return low.astype(F32) + moved.astype(F32), moved

    def near_pair(rows):
        blocks = rows.reshape(near_count, mp_count, own_rows, model)
        return lax.dynamic_index_in_dim(blocks, mp_at, 1, keepdims=False)

    def here(pair):
        return lax.dynamic_index_in_dim(pair, near_at, 0, keepdims=False)

    attn_sent = attention_blocks(
        (w_query, w_key, w_value), w_out, attn_scale.reshape(1, shard), rel_table, seqs, members
    )
    gate_up_parts = for_column(
        jnp.moveaxis(
            jnp.concatenate(
                [by_member(scaled(w_gate, ffn_scale)), by_member(scaled(w_up, ffn_scale))], 2
            ),
            1,
            0,
        )
    )
    down_parts = for_column(w_down.astype(LOW).reshape(members, hidden_width, shard))

    attn_got = exchange(attn_sent, COLUMN)
    attn_weights = attn_got[:, :shard].reshape(model, 4 * width)
    qkv_weight = attn_weights[:, : 3 * width]
    out_weight_t = attn_weights[:, 3 * width :]
    table = attn_got[:, shard : shard + table_rows, :heads_mp].reshape(buckets, heads_mp)

    mine_inputs = near_block_rows(inputs)
    mine_values = mine_inputs.astype(F32)
    mine_normed = (mine_values * rms(mine_values)).astype(LOW)
    normed_rows = jnp.concatenate([mine_normed, swap(mine_normed, "core")], 0)
    row_valid = (member_at * tok_rows + lax.iota(jnp.int32, tok_rows) < length)[:, None]
    masked = jnp.where(row_valid, cotangent, jnp.zeros_like(cotangent))
    mine_grad = near_block_rows(masked)
    other_grad = swap(mine_grad, "core")

    normed_rows = after(normed_rows, gate_up_parts, down_parts)
    down_got = exchange(after(down_parts, attn_got), COLUMN)
    down_weight = jnp.moveaxis(down_got, 0, 1).reshape(hidden_width, model)

    qkv = rows_dot(normed_rows, qkv_weight).astype(LOW)
    attended, prob = attention_forward(qkv, table, place, heads, tok_rows)
    attended = after(attended, mine_grad, other_grad)
    mixed, mixed_moved = sum_near_both(
        after(
            sum_mp(
                sum_cores(
                    contract_cols(attended[:half_rows], out_weight_t),
                    contract_cols(attended[half_rows:], out_weight_t),
                )
            ),
            down_got,
        )
    )
    gate_up_weight = exchange(after(gate_up_parts, mixed_moved), COLUMN).reshape(model, 2 * hidden_width)

    pair_inputs = near_pair(after(mine_inputs, normed_rows)).astype(F32)
    pair_cotangent = near_pair(mine_grad).astype(F32)
    after_attn = pair_inputs + mixed
    inv_two = rms(after_attn)
    normed_two = after_attn * inv_two
    halves = gather_rows(normed_two.astype(LOW))

    grads = (mine_grad, other_grad)
    ups, gelus, acts = [], [], []
    for rows in halves:
        gate_up = rows_dot(rows, gate_up_weight)
        gelus.append(jax.vjp(gelu_tanh, gate_up[:, :hidden_width]))
        ups.append(gate_up[:, hidden_width:])
        acts.append((gelus[-1][0] * ups[-1]).astype(LOW))
    d_down_w = (contract_rows(acts[0], grads[0]) + contract_rows(acts[1], grads[1])).astype(LOW)
    d_gate_ups, d_norms = [], []
    for grad, up_pre, (gelu_value, gelu_pull) in zip(grads, ups, gelus):
        d_hidden = contract_cols(after(grad, d_down_w), down_weight)
        (d_gate_pre,) = gelu_pull(d_hidden * up_pre)
        d_gate_ups.append(
            jnp.concatenate([d_gate_pre.astype(LOW), (d_hidden * gelu_value).astype(LOW)], 1)
        )
        d_norms.append(contract_cols(d_gate_ups[-1], gate_up_weight))
    inner_cores = sum_cores(*d_norms)
    d_gate_ups = [after(grad, *d_norms) for grad in d_gate_ups]

    def to_owners(grad):
        return exchange(grad, COLUMN)

    def by_rows(got):
        parts = got.reshape((seqs, members) + got.shape[1:]).astype(F32)
        return jnp.sum(parts, axis=0).reshape(-1, shard)

    d_down = to_owners(jnp.moveaxis(d_down_w.reshape(hidden_width, sources, shard), 1, 0))
    inner_two, inner_moved = sum_near_both(after(sum_mp(inner_cores), d_down))
    d_gate_up_w = (
        contract_rows(halves[0], d_gate_ups[0]) + contract_rows(halves[1], d_gate_ups[1])
    ).astype(LOW)
    d_gate_up = to_owners(after(d_gate_up_w, inner_moved).reshape(sources, shard, -1))

    pair_first = (
        lax.broadcasted_iota(jnp.int32, (near_count, own_rows, 1), 0) * (CORES * tok_rows)
        + lax.broadcasted_iota(jnp.int32, (near_count, own_rows, 1), 1)
        + (core_at * tok_rows + mp_at * own_rows)
    )
    pair_valid = pair_first < length
    grad_one = pair_cotangent + norm_grad(inner_two, normed_two, inv_two)
    mine_one, other_one = gather_rows(grad_one.astype(LOW))
    ffn_cores = sum_cores(*[rows_dot(after(act, inner_moved), down_weight) for act in acts])
    d_attended = jnp.concatenate(
        [rows_dot(mine_one, out_weight_t), rows_dot(other_one, out_weight_t)], 0
    ).astype(LOW)
    d_qkv, d_table = attention_backward(prob, d_attended, qkv, place, heads, tok_rows, buckets)
    inner_cores = sum_cores(
        contract_cols(d_qkv[:half_rows], qkv_weight), contract_cols(d_qkv[half_rows:], qkv_weight)
    )
    ffn_moved, ffn_kept = send_mp([after(rows, mine_one) for rows in ffn_cores])
    ffn_moved = [after(rows, d_qkv) for rows in ffn_moved]
    last_moved, last_kept = send_mp(inner_cores)
    inner_one = sum_near(sum((piece.astype(F32) for piece in last_moved), last_kept))
    table_sent = d_table[:, :heads].astype(LOW).reshape(sources, table_rows, heads)
    table_sent = jnp.pad(
        table_sent, ((0, 0), (0, EXTRA - table_rows), (0, 3 * width - heads))
    )
    d_qkv_w = contract_rows(normed_rows, d_qkv).astype(LOW).reshape(sources, shard, -1)
    d_qkv_sent = jnp.concatenate([d_qkv_w, table_sent], 1)
    d_qkv_got = to_owners(after(d_qkv_sent, d_gate_up, last_moved[0]))
    later_attended = after(attended, inner_cores[0])
    d_out = contract_rows(later_attended[:half_rows], mine_one) + contract_rows(
        later_attended[half_rows:], other_one
    )
    d_out = jnp.moveaxis(d_out.astype(LOW).reshape(width, sources, shard), 1, 0)
    d_out = to_owners(after(d_out, d_qkv_got))

    own_inputs = here(pair_inputs)
    normed_one = own_inputs * rms(own_inputs)
    grad_input = here(grad_one) + norm_grad(inner_one, normed_one, rms(own_inputs))
    d_inputs = over_mp(grad_input.astype(LOW), 0).reshape(tok_rows, model)
    ffn_pair = sum((piece.astype(F32) for piece in ffn_moved), ffn_kept)
    after_ffn = here(after_attn) + sum_near(after(ffn_pair, inner_one))
    own_out = jnp.where(here(pair_valid), after_ffn, 0.0).astype(LOW)
    layer_out = over_mp(after(own_out, d_qkv_got), 0).reshape(tok_rows, model)

    (d_w_gate, d_w_up), ffn_gain, _ = owner_grads(
        after(d_gate_up, inner_cores[0]), (w_gate, w_up), ffn_scale.reshape(1, shard), members, None
    )
    (d_w_query, d_w_key, d_w_value), attn_gain, d_rel_table = owner_grads(
        d_qkv_got,
        (w_query, w_key, w_value),
        attn_scale.reshape(1, shard),
        members,
        (table_rows, heads_mp),
    )
    gains = jnp.concatenate([attn_gain, ffn_gain], 0)
    gains = sum((shifted(gains, away) for away in range(1, mp_count)), gains)
    return (
        layer_out,
        d_inputs,
        gains[0],
        d_w_query,
        d_w_key,
        d_w_value,
        by_rows(d_out),
        d_rel_table,
        gains[1],
        d_w_gate,
        d_w_up,
        by_rows(after(d_down, d_qkv)),
    )


def solution(mesh):
    fsdp, mp = mesh.shape["fsdp"], mesh.shape["mp"]

    def run(*args):
        seqs = args[2].shape[0]
        members = fsdp // seqs
        inner = Mesh(
            mesh.devices.reshape(seqs, members // CORES, CORES, mp), ("seq", "near", "core", "mp")
        )
        rows, columns, first = P(COLUMN, None), P("mp", COLUMN), P(COLUMN)
        both = P(COLUMN, "mp")
        in_specs = (
            rows, rows, P(), first, both, both, both, columns, both, first, both, both, columns,
        )
        out_specs = (
            rows, rows, first, both, both, both, columns, both, first, both, both, columns,
        )
        return jax.shard_map(
            local, mesh=inner, in_specs=in_specs, out_specs=out_specs, check_vma=False
        )(*args)

    return run
```

```python
import functools

import jax
import jax.numpy as jnp
from jax import lax
from jax.experimental import pallas as pl
from jax.experimental.pallas import tpu as pltpu
from jax.sharding import Mesh, PartitionSpec as P

LOW = jnp.bfloat16
F32 = jnp.float32
CORES = 2
THRESHOLDS = (12, 16, 23, 32, 46, 64, 91)
EPSILON = 1e-06
MASKED = -1e30
SKEW = 128


def bucket_of(rel_offset):
    distance = jnp.abs(rel_offset)
    far_bucket = 8 + sum(((distance >= threshold).astype(jnp.int32) for threshold in THRESHOLDS))
    bucket_abs = jnp.where(distance < 8, distance, far_bucket)
    return bucket_abs + jnp.where(rel_offset > 0, 16, 0)


def bucket_onehot(buckets, seq_len):
    offset = lax.broadcasted_iota(jnp.int32, (buckets, 2 * seq_len), 1) - seq_len
    bucket = lax.broadcasted_iota(jnp.int32, (buckets, 2 * seq_len), 0)
    return bucket_of(offset) == bucket


def head_lanes(rows, width, head_width, head):
    lane = lax.broadcasted_iota(jnp.int32, (rows, width), 1)
    return (lane >= head * head_width) & (lane < (head + 1) * head_width)


def only(mask, values):
    return jnp.where(mask, values, jnp.zeros_like(values))


def block_place(block, core, near_count):
    return lax.rem(block, near_count) * CORES + lax.bitwise_xor(lax.div(block, near_count), core)


def bias_places(place_ref, step, blocks, rows, seq_len):
    core, near_count = place_ref[1], blocks // CORES
    query = block_place(step, core, near_count) * rows
    return [
        [
            pl.multiple_of(
                block_place(block, core, near_count) * rows - query - part * SKEW + seq_len - SKEW,
                SKEW,
            )
            for block in range(blocks)
        ]
        for part in range(rows // SKEW)
    ]


def forward_kernel(heads, rows, place_ref, qkv_ref, table_ref, o_ref, p_ref, skew_ref):
    step = pl.program_id(0)
    seq_len = qkv_ref.shape[0]
    width = qkv_ref.shape[1] // 3
    head_width = width // heads
    span = 2 * seq_len
    blocks = seq_len // rows

    @pl.when(step == 0)
    def _():
        one_hot = bucket_onehot(table_ref.shape[0], seq_len)
        table = table_ref[...].astype(F32)
        column = lax.broadcasted_iota(jnp.int32, table.shape, 1)
        for head in range(heads):
            here = column == place_ref[2] * heads + head
            levels = jnp.sum(jnp.where(here, table, 0.0), axis=1, keepdims=True)
            line = jnp.sum(jnp.where(one_hot, levels, 0.0), axis=0, keepdims=True)
            line = jnp.broadcast_to(line, (SKEW, span))
            skew_ref[head] = pltpu.roll(line, span - SKEW, 1, stride=1, stride_axis=0)

    row = lax.broadcasted_iota(jnp.int32, (1, rows), 1)
    allowed = jnp.concatenate(
        [
            block_place(block, place_ref[1], blocks // CORES) * rows + row < place_ref[0]
            for block in range(blocks)
        ],
        1,
    )
    queries = qkv_ref[pl.ds(pl.multiple_of(step * rows, rows), rows), :width]
    keys = qkv_ref[:, width : 2 * width]
    values = qkv_ref[:, 2 * width :]
    total = jnp.zeros((rows, width), F32)
    places = bias_places(place_ref, step, blocks, rows, seq_len)
    for head in range(heads):
        scores = lax.dot_general(
            only(head_lanes(rows, width, head_width, head), queries),
            keys,
            (((1,), (1,)), ((), ())),
            preferred_element_type=F32,
        )
        bias = jnp.concatenate(
            [
                jnp.concatenate([skew_ref[head, :, pl.ds(place, rows)] for place in part], 1)
                for part in places
            ],
            0,
        )
        scores = jnp.where(allowed, scores + bias, MASKED)
        grown = jnp.exp(scores - jnp.max(scores, axis=1, keepdims=True))
        prob = (grown * (1.0 / jnp.sum(grown, axis=1, keepdims=True))).astype(LOW)
        p_ref[head] = prob
        total = total + jnp.dot(
            prob,
            only(head_lanes(seq_len, width, head_width, head), values),
            preferred_element_type=F32,
        )
    o_ref[...] = total.astype(LOW)


def attention_forward(qkv, table, place, heads, rows):
    seq_len, width = qkv.shape[0], qkv.shape[1] // 3
    return pl.pallas_call(
        functools.partial(forward_kernel, heads, rows),
        grid=(seq_len // rows,),
        in_specs=[
            pl.BlockSpec(memory_space=pltpu.SMEM),
            pl.BlockSpec(qkv.shape, lambda i: (0, 0)),
            pl.BlockSpec(table.shape, lambda i: (0, 0)),
        ],
        out_specs=[
            pl.BlockSpec((rows, width), lambda i: (i, 0)),
            pl.BlockSpec((heads, rows, seq_len), lambda i: (0, i, 0)),
        ],
        out_shape=[
            jax.ShapeDtypeStruct((seq_len, width), LOW),
            jax.ShapeDtypeStruct((heads, seq_len, seq_len), LOW),
        ],
        scratch_shapes=[pltpu.VMEM((heads, SKEW, 2 * seq_len), F32)],
        compiler_params=pltpu.CompilerParams(vmem_limit_bytes=32 * 2**20),
        cost_estimate=pl.CostEstimate(
            flops=4 * seq_len * seq_len * width,
            bytes_accessed=2 * heads * seq_len * seq_len,
            transcendentals=0,
        ),
        name="attention_forward",
    )(place, qkv, table)


def backward_kernel(
    heads, rows, place_ref, p_ref, do_ref, qkv_ref, d_ref, dt_ref, dk_sum, dv_sum, skew_ref
):
    step = pl.program_id(0)
    seq_len = qkv_ref.shape[0]
    width = qkv_ref.shape[1] // 3
    head_width = width // heads
    span = 2 * seq_len
    blocks = seq_len // rows

    @pl.when(step == 0)
    def _():
        dk_sum[...] = jnp.zeros_like(dk_sum)
        dv_sum[...] = jnp.zeros_like(dv_sum)
        skew_ref[...] = jnp.zeros_like(skew_ref)

    here = pl.ds(pl.multiple_of(step * rows, rows), rows)
    queries = qkv_ref[here, :width]
    keys = qkv_ref[:, width : 2 * width]
    values = qkv_ref[:, 2 * width :]
    grads = do_ref[...]
    total = jnp.zeros((rows, width), F32)
    places = bias_places(place_ref, step, blocks, rows, seq_len)
    for head in range(heads):
        own = head_lanes(rows, width, head_width, head)
        own_grads = only(own, grads)
        d_prob = lax.dot_general(
            own_grads, values, (((1,), (1,)), ((), ())), preferred_element_type=F32
        )
        prob_low = p_ref[head]
        prob = prob_low.astype(F32)
        weighed = prob * d_prob
        d_scores = (weighed - prob * jnp.sum(weighed, axis=1, keepdims=True)).astype(LOW)
        total = total + jnp.dot(
            d_scores,
            only(head_lanes(seq_len, width, head_width, head), keys),
            preferred_element_type=F32,
        )
        dk_sum[...] += lax.dot_general(
            d_scores, only(own, queries), (((0,), (0,)), ((), ())), preferred_element_type=F32
        )
        dv_sum[...] += lax.dot_general(
            prob_low, own_grads, (((0,), (0,)), ((), ())), preferred_element_type=F32
        )
        for part in range(rows // SKEW):
            for block in range(blocks):
                skew_ref[head, :, pl.ds(places[part][block], rows)] += d_scores[
                    part * SKEW : (part + 1) * SKEW, block * rows : (block + 1) * rows
                ].astype(F32)
    d_ref[here, :width] = total.astype(LOW)

    @pl.when(step == pl.num_programs(0) - 1)
    def _():
        d_ref[:, width : 2 * width] = dk_sum[...].astype(LOW)
        d_ref[:, 2 * width :] = dv_sum[...].astype(LOW)
        one_hot = bucket_onehot(dt_ref.shape[0], seq_len)
        row = lax.broadcasted_iota(jnp.int32, (SKEW, span), 0)
        column = lax.broadcasted_iota(jnp.int32, dt_ref.shape, 1)
        result = jnp.zeros(dt_ref.shape, F32)
        for head in range(heads):
            level = pltpu.roll(skew_ref[head], SKEW, 1)
            bit = 1
            while bit < SKEW:
                level = jnp.where((row & bit) != 0, pltpu.roll(level, span - bit, 1), level)
                bit *= 2
            line = jnp.sum(level, axis=0, keepdims=True)
            summed = jnp.sum(jnp.where(one_hot, line, 0.0), axis=1, keepdims=True)
            result = jnp.where(column == head, summed, result)
        dt_ref[...] = result


def attention_backward(prob, d_out, qkv, place, heads, rows, buckets):
    seq_len, width = d_out.shape
    return pl.pallas_call(
        functools.partial(backward_kernel, heads, rows),
        grid=(seq_len // rows,),
        in_specs=[
            pl.BlockSpec(memory_space=pltpu.SMEM),
            pl.BlockSpec((heads, rows, seq_len), lambda i: (0, i, 0)),
            pl.BlockSpec((rows, width), lambda i: (i, 0)),
            pl.BlockSpec(qkv.shape, lambda i: (0, 0)),
        ],
        out_specs=[
            pl.BlockSpec(qkv.shape, lambda i: (0, 0)),
            pl.BlockSpec((buckets, 128), lambda i: (0, 0)),
        ],
        out_shape=[
            jax.ShapeDtypeStruct(qkv.shape, LOW),
            jax.ShapeDtypeStruct((buckets, 128), F32),
        ],
        scratch_shapes=[
            pltpu.VMEM((seq_len, width), F32),
            pltpu.VMEM((seq_len, width), F32),
            pltpu.VMEM((heads, SKEW, 2 * seq_len), F32),
        ],
        compiler_params=pltpu.CompilerParams(vmem_limit_bytes=40 * 2**20),
        cost_estimate=pl.CostEstimate(
            flops=8 * seq_len * seq_len * width * 4,
            bytes_accessed=2 * heads * seq_len * seq_len,
            transcendentals=0,
        ),
        name="attention_backward",
    )(place, prob, d_out, qkv)


EXTRA = 8
OWNER_ROWS = 64


def as_column(row, first, count):
    size = row.shape[1]
    here = lax.broadcasted_iota(jnp.int32, (count, size), 1) == first + lax.broadcasted_iota(
        jnp.int32, (count, size), 0
    )
    return jnp.sum(jnp.where(here, row, 0.0), axis=1, keepdims=True)


def blocks_kernel(seqs, members, q_ref, k_ref, v_ref, o_ref, gain_ref, table_ref, sent_ref):
    shard = q_ref.shape[0]
    width = q_ref.shape[1] // members
    gain = as_column(gain_ref[...].astype(LOW).astype(F32), 0, shard)
    parts = [
        (ref[...].astype(LOW).astype(F32) * gain).astype(LOW) for ref in (q_ref, k_ref, v_ref)
    ]
    parts.append(o_ref[...].T.astype(LOW))
    rest = jnp.zeros((EXTRA, sent_ref.shape[2]), LOW)
    table_rows, heads = table_ref.shape
    for seq in range(seqs):
        for member in range(members):
            at = seq * members + member
            for i, part in enumerate(parts):
                sent_ref[at, :shard, i * width : (i + 1) * width] = part[
                    :, member * width : (member + 1) * width
                ]
            sent_ref[at, shard:, :] = rest
            sent_ref[at, shard : shard + table_rows, :heads] = table_ref[...].astype(LOW)


def attention_blocks(weights, w_out, gain, table, seqs, members):
    shard, columns = weights[0].shape
    return pl.pallas_call(
        functools.partial(blocks_kernel, seqs, members),
        out_shape=jax.ShapeDtypeStruct(
            (seqs * members, shard + EXTRA, 4 * columns // members), LOW
        ),
        compiler_params=pltpu.CompilerParams(vmem_limit_bytes=32 * 2**20),
        cost_estimate=pl.CostEstimate(
            flops=0, bytes_accessed=16 * shard * columns, transcendentals=0
        ),
        name="attention_blocks",
    )(*weights, w_out, gain, table)


def owner_kernel(count, members, table_shape, *refs):
    got_ref, extra_ref = refs[:2]
    weight_refs = refs[2 : 2 + count]
    gain_ref = refs[2 + count]
    grad_refs = refs[3 + count : 3 + 2 * count]
    sum_ref = refs[3 + 2 * count]
    step = pl.program_id(0)
    rows = got_ref.shape[1]
    seqs = got_ref.shape[0] // members
    width = got_ref.shape[2] // count
    size = sum_ref.shape[1]
    gain = as_column(gain_ref[...].astype(LOW).astype(F32), step * rows, rows)
    total = jnp.zeros((rows, 1), F32)
    for member in range(members):
        product = sum(got_ref[seq * members + member].astype(F32) for seq in range(seqs))
        for i in range(count):
            part = product[:, i * width : (i + 1) * width]
            here = pl.ds(member * width, width)
            grad_refs[i][:, here] = part * gain
            weight = weight_refs[i][:, here].astype(LOW).astype(F32)
            total = total + jnp.sum(weight * part, axis=1, keepdims=True)

    @pl.when(step == 0)
    def _():
        sum_ref[...] = jnp.zeros_like(sum_ref)

    diagonal = lax.broadcasted_iota(jnp.int32, (rows, size), 1) == step * rows + (
        lax.broadcasted_iota(jnp.int32, (rows, size), 0)
    )
    sum_ref[...] += jnp.sum(jnp.where(diagonal, total, 0.0), axis=0, keepdims=True)
    if table_shape is not None:
        table_rows, heads = table_shape
        each = heads // members
        for member in range(members):
            piece = sum(extra_ref[seq * members + member].astype(F32) for seq in range(seqs))
            refs[-1][:, member * each : (member + 1) * each] = piece[:table_rows, :each]


def owner_grads(got, weights, gain, members, table_shape):
    sources, height, columns = got.shape
    shard, wide = weights[0].shape
    count = len(weights)
    rows = min(OWNER_ROWS, shard)
    step_rows = pl.BlockSpec((rows, wide), lambda i: (i, 0))
    row = pl.BlockSpec((1, shard), lambda i: (0, 0))
    last = height // EXTRA - 1
    out_specs = [step_rows] * count + [row]
    out_shape = [jax.ShapeDtypeStruct((shard, wide), F32)] * count
    out_shape.append(jax.ShapeDtypeStruct((1, shard), F32))
    if table_shape is not None:
        out_specs.append(pl.BlockSpec(table_shape, lambda i: (0, 0)))
        out_shape.append(jax.ShapeDtypeStruct(table_shape, F32))
    outs = pl.pallas_call(
        functools.partial(owner_kernel, count, members, table_shape),
        grid=(shard // rows,),
        in_specs=[
            pl.BlockSpec((sources, rows, columns), lambda i: (0, i, 0)),
            pl.BlockSpec((sources, EXTRA, columns), lambda i: (0, last, 0)),
        ]
        + [step_rows] * count
        + [row],
        out_specs=out_specs,
        out_shape=out_shape,
        compiler_params=pltpu.CompilerParams(vmem_limit_bytes=32 * 2**20),
        cost_estimate=pl.CostEstimate(
            flops=0, bytes_accessed=10 * count * shard * wide, transcendentals=0
        ),
        name="owner_grads",
    )(got, got, *weights, gain)
    return outs[:count], outs[count], outs[-1] if table_shape is not None else None


def rows_dot(left, right):
    return jnp.dot(left, right, preferred_element_type=F32)


def contract_cols(left, right):
    return lax.dot_general(left, right, (((1,), (1,)), ((), ())), preferred_element_type=F32)


def contract_rows(left, right):
    return lax.dot_general(left, right, (((0,), (0,)), ((), ())), preferred_element_type=F32)

def row_block(step, near_count):
    return lax.rem(step + near_count, CORES * near_count)


def send_rows(step, near_count, mp_at, held_ref, other_refs, mine_refs):
    count = len(other_refs)
    own_rows = held_ref.shape[0] // count

    def write(refs):
        for away, ref in enumerate(refs):
            first = pl.multiple_of(lax.bitwise_xor(mp_at, away) * own_rows, own_rows)
            ref[0] = held_ref[pl.ds(first, own_rows), :]

    @pl.when(step < near_count)
    def _():
        write(other_refs)

    @pl.when(step >= near_count)
    def _():
        write(mine_refs)


def sent_specs(near_count, count, own_rows, model):
    other = pl.BlockSpec((1, own_rows, model), lambda i: (jnp.minimum(i, near_count - 1), 0, 0))
    mine = pl.BlockSpec((1, own_rows, model), lambda i: (jnp.maximum(i - near_count, 0), 0, 0))
    shape = jax.ShapeDtypeStruct((near_count, own_rows, model), LOW)
    return [other] * count + [mine] * count, [shape] * (2 * count)


def partial_kernel(near_count, count, product, place_ref, left_ref, weight_ref, *refs):
    held_ref = refs[-1]
    product(left_ref, weight_ref, held_ref)
    send_rows(
        pl.program_id(0), near_count, place_ref[3], held_ref, refs[:count], refs[count : 2 * count]
    )


def partial_rows(left, weight, model, place, near_count, count, product, name):
    seq_len, depth = left.shape
    rows = seq_len // (CORES * near_count)
    out_specs, out_shape = sent_specs(near_count, count, rows // count, model)
    outs = pl.pallas_call(
        functools.partial(partial_kernel, near_count, count, product),
        grid=(CORES * near_count,),
        in_specs=[
            pl.BlockSpec(memory_space=pltpu.SMEM),
            pl.BlockSpec((rows, depth), lambda i: (row_block(i, near_count), 0)),
            pl.BlockSpec(weight.shape, lambda i: (0, 0, 0)),
        ],
        out_specs=out_specs,
        out_shape=out_shape,
        scratch_shapes=[pltpu.VMEM((rows, model), LOW)],
        compiler_params=pltpu.CompilerParams(vmem_limit_bytes=40 * 2**20),
        cost_estimate=pl.CostEstimate(
            flops=2 * seq_len * depth * model, bytes_accessed=2 * seq_len * model, transcendentals=0
        ),
        name=name,
    )(place, left, weight)
    return outs[count:], outs[:count]


def column_product(shard, first, last, left_ref, weight_ref, held_ref):
    weight = weight_ref[:, :shard, first:last]
    weight = weight.reshape(weight.shape[0] * shard, last - first)
    held_ref[...] = contract_cols(left_ref[...], weight).astype(LOW)


def row_product(height, left_ref, weight_ref, held_ref):
    left = left_ref[...]
    width = weight_ref.shape[2]
    for at in range(weight_ref.shape[0]):
        held_ref[:, at * width : (at + 1) * width] = rows_dot(
            left, weight_ref[at, :height, :]
        ).astype(LOW)


def ffn_blocks_kernel(seqs, members, gate_ref, up_ref, down_ref, gain_ref, first_ref, second_ref):
    shard = gate_ref.shape[0]
    width = gate_ref.shape[1] // members
    gain = as_column(gain_ref[...].astype(LOW).astype(F32), 0, shard)
    for member in range(members):
        here = slice(member * width, (member + 1) * width)
        parts = [
            (ref[:, here].astype(LOW).astype(F32) * gain).astype(LOW) for ref in (gate_ref, up_ref)
        ]
        both = jnp.concatenate(parts, 1)
        down = down_ref[here, :].astype(LOW)
        for seq in range(seqs):
            at = seq * members + member
            first_ref[at, :width, :] = down
            first_ref[at, width:, :] = both[:, :shard]
            second_ref[at] = both[:, shard:]


def ffn_blocks(w_gate, w_up, w_down, gain, seqs, members):
    shard, columns = w_gate.shape
    width = columns // members
    return pl.pallas_call(
        functools.partial(ffn_blocks_kernel, seqs, members),
        out_shape=[
            jax.ShapeDtypeStruct((seqs * members, width + shard, shard), LOW),
            jax.ShapeDtypeStruct((seqs * members, shard, 2 * width - shard), LOW),
        ],
        compiler_params=pltpu.CompilerParams(vmem_limit_bytes=40 * 2**20),
        cost_estimate=pl.CostEstimate(
            flops=0, bytes_accessed=18 * shard * columns, transcendentals=0
        ),
        name="ffn_blocks",
    )(w_gate, w_up, w_down, gain)


def ffn_kernel(
    near_count, count, place_ref, rows_ref, grad_ref, first_ref, second_ref, *refs
):
    other_refs, mine_refs = refs[:count], refs[count : 2 * count]
    act_ref, d_ref, down_ref, held_ref, sum_ref = refs[2 * count :]
    step = pl.program_id(0)
    sources, height, shard = first_ref.shape
    width = height - shard
    rows = rows_ref[...]
    grads = grad_ref[...]
    early = first_ref[:, width:, :].reshape(sources * shard, shard)
    late = second_ref[...].reshape(sources * shard, 2 * width - shard)
    both = jnp.concatenate([rows_dot(rows, early), rows_dot(rows, late)], 1)
    gate, up = both[:, :width], both[:, width:]
    scale, cubic = 0.7978845608028654, 0.044715
    square = gate * gate
    bent = jnp.tanh(scale * (gate + cubic * square * gate))
    half = 0.5 * (1.0 + bent)
    value = gate * half
    slope = half + 0.5 * gate * (1.0 - bent * bent) * (scale * (1.0 + 3.0 * cubic * square))
    act = (value * up).astype(LOW)
    act_ref[...] = act
    d_hidden = jnp.zeros((rows.shape[0], width), F32)
    for at in range(sources):
        d_hidden = d_hidden + contract_cols(
            grads[:, at * shard : (at + 1) * shard], first_ref[at, :width, :]
        )
    d_both = jnp.concatenate(
        [(d_hidden * up * slope).astype(LOW), (d_hidden * value).astype(LOW)], 1
    )
    d_ref[...] = d_both
    held_ref[...] = (
        contract_cols(d_both[:, :shard], early) + contract_cols(d_both[:, shard:], late)
    ).astype(LOW)
    send_rows(step, near_count, place_ref[3], held_ref, other_refs, mine_refs)
    product = contract_rows(act, grads)

    @pl.when(step == 0)
    def _():
        sum_ref[...] = product

    @pl.when(step > 0)
    def _():
        sum_ref[...] += product

    @pl.when(step == pl.num_programs(0) - 1)
    def _():
        for at in range(sources):
            down_ref[at] = sum_ref[:, at * shard : (at + 1) * shard].astype(LOW)


def feed_forward(rows_all, grads, first, second, place, near_count, count):
    seq_len, model = rows_all.shape
    sources, height, shard = first.shape
    width = height - shard
    rows = seq_len // (CORES * near_count)
    out_specs, out_shape = sent_specs(near_count, count, rows // count, model)

    def blocks(columns):
        return pl.BlockSpec((rows, columns), lambda i: (row_block(i, near_count), 0))

    outs = pl.pallas_call(
        functools.partial(ffn_kernel, near_count, count),
        grid=(CORES * near_count,),
        in_specs=[
            pl.BlockSpec(memory_space=pltpu.SMEM),
            blocks(model),
            blocks(model),
            pl.BlockSpec(first.shape, lambda i: (0, 0, 0)),
            pl.BlockSpec(second.shape, lambda i: (0, 0, 0)),
        ],
        out_specs=out_specs
        + [
            blocks(width),
            blocks(2 * width),
            pl.BlockSpec((sources, width, shard), lambda i: (0, 0, 0)),
        ],
        out_shape=out_shape
        + [
            jax.ShapeDtypeStruct((seq_len, width), LOW),
            jax.ShapeDtypeStruct((seq_len, 2 * width), LOW),
            jax.ShapeDtypeStruct((sources, width, shard), LOW),
        ],
        scratch_shapes=[pltpu.VMEM((rows, model), LOW), pltpu.VMEM((width, model), F32)],
        compiler_params=pltpu.CompilerParams(vmem_limit_bytes=52 * 2**20),
        cost_estimate=pl.CostEstimate(
            flops=12 * seq_len * model * width, bytes_accessed=12 * seq_len * model, transcendentals=0
        ),
        name="feed_forward",
    )(place, rows_all, grads, first, second)
    return outs[count : 2 * count], outs[:count], *outs[2 * count :]


COLUMN = ("seq", "near", "core")


def exchange(blocks, axes):
    return lax.all_to_all(blocks, axes, split_axis=0, concat_axis=0, tiled=True)


def swap(block, axis):
    return lax.ppermute(block, axis, [(0, 1), (1, 0)])


def after(value, *done):
    return lax.optimization_barrier((value,) + done)[0]


def rms(values):
    return lax.rsqrt(jnp.mean(values * values, axis=-1, keepdims=True) + EPSILON)


def norm_grad(inner, normed, inverse):
    return inverse * (inner - normed * jnp.mean(inner * normed, axis=-1, keepdims=True))


def local(
    inputs,
    cotangent,
    lengths,
    attn_scale,
    w_query,
    w_key,
    w_value,
    w_out,
    rel_table,
    ffn_scale,
    w_gate,
    w_up,
    w_down,
):
    seqs = lax.axis_size("seq")
    near_count = lax.axis_size("near")
    mp_count = lax.axis_size("mp")
    members = near_count * CORES
    sources = seqs * members
    tok_rows, model = inputs.shape
    seq_len = tok_rows * members
    own_rows = tok_rows // mp_count
    half_rows = seq_len // CORES
    shard = attn_scale.shape[0]
    table_rows, heads_mp = rel_table.shape
    buckets = table_rows * sources
    heads = heads_mp // members
    width = w_query.shape[1] // members
    hidden_width = w_gate.shape[1] // members

    near_at = lax.axis_index("near")
    core_at = lax.axis_index("core")
    mp_at = lax.axis_index("mp")
    member_at = near_at * CORES + core_at
    length = lax.dynamic_slice_in_dim(lengths, lax.axis_index("seq"), 1, 0)
    place = jnp.stack(
        [length[0]] + [at.astype(jnp.int32) for at in (core_at, member_at, mp_at)]
    )

    def over_mp(own, axis):
        shape = own.shape[:axis] + (mp_count,) + own.shape[axis:]
        blocks = lax.dynamic_update_index_in_dim(jnp.zeros(shape, own.dtype), own, mp_at, axis)
        moved = [(away, shifted(own, away)) for away in reversed(range(1, mp_count))]
        for away, block in moved:
            blocks = lax.dynamic_update_index_in_dim(blocks, block, mp_at ^ away, axis)
        return blocks

    def shifted(block, away):
        return lax.ppermute(block, "mp", [(i, i ^ away) for i in range(mp_count)])

    def in_near_order(own, moved):
        return jnp.stack(
            [jnp.where(near_at == 0, own, moved), jnp.where(near_at == 0, moved, own)], 0
        )

    def near_block_rows(block):
        own = lax.dynamic_slice_in_dim(block, mp_at * own_rows, own_rows, 0)
        moved = over_mp(swap(own, "near"), 0).reshape(tok_rows, model)
        return in_near_order(block, moved).reshape(half_rows, model)

    def gather_rows(near):
        blocks = [(0, near)] + [(away, shifted(near, away)) for away in range(1, mp_count)]
        rows = jnp.zeros((CORES, near_count, mp_count, own_rows, model), near.dtype)
        for away, block in blocks:
            for other, part in enumerate((block, swap(block, "core"))):
                rows = lax.dynamic_update_slice(
                    rows, part[None, :, None], (other, 0, mp_at ^ away, 0, 0)
                )
        return rows.reshape(seq_len, model), [block for _, block in blocks[1:]]

    def sum_cores(mine, other):
        return [
            kept.astype(F32) + swap(sent, "core").astype(F32) for kept, sent in zip(mine, other)
        ]

    def send_mp(sums):
        moved = [shifted(sums[away].astype(LOW), away) for away in reversed(range(1, mp_count))]
        return moved, sums[0]

    def sum_mp(sums):
        moved, kept = send_mp(sums)
        return sum((piece.astype(F32) for piece in moved), kept)

    def sum_near(pair):
        sent = jnp.where(near_at == 0, pair[1], pair[0]).astype(LOW)
        kept = jnp.where(near_at == 0, pair[0], pair[1])
        return kept + swap(sent, "near").astype(F32)

    def sum_near_both(pair):
        low = pair.astype(LOW)
        moved = swap(low, "near")
        return low.astype(F32) + moved.astype(F32), moved

    def near_pair(rows):
        blocks = rows.reshape(near_count, mp_count, own_rows, model)
        return lax.dynamic_index_in_dim(blocks, mp_at, 1, keepdims=False)

    def here(pair):
        return lax.dynamic_index_in_dim(pair, near_at, 0, keepdims=False)

    attn_sent = attention_blocks(
        (w_query, w_key, w_value), w_out, attn_scale.reshape(1, shard), rel_table, seqs, members
    )
    ffn_first, ffn_second = ffn_blocks(
        w_gate, w_up, w_down, ffn_scale.reshape(1, shard), seqs, members
    )

    attn_got = exchange(attn_sent, COLUMN)
    attn_weights = attn_got[:, :shard].reshape(model, 4 * width)
    qkv_weight = attn_weights[:, : 3 * width]
    out_weight_t = attn_weights[:, 3 * width :]

    def partial(left, weight, product, name):
        return partial_rows(left, weight, model, place, near_count, mp_count, product, name)

    table = attn_got[:, shard : shard + table_rows, :heads_mp].reshape(buckets, heads_mp)

    mine_inputs = near_block_rows(inputs)
    mine_values = mine_inputs.astype(F32)
    mine_normed = (mine_values * rms(mine_values)).astype(LOW)
    normed_rows = jnp.concatenate([mine_normed, swap(mine_normed, "core")], 0)
    row_valid = (member_at * tok_rows + lax.iota(jnp.int32, tok_rows) < length)[:, None]
    masked = jnp.where(row_valid, cotangent, jnp.zeros_like(cotangent))
    mine_grad = near_block_rows(masked)
    grad_two = jnp.concatenate([mine_grad, swap(mine_grad, "core")], 0)

    normed_rows = after(normed_rows, ffn_first, ffn_second)
    first_got = exchange(after(ffn_first, attn_got), COLUMN)

    qkv = rows_dot(normed_rows, qkv_weight).astype(LOW)
    attended, prob = attention_forward(qkv, table, place, heads, tok_rows)
    attended = after(attended, mine_grad)
    out_product = functools.partial(column_product, shard, 3 * width, 4 * width)
    mixed, mixed_moved = sum_near_both(
        after(
            sum_mp(sum_cores(*partial(attended, attn_got, out_product, "attention_out"))), first_got
        )
    )
    second_got = exchange(after(ffn_second, mixed_moved), COLUMN)

    pair_inputs = near_pair(after(mine_inputs, normed_rows)).astype(F32)
    pair_cotangent = near_pair(mine_grad).astype(F32)
    after_attn = pair_inputs + mixed
    inv_two = rms(after_attn)
    normed_two = after_attn * inv_two
    hidden_two, _ = gather_rows(normed_two.astype(LOW))

    d_mine, d_other, acts, d_both, d_down_w = feed_forward(
        hidden_two, grad_two, first_got, second_got, place, near_count, mp_count
    )
    inner_cores = sum_cores(d_mine, d_other)

    def to_owners(grad):
        return exchange(grad, COLUMN)

    def by_rows(got):
        parts = got.reshape((seqs, members) + got.shape[1:]).astype(F32)
        return jnp.sum(parts, axis=0).reshape(-1, shard)

    d_down = to_owners(d_down_w)
    inner_two, inner_moved = sum_near_both(after(sum_mp(inner_cores), d_down))
    d_gate_up_w = contract_rows(hidden_two, after(d_both, *inner_cores)).astype(LOW)
    d_gate_up = to_owners(after(d_gate_up_w, inner_moved).reshape(sources, shard, -1))

    pair_first = (
        lax.broadcasted_iota(jnp.int32, (near_count, own_rows, 1), 0) * (CORES * tok_rows)
        + lax.broadcasted_iota(jnp.int32, (near_count, own_rows, 1), 1)
        + (core_at * tok_rows + mp_at * own_rows)
    )
    pair_valid = pair_first < length
    grad_one = pair_cotangent + norm_grad(inner_two, normed_two, inv_two)
    rows_one, came_one = gather_rows(grad_one.astype(LOW))
    down_product = functools.partial(row_product, hidden_width)
    ffn_cores = sum_cores(*partial(after(acts, inner_moved), first_got, down_product, "ffn_out"))
    d_attended = rows_dot(rows_one, out_weight_t).astype(LOW)
    d_qkv, d_table = attention_backward(prob, d_attended, qkv, place, heads, tok_rows, buckets)
    qkv_product = functools.partial(column_product, shard, 0, 3 * width)
    ffn_moved, ffn_kept = send_mp([after(rows, *came_one) for rows in ffn_cores])
    inner_cores = sum_cores(
        *partial(after(d_qkv, *ffn_moved), attn_got, qkv_product, "attention_in")
    )
    last_moved, last_kept = send_mp(inner_cores)
    inner_one = sum_near(sum((piece.astype(F32) for piece in last_moved), last_kept))
    table_sent = d_table[:, :heads].astype(LOW).reshape(sources, table_rows, heads)
    table_sent = jnp.pad(
        table_sent, ((0, 0), (0, EXTRA - table_rows), (0, 3 * width - heads))
    )
    d_qkv_w = contract_rows(normed_rows, d_qkv).astype(LOW).reshape(sources, shard, -1)
    d_qkv_sent = jnp.concatenate([d_qkv_w, table_sent], 1)
    d_qkv_got = to_owners(after(d_qkv_sent, d_gate_up, last_moved[0]))
    d_out = contract_rows(after(attended, inner_cores[0]), rows_one)
    d_out = jnp.moveaxis(d_out.astype(LOW).reshape(width, sources, shard), 1, 0)
    d_out = to_owners(after(d_out, d_qkv_got))

    own_inputs = here(pair_inputs)
    normed_one = own_inputs * rms(own_inputs)
    grad_input = here(grad_one) + norm_grad(inner_one, normed_one, rms(own_inputs))
    d_inputs = over_mp(grad_input.astype(LOW), 0).reshape(tok_rows, model)
    ffn_pair = sum((piece.astype(F32) for piece in ffn_moved), ffn_kept)
    after_ffn = here(after_attn) + sum_near(after(ffn_pair, d_qkv_got))
    own_out = jnp.where(here(pair_valid), after_ffn, 0.0).astype(LOW)
    layer_out = over_mp(own_out, 0).reshape(tok_rows, model)

    (d_w_gate, d_w_up), ffn_gain, _ = owner_grads(
        after(d_gate_up, inner_cores[0]), (w_gate, w_up), ffn_scale.reshape(1, shard), members, None
    )
    (d_w_query, d_w_key, d_w_value), attn_gain, d_rel_table = owner_grads(
        d_qkv_got,
        (w_query, w_key, w_value),
        attn_scale.reshape(1, shard),
        members,
        (table_rows, heads_mp),
    )
    gains = jnp.concatenate([attn_gain, ffn_gain], 0)
    gains = sum((shifted(gains, away) for away in range(1, mp_count)), gains)
    return (
        layer_out,
        d_inputs,
        gains[0],
        d_w_query,
        d_w_key,
        d_w_value,
        by_rows(d_out),
        d_rel_table,
        gains[1],
        d_w_gate,
        d_w_up,
        by_rows(after(d_down, d_qkv)),
    )


def solution(mesh):
    fsdp, mp = mesh.shape["fsdp"], mesh.shape["mp"]

    def run(*args):
        seqs = args[2].shape[0]
        members = fsdp // seqs
        inner = Mesh(
            mesh.devices.reshape(seqs, members // CORES, CORES, mp), ("seq", "near", "core", "mp")
        )
        rows, columns, first = P(COLUMN, None), P("mp", COLUMN), P(COLUMN)
        both = P(COLUMN, "mp")
        in_specs = (
            rows, rows, P(), first, both, both, both, columns, both, first, both, both, columns,
        )
        out_specs = (
            rows, rows, first, both, both, both, columns, both, first, both, both, columns,
        )
        return jax.shard_map(
            local, mesh=inner, in_specs=in_specs, out_specs=out_specs, check_vma=False
        )(*args)

    return run
```

```python
import functools

import jax
import jax.numpy as jnp
from jax import lax
from jax.experimental import pallas as pl
from jax.experimental.pallas import tpu as pltpu
from jax.sharding import Mesh, PartitionSpec as P

LOW = jnp.bfloat16
F32 = jnp.float32
CORES = 2
THRESHOLDS = (12, 16, 23, 32, 46, 64, 91)
EPSILON = 1e-06
MASKED = -1e30
SKEW = 128


def bucket_of(rel_offset):
    distance = jnp.abs(rel_offset)
    far_bucket = 8 + sum(((distance >= threshold).astype(jnp.int32) for threshold in THRESHOLDS))
    bucket_abs = jnp.where(distance < 8, distance, far_bucket)
    return bucket_abs + jnp.where(rel_offset > 0, 16, 0)


def bucket_onehot(buckets, seq_len):
    offset = lax.broadcasted_iota(jnp.int32, (buckets, 2 * seq_len), 1) - seq_len
    bucket = lax.broadcasted_iota(jnp.int32, (buckets, 2 * seq_len), 0)
    return bucket_of(offset) == bucket


def head_lanes(rows, width, head_width, head):
    lane = lax.broadcasted_iota(jnp.int32, (rows, width), 1)
    return (lane >= head * head_width) & (lane < (head + 1) * head_width)


def only(mask, values):
    return jnp.where(mask, values, jnp.zeros_like(values))


def block_place(block, core, near_count):
    return lax.rem(block, near_count) * CORES + lax.bitwise_xor(lax.div(block, near_count), core)


def bias_places(place_ref, step, blocks, rows, seq_len):
    core, near_count = place_ref[1], blocks // CORES
    query = block_place(step, core, near_count) * rows
    return [
        [
            pl.multiple_of(
                block_place(block, core, near_count) * rows - query - part * SKEW + seq_len - SKEW,
                SKEW,
            )
            for block in range(blocks)
        ]
        for part in range(rows // SKEW)
    ]


def forward_kernel(heads, shard, near_count, count, place_ref, *refs):
    own_ref, moved_ref, core_ref, core_moved_ref, got_ref, table_ref = refs[:6]
    qkv_ref, o_ref, p_ref = refs[6:9]
    other_refs, mine_refs = refs[9 : 9 + count], refs[9 + count : 9 + 2 * count]
    skew_ref, held_ref = refs[9 + 2 * count :]
    step = pl.program_id(0)
    seq_len = qkv_ref.shape[0]
    rows, width = o_ref.shape
    model = held_ref.shape[1]
    head_width = width // heads
    span = 2 * seq_len
    blocks = seq_len // rows
    block = row_block(step, near_count)

    @pl.when(step == 0)
    def _():
        weight = got_ref[:, :shard, : 3 * width].reshape(model, 3 * width)
        near = place_ref[4]
        for at, ref in enumerate((own_ref, moved_ref, core_ref, core_moved_ref)):
            first = (at // 2) * near_count + lax.bitwise_xor(near, at % 2)
            qkv_ref[pl.ds(pl.multiple_of(first * rows, rows), rows), :] = rows_dot(
                ref[...], weight
            ).astype(LOW)
        one_hot = bucket_onehot(table_ref.shape[0], seq_len)
        table = table_ref[...].astype(F32)
        column = lax.broadcasted_iota(jnp.int32, table.shape, 1)
        for head in range(heads):
            here = column == place_ref[2] * heads + head
            levels = jnp.sum(jnp.where(here, table, 0.0), axis=1, keepdims=True)
            line = jnp.sum(jnp.where(one_hot, levels, 0.0), axis=0, keepdims=True)
            line = jnp.broadcast_to(line, (SKEW, span))
            skew_ref[head] = pltpu.roll(line, span - SKEW, 1, stride=1, stride_axis=0)

    row = lax.broadcasted_iota(jnp.int32, (1, rows), 1)
    allowed = jnp.concatenate(
        [
            block_place(at, place_ref[1], near_count) * rows + row < place_ref[0]
            for at in range(blocks)
        ],
        1,
    )
    queries = qkv_ref[pl.ds(pl.multiple_of(block * rows, rows), rows), :width]
    keys = qkv_ref[:, width : 2 * width]
    values = qkv_ref[:, 2 * width :]
    total = jnp.zeros((rows, width), F32)
    places = bias_places(place_ref, block, blocks, rows, seq_len)
    for head in range(heads):
        scores = lax.dot_general(
            only(head_lanes(rows, width, head_width, head), queries),
            keys,
            (((1,), (1,)), ((), ())),
            preferred_element_type=F32,
        )
        bias = jnp.concatenate(
            [
                jnp.concatenate([skew_ref[head, :, pl.ds(place, rows)] for place in part], 1)
                for part in places
            ],
            0,
        )
        scores = jnp.where(allowed, scores + bias, MASKED)
        grown = jnp.exp(scores - jnp.max(scores, axis=1, keepdims=True))
        prob = (grown * (1.0 / jnp.sum(grown, axis=1, keepdims=True))).astype(LOW)
        p_ref[head] = prob
        total = total + jnp.dot(
            prob,
            only(head_lanes(seq_len, width, head_width, head), values),
            preferred_element_type=F32,
        )
    attended = total.astype(LOW)
    o_ref[...] = attended
    weight = got_ref[:, :shard, 3 * width :].reshape(model, width)
    held_ref[...] = contract_cols(attended, weight).astype(LOW)
    send_rows(step, near_count, place_ref[3], held_ref, other_refs, mine_refs)


def attention_forward(parts, got, table, place, heads, shard, count):
    rows, model = parts[0].shape
    blocks = len(parts)
    near_count = blocks // CORES
    seq_len, width = rows * blocks, got.shape[2] // 4
    out_specs, out_shape = sent_specs(near_count, count, rows // count, model)

    def fixed(shape):
        return pl.BlockSpec(shape, lambda i: (0,) * len(shape))

    outs = pl.pallas_call(
        functools.partial(forward_kernel, heads, shard, near_count, count),
        grid=(blocks,),
        in_specs=[pl.BlockSpec(memory_space=pltpu.SMEM)]
        + [fixed(part.shape) for part in parts]
        + [fixed(got.shape), fixed(table.shape)],
        out_specs=[
            fixed((seq_len, 3 * width)),
            pl.BlockSpec((rows, width), lambda i: (row_block(i, near_count), 0)),
            pl.BlockSpec((heads, rows, seq_len), lambda i: (0, row_block(i, near_count), 0)),
        ]
        + out_specs,
        out_shape=[
            jax.ShapeDtypeStruct((seq_len, 3 * width), LOW),
            jax.ShapeDtypeStruct((seq_len, width), LOW),
            jax.ShapeDtypeStruct((heads, seq_len, seq_len), LOW),
        ]
        + out_shape,
        scratch_shapes=[
            pltpu.VMEM((heads, SKEW, 2 * seq_len), F32),
            pltpu.VMEM((rows, model), LOW),
        ],
        compiler_params=pltpu.CompilerParams(vmem_limit_bytes=34 * 2**20),
        cost_estimate=pl.CostEstimate(
            flops=4 * seq_len * seq_len * width,
            bytes_accessed=2 * heads * seq_len * seq_len,
            transcendentals=0,
        ),
        name="attention_forward",
    )(place, *parts, got, table)
    return (*outs[:3], outs[3 + count :], outs[3 : 3 + count])


def backward_kernel(heads, shard, near_count, count, place_ref, *refs):
    came, refs = refs[: 2 * count], refs[2 * count :]
    p_ref, got_ref, qkv_ref, d_ref, dt_ref, rows_ref, dk_sum, dv_sum, skew_ref = refs
    step = pl.program_id(0)
    block = row_block(step, near_count)
    take_rows(step, near_count, place_ref[3], came[:count], came[count:], rows_ref)
    rows, model = rows_ref.shape
    seq_len = qkv_ref.shape[0]
    width = qkv_ref.shape[1] // 3
    head_width = width // heads
    span = 2 * seq_len
    blocks = seq_len // rows

    @pl.when(step == 0)
    def _():
        dk_sum[...] = jnp.zeros_like(dk_sum)
        dv_sum[...] = jnp.zeros_like(dv_sum)
        skew_ref[...] = jnp.zeros_like(skew_ref)

    here = pl.ds(pl.multiple_of(block * rows, rows), rows)
    queries = qkv_ref[here, :width]
    keys = qkv_ref[:, width : 2 * width]
    values = qkv_ref[:, 2 * width :]
    weight = got_ref[:, :shard, 3 * width :].reshape(model, width)
    grads = rows_dot(rows_ref[...], weight).astype(LOW)
    total = jnp.zeros((rows, width), F32)
    places = bias_places(place_ref, block, blocks, rows, seq_len)
    for head in range(heads):
        own = head_lanes(rows, width, head_width, head)
        own_grads = only(own, grads)
        d_prob = lax.dot_general(
            own_grads, values, (((1,), (1,)), ((), ())), preferred_element_type=F32
        )
        prob_low = p_ref[head]
        prob = prob_low.astype(F32)
        weighed = prob * d_prob
        d_scores = (weighed - prob * jnp.sum(weighed, axis=1, keepdims=True)).astype(LOW)
        total = total + jnp.dot(
            d_scores,
            only(head_lanes(seq_len, width, head_width, head), keys),
            preferred_element_type=F32,
        )
        dk_sum[...] += lax.dot_general(
            d_scores, only(own, queries), (((0,), (0,)), ((), ())), preferred_element_type=F32
        )
        dv_sum[...] += lax.dot_general(
            prob_low, own_grads, (((0,), (0,)), ((), ())), preferred_element_type=F32
        )
        for part in range(rows // SKEW):
            for at in range(blocks):
                skew_ref[head, :, pl.ds(places[part][at], rows)] += d_scores[
                    part * SKEW : (part + 1) * SKEW, at * rows : (at + 1) * rows
                ].astype(F32)
    d_ref[here, :width] = total.astype(LOW)

    @pl.when(step == pl.num_programs(0) - 1)
    def _():
        d_ref[:, width : 2 * width] = dk_sum[...].astype(LOW)
        d_ref[:, 2 * width :] = dv_sum[...].astype(LOW)
        one_hot = bucket_onehot(dt_ref.shape[0], seq_len)
        row = lax.broadcasted_iota(jnp.int32, (SKEW, span), 0)
        column = lax.broadcasted_iota(jnp.int32, dt_ref.shape, 1)
        result = jnp.zeros(dt_ref.shape, F32)
        for head in range(heads):
            level = pltpu.roll(skew_ref[head], SKEW, 1)
            bit = 1
            while bit < SKEW:
                level = jnp.where((row & bit) != 0, pltpu.roll(level, span - bit, 1), level)
                bit *= 2
            line = jnp.sum(level, axis=0, keepdims=True)
            summed = jnp.sum(jnp.where(one_hot, line, 0.0), axis=1, keepdims=True)
            result = jnp.where(column == head, summed, result)
        dt_ref[...] = result


def attention_backward(prob, mine, other, got, qkv, place, heads, shard, buckets):
    seq_len, width = qkv.shape[0], qkv.shape[1] // 3
    near_count, own_rows, model = mine[0].shape
    count = len(mine)
    rows = count * own_rows
    came_specs, _ = sent_specs(near_count, count, own_rows, model)
    return pl.pallas_call(
        functools.partial(backward_kernel, heads, shard, near_count, count),
        grid=(seq_len // rows,),
        in_specs=[
            pl.BlockSpec(memory_space=pltpu.SMEM),
            *came_specs,
            pl.BlockSpec((heads, rows, seq_len), lambda i: (0, row_block(i, near_count), 0)),
            pl.BlockSpec(got.shape, lambda i: (0, 0, 0)),
            pl.BlockSpec(qkv.shape, lambda i: (0, 0)),
        ],
        out_specs=[
            pl.BlockSpec(qkv.shape, lambda i: (0, 0)),
            pl.BlockSpec((buckets, 128), lambda i: (0, 0)),
            pl.BlockSpec((rows, model), lambda i: (row_block(i, near_count), 0)),
        ],
        out_shape=[
            jax.ShapeDtypeStruct(qkv.shape, LOW),
            jax.ShapeDtypeStruct((buckets, 128), F32),
            jax.ShapeDtypeStruct((seq_len, model), LOW),
        ],
        scratch_shapes=[
            pltpu.VMEM((seq_len, width), F32),
            pltpu.VMEM((seq_len, width), F32),
            pltpu.VMEM((heads, SKEW, 2 * seq_len), F32),
        ],
        compiler_params=pltpu.CompilerParams(vmem_limit_bytes=34 * 2**20),
        cost_estimate=pl.CostEstimate(
            flops=8 * seq_len * seq_len * width * 4,
            bytes_accessed=2 * heads * seq_len * seq_len,
            transcendentals=0,
        ),
        name="attention_backward",
    )(place, *other, *mine, prob, got, qkv)


EXTRA = 8
OWNER_ROWS = 64


def as_column(row, first, count):
    size = row.shape[1]
    here = lax.broadcasted_iota(jnp.int32, (count, size), 1) == first + lax.broadcasted_iota(
        jnp.int32, (count, size), 0
    )
    return jnp.sum(jnp.where(here, row, 0.0), axis=1, keepdims=True)


def blocks_kernel(seqs, members, q_ref, k_ref, v_ref, o_ref, gain_ref, table_ref, sent_ref):
    shard = q_ref.shape[0]
    width = q_ref.shape[1] // members
    gain = as_column(gain_ref[...].astype(LOW).astype(F32), 0, shard)
    parts = [
        (ref[...].astype(LOW).astype(F32) * gain).astype(LOW) for ref in (q_ref, k_ref, v_ref)
    ]
    parts.append(o_ref[...].T.astype(LOW))
    rest = jnp.zeros((EXTRA, sent_ref.shape[2]), LOW)
    table_rows, heads = table_ref.shape
    for seq in range(seqs):
        for member in range(members):
            at = seq * members + member
            for i, part in enumerate(parts):
                sent_ref[at, :shard, i * width : (i + 1) * width] = part[
                    :, member * width : (member + 1) * width
                ]
            sent_ref[at, shard:, :] = rest
            sent_ref[at, shard : shard + table_rows, :heads] = table_ref[...].astype(LOW)


def attention_blocks(weights, w_out, gain, table, seqs, members):
    shard, columns = weights[0].shape
    return pl.pallas_call(
        functools.partial(blocks_kernel, seqs, members),
        out_shape=jax.ShapeDtypeStruct(
            (seqs * members, shard + EXTRA, 4 * columns // members), LOW
        ),
        compiler_params=pltpu.CompilerParams(vmem_limit_bytes=60 * 2**20),
        cost_estimate=pl.CostEstimate(
            flops=0, bytes_accessed=16 * shard * columns, transcendentals=0
        ),
        name="attention_blocks",
    )(*weights, w_out, gain, table)


def owner_kernel(count, members, table_shape, *refs):
    got_ref, extra_ref = refs[:2]
    weight_refs = refs[2 : 2 + count]
    gain_ref = refs[2 + count]
    grad_refs = refs[3 + count : 3 + 2 * count]
    sum_ref = refs[3 + 2 * count]
    step = pl.program_id(0)
    rows = got_ref.shape[1]
    seqs = got_ref.shape[0] // members
    width = got_ref.shape[2] // count
    size = sum_ref.shape[1]
    gain = as_column(gain_ref[...].astype(LOW).astype(F32), step * rows, rows)
    total = jnp.zeros((rows, 1), F32)
    for member in range(members):
        product = sum(got_ref[seq * members + member].astype(F32) for seq in range(seqs))
        for i in range(count):
            part = product[:, i * width : (i + 1) * width]
            here = pl.ds(member * width, width)
            grad_refs[i][:, here] = part * gain
            weight = weight_refs[i][:, here].astype(LOW).astype(F32)
            total = total + jnp.sum(weight * part, axis=1, keepdims=True)

    @pl.when(step == 0)
    def _():
        sum_ref[...] = jnp.zeros_like(sum_ref)

    diagonal = lax.broadcasted_iota(jnp.int32, (rows, size), 1) == step * rows + (
        lax.broadcasted_iota(jnp.int32, (rows, size), 0)
    )
    sum_ref[...] += jnp.sum(jnp.where(diagonal, total, 0.0), axis=0, keepdims=True)
    if table_shape is not None:
        table_rows, heads = table_shape
        each = heads // members
        for member in range(members):
            piece = sum(extra_ref[seq * members + member].astype(F32) for seq in range(seqs))
            refs[-1][:, member * each : (member + 1) * each] = piece[:table_rows, :each]


def owner_grads(got, weights, gain, members, table_shape):
    sources, height, columns = got.shape
    shard, wide = weights[0].shape
    count = len(weights)
    rows = min(OWNER_ROWS, shard)
    step_rows = pl.BlockSpec((rows, wide), lambda i: (i, 0))
    row = pl.BlockSpec((1, shard), lambda i: (0, 0))
    last = height // EXTRA - 1
    out_specs = [step_rows] * count + [row]
    out_shape = [jax.ShapeDtypeStruct((shard, wide), F32)] * count
    out_shape.append(jax.ShapeDtypeStruct((1, shard), F32))
    if table_shape is not None:
        out_specs.append(pl.BlockSpec(table_shape, lambda i: (0, 0)))
        out_shape.append(jax.ShapeDtypeStruct(table_shape, F32))
    outs = pl.pallas_call(
        functools.partial(owner_kernel, count, members, table_shape),
        grid=(shard // rows,),
        in_specs=[
            pl.BlockSpec((sources, rows, columns), lambda i: (0, i, 0)),
            pl.BlockSpec((sources, EXTRA, columns), lambda i: (0, last, 0)),
        ]
        + [step_rows] * count
        + [row],
        out_specs=out_specs,
        out_shape=out_shape,
        compiler_params=pltpu.CompilerParams(vmem_limit_bytes=32 * 2**20),
        cost_estimate=pl.CostEstimate(
            flops=0, bytes_accessed=10 * count * shard * wide, transcendentals=0
        ),
        name="owner_grads",
    )(got, got, *weights, gain)
    return outs[:count], outs[count], outs[-1] if table_shape is not None else None


def rows_dot(left, right):
    return jnp.dot(left, right, preferred_element_type=F32)


def contract_cols(left, right):
    return lax.dot_general(left, right, (((1,), (1,)), ((), ())), preferred_element_type=F32)


def contract_rows(left, right):
    return lax.dot_general(left, right, (((0,), (0,)), ((), ())), preferred_element_type=F32)

def row_block(step, near_count):
    return lax.rem(step + near_count, CORES * near_count)


def send_rows(step, near_count, mp_at, held_ref, other_refs, mine_refs):
    count = len(other_refs)
    own_rows = held_ref.shape[0] // count

    def write(refs):
        for away, ref in enumerate(refs):
            first = pl.multiple_of(lax.bitwise_xor(mp_at, away) * own_rows, own_rows)
            ref[0] = held_ref[pl.ds(first, own_rows), :]

    @pl.when(step < near_count)
    def _():
        write(other_refs)

    @pl.when(step >= near_count)
    def _():
        write(mine_refs)


def take_rows(step, near_count, mp_at, other_refs, mine_refs, rows_ref):
    own_rows = other_refs[0].shape[1]

    def read(refs):
        for away, ref in enumerate(refs):
            first = pl.multiple_of(lax.bitwise_xor(mp_at, away) * own_rows, own_rows)
            rows_ref[pl.ds(first, own_rows), :] = ref[0]

    @pl.when(step < near_count)
    def _():
        read(other_refs)

    @pl.when(step >= near_count)
    def _():
        read(mine_refs)


def sent_specs(near_count, count, own_rows, model):
    other = pl.BlockSpec((1, own_rows, model), lambda i: (jnp.minimum(i, near_count - 1), 0, 0))
    mine = pl.BlockSpec((1, own_rows, model), lambda i: (jnp.maximum(i - near_count, 0), 0, 0))
    shape = jax.ShapeDtypeStruct((near_count, own_rows, model), LOW)
    return [other] * count + [mine] * count, [shape] * (2 * count)


def partial_kernel(near_count, count, product, place_ref, left_ref, weight_ref, *refs):
    held_ref = refs[-1]
    product(left_ref, weight_ref, held_ref)
    send_rows(
        pl.program_id(0), near_count, place_ref[3], held_ref, refs[:count], refs[count : 2 * count]
    )


def partial_rows(left, weight, model, place, near_count, count, product, name):
    seq_len, depth = left.shape
    rows = seq_len // (CORES * near_count)
    out_specs, out_shape = sent_specs(near_count, count, rows // count, model)
    outs = pl.pallas_call(
        functools.partial(partial_kernel, near_count, count, product),
        grid=(CORES * near_count,),
        in_specs=[
            pl.BlockSpec(memory_space=pltpu.SMEM),
            pl.BlockSpec((rows, depth), lambda i: (row_block(i, near_count), 0)),
            pl.BlockSpec(weight.shape, lambda i: (0, 0, 0)),
        ],
        out_specs=out_specs,
        out_shape=out_shape,
        scratch_shapes=[pltpu.VMEM((rows, model), LOW)],
        compiler_params=pltpu.CompilerParams(vmem_limit_bytes=40 * 2**20),
        cost_estimate=pl.CostEstimate(
            flops=2 * seq_len * depth * model, bytes_accessed=2 * seq_len * model, transcendentals=0
        ),
        name=name,
    )(place, left, weight)
    return outs[count:], outs[:count]


def column_product(shard, first, last, left_ref, weight_ref, held_ref):
    weight = weight_ref[:, :shard, first:last]
    weight = weight.reshape(weight.shape[0] * shard, last - first)
    held_ref[...] = contract_cols(left_ref[...], weight).astype(LOW)


def row_product(height, left_ref, weight_ref, held_ref):
    left = left_ref[...]
    width = weight_ref.shape[2]
    for at in range(weight_ref.shape[0]):
        held_ref[:, at * width : (at + 1) * width] = rows_dot(
            left, weight_ref[at, :height, :]
        ).astype(LOW)


def ffn_blocks_kernel(seqs, members, gate_ref, up_ref, down_ref, gain_ref, first_ref, second_ref):
    shard = gate_ref.shape[0]
    width = gate_ref.shape[1] // members
    gain = as_column(gain_ref[...].astype(LOW).astype(F32), 0, shard)
    for member in range(members):
        here = slice(member * width, (member + 1) * width)
        parts = [
            (ref[:, here].astype(LOW).astype(F32) * gain).astype(LOW) for ref in (gate_ref, up_ref)
        ]
        both = jnp.concatenate(parts, 1)
        down = down_ref[here, :].astype(LOW)
        for seq in range(seqs):
            at = seq * members + member
            first_ref[at, :width, :] = down
            first_ref[at, width:, :] = both[:, :shard]
            second_ref[at] = both[:, shard:]


def ffn_blocks(w_gate, w_up, w_down, gain, seqs, members):
    shard, columns = w_gate.shape
    width = columns // members
    return pl.pallas_call(
        functools.partial(ffn_blocks_kernel, seqs, members),
        out_shape=[
            jax.ShapeDtypeStruct((seqs * members, width + shard, shard), LOW),
            jax.ShapeDtypeStruct((seqs * members, shard, 2 * width - shard), LOW),
        ],
        compiler_params=pltpu.CompilerParams(vmem_limit_bytes=40 * 2**20),
        cost_estimate=pl.CostEstimate(
            flops=0, bytes_accessed=18 * shard * columns, transcendentals=0
        ),
        name="ffn_blocks",
    )(w_gate, w_up, w_down, gain)


def ffn_kernel(near_count, count, place_ref, *refs):
    came, refs = refs[: 2 * count], refs[2 * count :]
    grad_ref, first_ref, second_ref = refs[:3]
    other_refs, mine_refs = refs[3 : 3 + count], refs[3 + count : 3 + 2 * count]
    rows_ref, act_ref, d_ref, down_ref, held_ref, sum_ref = refs[3 + 2 * count :]
    step = pl.program_id(0)
    take_rows(step, near_count, place_ref[3], came[:count], came[count:], rows_ref)
    sources, height, shard = first_ref.shape
    width = height - shard
    rows = rows_ref[...]
    block = row_block(step, near_count)
    first = block_place(block, place_ref[1], near_count) * rows.shape[0]
    valid = first + lax.broadcasted_iota(jnp.int32, (rows.shape[0], 1), 0) < place_ref[0]
    grads = only(valid, grad_ref[...])
    early = first_ref[:, width:, :].reshape(sources * shard, shard)
    late = second_ref[...].reshape(sources * shard, 2 * width - shard)
    both = jnp.concatenate([rows_dot(rows, early), rows_dot(rows, late)], 1)
    gate, up = both[:, :width], both[:, width:]
    scale, cubic = 0.7978845608028654, 0.044715
    square = gate * gate
    bent = jnp.tanh(scale * (gate + cubic * square * gate))
    half = 0.5 * (1.0 + bent)
    value = gate * half
    slope = half + 0.5 * gate * (1.0 - bent * bent) * (scale * (1.0 + 3.0 * cubic * square))
    act = (value * up).astype(LOW)
    act_ref[...] = act
    d_hidden = jnp.zeros((rows.shape[0], width), F32)
    for at in range(sources):
        d_hidden = d_hidden + contract_cols(
            grads[:, at * shard : (at + 1) * shard], first_ref[at, :width, :]
        )
    d_both = jnp.concatenate(
        [(d_hidden * up * slope).astype(LOW), (d_hidden * value).astype(LOW)], 1
    )
    d_ref[...] = d_both
    held_ref[...] = (
        contract_cols(d_both[:, :shard], early) + contract_cols(d_both[:, shard:], late)
    ).astype(LOW)
    send_rows(step, near_count, place_ref[3], held_ref, other_refs, mine_refs)
    product = contract_rows(act, grads)

    @pl.when(step == 0)
    def _():
        sum_ref[...] = product

    @pl.when(step > 0)
    def _():
        sum_ref[...] += product

    @pl.when(step == pl.num_programs(0) - 1)
    def _():
        for at in range(sources):
            down_ref[at] = sum_ref[:, at * shard : (at + 1) * shard].astype(LOW)


def feed_forward(mine, other, grads, first, second, place):
    seq_len, model = grads.shape
    near_count, count = mine[0].shape[0], len(mine)
    sources, height, shard = first.shape
    width = height - shard
    rows = seq_len // (CORES * near_count)
    out_specs, out_shape = sent_specs(near_count, count, rows // count, model)

    def blocks(columns):
        return pl.BlockSpec((rows, columns), lambda i: (row_block(i, near_count), 0))

    outs = pl.pallas_call(
        functools.partial(ffn_kernel, near_count, count),
        grid=(CORES * near_count,),
        in_specs=[
            pl.BlockSpec(memory_space=pltpu.SMEM),
            *out_specs,
            blocks(model),
            pl.BlockSpec(first.shape, lambda i: (0, 0, 0)),
            pl.BlockSpec(second.shape, lambda i: (0, 0, 0)),
        ],
        out_specs=out_specs
        + [
            blocks(model),
            blocks(width),
            blocks(2 * width),
            pl.BlockSpec((sources, width, shard), lambda i: (0, 0, 0)),
        ],
        out_shape=out_shape
        + [
            jax.ShapeDtypeStruct((seq_len, model), LOW),
            jax.ShapeDtypeStruct((seq_len, width), LOW),
            jax.ShapeDtypeStruct((seq_len, 2 * width), LOW),
            jax.ShapeDtypeStruct((sources, width, shard), LOW),
        ],
        scratch_shapes=[pltpu.VMEM((rows, model), LOW), pltpu.VMEM((width, model), F32)],
        compiler_params=pltpu.CompilerParams(vmem_limit_bytes=38 * 2**20),
        cost_estimate=pl.CostEstimate(
            flops=12 * seq_len * model * width, bytes_accessed=12 * seq_len * model, transcendentals=0
        ),
        name="feed_forward",
    )(place, *other, *mine, grads, first, second)
    return outs[count : 2 * count], outs[:count], *outs[2 * count :]


COLUMN = ("seq", "near", "core")


def exchange(blocks, axes):
    return lax.all_to_all(blocks, axes, split_axis=0, concat_axis=0, tiled=True)


def swap(block, axis):
    return lax.ppermute(block, axis, [(0, 1), (1, 0)])


def after(value, *done):
    return lax.optimization_barrier((value,) + done)[0]


def rms(values):
    return lax.rsqrt(jnp.mean(values * values, axis=-1, keepdims=True) + EPSILON)


def norm_grad(inner, normed, inverse):
    return inverse * (inner - normed * jnp.mean(inner * normed, axis=-1, keepdims=True))


def local(
    inputs,
    cotangent,
    lengths,
    attn_scale,
    w_query,
    w_key,
    w_value,
    w_out,
    rel_table,
    ffn_scale,
    w_gate,
    w_up,
    w_down,
):
    seqs = lax.axis_size("seq")
    near_count = lax.axis_size("near")
    mp_count = lax.axis_size("mp")
    members = near_count * CORES
    sources = seqs * members
    tok_rows, model = inputs.shape
    seq_len = tok_rows * members
    own_rows = tok_rows // mp_count
    half_rows = seq_len // CORES
    shard = attn_scale.shape[0]
    table_rows, heads_mp = rel_table.shape
    buckets = table_rows * sources
    heads = heads_mp // members
    width = w_query.shape[1] // members
    hidden_width = w_gate.shape[1] // members

    near_at = lax.axis_index("near")
    core_at = lax.axis_index("core")
    mp_at = lax.axis_index("mp")
    member_at = near_at * CORES + core_at
    length = lax.dynamic_slice_in_dim(lengths, lax.axis_index("seq"), 1, 0)
    place = jnp.stack(
        [length[0]] + [at.astype(jnp.int32) for at in (core_at, member_at, mp_at, near_at)]
    )

    def over_mp(own, axis):
        shape = own.shape[:axis] + (mp_count,) + own.shape[axis:]
        blocks = lax.dynamic_update_index_in_dim(jnp.zeros(shape, own.dtype), own, mp_at, axis)
        moved = [(away, shifted(own, away)) for away in reversed(range(1, mp_count))]
        for away, block in moved:
            blocks = lax.dynamic_update_index_in_dim(blocks, block, mp_at ^ away, axis)
        return blocks

    def shifted(block, away):
        return lax.ppermute(block, "mp", [(i, i ^ away) for i in range(mp_count)])

    def in_near_order(own, moved):
        return jnp.stack(
            [jnp.where(near_at == 0, own, moved), jnp.where(near_at == 0, moved, own)], 0
        )

    def near_rows(blocks):
        own = [lax.dynamic_slice_in_dim(block, mp_at * own_rows, own_rows, 0) for block in blocks]
        near = swap(jnp.stack(own), "near")
        came = [(0, near)] + [(away, shifted(near, away)) for away in range(1, mp_count)]
        halves = []
        for half in (came, [(away, swap(block, "core")) for away, block in came]):
            rows = jnp.zeros((len(blocks), mp_count, own_rows, model), near.dtype)
            for away, block in half:
                rows = lax.dynamic_update_index_in_dim(rows, block, mp_at ^ away, 1)
            halves.append([rows[i].reshape(tok_rows, model) for i in range(len(blocks))])
        return halves

    def in_order(own, moved, core, core_moved):
        rows = jnp.zeros((CORES, near_count, tok_rows, model), own.dtype)
        for at, block in enumerate((own, moved, core, core_moved)):
            rows = lax.dynamic_update_slice(
                rows, block[None, None], (at // 2, near_at ^ (at % 2), 0, 0)
            )
        return rows.reshape(seq_len, model)

    def gather_rows(near):
        mine = [near] + [shifted(near, away) for away in range(1, mp_count)]
        return mine, [swap(block, "core") for block in mine]

    def sum_cores(mine, other):
        return [
            kept.astype(F32) + swap(sent, "core").astype(F32) for kept, sent in zip(mine, other)
        ]

    def send_mp(sums):
        moved = [shifted(sums[away].astype(LOW), away) for away in reversed(range(1, mp_count))]
        return moved, sums[0]

    def sum_mp(sums):
        moved, kept = send_mp(sums)
        return sum((piece.astype(F32) for piece in moved), kept)

    def sum_near(pair):
        sent = jnp.where(near_at == 0, pair[1], pair[0]).astype(LOW)
        kept = jnp.where(near_at == 0, pair[0], pair[1])
        return kept + swap(sent, "near").astype(F32)

    def sum_near_both(pair):
        low = pair.astype(LOW)
        moved = swap(low, "near")
        return low.astype(F32) + moved.astype(F32), moved

    def near_pair(own, moved):
        pair = [
            lax.dynamic_slice_in_dim(block, mp_at * own_rows, own_rows, 0)
            for block in (own, moved)
        ]
        return in_near_order(*pair)

    def here(pair):
        return lax.dynamic_index_in_dim(pair, near_at, 0, keepdims=False)

    attn_sent = attention_blocks(
        (w_query, w_key, w_value), w_out, attn_scale.reshape(1, shard), rel_table, seqs, members
    )
    ffn_first, ffn_second = ffn_blocks(
        w_gate, w_up, w_down, ffn_scale.reshape(1, shard), seqs, members
    )

    attn_got = exchange(attn_sent, COLUMN)
    def partial(left, weight, product, name):
        return partial_rows(left, weight, model, place, near_count, mp_count, product, name)

    table = attn_got[:, shard : shard + table_rows, :heads_mp].reshape(buckets, heads_mp)

    def normed(rows):
        values = rows.astype(F32)
        return (values * rms(values)).astype(LOW)

    (moved_inputs, moved_cotangent), core_moved = near_rows([inputs, cotangent])
    input_parts = [inputs, moved_inputs, swap(inputs, "core"), core_moved[0]]
    grad_parts = [cotangent, moved_cotangent, swap(cotangent, "core"), core_moved[1]]
    parts = [normed(part) for part in input_parts]
    parts = lax.optimization_barrier((*parts, ffn_first, ffn_second))[:4]
    first_got = exchange(after(ffn_first, attn_got), COLUMN)

    qkv, attended, prob, out_mine, out_other = attention_forward(
        parts, attn_got, table, place, heads, shard, mp_count
    )
    normed_rows = in_order(*parts)
    grad_two = in_order(*grad_parts)
    mixed, mixed_moved = sum_near_both(
        after(sum_mp(sum_cores(out_mine, out_other)), first_got, grad_two)
    )
    second_got = exchange(after(ffn_second, mixed_moved), COLUMN)

    pair_inputs = near_pair(inputs, moved_inputs).astype(F32)
    after_attn = pair_inputs + mixed
    inv_two = rms(after_attn)
    normed_two = after_attn * inv_two
    mine_two, other_two = gather_rows(normed_two.astype(LOW))

    d_mine, d_other, hidden_two, acts, d_both, d_down_w = feed_forward(
        mine_two, other_two, grad_two, first_got, second_got, place
    )
    inner_cores = sum_cores(d_mine, d_other)

    def to_owners(grad):
        return exchange(grad, COLUMN)

    def by_rows(got):
        parts = got.reshape((seqs, members) + got.shape[1:]).astype(F32)
        return jnp.sum(parts, axis=0).reshape(-1, shard)

    d_down = to_owners(d_down_w)
    d_gate_up_w = contract_rows(hidden_two, after(d_both, *inner_cores)).astype(LOW)
    inner_two, inner_moved = sum_near_both(
        after(sum_mp(inner_cores), d_down, d_gate_up_w)
    )
    d_gate_up = to_owners(after(d_gate_up_w, inner_moved).reshape(sources, shard, -1))

    pair_first = (
        lax.broadcasted_iota(jnp.int32, (near_count, own_rows, 1), 0) * (CORES * tok_rows)
        + lax.broadcasted_iota(jnp.int32, (near_count, own_rows, 1), 1)
        + (core_at * tok_rows + mp_at * own_rows)
    )
    pair_valid = pair_first < length
    pair_grad = near_pair(cotangent, moved_cotangent).astype(F32)
    grad_one = jnp.where(pair_valid, pair_grad, 0.0) + norm_grad(inner_two, normed_two, inv_two)
    mine_one, other_one = gather_rows(grad_one.astype(LOW))
    down_product = functools.partial(row_product, hidden_width)
    ffn_cores = sum_cores(*partial(after(acts, inner_moved), first_got, down_product, "ffn_out"))
    d_qkv, d_table, rows_one = attention_backward(
        prob, mine_one, other_one, attn_got, qkv, place, heads, shard, buckets
    )
    qkv_product = functools.partial(column_product, shard, 0, 3 * width)
    ffn_moved, ffn_kept = send_mp([after(rows, *mine_one[1:]) for rows in ffn_cores])
    inner_cores = sum_cores(
        *partial(after(d_qkv, *ffn_moved), attn_got, qkv_product, "attention_in")
    )
    last_moved, last_kept = send_mp(inner_cores)
    inner_one = sum_near(sum((piece.astype(F32) for piece in last_moved), last_kept))
    table_sent = d_table[:, :heads].astype(LOW).reshape(sources, table_rows, heads)
    table_sent = jnp.pad(
        table_sent, ((0, 0), (0, EXTRA - table_rows), (0, 3 * width - heads))
    )
    d_qkv_w = contract_rows(normed_rows, d_qkv).astype(LOW).reshape(sources, shard, -1)
    d_qkv_sent = jnp.concatenate([d_qkv_w, table_sent], 1)
    d_qkv_got = to_owners(after(d_qkv_sent, d_gate_up, last_moved[0]))
    d_out = contract_rows(after(attended, inner_cores[0]), rows_one)
    d_out = jnp.moveaxis(d_out.astype(LOW).reshape(width, sources, shard), 1, 0)
    d_out = to_owners(after(d_out, d_qkv_got))

    own_inputs = here(pair_inputs)
    normed_one = own_inputs * rms(own_inputs)
    grad_input = here(grad_one) + norm_grad(inner_one, normed_one, rms(own_inputs))
    d_inputs = over_mp(grad_input.astype(LOW), 0).reshape(tok_rows, model)
    ffn_pair = sum((piece.astype(F32) for piece in ffn_moved), ffn_kept)
    after_ffn = here(after_attn) + sum_near(after(ffn_pair, d_qkv_got))
    own_out = jnp.where(here(pair_valid), after_ffn, 0.0).astype(LOW)
    layer_out = over_mp(own_out, 0).reshape(tok_rows, model)

    (d_w_gate, d_w_up), ffn_gain, _ = owner_grads(
        after(d_gate_up, inner_cores[0]), (w_gate, w_up), ffn_scale.reshape(1, shard), members, None
    )
    (d_w_query, d_w_key, d_w_value), attn_gain, d_rel_table = owner_grads(
        d_qkv_got,
        (w_query, w_key, w_value),
        attn_scale.reshape(1, shard),
        members,
        (table_rows, heads_mp),
    )
    gains = jnp.concatenate([attn_gain, ffn_gain], 0)
    gains = sum((shifted(gains, away) for away in range(1, mp_count)), gains)
    return (
        layer_out,
        d_inputs,
        gains[0],
        d_w_query,
        d_w_key,
        d_w_value,
        by_rows(d_out),
        d_rel_table,
        gains[1],
        d_w_gate,
        d_w_up,
        by_rows(after(d_down, d_qkv)),
    )


def solution(mesh):
    fsdp, mp = mesh.shape["fsdp"], mesh.shape["mp"]

    def run(*args):
        seqs = args[2].shape[0]
        members = fsdp // seqs
        inner = Mesh(
            mesh.devices.reshape(seqs, members // CORES, CORES, mp), ("seq", "near", "core", "mp")
        )
        rows, columns, first = P(COLUMN, None), P("mp", COLUMN), P(COLUMN)
        both = P(COLUMN, "mp")
        in_specs = (
            rows, rows, P(), first, both, both, both, columns, both, first, both, both, columns,
        )
        out_specs = (
            rows, rows, first, both, both, both, columns, both, first, both, both, columns,
        )
        return jax.shard_map(
            local, mesh=inner, in_specs=in_specs, out_specs=out_specs, check_vma=False
        )(*args)

    return run
```

```python
import functools

import jax
import jax.numpy as jnp
from jax import lax
from jax.experimental import pallas as pl
from jax.experimental.pallas import tpu as pltpu
from jax.sharding import Mesh, PartitionSpec as P

LOW = jnp.bfloat16
F32 = jnp.float32
CORES = 2
THRESHOLDS = (12, 16, 23, 32, 46, 64, 91)
EPSILON = 1e-06
MASKED = -1e30
SKEW = 128


def bucket_of(rel_offset):
    distance = jnp.abs(rel_offset)
    far_bucket = 8 + sum(((distance >= threshold).astype(jnp.int32) for threshold in THRESHOLDS))
    bucket_abs = jnp.where(distance < 8, distance, far_bucket)
    return bucket_abs + jnp.where(rel_offset > 0, 16, 0)


def bucket_onehot(buckets, seq_len):
    offset = lax.broadcasted_iota(jnp.int32, (buckets, 2 * seq_len), 1) - seq_len
    bucket = lax.broadcasted_iota(jnp.int32, (buckets, 2 * seq_len), 0)
    return bucket_of(offset) == bucket


def head_lanes(rows, width, head_width, head):
    lane = lax.broadcasted_iota(jnp.int32, (rows, width), 1)
    return (lane >= head * head_width) & (lane < (head + 1) * head_width)


def only(mask, values):
    return jnp.where(mask, values, jnp.zeros_like(values))


def block_place(block, core, near_count):
    return lax.rem(block, near_count) * CORES + lax.bitwise_xor(lax.div(block, near_count), core)


def bias_places(place_ref, step, blocks, rows, seq_len):
    core, near_count = place_ref[1], blocks // CORES
    query = block_place(step, core, near_count) * rows
    return [
        [
            pl.multiple_of(
                block_place(block, core, near_count) * rows - query - part * SKEW + seq_len - SKEW,
                SKEW,
            )
            for block in range(blocks)
        ]
        for part in range(rows // SKEW)
    ]


def forward_kernel(heads, shard, near_count, count, place_ref, *refs):
    own_ref, moved_ref, core_ref, core_moved_ref, got_ref, table_ref = refs[:6]
    qkv_ref, o_ref, p_ref = refs[6:9]
    other_refs, mine_refs = refs[9 : 9 + count], refs[9 + count : 9 + 2 * count]
    skew_ref, held_ref = refs[9 + 2 * count :]
    step = pl.program_id(0)
    seq_len = qkv_ref.shape[0]
    rows, width = o_ref.shape
    model = held_ref.shape[1]
    head_width = width // heads
    span = 2 * seq_len
    blocks = seq_len // rows
    block = row_block(step, near_count)

    @pl.when(step == 0)
    def _():
        weight = got_ref[:, :shard, : 3 * width].reshape(model, 3 * width)
        near = place_ref[4]
        for at, ref in enumerate((own_ref, moved_ref, core_ref, core_moved_ref)):
            first = (at // 2) * near_count + lax.bitwise_xor(near, at % 2)
            qkv_ref[pl.ds(pl.multiple_of(first * rows, rows), rows), :] = rows_dot(
                ref[...], weight
            ).astype(LOW)
        one_hot = bucket_onehot(table_ref.shape[0], seq_len)
        table = table_ref[...].astype(F32)
        column = lax.broadcasted_iota(jnp.int32, table.shape, 1)
        for head in range(heads):
            here = column == place_ref[2] * heads + head
            levels = jnp.sum(jnp.where(here, table, 0.0), axis=1, keepdims=True)
            line = jnp.sum(jnp.where(one_hot, levels, 0.0), axis=0, keepdims=True)
            line = jnp.broadcast_to(line, (SKEW, span))
            skew_ref[head] = pltpu.roll(line, span - SKEW, 1, stride=1, stride_axis=0)

    row = lax.broadcasted_iota(jnp.int32, (1, rows), 1)
    allowed = jnp.concatenate(
        [
            block_place(at, place_ref[1], near_count) * rows + row < place_ref[0]
            for at in range(blocks)
        ],
        1,
    )
    queries = qkv_ref[pl.ds(pl.multiple_of(block * rows, rows), rows), :width]
    keys = qkv_ref[:, width : 2 * width]
    values = qkv_ref[:, 2 * width :]
    total = jnp.zeros((rows, width), F32)
    places = bias_places(place_ref, block, blocks, rows, seq_len)
    for head in range(heads):
        scores = lax.dot_general(
            only(head_lanes(rows, width, head_width, head), queries),
            keys,
            (((1,), (1,)), ((), ())),
            preferred_element_type=F32,
        )
        bias = jnp.concatenate(
            [
                jnp.concatenate([skew_ref[head, :, pl.ds(place, rows)] for place in part], 1)
                for part in places
            ],
            0,
        )
        scores = jnp.where(allowed, scores + bias, MASKED)
        grown = jnp.exp(scores - jnp.max(scores, axis=1, keepdims=True))
        prob = (grown * (1.0 / jnp.sum(grown, axis=1, keepdims=True))).astype(LOW)
        p_ref[head] = prob
        total = total + jnp.dot(
            prob,
            only(head_lanes(seq_len, width, head_width, head), values),
            preferred_element_type=F32,
        )
    attended = total.astype(LOW)
    o_ref[...] = attended
    weight = got_ref[:, :shard, 3 * width :].reshape(model, width)
    held_ref[...] = contract_cols(attended, weight).astype(LOW)
    send_rows(step, near_count, place_ref[3], held_ref, other_refs, mine_refs)


def attention_forward(parts, got, table, place, heads, shard, count):
    rows, model = parts[0].shape
    blocks = len(parts)
    near_count = blocks // CORES
    seq_len, width = rows * blocks, got.shape[2] // 4
    out_specs, out_shape = sent_specs(near_count, count, rows // count, model)

    def fixed(shape):
        return pl.BlockSpec(shape, lambda i: (0,) * len(shape))

    outs = pl.pallas_call(
        functools.partial(forward_kernel, heads, shard, near_count, count),
        grid=(blocks,),
        in_specs=[pl.BlockSpec(memory_space=pltpu.SMEM)]
        + [fixed(part.shape) for part in parts]
        + [fixed(got.shape), fixed(table.shape)],
        out_specs=[
            fixed((seq_len, 3 * width)),
            pl.BlockSpec((rows, width), lambda i: (row_block(i, near_count), 0)),
            pl.BlockSpec((heads, rows, seq_len), lambda i: (0, row_block(i, near_count), 0)),
        ]
        + out_specs,
        out_shape=[
            jax.ShapeDtypeStruct((seq_len, 3 * width), LOW),
            jax.ShapeDtypeStruct((seq_len, width), LOW),
            jax.ShapeDtypeStruct((heads, seq_len, seq_len), LOW),
        ]
        + out_shape,
        scratch_shapes=[
            pltpu.VMEM((heads, SKEW, 2 * seq_len), F32),
            pltpu.VMEM((rows, model), LOW),
        ],
        compiler_params=pltpu.CompilerParams(vmem_limit_bytes=56 * 2**20),
        cost_estimate=pl.CostEstimate(
            flops=4 * seq_len * seq_len * width,
            bytes_accessed=2 * heads * seq_len * seq_len,
            transcendentals=0,
        ),
        name="attention_forward",
    )(place, *parts, got, table)
    return (*outs[:3], outs[3 + count :], outs[3 : 3 + count])


def backward_kernel(heads, shard, near_count, count, place_ref, *refs):
    came, refs = refs[: 2 * count], refs[2 * count :]
    p_ref, got_ref, qkv_ref, d_ref, dt_ref, rows_ref, dk_sum, dv_sum, skew_ref = refs
    step = pl.program_id(0)
    block = row_block(step, near_count)
    take_rows(step, near_count, place_ref[3], came[:count], came[count:], rows_ref)
    rows, model = rows_ref.shape
    seq_len = qkv_ref.shape[0]
    width = qkv_ref.shape[1] // 3
    head_width = width // heads
    span = 2 * seq_len
    blocks = seq_len // rows

    @pl.when(step == 0)
    def _():
        dk_sum[...] = jnp.zeros_like(dk_sum)
        dv_sum[...] = jnp.zeros_like(dv_sum)
        skew_ref[...] = jnp.zeros_like(skew_ref)

    here = pl.ds(pl.multiple_of(block * rows, rows), rows)
    queries = qkv_ref[here, :width]
    keys = qkv_ref[:, width : 2 * width]
    values = qkv_ref[:, 2 * width :]
    weight = got_ref[:, :shard, 3 * width :].reshape(model, width)
    grads = rows_dot(rows_ref[...], weight).astype(LOW)
    total = jnp.zeros((rows, width), F32)
    places = bias_places(place_ref, block, blocks, rows, seq_len)
    for head in range(heads):
        own = head_lanes(rows, width, head_width, head)
        own_grads = only(own, grads)
        d_prob = lax.dot_general(
            own_grads, values, (((1,), (1,)), ((), ())), preferred_element_type=F32
        )
        prob_low = p_ref[head]
        prob = prob_low.astype(F32)
        weighed = prob * d_prob
        d_scores = (weighed - prob * jnp.sum(weighed, axis=1, keepdims=True)).astype(LOW)
        total = total + jnp.dot(
            d_scores,
            only(head_lanes(seq_len, width, head_width, head), keys),
            preferred_element_type=F32,
        )
        dk_sum[...] += lax.dot_general(
            d_scores, only(own, queries), (((0,), (0,)), ((), ())), preferred_element_type=F32
        )
        dv_sum[...] += lax.dot_general(
            prob_low, own_grads, (((0,), (0,)), ((), ())), preferred_element_type=F32
        )
        for part in range(rows // SKEW):
            for at in range(blocks):
                skew_ref[head, :, pl.ds(places[part][at], rows)] += d_scores[
                    part * SKEW : (part + 1) * SKEW, at * rows : (at + 1) * rows
                ].astype(F32)
    d_ref[here, :width] = total.astype(LOW)

    @pl.when(step == pl.num_programs(0) - 1)
    def _():
        d_ref[:, width : 2 * width] = dk_sum[...].astype(LOW)
        d_ref[:, 2 * width :] = dv_sum[...].astype(LOW)
        one_hot = bucket_onehot(dt_ref.shape[0], seq_len)
        row = lax.broadcasted_iota(jnp.int32, (SKEW, span), 0)
        column = lax.broadcasted_iota(jnp.int32, dt_ref.shape, 1)
        result = jnp.zeros(dt_ref.shape, F32)
        for head in range(heads):
            level = pltpu.roll(skew_ref[head], SKEW, 1)
            bit = 1
            while bit < SKEW:
                level = jnp.where((row & bit) != 0, pltpu.roll(level, span - bit, 1), level)
                bit *= 2
            line = jnp.sum(level, axis=0, keepdims=True)
            summed = jnp.sum(jnp.where(one_hot, line, 0.0), axis=1, keepdims=True)
            result = jnp.where(column == head, summed, result)
        dt_ref[...] = result


def attention_backward(prob, mine, other, got, qkv, place, heads, shard, buckets):
    seq_len, width = qkv.shape[0], qkv.shape[1] // 3
    near_count, own_rows, model = mine[0].shape
    count = len(mine)
    rows = count * own_rows
    came_specs, _ = sent_specs(near_count, count, own_rows, model)
    return pl.pallas_call(
        functools.partial(backward_kernel, heads, shard, near_count, count),
        grid=(seq_len // rows,),
        in_specs=[
            pl.BlockSpec(memory_space=pltpu.SMEM),
            *came_specs,
            pl.BlockSpec((heads, rows, seq_len), lambda i: (0, row_block(i, near_count), 0)),
            pl.BlockSpec(got.shape, lambda i: (0, 0, 0)),
            pl.BlockSpec(qkv.shape, lambda i: (0, 0)),
        ],
        out_specs=[
            pl.BlockSpec(qkv.shape, lambda i: (0, 0)),
            pl.BlockSpec((buckets, 128), lambda i: (0, 0)),
            pl.BlockSpec((rows, model), lambda i: (row_block(i, near_count), 0)),
        ],
        out_shape=[
            jax.ShapeDtypeStruct(qkv.shape, LOW),
            jax.ShapeDtypeStruct((buckets, 128), F32),
            jax.ShapeDtypeStruct((seq_len, model), LOW),
        ],
        scratch_shapes=[
            pltpu.VMEM((seq_len, width), F32),
            pltpu.VMEM((seq_len, width), F32),
            pltpu.VMEM((heads, SKEW, 2 * seq_len), F32),
        ],
        compiler_params=pltpu.CompilerParams(vmem_limit_bytes=56 * 2**20),
        cost_estimate=pl.CostEstimate(
            flops=8 * seq_len * seq_len * width * 4,
            bytes_accessed=2 * heads * seq_len * seq_len,
            transcendentals=0,
        ),
        name="attention_backward",
    )(place, *other, *mine, prob, got, qkv)


EXTRA = 8
OWNER_ROWS = 64


def as_column(row, first, count):
    size = row.shape[1]
    here = lax.broadcasted_iota(jnp.int32, (count, size), 1) == first + lax.broadcasted_iota(
        jnp.int32, (count, size), 0
    )
    return jnp.sum(jnp.where(here, row, 0.0), axis=1, keepdims=True)


def blocks_kernel(seqs, members, q_ref, k_ref, v_ref, o_ref, gain_ref, table_ref, sent_ref):
    shard = q_ref.shape[0]
    width = q_ref.shape[1] // members
    gain = as_column(gain_ref[...].astype(LOW).astype(F32), 0, shard)
    parts = [
        (ref[...].astype(LOW).astype(F32) * gain).astype(LOW) for ref in (q_ref, k_ref, v_ref)
    ]
    parts.append(o_ref[...].T.astype(LOW))
    rest = jnp.zeros((EXTRA, sent_ref.shape[2]), LOW)
    table_rows, heads = table_ref.shape
    for seq in range(seqs):
        for member in range(members):
            at = seq * members + member
            for i, part in enumerate(parts):
                sent_ref[at, :shard, i * width : (i + 1) * width] = part[
                    :, member * width : (member + 1) * width
                ]
            sent_ref[at, shard:, :] = rest
            sent_ref[at, shard : shard + table_rows, :heads] = table_ref[...].astype(LOW)


def attention_blocks(weights, w_out, gain, table, seqs, members):
    shard, columns = weights[0].shape
    return pl.pallas_call(
        functools.partial(blocks_kernel, seqs, members),
        out_shape=jax.ShapeDtypeStruct(
            (seqs * members, shard + EXTRA, 4 * columns // members), LOW
        ),
        compiler_params=pltpu.CompilerParams(vmem_limit_bytes=60 * 2**20),
        cost_estimate=pl.CostEstimate(
            flops=0, bytes_accessed=16 * shard * columns, transcendentals=0
        ),
        name="attention_blocks",
    )(*weights, w_out, gain, table)


def owner_kernel(count, members, table_shape, *refs):
    got_ref, extra_ref = refs[:2]
    weight_refs = refs[2 : 2 + count]
    gain_ref = refs[2 + count]
    grad_refs = refs[3 + count : 3 + 2 * count]
    sum_ref = refs[3 + 2 * count]
    step = pl.program_id(0)
    rows = got_ref.shape[1]
    seqs = got_ref.shape[0] // members
    width = got_ref.shape[2] // count
    size = sum_ref.shape[1]
    gain = as_column(gain_ref[...].astype(LOW).astype(F32), step * rows, rows)
    total = jnp.zeros((rows, 1), F32)
    for member in range(members):
        product = sum(got_ref[seq * members + member].astype(F32) for seq in range(seqs))
        for i in range(count):
            part = product[:, i * width : (i + 1) * width]
            here = pl.ds(member * width, width)
            grad_refs[i][:, here] = part * gain
            weight = weight_refs[i][:, here].astype(LOW).astype(F32)
            total = total + jnp.sum(weight * part, axis=1, keepdims=True)

    @pl.when(step == 0)
    def _():
        sum_ref[...] = jnp.zeros_like(sum_ref)

    diagonal = lax.broadcasted_iota(jnp.int32, (rows, size), 1) == step * rows + (
        lax.broadcasted_iota(jnp.int32, (rows, size), 0)
    )
    sum_ref[...] += jnp.sum(jnp.where(diagonal, total, 0.0), axis=0, keepdims=True)
    if table_shape is not None:
        table_rows, heads = table_shape
        each = heads // members
        for member in range(members):
            piece = sum(extra_ref[seq * members + member].astype(F32) for seq in range(seqs))
            refs[-1][:, member * each : (member + 1) * each] = piece[:table_rows, :each]


def owner_grads(got, weights, gain, members, table_shape):
    sources, height, columns = got.shape
    shard, wide = weights[0].shape
    count = len(weights)
    rows = min(OWNER_ROWS, shard)
    step_rows = pl.BlockSpec((rows, wide), lambda i: (i, 0))
    row = pl.BlockSpec((1, shard), lambda i: (0, 0))
    last = height // EXTRA - 1
    out_specs = [step_rows] * count + [row]
    out_shape = [jax.ShapeDtypeStruct((shard, wide), F32)] * count
    out_shape.append(jax.ShapeDtypeStruct((1, shard), F32))
    if table_shape is not None:
        out_specs.append(pl.BlockSpec(table_shape, lambda i: (0, 0)))
        out_shape.append(jax.ShapeDtypeStruct(table_shape, F32))
    outs = pl.pallas_call(
        functools.partial(owner_kernel, count, members, table_shape),
        grid=(shard // rows,),
        in_specs=[
            pl.BlockSpec((sources, rows, columns), lambda i: (0, i, 0)),
            pl.BlockSpec((sources, EXTRA, columns), lambda i: (0, last, 0)),
        ]
        + [step_rows] * count
        + [row],
        out_specs=out_specs,
        out_shape=out_shape,
        compiler_params=pltpu.CompilerParams(vmem_limit_bytes=32 * 2**20),
        cost_estimate=pl.CostEstimate(
            flops=0, bytes_accessed=10 * count * shard * wide, transcendentals=0
        ),
        name="owner_grads",
    )(got, got, *weights, gain)
    return outs[:count], outs[count], outs[-1] if table_shape is not None else None


def rows_dot(left, right):
    return jnp.dot(left, right, preferred_element_type=F32)


def contract_cols(left, right):
    return lax.dot_general(left, right, (((1,), (1,)), ((), ())), preferred_element_type=F32)


def contract_rows(left, right):
    return lax.dot_general(left, right, (((0,), (0,)), ((), ())), preferred_element_type=F32)

def row_block(step, near_count):
    return lax.rem(step + near_count, CORES * near_count)


def send_rows(step, near_count, mp_at, held_ref, other_refs, mine_refs):
    count = len(other_refs)
    own_rows = held_ref.shape[0] // count

    def write(refs):
        for away, ref in enumerate(refs):
            first = pl.multiple_of(lax.bitwise_xor(mp_at, away) * own_rows, own_rows)
            ref[0] = held_ref[pl.ds(first, own_rows), :]

    @pl.when(step < near_count)
    def _():
        write(other_refs)

    @pl.when(step >= near_count)
    def _():
        write(mine_refs)


def take_rows(step, near_count, mp_at, other_refs, mine_refs, rows_ref):
    own_rows = other_refs[0].shape[1]

    def read(refs):
        for away, ref in enumerate(refs):
            first = pl.multiple_of(lax.bitwise_xor(mp_at, away) * own_rows, own_rows)
            rows_ref[pl.ds(first, own_rows), :] = ref[0]

    @pl.when(step < near_count)
    def _():
        read(other_refs)

    @pl.when(step >= near_count)
    def _():
        read(mine_refs)


def sent_specs(near_count, count, own_rows, model):
    other = pl.BlockSpec((1, own_rows, model), lambda i: (jnp.minimum(i, near_count - 1), 0, 0))
    mine = pl.BlockSpec((1, own_rows, model), lambda i: (jnp.maximum(i - near_count, 0), 0, 0))
    shape = jax.ShapeDtypeStruct((near_count, own_rows, model), LOW)
    return [other] * count + [mine] * count, [shape] * (2 * count)


def partial_kernel(near_count, count, product, place_ref, left_ref, weight_ref, *refs):
    held_ref = refs[-1]
    product(left_ref, weight_ref, held_ref)
    send_rows(
        pl.program_id(0), near_count, place_ref[3], held_ref, refs[:count], refs[count : 2 * count]
    )


def partial_rows(left, weight, model, place, near_count, count, product, name):
    seq_len, depth = left.shape
    rows = seq_len // (CORES * near_count)
    out_specs, out_shape = sent_specs(near_count, count, rows // count, model)
    outs = pl.pallas_call(
        functools.partial(partial_kernel, near_count, count, product),
        grid=(CORES * near_count,),
        in_specs=[
            pl.BlockSpec(memory_space=pltpu.SMEM),
            pl.BlockSpec((rows, depth), lambda i: (row_block(i, near_count), 0)),
            pl.BlockSpec(weight.shape, lambda i: (0, 0, 0)),
        ],
        out_specs=out_specs,
        out_shape=out_shape,
        scratch_shapes=[pltpu.VMEM((rows, model), LOW)],
        compiler_params=pltpu.CompilerParams(vmem_limit_bytes=40 * 2**20),
        cost_estimate=pl.CostEstimate(
            flops=2 * seq_len * depth * model, bytes_accessed=2 * seq_len * model, transcendentals=0
        ),
        name=name,
    )(place, left, weight)
    return outs[count:], outs[:count]


def column_product(shard, first, last, left_ref, weight_ref, held_ref):
    weight = weight_ref[:, :shard, first:last]
    weight = weight.reshape(weight.shape[0] * shard, last - first)
    held_ref[...] = contract_cols(left_ref[...], weight).astype(LOW)


def row_product(height, left_ref, weight_ref, held_ref):
    left = left_ref[...]
    width = weight_ref.shape[2]
    for at in range(weight_ref.shape[0]):
        held_ref[:, at * width : (at + 1) * width] = rows_dot(
            left, weight_ref[at, :height, :]
        ).astype(LOW)


def ffn_blocks_kernel(seqs, members, gate_ref, up_ref, down_ref, gain_ref, first_ref, second_ref):
    shard = gate_ref.shape[0]
    width = gate_ref.shape[1] // members
    gain = as_column(gain_ref[...].astype(LOW).astype(F32), 0, shard)
    for member in range(members):
        here = slice(member * width, (member + 1) * width)
        parts = [
            (ref[:, here].astype(LOW).astype(F32) * gain).astype(LOW) for ref in (gate_ref, up_ref)
        ]
        both = jnp.concatenate(parts, 1)
        down = down_ref[here, :].astype(LOW)
        for seq in range(seqs):
            at = seq * members + member
            first_ref[at, :width, :] = down
            first_ref[at, width:, :] = both[:, :shard]
            second_ref[at] = both[:, shard:]


def ffn_blocks(w_gate, w_up, w_down, gain, seqs, members):
    shard, columns = w_gate.shape
    width = columns // members
    return pl.pallas_call(
        functools.partial(ffn_blocks_kernel, seqs, members),
        out_shape=[
            jax.ShapeDtypeStruct((seqs * members, width + shard, shard), LOW),
            jax.ShapeDtypeStruct((seqs * members, shard, 2 * width - shard), LOW),
        ],
        compiler_params=pltpu.CompilerParams(vmem_limit_bytes=40 * 2**20),
        cost_estimate=pl.CostEstimate(
            flops=0, bytes_accessed=18 * shard * columns, transcendentals=0
        ),
        name="ffn_blocks",
    )(w_gate, w_up, w_down, gain)


def ffn_kernel(near_count, count, place_ref, *refs):
    came, refs = refs[: 2 * count], refs[2 * count :]
    grad_ref, first_ref, second_ref = refs[:3]
    other_refs, mine_refs = refs[3 : 3 + count], refs[3 + count : 3 + 2 * count]
    rows_ref, act_ref, d_ref, down_ref, held_ref, sum_ref = refs[3 + 2 * count :]
    step = pl.program_id(0)
    take_rows(step, near_count, place_ref[3], came[:count], came[count:], rows_ref)
    sources, height, shard = first_ref.shape
    width = height - shard
    rows = rows_ref[...]
    block = row_block(step, near_count)
    first = block_place(block, place_ref[1], near_count) * rows.shape[0]
    valid = first + lax.broadcasted_iota(jnp.int32, (rows.shape[0], 1), 0) < place_ref[0]
    grads = only(valid, grad_ref[...])
    early = first_ref[:, width:, :].reshape(sources * shard, shard)
    late = second_ref[...].reshape(sources * shard, 2 * width - shard)
    both = jnp.concatenate([rows_dot(rows, early), rows_dot(rows, late)], 1)
    gate, up = both[:, :width], both[:, width:]
    scale, cubic = 0.7978845608028654, 0.044715
    square = gate * gate
    bent = jnp.tanh(scale * (gate + cubic * square * gate))
    half = 0.5 * (1.0 + bent)
    value = gate * half
    slope = half + 0.5 * gate * (1.0 - bent * bent) * (scale * (1.0 + 3.0 * cubic * square))
    act = (value * up).astype(LOW)
    act_ref[...] = act
    d_hidden = jnp.zeros((rows.shape[0], width), F32)
    for at in range(sources):
        d_hidden = d_hidden + contract_cols(
            grads[:, at * shard : (at + 1) * shard], first_ref[at, :width, :]
        )
    d_both = jnp.concatenate(
        [(d_hidden * up * slope).astype(LOW), (d_hidden * value).astype(LOW)], 1
    )
    d_ref[...] = d_both
    held_ref[...] = (
        contract_cols(d_both[:, :shard], early) + contract_cols(d_both[:, shard:], late)
    ).astype(LOW)
    send_rows(step, near_count, place_ref[3], held_ref, other_refs, mine_refs)
    product = contract_rows(act, grads)

    @pl.when(step == 0)
    def _():
        sum_ref[...] = product

    @pl.when(step > 0)
    def _():
        sum_ref[...] += product

    @pl.when(step == pl.num_programs(0) - 1)
    def _():
        for at in range(sources):
            down_ref[at] = sum_ref[:, at * shard : (at + 1) * shard].astype(LOW)


def feed_forward(mine, other, grads, first, second, place):
    seq_len, model = grads.shape
    near_count, count = mine[0].shape[0], len(mine)
    sources, height, shard = first.shape
    width = height - shard
    rows = seq_len // (CORES * near_count)
    out_specs, out_shape = sent_specs(near_count, count, rows // count, model)

    def blocks(columns):
        return pl.BlockSpec((rows, columns), lambda i: (row_block(i, near_count), 0))

    outs = pl.pallas_call(
        functools.partial(ffn_kernel, near_count, count),
        grid=(CORES * near_count,),
        in_specs=[
            pl.BlockSpec(memory_space=pltpu.SMEM),
            *out_specs,
            blocks(model),
            pl.BlockSpec(first.shape, lambda i: (0, 0, 0)),
            pl.BlockSpec(second.shape, lambda i: (0, 0, 0)),
        ],
        out_specs=out_specs
        + [
            blocks(model),
            blocks(width),
            blocks(2 * width),
            pl.BlockSpec((sources, width, shard), lambda i: (0, 0, 0)),
        ],
        out_shape=out_shape
        + [
            jax.ShapeDtypeStruct((seq_len, model), LOW),
            jax.ShapeDtypeStruct((seq_len, width), LOW),
            jax.ShapeDtypeStruct((seq_len, 2 * width), LOW),
            jax.ShapeDtypeStruct((sources, width, shard), LOW),
        ],
        scratch_shapes=[pltpu.VMEM((rows, model), LOW), pltpu.VMEM((width, model), F32)],
        compiler_params=pltpu.CompilerParams(vmem_limit_bytes=56 * 2**20),
        cost_estimate=pl.CostEstimate(
            flops=12 * seq_len * model * width, bytes_accessed=12 * seq_len * model, transcendentals=0
        ),
        name="feed_forward",
    )(place, *other, *mine, grads, first, second)
    return outs[count : 2 * count], outs[:count], *outs[2 * count :]


COLUMN = ("seq", "near", "core")


def exchange(blocks, axes):
    return lax.all_to_all(blocks, axes, split_axis=0, concat_axis=0, tiled=True)


def swap(block, axis):
    return lax.ppermute(block, axis, [(0, 1), (1, 0)])


def after(value, *done):
    return lax.optimization_barrier((value,) + done)[0]


def rms(values):
    return lax.rsqrt(jnp.mean(values * values, axis=-1, keepdims=True) + EPSILON)


def norm_grad(inner, normed, inverse):
    return inverse * (inner - normed * jnp.mean(inner * normed, axis=-1, keepdims=True))


def local(
    inputs,
    cotangent,
    lengths,
    attn_scale,
    w_query,
    w_key,
    w_value,
    w_out,
    rel_table,
    ffn_scale,
    w_gate,
    w_up,
    w_down,
):
    seqs = lax.axis_size("seq")
    near_count = lax.axis_size("near")
    mp_count = lax.axis_size("mp")
    members = near_count * CORES
    sources = seqs * members
    tok_rows, model = inputs.shape
    seq_len = tok_rows * members
    own_rows = tok_rows // mp_count
    half_rows = seq_len // CORES
    shard = attn_scale.shape[0]
    table_rows, heads_mp = rel_table.shape
    buckets = table_rows * sources
    heads = heads_mp // members
    width = w_query.shape[1] // members
    hidden_width = w_gate.shape[1] // members

    near_at = lax.axis_index("near")
    core_at = lax.axis_index("core")
    mp_at = lax.axis_index("mp")
    member_at = near_at * CORES + core_at
    length = lax.dynamic_slice_in_dim(lengths, lax.axis_index("seq"), 1, 0)
    place = jnp.stack(
        [length[0]] + [at.astype(jnp.int32) for at in (core_at, member_at, mp_at, near_at)]
    )

    def over_mp(own, axis):
        shape = own.shape[:axis] + (mp_count,) + own.shape[axis:]
        blocks = lax.dynamic_update_index_in_dim(jnp.zeros(shape, own.dtype), own, mp_at, axis)
        moved = [(away, shifted(own, away)) for away in reversed(range(1, mp_count))]
        for away, block in moved:
            blocks = lax.dynamic_update_index_in_dim(blocks, block, mp_at ^ away, axis)
        return blocks

    def shifted(block, away):
        return lax.ppermute(block, "mp", [(i, i ^ away) for i in range(mp_count)])

    def in_near_order(own, moved):
        return jnp.stack(
            [jnp.where(near_at == 0, own, moved), jnp.where(near_at == 0, moved, own)], 0
        )

    def over_near(blocks):
        own = [lax.dynamic_slice_in_dim(block, mp_at * own_rows, own_rows, 0) for block in blocks]
        return swap(jnp.stack(own), "near")

    def near_rows(near):
        came = [(0, near)] + [(away, shifted(near, away)) for away in range(1, mp_count)]
        halves = []
        for half in (came, [(away, swap(block, "core")) for away, block in came]):
            rows = jnp.zeros((mp_count, own_rows, model), near.dtype)
            for away, block in half:
                rows = lax.dynamic_update_index_in_dim(rows, block, mp_at ^ away, 0)
            halves.append(rows.reshape(tok_rows, model))
        return halves

    def in_order(own, moved, core, core_moved):
        rows = jnp.zeros((CORES, near_count, tok_rows, model), own.dtype)
        for at, block in enumerate((own, moved, core, core_moved)):
            rows = lax.dynamic_update_slice(
                rows, block[None, None], (at // 2, near_at ^ (at % 2), 0, 0)
            )
        return rows.reshape(seq_len, model)

    def gather_rows(near):
        mine = [near] + [shifted(near, away) for away in range(1, mp_count)]
        return mine, [swap(block, "core") for block in mine]

    def sum_cores(mine, other):
        return [
            kept.astype(F32) + swap(sent, "core").astype(F32) for kept, sent in zip(mine, other)
        ]

    def send_mp(sums):
        return [shifted(sums[away].astype(LOW), away) for away in reversed(range(1, mp_count))]

    def sum_mp(sums):
        return sum((piece.astype(F32) for piece in send_mp(sums)), sums[0])

    def split_near(pair):
        sent = jnp.where(near_at == 0, pair[1], pair[0]).astype(LOW)
        return sent, jnp.where(near_at == 0, pair[0], pair[1])

    def sum_near_both(pair):
        low = pair.astype(LOW)
        moved = swap(low, "near")
        return low.astype(F32) + moved.astype(F32), moved

    def near_pair(own, moved):
        pair = [
            lax.dynamic_slice_in_dim(block, mp_at * own_rows, own_rows, 0)
            for block in (own, moved)
        ]
        return in_near_order(*pair)

    def here(pair):
        return lax.dynamic_index_in_dim(pair, near_at, 0, keepdims=False)

    attn_sent = attention_blocks(
        (w_query, w_key, w_value), w_out, attn_scale.reshape(1, shard), rel_table, seqs, members
    )
    ffn_first, ffn_second = ffn_blocks(
        w_gate, w_up, w_down, ffn_scale.reshape(1, shard), seqs, members
    )

    attn_got = exchange(attn_sent, COLUMN)
    def partial(left, weight, product, name):
        return partial_rows(left, weight, model, place, near_count, mp_count, product, name)

    table = attn_got[:, shard : shard + table_rows, :heads_mp].reshape(buckets, heads_mp)

    def normed(rows):
        values = rows.astype(F32)
        return (values * rms(values)).astype(LOW)

    near = over_near([inputs, cotangent])
    moved_inputs, core_moved = near_rows(near[0])
    input_parts = [inputs, moved_inputs, swap(inputs, "core"), core_moved]
    moved_cotangent, core_moved = near_rows(after(near[1], moved_inputs))
    grad_parts = [cotangent, moved_cotangent, swap(cotangent, "core"), core_moved]
    parts = [normed(part) for part in input_parts]
    parts = lax.optimization_barrier((*parts, ffn_first, ffn_second, moved_cotangent))[:4]
    first_got = exchange(after(ffn_first, attn_got), COLUMN)

    qkv, attended, prob, out_mine, out_other = attention_forward(
        parts, attn_got, table, place, heads, shard, mp_count
    )
    normed_rows = in_order(*parts)
    grad_two = in_order(*grad_parts)
    mixed, mixed_moved = sum_near_both(
        after(sum_mp(sum_cores(out_mine, out_other)), first_got, grad_two)
    )
    second_got = exchange(after(ffn_second, mixed_moved), COLUMN)

    pair_inputs = near_pair(inputs, moved_inputs).astype(F32)
    after_attn = pair_inputs + mixed
    inv_two = rms(after_attn)
    normed_two = after_attn * inv_two
    mine_two, other_two = gather_rows(normed_two.astype(LOW))

    d_mine, d_other, hidden_two, acts, d_both, d_down_w = feed_forward(
        mine_two, other_two, grad_two, first_got, second_got, place
    )
    inner_cores = sum_cores(d_mine, d_other)

    def to_owners(grad):
        return exchange(grad, COLUMN)

    def by_rows(got):
        parts = got.reshape((seqs, members) + got.shape[1:]).astype(F32)
        return jnp.sum(parts, axis=0).reshape(-1, shard)

    d_down = to_owners(d_down_w)
    d_gate_up_w = contract_rows(hidden_two, after(d_both, *inner_cores)).astype(LOW)
    inner_two, inner_moved = sum_near_both(
        after(sum_mp(inner_cores), d_down, d_gate_up_w)
    )
    d_gate_up = to_owners(after(d_gate_up_w, inner_moved).reshape(sources, shard, -1))

    pair_first = (
        lax.broadcasted_iota(jnp.int32, (near_count, own_rows, 1), 0) * (CORES * tok_rows)
        + lax.broadcasted_iota(jnp.int32, (near_count, own_rows, 1), 1)
        + (core_at * tok_rows + mp_at * own_rows)
    )
    pair_valid = pair_first < length
    pair_grad = near_pair(cotangent, moved_cotangent).astype(F32)
    grad_one = jnp.where(pair_valid, pair_grad, 0.0) + norm_grad(inner_two, normed_two, inv_two)
    mine_one, other_one = gather_rows(grad_one.astype(LOW))
    down_product = functools.partial(row_product, hidden_width)
    ffn_cores = sum_cores(*partial(after(acts, mine_one[1]), first_got, down_product, "ffn_out"))
    d_qkv, d_table, rows_one = attention_backward(
        prob, mine_one, other_one, attn_got, qkv, place, heads, shard, buckets
    )
    qkv_product = functools.partial(column_product, shard, 0, 3 * width)
    ffn_moved = send_mp([after(rows, *mine_one[1:]) for rows in ffn_cores])
    inner_cores = sum_cores(
        *partial(after(d_qkv, *ffn_moved), attn_got, qkv_product, "attention_in")
    )
    inner_pair = sum_mp(inner_cores)
    table_sent = d_table[:, :heads].astype(LOW).reshape(sources, table_rows, heads)
    table_sent = jnp.pad(
        table_sent, ((0, 0), (0, EXTRA - table_rows), (0, 3 * width - heads))
    )
    d_qkv_w = contract_rows(normed_rows, d_qkv).astype(LOW).reshape(sources, shard, -1)
    d_qkv_sent = jnp.concatenate([d_qkv_w, table_sent], 1)
    d_qkv_got = to_owners(after(d_qkv_sent, d_gate_up))
    d_out = contract_rows(after(attended, inner_cores[0]), rows_one)
    d_out = jnp.moveaxis(d_out.astype(LOW).reshape(width, sources, shard), 1, 0)
    d_out = to_owners(after(d_out, d_qkv_got))

    (d_w_gate, d_w_up), ffn_gain, _ = owner_grads(
        after(d_gate_up, inner_cores[0]), (w_gate, w_up), ffn_scale.reshape(1, shard), members, None
    )
    d_w_down = by_rows(after(d_down, d_qkv))

    ffn_sent, ffn_kept = split_near(
        sum((piece.astype(F32) for piece in ffn_moved), ffn_cores[0])
    )
    inner_sent, inner_kept = split_near(inner_pair)
    came = swap(
        after(jnp.stack([ffn_sent, inner_sent]), d_qkv_got, ffn_gain, d_w_down), "near"
    ).astype(F32)
    own_inputs = here(pair_inputs)
    inv_one = rms(own_inputs)
    grad_input = here(grad_one) + norm_grad(inner_kept + came[1], own_inputs * inv_one, inv_one)
    own_out = jnp.where(here(pair_valid), here(after_attn) + ffn_kept + came[0], 0.0)
    owned = jnp.stack([own_out.astype(LOW), grad_input.astype(LOW)])
    rows_out = [jnp.zeros((mp_count, own_rows, model), LOW)] * 2
    for away in range(mp_count):
        block = shifted(owned, away) if away else owned
        rows_out = [
            lax.dynamic_update_index_in_dim(rows, block[i], mp_at ^ away, 0)
            for i, rows in enumerate(rows_out)
        ]
    layer_out, d_inputs = (rows.reshape(tok_rows, model) for rows in rows_out)

    (d_w_query, d_w_key, d_w_value), attn_gain, d_rel_table = owner_grads(
        d_qkv_got,
        (w_query, w_key, w_value),
        attn_scale.reshape(1, shard),
        members,
        (table_rows, heads_mp),
    )
    gains = jnp.concatenate([attn_gain, ffn_gain], 0)
    gains = sum((shifted(gains, away) for away in range(1, mp_count)), gains)
    return (
        layer_out,
        d_inputs,
        gains[0],
        d_w_query,
        d_w_key,
        d_w_value,
        by_rows(d_out),
        d_rel_table,
        gains[1],
        d_w_gate,
        d_w_up,
        d_w_down,
    )


def solution(mesh):
    fsdp, mp = mesh.shape["fsdp"], mesh.shape["mp"]

    def run(*args):
        seqs = args[2].shape[0]
        members = fsdp // seqs
        inner = Mesh(
            mesh.devices.reshape(seqs, members // CORES, CORES, mp), ("seq", "near", "core", "mp")
        )
        rows, columns, first = P(COLUMN, None), P("mp", COLUMN), P(COLUMN)
        both = P(COLUMN, "mp")
        in_specs = (
            rows, rows, P(), first, both, both, both, columns, both, first, both, both, columns,
        )
        out_specs = (
            rows, rows, first, both, both, both, columns, both, first, both, both, columns,
        )
        return jax.shard_map(
            local, mesh=inner, in_specs=in_specs, out_specs=out_specs, check_vma=False
        )(*args)

    return run
```

```python
import functools

import jax
import jax.numpy as jnp
from jax import lax
from jax.experimental import pallas as pl
from jax.experimental.pallas import tpu as pltpu
from jax.sharding import Mesh, PartitionSpec as P

LOW = jnp.bfloat16
F32 = jnp.float32
CORES = 2
THRESHOLDS = (12, 16, 23, 32, 46, 64, 91)
EPSILON = 1e-06
MASKED = -1e30
SKEW = 128


def bucket_of(rel_offset):
    distance = jnp.abs(rel_offset)
    far_bucket = 8 + sum(((distance >= threshold).astype(jnp.int32) for threshold in THRESHOLDS))
    bucket_abs = jnp.where(distance < 8, distance, far_bucket)
    return bucket_abs + jnp.where(rel_offset > 0, 16, 0)


def bucket_onehot(buckets, seq_len):
    offset = lax.broadcasted_iota(jnp.int32, (buckets, 2 * seq_len), 1) - seq_len
    bucket = lax.broadcasted_iota(jnp.int32, (buckets, 2 * seq_len), 0)
    return bucket_of(offset) == bucket


def head_lanes(rows, width, head_width, head):
    lane = lax.broadcasted_iota(jnp.int32, (rows, width), 1)
    return (lane >= head * head_width) & (lane < (head + 1) * head_width)


def only(mask, values):
    return jnp.where(mask, values, jnp.zeros_like(values))


def block_place(block, core, near_count):
    return lax.rem(block, near_count) * CORES + lax.bitwise_xor(lax.div(block, near_count), core)


def bias_places(place_ref, step, blocks, rows, seq_len):
    core, near_count = place_ref[1], blocks // CORES
    query = block_place(step, core, near_count) * rows
    return [
        [
            pl.multiple_of(
                block_place(block, core, near_count) * rows - query - part * SKEW + seq_len - SKEW,
                SKEW,
            )
            for block in range(blocks)
        ]
        for part in range(rows // SKEW)
    ]


def forward_kernel(heads, shard, near_count, count, place_ref, *refs):
    own_ref, moved_ref, core_ref, core_moved_ref, got_ref, table_ref = refs[:6]
    qkv_ref, o_ref, p_ref = refs[6:9]
    other_refs, mine_refs = refs[9 : 9 + count], refs[9 + count : 9 + 2 * count]
    skew_ref, held_ref = refs[9 + 2 * count :]
    step = pl.program_id(0)
    seq_len = qkv_ref.shape[0]
    rows, width = o_ref.shape
    model = held_ref.shape[1]
    head_width = width // heads
    span = 2 * seq_len
    blocks = seq_len // rows
    block = row_block(step, near_count)

    @pl.when(step == 0)
    def _():
        weight = got_ref[:, :shard, : 3 * width].reshape(model, 3 * width)
        near = place_ref[4]
        for at, ref in enumerate((own_ref, moved_ref, core_ref, core_moved_ref)):
            first = (at // 2) * near_count + lax.bitwise_xor(near, at % 2)
            qkv_ref[pl.ds(pl.multiple_of(first * rows, rows), rows), :] = rows_dot(
                ref[...], weight
            ).astype(LOW)
        one_hot = bucket_onehot(table_ref.shape[0], seq_len)
        table = table_ref[...].astype(F32)
        column = lax.broadcasted_iota(jnp.int32, table.shape, 1)
        for head in range(heads):
            here = column == place_ref[2] * heads + head
            levels = jnp.sum(jnp.where(here, table, 0.0), axis=1, keepdims=True)
            line = jnp.sum(jnp.where(one_hot, levels, 0.0), axis=0, keepdims=True)
            line = jnp.broadcast_to(line, (SKEW, span))
            skew_ref[head] = pltpu.roll(line, span - SKEW, 1, stride=1, stride_axis=0)

    row = lax.broadcasted_iota(jnp.int32, (1, rows), 1)
    allowed = jnp.concatenate(
        [
            block_place(at, place_ref[1], near_count) * rows + row < place_ref[0]
            for at in range(blocks)
        ],
        1,
    )
    queries = qkv_ref[pl.ds(pl.multiple_of(block * rows, rows), rows), :width]
    keys = qkv_ref[:, width : 2 * width]
    values = qkv_ref[:, 2 * width :]
    total = jnp.zeros((rows, width), F32)
    places = bias_places(place_ref, block, blocks, rows, seq_len)
    for head in range(heads):
        scores = lax.dot_general(
            only(head_lanes(rows, width, head_width, head), queries),
            keys,
            (((1,), (1,)), ((), ())),
            preferred_element_type=F32,
        )
        bias = jnp.concatenate(
            [
                jnp.concatenate([skew_ref[head, :, pl.ds(place, rows)] for place in part], 1)
                for part in places
            ],
            0,
        )
        scores = jnp.where(allowed, scores + bias, MASKED)
        grown = jnp.exp(scores - jnp.max(scores, axis=1, keepdims=True))
        prob = (grown * (1.0 / jnp.sum(grown, axis=1, keepdims=True))).astype(LOW)
        p_ref[head] = prob
        total = total + jnp.dot(
            prob,
            only(head_lanes(seq_len, width, head_width, head), values),
            preferred_element_type=F32,
        )
    attended = total.astype(LOW)
    o_ref[...] = attended
    weight = got_ref[:, :shard, 3 * width :].reshape(model, width)
    held_ref[...] = contract_cols(attended, weight).astype(LOW)
    send_rows(step, near_count, place_ref[3], held_ref, other_refs, mine_refs)


def attention_forward(parts, got, table, place, heads, shard, count):
    rows, model = parts[0].shape
    blocks = len(parts)
    near_count = blocks // CORES
    seq_len, width = rows * blocks, got.shape[2] // 4
    out_specs, out_shape = sent_specs(near_count, count, rows // count, model)

    def fixed(shape):
        return pl.BlockSpec(shape, lambda i: (0,) * len(shape))

    outs = pl.pallas_call(
        functools.partial(forward_kernel, heads, shard, near_count, count),
        grid=(blocks,),
        in_specs=[pl.BlockSpec(memory_space=pltpu.SMEM)]
        + [fixed(part.shape) for part in parts]
        + [fixed(got.shape), fixed(table.shape)],
        out_specs=[
            fixed((seq_len, 3 * width)),
            pl.BlockSpec((rows, width), lambda i: (row_block(i, near_count), 0)),
            pl.BlockSpec((heads, rows, seq_len), lambda i: (0, row_block(i, near_count), 0)),
        ]
        + out_specs,
        out_shape=[
            jax.ShapeDtypeStruct((seq_len, 3 * width), LOW),
            jax.ShapeDtypeStruct((seq_len, width), LOW),
            jax.ShapeDtypeStruct((heads, seq_len, seq_len), LOW),
        ]
        + out_shape,
        scratch_shapes=[
            pltpu.VMEM((heads, SKEW, 2 * seq_len), F32),
            pltpu.VMEM((rows, model), LOW),
        ],
        compiler_params=pltpu.CompilerParams(vmem_limit_bytes=34 * 2**20),
        cost_estimate=pl.CostEstimate(
            flops=4 * seq_len * seq_len * width,
            bytes_accessed=2 * heads * seq_len * seq_len,
            transcendentals=0,
        ),
        name="attention_forward",
    )(place, *parts, got, table)
    return (*outs[:3], outs[3 + count :], outs[3 : 3 + count])


def backward_kernel(heads, shard, near_count, count, place_ref, *refs):
    came, refs = refs[: 2 * count], refs[2 * count :]
    p_ref, got_ref, qkv_ref, d_ref, dt_ref, rows_ref, dk_sum, dv_sum, skew_ref = refs
    step = pl.program_id(0)
    block = row_block(step, near_count)
    take_rows(step, near_count, place_ref[3], came[:count], came[count:], rows_ref)
    rows, model = rows_ref.shape
    seq_len = qkv_ref.shape[0]
    width = qkv_ref.shape[1] // 3
    head_width = width // heads
    span = 2 * seq_len
    blocks = seq_len // rows

    @pl.when(step == 0)
    def _():
        dk_sum[...] = jnp.zeros_like(dk_sum)
        dv_sum[...] = jnp.zeros_like(dv_sum)
        skew_ref[...] = jnp.zeros_like(skew_ref)

    here = pl.ds(pl.multiple_of(block * rows, rows), rows)
    queries = qkv_ref[here, :width]
    keys = qkv_ref[:, width : 2 * width]
    values = qkv_ref[:, 2 * width :]
    weight = got_ref[:, :shard, 3 * width :].reshape(model, width)
    grads = rows_dot(rows_ref[...], weight).astype(LOW)
    total = jnp.zeros((rows, width), F32)
    places = bias_places(place_ref, block, blocks, rows, seq_len)
    for head in range(heads):
        own = head_lanes(rows, width, head_width, head)
        own_grads = only(own, grads)
        d_prob = lax.dot_general(
            own_grads, values, (((1,), (1,)), ((), ())), preferred_element_type=F32
        )
        prob_low = p_ref[head]
        prob = prob_low.astype(F32)
        weighed = prob * d_prob
        d_scores = (weighed - prob * jnp.sum(weighed, axis=1, keepdims=True)).astype(LOW)
        total = total + jnp.dot(
            d_scores,
            only(head_lanes(seq_len, width, head_width, head), keys),
            preferred_element_type=F32,
        )
        dk_sum[...] += lax.dot_general(
            d_scores, only(own, queries), (((0,), (0,)), ((), ())), preferred_element_type=F32
        )
        dv_sum[...] += lax.dot_general(
            prob_low, own_grads, (((0,), (0,)), ((), ())), preferred_element_type=F32
        )
        for part in range(rows // SKEW):
            for at in range(blocks):
                skew_ref[head, :, pl.ds(places[part][at], rows)] += d_scores[
                    part * SKEW : (part + 1) * SKEW, at * rows : (at + 1) * rows
                ].astype(F32)
    d_ref[here, :width] = total.astype(LOW)

    @pl.when(step == pl.num_programs(0) - 1)
    def _():
        d_ref[:, width : 2 * width] = dk_sum[...].astype(LOW)
        d_ref[:, 2 * width :] = dv_sum[...].astype(LOW)
        one_hot = bucket_onehot(dt_ref.shape[0], seq_len)
        row = lax.broadcasted_iota(jnp.int32, (SKEW, span), 0)
        column = lax.broadcasted_iota(jnp.int32, dt_ref.shape, 1)
        result = jnp.zeros(dt_ref.shape, F32)
        for head in range(heads):
            level = pltpu.roll(skew_ref[head], SKEW, 1)
            bit = 1
            while bit < SKEW:
                level = jnp.where((row & bit) != 0, pltpu.roll(level, span - bit, 1), level)
                bit *= 2
            line = jnp.sum(level, axis=0, keepdims=True)
            summed = jnp.sum(jnp.where(one_hot, line, 0.0), axis=1, keepdims=True)
            result = jnp.where(column == head, summed, result)
        dt_ref[...] = result


def attention_backward(prob, mine, other, got, qkv, place, heads, shard, buckets):
    seq_len, width = qkv.shape[0], qkv.shape[1] // 3
    near_count, own_rows, model = mine[0].shape
    count = len(mine)
    rows = count * own_rows
    came_specs, _ = sent_specs(near_count, count, own_rows, model)
    return pl.pallas_call(
        functools.partial(backward_kernel, heads, shard, near_count, count),
        grid=(seq_len // rows,),
        in_specs=[
            pl.BlockSpec(memory_space=pltpu.SMEM),
            *came_specs,
            pl.BlockSpec((heads, rows, seq_len), lambda i: (0, row_block(i, near_count), 0)),
            pl.BlockSpec(got.shape, lambda i: (0, 0, 0)),
            pl.BlockSpec(qkv.shape, lambda i: (0, 0)),
        ],
        out_specs=[
            pl.BlockSpec(qkv.shape, lambda i: (0, 0)),
            pl.BlockSpec((buckets, 128), lambda i: (0, 0)),
            pl.BlockSpec((rows, model), lambda i: (row_block(i, near_count), 0)),
        ],
        out_shape=[
            jax.ShapeDtypeStruct(qkv.shape, LOW),
            jax.ShapeDtypeStruct((buckets, 128), F32),
            jax.ShapeDtypeStruct((seq_len, model), LOW),
        ],
        scratch_shapes=[
            pltpu.VMEM((seq_len, width), F32),
            pltpu.VMEM((seq_len, width), F32),
            pltpu.VMEM((heads, SKEW, 2 * seq_len), F32),
        ],
        compiler_params=pltpu.CompilerParams(vmem_limit_bytes=34 * 2**20),
        cost_estimate=pl.CostEstimate(
            flops=8 * seq_len * seq_len * width * 4,
            bytes_accessed=2 * heads * seq_len * seq_len,
            transcendentals=0,
        ),
        name="attention_backward",
    )(place, *other, *mine, prob, got, qkv)


EXTRA = 8
OWNER_ROWS = 64


def as_column(row, first, count):
    size = row.shape[1]
    here = lax.broadcasted_iota(jnp.int32, (count, size), 1) == first + lax.broadcasted_iota(
        jnp.int32, (count, size), 0
    )
    return jnp.sum(jnp.where(here, row, 0.0), axis=1, keepdims=True)


def blocks_kernel(seqs, members, q_ref, k_ref, v_ref, o_ref, gain_ref, table_ref, sent_ref):
    shard = q_ref.shape[0]
    width = q_ref.shape[1] // members
    gain = as_column(gain_ref[...].astype(LOW).astype(F32), 0, shard)
    parts = [
        (ref[...].astype(LOW).astype(F32) * gain).astype(LOW) for ref in (q_ref, k_ref, v_ref)
    ]
    parts.append(o_ref[...].T.astype(LOW))
    rest = jnp.zeros((EXTRA, sent_ref.shape[2]), LOW)
    table_rows, heads = table_ref.shape
    for seq in range(seqs):
        for member in range(members):
            at = seq * members + member
            for i, part in enumerate(parts):
                sent_ref[at, :shard, i * width : (i + 1) * width] = part[
                    :, member * width : (member + 1) * width
                ]
            sent_ref[at, shard:, :] = rest
            sent_ref[at, shard : shard + table_rows, :heads] = table_ref[...].astype(LOW)


def attention_blocks(weights, w_out, gain, table, seqs, members):
    shard, columns = weights[0].shape
    return pl.pallas_call(
        functools.partial(blocks_kernel, seqs, members),
        out_shape=jax.ShapeDtypeStruct(
            (seqs * members, shard + EXTRA, 4 * columns // members), LOW
        ),
        compiler_params=pltpu.CompilerParams(vmem_limit_bytes=60 * 2**20),
        cost_estimate=pl.CostEstimate(
            flops=0, bytes_accessed=16 * shard * columns, transcendentals=0
        ),
        name="attention_blocks",
    )(*weights, w_out, gain, table)


def owner_kernel(count, members, table_shape, *refs):
    got_ref, extra_ref = refs[:2]
    weight_refs = refs[2 : 2 + count]
    gain_ref = refs[2 + count]
    grad_refs = refs[3 + count : 3 + 2 * count]
    sum_ref = refs[3 + 2 * count]
    step = pl.program_id(0)
    rows = got_ref.shape[1]
    seqs = got_ref.shape[0] // members
    width = got_ref.shape[2] // count
    size = sum_ref.shape[1]
    gain = as_column(gain_ref[...].astype(LOW).astype(F32), step * rows, rows)
    total = jnp.zeros((rows, 1), F32)
    for member in range(members):
        product = sum(got_ref[seq * members + member].astype(F32) for seq in range(seqs))
        for i in range(count):
            part = product[:, i * width : (i + 1) * width]
            here = pl.ds(member * width, width)
            grad_refs[i][:, here] = part * gain
            weight = weight_refs[i][:, here].astype(LOW).astype(F32)
            total = total + jnp.sum(weight * part, axis=1, keepdims=True)

    @pl.when(step == 0)
    def _():
        sum_ref[...] = jnp.zeros_like(sum_ref)

    diagonal = lax.broadcasted_iota(jnp.int32, (rows, size), 1) == step * rows + (
        lax.broadcasted_iota(jnp.int32, (rows, size), 0)
    )
    sum_ref[...] += jnp.sum(jnp.where(diagonal, total, 0.0), axis=0, keepdims=True)
    if table_shape is not None:
        table_rows, heads = table_shape
        each = heads // members
        for member in range(members):
            piece = sum(extra_ref[seq * members + member].astype(F32) for seq in range(seqs))
            refs[-1][:, member * each : (member + 1) * each] = piece[:table_rows, :each]


def owner_grads(got, weights, gain, members, table_shape):
    sources, height, columns = got.shape
    shard, wide = weights[0].shape
    count = len(weights)
    rows = min(OWNER_ROWS, shard)
    step_rows = pl.BlockSpec((rows, wide), lambda i: (i, 0))
    row = pl.BlockSpec((1, shard), lambda i: (0, 0))
    last = height // EXTRA - 1
    out_specs = [step_rows] * count + [row]
    out_shape = [jax.ShapeDtypeStruct((shard, wide), F32)] * count
    out_shape.append(jax.ShapeDtypeStruct((1, shard), F32))
    if table_shape is not None:
        out_specs.append(pl.BlockSpec(table_shape, lambda i: (0, 0)))
        out_shape.append(jax.ShapeDtypeStruct(table_shape, F32))
    outs = pl.pallas_call(
        functools.partial(owner_kernel, count, members, table_shape),
        grid=(shard // rows,),
        in_specs=[
            pl.BlockSpec((sources, rows, columns), lambda i: (0, i, 0)),
            pl.BlockSpec((sources, EXTRA, columns), lambda i: (0, last, 0)),
        ]
        + [step_rows] * count
        + [row],
        out_specs=out_specs,
        out_shape=out_shape,
        compiler_params=pltpu.CompilerParams(vmem_limit_bytes=32 * 2**20),
        cost_estimate=pl.CostEstimate(
            flops=0, bytes_accessed=10 * count * shard * wide, transcendentals=0
        ),
        name="owner_grads",
    )(got, got, *weights, gain)
    return outs[:count], outs[count], outs[-1] if table_shape is not None else None


def rows_dot(left, right):
    return jnp.dot(left, right, preferred_element_type=F32)


def contract_cols(left, right):
    return lax.dot_general(left, right, (((1,), (1,)), ((), ())), preferred_element_type=F32)


def contract_rows(left, right):
    return lax.dot_general(left, right, (((0,), (0,)), ((), ())), preferred_element_type=F32)

def row_block(step, near_count):
    return lax.rem(step + near_count, CORES * near_count)


def send_rows(step, near_count, mp_at, held_ref, other_refs, mine_refs):
    count = len(other_refs)
    own_rows = held_ref.shape[0] // count

    def write(refs):
        for away, ref in enumerate(refs):
            first = pl.multiple_of(lax.bitwise_xor(mp_at, away) * own_rows, own_rows)
            ref[0] = held_ref[pl.ds(first, own_rows), :]

    @pl.when(step < near_count)
    def _():
        write(other_refs)

    @pl.when(step >= near_count)
    def _():
        write(mine_refs)


def take_rows(step, near_count, mp_at, other_refs, mine_refs, rows_ref):
    own_rows = other_refs[0].shape[1]

    def read(refs):
        for away, ref in enumerate(refs):
            first = pl.multiple_of(lax.bitwise_xor(mp_at, away) * own_rows, own_rows)
            rows_ref[pl.ds(first, own_rows), :] = ref[0]

    @pl.when(step < near_count)
    def _():
        read(other_refs)

    @pl.when(step >= near_count)
    def _():
        read(mine_refs)


def sent_specs(near_count, count, own_rows, model):
    other = pl.BlockSpec((1, own_rows, model), lambda i: (jnp.minimum(i, near_count - 1), 0, 0))
    mine = pl.BlockSpec((1, own_rows, model), lambda i: (jnp.maximum(i - near_count, 0), 0, 0))
    shape = jax.ShapeDtypeStruct((near_count, own_rows, model), LOW)
    return [other] * count + [mine] * count, [shape] * (2 * count)


def partial_kernel(near_count, count, product, place_ref, left_ref, weight_ref, *refs):
    held_ref = refs[-1]
    product(left_ref, weight_ref, held_ref)
    send_rows(
        pl.program_id(0), near_count, place_ref[3], held_ref, refs[:count], refs[count : 2 * count]
    )


def partial_rows(left, weight, model, place, near_count, count, product, name):
    seq_len, depth = left.shape
    rows = seq_len // (CORES * near_count)
    out_specs, out_shape = sent_specs(near_count, count, rows // count, model)
    outs = pl.pallas_call(
        functools.partial(partial_kernel, near_count, count, product),
        grid=(CORES * near_count,),
        in_specs=[
            pl.BlockSpec(memory_space=pltpu.SMEM),
            pl.BlockSpec((rows, depth), lambda i: (row_block(i, near_count), 0)),
            pl.BlockSpec(weight.shape, lambda i: (0, 0, 0)),
        ],
        out_specs=out_specs,
        out_shape=out_shape,
        scratch_shapes=[pltpu.VMEM((rows, model), LOW)],
        compiler_params=pltpu.CompilerParams(vmem_limit_bytes=40 * 2**20),
        cost_estimate=pl.CostEstimate(
            flops=2 * seq_len * depth * model, bytes_accessed=2 * seq_len * model, transcendentals=0
        ),
        name=name,
    )(place, left, weight)
    return outs[count:], outs[:count]


def column_product(shard, first, last, left_ref, weight_ref, held_ref):
    weight = weight_ref[:, :shard, first:last]
    weight = weight.reshape(weight.shape[0] * shard, last - first)
    held_ref[...] = contract_cols(left_ref[...], weight).astype(LOW)


def row_product(height, left_ref, weight_ref, held_ref):
    left = left_ref[...]
    width = weight_ref.shape[2]
    for at in range(weight_ref.shape[0]):
        held_ref[:, at * width : (at + 1) * width] = rows_dot(
            left, weight_ref[at, :height, :]
        ).astype(LOW)


def ffn_blocks_kernel(seqs, members, gate_ref, up_ref, down_ref, gain_ref, first_ref, second_ref):
    shard = gate_ref.shape[0]
    width = gate_ref.shape[1] // members
    gain = as_column(gain_ref[...].astype(LOW).astype(F32), 0, shard)
    for member in range(members):
        here = slice(member * width, (member + 1) * width)
        parts = [
            (ref[:, here].astype(LOW).astype(F32) * gain).astype(LOW) for ref in (gate_ref, up_ref)
        ]
        both = jnp.concatenate(parts, 1)
        down = down_ref[here, :].astype(LOW)
        for seq in range(seqs):
            at = seq * members + member
            first_ref[at, :width, :] = down
            first_ref[at, width:, :] = both[:, :shard]
            second_ref[at] = both[:, shard:]


def ffn_blocks(w_gate, w_up, w_down, gain, seqs, members):
    shard, columns = w_gate.shape
    width = columns // members
    return pl.pallas_call(
        functools.partial(ffn_blocks_kernel, seqs, members),
        out_shape=[
            jax.ShapeDtypeStruct((seqs * members, width + shard, shard), LOW),
            jax.ShapeDtypeStruct((seqs * members, shard, 2 * width - shard), LOW),
        ],
        compiler_params=pltpu.CompilerParams(vmem_limit_bytes=40 * 2**20),
        cost_estimate=pl.CostEstimate(
            flops=0, bytes_accessed=18 * shard * columns, transcendentals=0
        ),
        name="ffn_blocks",
    )(w_gate, w_up, w_down, gain)


def ffn_kernel(near_count, count, place_ref, *refs):
    came, refs = refs[: 2 * count], refs[2 * count :]
    grad_ref, first_ref, second_ref = refs[:3]
    other_refs, mine_refs = refs[3 : 3 + count], refs[3 + count : 3 + 2 * count]
    rows_ref, act_ref, d_ref, down_ref, held_ref, sum_ref = refs[3 + 2 * count :]
    step = pl.program_id(0)
    take_rows(step, near_count, place_ref[3], came[:count], came[count:], rows_ref)
    sources, height, shard = first_ref.shape
    width = height - shard
    rows = rows_ref[...]
    block = row_block(step, near_count)
    first = block_place(block, place_ref[1], near_count) * rows.shape[0]
    valid = first + lax.broadcasted_iota(jnp.int32, (rows.shape[0], 1), 0) < place_ref[0]
    grads = only(valid, grad_ref[...])
    early = first_ref[:, width:, :].reshape(sources * shard, shard)
    late = second_ref[...].reshape(sources * shard, 2 * width - shard)
    both = jnp.concatenate([rows_dot(rows, early), rows_dot(rows, late)], 1)
    gate, up = both[:, :width], both[:, width:]
    scale, cubic = 0.7978845608028654, 0.044715
    square = gate * gate
    bent = jnp.tanh(scale * (gate + cubic * square * gate))
    half = 0.5 * (1.0 + bent)
    value = gate * half
    slope = half + 0.5 * gate * (1.0 - bent * bent) * (scale * (1.0 + 3.0 * cubic * square))
    act = (value * up).astype(LOW)
    act_ref[...] = act
    d_hidden = jnp.zeros((rows.shape[0], width), F32)
    for at in range(sources):
        d_hidden = d_hidden + contract_cols(
            grads[:, at * shard : (at + 1) * shard], first_ref[at, :width, :]
        )
    d_both = jnp.concatenate(
        [(d_hidden * up * slope).astype(LOW), (d_hidden * value).astype(LOW)], 1
    )
    d_ref[...] = d_both
    held_ref[...] = (
        contract_cols(d_both[:, :shard], early) + contract_cols(d_both[:, shard:], late)
    ).astype(LOW)
    send_rows(step, near_count, place_ref[3], held_ref, other_refs, mine_refs)
    product = contract_rows(act, grads)

    @pl.when(step == 0)
    def _():
        sum_ref[...] = product

    @pl.when(step > 0)
    def _():
        sum_ref[...] += product

    @pl.when(step == pl.num_programs(0) - 1)
    def _():
        for at in range(sources):
            down_ref[at] = sum_ref[:, at * shard : (at + 1) * shard].astype(LOW)


def feed_forward(mine, other, grads, first, second, place):
    seq_len, model = grads.shape
    near_count, count = mine[0].shape[0], len(mine)
    sources, height, shard = first.shape
    width = height - shard
    rows = seq_len // (CORES * near_count)
    out_specs, out_shape = sent_specs(near_count, count, rows // count, model)

    def blocks(columns):
        return pl.BlockSpec((rows, columns), lambda i: (row_block(i, near_count), 0))

    outs = pl.pallas_call(
        functools.partial(ffn_kernel, near_count, count),
        grid=(CORES * near_count,),
        in_specs=[
            pl.BlockSpec(memory_space=pltpu.SMEM),
            *out_specs,
            blocks(model),
            pl.BlockSpec(first.shape, lambda i: (0, 0, 0)),
            pl.BlockSpec(second.shape, lambda i: (0, 0, 0)),
        ],
        out_specs=out_specs
        + [
            blocks(model),
            blocks(width),
            blocks(2 * width),
            pl.BlockSpec((sources, width, shard), lambda i: (0, 0, 0)),
        ],
        out_shape=out_shape
        + [
            jax.ShapeDtypeStruct((seq_len, model), LOW),
            jax.ShapeDtypeStruct((seq_len, width), LOW),
            jax.ShapeDtypeStruct((seq_len, 2 * width), LOW),
            jax.ShapeDtypeStruct((sources, width, shard), LOW),
        ],
        scratch_shapes=[pltpu.VMEM((rows, model), LOW), pltpu.VMEM((width, model), F32)],
        compiler_params=pltpu.CompilerParams(vmem_limit_bytes=56 * 2**20),
        cost_estimate=pl.CostEstimate(
            flops=12 * seq_len * model * width, bytes_accessed=12 * seq_len * model, transcendentals=0
        ),
        name="feed_forward",
    )(place, *other, *mine, grads, first, second)
    return outs[count : 2 * count], outs[:count], *outs[2 * count :]


COLUMN = ("seq", "near", "core")


def exchange(blocks, axes):
    return lax.all_to_all(blocks, axes, split_axis=0, concat_axis=0, tiled=True)


def swap(block, axis):
    return lax.ppermute(block, axis, [(0, 1), (1, 0)])


def after(value, *done):
    return lax.optimization_barrier((value,) + done)[0]


def rms(values):
    return lax.rsqrt(jnp.mean(values * values, axis=-1, keepdims=True) + EPSILON)


def norm_grad(inner, normed, inverse):
    return inverse * (inner - normed * jnp.mean(inner * normed, axis=-1, keepdims=True))


def local(
    inputs,
    cotangent,
    lengths,
    attn_scale,
    w_query,
    w_key,
    w_value,
    w_out,
    rel_table,
    ffn_scale,
    w_gate,
    w_up,
    w_down,
):
    seqs = lax.axis_size("seq")
    near_count = lax.axis_size("near")
    mp_count = lax.axis_size("mp")
    members = near_count * CORES
    sources = seqs * members
    tok_rows, model = inputs.shape
    seq_len = tok_rows * members
    own_rows = tok_rows // mp_count
    half_rows = seq_len // CORES
    shard = attn_scale.shape[0]
    table_rows, heads_mp = rel_table.shape
    buckets = table_rows * sources
    heads = heads_mp // members
    width = w_query.shape[1] // members
    hidden_width = w_gate.shape[1] // members

    near_at = lax.axis_index("near")
    core_at = lax.axis_index("core")
    mp_at = lax.axis_index("mp")
    member_at = near_at * CORES + core_at
    length = lax.dynamic_slice_in_dim(lengths, lax.axis_index("seq"), 1, 0)
    place = jnp.stack(
        [length[0]] + [at.astype(jnp.int32) for at in (core_at, member_at, mp_at, near_at)]
    )

    def over_mp(own, axis):
        shape = own.shape[:axis] + (mp_count,) + own.shape[axis:]
        blocks = lax.dynamic_update_index_in_dim(jnp.zeros(shape, own.dtype), own, mp_at, axis)
        moved = [(away, shifted(own, away)) for away in reversed(range(1, mp_count))]
        for away, block in moved:
            blocks = lax.dynamic_update_index_in_dim(blocks, block, mp_at ^ away, axis)
        return blocks

    def shifted(block, away):
        return lax.ppermute(block, "mp", [(i, i ^ away) for i in range(mp_count)])

    def in_near_order(own, moved):
        return jnp.stack(
            [jnp.where(near_at == 0, own, moved), jnp.where(near_at == 0, moved, own)], 0
        )

    def near_rows(blocks):
        own = [lax.dynamic_slice_in_dim(block, mp_at * own_rows, own_rows, 0) for block in blocks]
        near = swap(jnp.stack(own), "near")
        came = [(0, near)] + [(away, shifted(near, away)) for away in range(1, mp_count)]
        halves = []
        for half in (came, [(away, swap(block, "core")) for away, block in came]):
            rows = jnp.zeros((len(blocks), mp_count, own_rows, model), near.dtype)
            for away, block in half:
                rows = lax.dynamic_update_index_in_dim(rows, block, mp_at ^ away, 1)
            halves.append([rows[i].reshape(tok_rows, model) for i in range(len(blocks))])
        return halves

    def in_order(own, moved, core, core_moved):
        rows = jnp.zeros((CORES, near_count, tok_rows, model), own.dtype)
        for at, block in enumerate((own, moved, core, core_moved)):
            rows = lax.dynamic_update_slice(
                rows, block[None, None], (at // 2, near_at ^ (at % 2), 0, 0)
            )
        return rows.reshape(seq_len, model)

    def gather_rows(near):
        mine = [near] + [shifted(near, away) for away in range(1, mp_count)]
        return mine, [swap(block, "core") for block in mine]

    def sum_cores(mine, other):
        return [
            kept.astype(F32) + swap(sent, "core").astype(F32) for kept, sent in zip(mine, other)
        ]

    def send_mp(sums):
        return [shifted(sums[away].astype(LOW), away) for away in reversed(range(1, mp_count))]

    def sum_mp(sums, *meanwhile):
        moved = send_mp(sums)
        if meanwhile:
            moved = [after(piece, *meanwhile) for piece in moved]
        return sum((piece.astype(F32) for piece in moved), sums[0])

    def split_near(pair):
        sent = jnp.where(near_at == 0, pair[1], pair[0]).astype(LOW)
        return sent, jnp.where(near_at == 0, pair[0], pair[1])

    def sum_near_both(pair):
        low = pair.astype(LOW)
        moved = swap(low, "near")
        return low.astype(F32) + moved.astype(F32), moved

    def near_pair(own, moved):
        pair = [
            lax.dynamic_slice_in_dim(block, mp_at * own_rows, own_rows, 0)
            for block in (own, moved)
        ]
        return in_near_order(*pair)

    def here(pair):
        return lax.dynamic_index_in_dim(pair, near_at, 0, keepdims=False)

    attn_sent = attention_blocks(
        (w_query, w_key, w_value), w_out, attn_scale.reshape(1, shard), rel_table, seqs, members
    )
    ffn_first, ffn_second = ffn_blocks(
        w_gate, w_up, w_down, ffn_scale.reshape(1, shard), seqs, members
    )

    attn_got = exchange(attn_sent, COLUMN)
    def partial(left, weight, product, name):
        return partial_rows(left, weight, model, place, near_count, mp_count, product, name)

    table = attn_got[:, shard : shard + table_rows, :heads_mp].reshape(buckets, heads_mp)

    def normed(rows):
        values = rows.astype(F32)
        return (values * rms(values)).astype(LOW)

    (moved_inputs, moved_cotangent), core_moved = near_rows([inputs, cotangent])
    input_parts = [inputs, moved_inputs, swap(inputs, "core"), core_moved[0]]
    grad_parts = [cotangent, moved_cotangent, swap(cotangent, "core"), core_moved[1]]
    parts = [normed(part) for part in input_parts]
    parts = lax.optimization_barrier((*parts, ffn_first, ffn_second))[:4]
    first_got = exchange(after(ffn_first, attn_got), COLUMN)

    qkv, attended, prob, out_mine, out_other = attention_forward(
        parts, attn_got, table, place, heads, shard, mp_count
    )
    normed_rows = in_order(*parts)
    grad_two = in_order(*grad_parts)
    mixed, mixed_moved = sum_near_both(
        after(sum_mp(sum_cores(out_mine, out_other)), first_got, grad_two, normed_rows)
    )
    second_got = exchange(after(ffn_second, mixed_moved), COLUMN)

    pair_inputs = near_pair(inputs, moved_inputs).astype(F32)
    after_attn = pair_inputs + mixed
    inv_two = rms(after_attn)
    normed_two = after_attn * inv_two
    mine_two, other_two = gather_rows(normed_two.astype(LOW))

    d_mine, d_other, hidden_two, acts, d_both, d_down_w = feed_forward(
        mine_two, other_two, grad_two, first_got, second_got, place
    )
    inner_cores = sum_cores(d_mine, d_other)
    down_product = functools.partial(row_product, hidden_width)
    ffn_partial = partial(after(acts, *inner_cores), first_got, down_product, "ffn_out")

    def to_owners(grad):
        return exchange(grad, COLUMN)

    def by_rows(got):
        parts = got.reshape((seqs, members) + got.shape[1:]).astype(F32)
        return jnp.sum(parts, axis=0).reshape(-1, shard)

    d_down = to_owners(after(d_down_w, *[rows.astype(LOW) for rows in inner_cores[1:]]))
    d_gate_up_w = contract_rows(hidden_two, after(d_both, *inner_cores)).astype(LOW)
    inner_two, inner_moved = sum_near_both(
        after(sum_mp(inner_cores, d_gate_up_w, *ffn_partial[0], *ffn_partial[1]), d_down)
    )
    d_gate_up = to_owners(after(d_gate_up_w, inner_moved).reshape(sources, shard, -1))

    pair_first = (
        lax.broadcasted_iota(jnp.int32, (near_count, own_rows, 1), 0) * (CORES * tok_rows)
        + lax.broadcasted_iota(jnp.int32, (near_count, own_rows, 1), 1)
        + (core_at * tok_rows + mp_at * own_rows)
    )
    pair_valid = pair_first < length
    pair_grad = near_pair(cotangent, moved_cotangent).astype(F32)
    grad_one = jnp.where(pair_valid, pair_grad, 0.0) + norm_grad(inner_two, normed_two, inv_two)
    mine_one, other_one = gather_rows(grad_one.astype(LOW))
    ffn_cores = sum_cores(*ffn_partial)
    d_qkv, d_table, rows_one = attention_backward(
        prob, mine_one, other_one, attn_got, qkv, place, heads, shard, buckets
    )
    qkv_product = functools.partial(column_product, shard, 0, 3 * width)
    ffn_moved = send_mp([after(rows, *mine_one[1:]) for rows in ffn_cores])
    inner_cores = sum_cores(
        *partial(after(d_qkv, *ffn_moved), attn_got, qkv_product, "attention_in")
    )
    inner_pair = sum_mp(inner_cores)
    table_sent = d_table[:, :heads].astype(LOW).reshape(sources, table_rows, heads)
    table_sent = jnp.pad(
        table_sent, ((0, 0), (0, EXTRA - table_rows), (0, 3 * width - heads))
    )
    d_qkv_w = contract_rows(normed_rows, d_qkv).astype(LOW).reshape(sources, shard, -1)
    d_qkv_sent = jnp.concatenate([d_qkv_w, table_sent], 1)
    d_qkv_got = to_owners(after(d_qkv_sent, d_gate_up))
    d_out = contract_rows(after(attended, inner_cores[0]), rows_one)
    d_out = jnp.moveaxis(d_out.astype(LOW).reshape(width, sources, shard), 1, 0)
    d_out = to_owners(after(d_out, d_qkv_got))

    (d_w_gate, d_w_up), ffn_gain, _ = owner_grads(
        after(d_gate_up, inner_cores[0]), (w_gate, w_up), ffn_scale.reshape(1, shard), members, None
    )
    d_w_down = by_rows(after(d_down, d_qkv))

    ffn_sent, ffn_kept = split_near(
        sum((piece.astype(F32) for piece in ffn_moved), ffn_cores[0])
    )
    inner_sent, inner_kept = split_near(inner_pair)
    came = swap(
        after(jnp.stack([ffn_sent, inner_sent]), d_qkv_got, ffn_gain, d_w_down), "near"
    )
    own_inputs = here(pair_inputs)
    inv_one = rms(own_inputs)
    grad_input = here(grad_one) + norm_grad(inner_kept + came[1].astype(F32), own_inputs * inv_one, inv_one)
    own_out = jnp.where(here(pair_valid), here(after_attn) + ffn_kept + came[0].astype(F32), 0.0)
    owned = jnp.stack([own_out.astype(LOW), grad_input.astype(LOW)])
    rows_out = [jnp.zeros((mp_count, own_rows, model), LOW)] * 2
    for away in range(mp_count):
        block = shifted(owned, away) if away else owned
        rows_out = [
            lax.dynamic_update_index_in_dim(rows, block[i], mp_at ^ away, 0)
            for i, rows in enumerate(rows_out)
        ]
    layer_out, d_inputs = (rows.reshape(tok_rows, model) for rows in rows_out)

    (d_w_query, d_w_key, d_w_value), attn_gain, d_rel_table = owner_grads(
        after(d_qkv_got, came),
        (w_query, w_key, w_value),
        attn_scale.reshape(1, shard),
        members,
        (table_rows, heads_mp),
    )
    gains = jnp.concatenate([attn_gain, ffn_gain], 0)
    gains = sum((shifted(gains, away) for away in range(1, mp_count)), gains)
    return (
        layer_out,
        d_inputs,
        gains[0],
        d_w_query,
        d_w_key,
        d_w_value,
        by_rows(d_out),
        d_rel_table,
        gains[1],
        d_w_gate,
        d_w_up,
        d_w_down,
    )


def solution(mesh):
    fsdp, mp = mesh.shape["fsdp"], mesh.shape["mp"]

    def run(*args):
        seqs = args[2].shape[0]
        members = fsdp // seqs
        inner = Mesh(
            mesh.devices.reshape(seqs, members // CORES, CORES, mp), ("seq", "near", "core", "mp")
        )
        rows, columns, first = P(COLUMN, None), P("mp", COLUMN), P(COLUMN)
        both = P(COLUMN, "mp")
        in_specs = (
            rows, rows, P(), first, both, both, both, columns, both, first, both, both, columns,
        )
        out_specs = (
            rows, rows, first, both, both, both, columns, both, first, both, both, columns,
        )
        return jax.shard_map(
            local, mesh=inner, in_specs=in_specs, out_specs=out_specs, check_vma=False
        )(*args)

    return run
```

```python
import functools

import jax
import jax.numpy as jnp
from jax import lax
from jax.experimental import pallas as pl
from jax.experimental.pallas import tpu as pltpu
from jax.sharding import Mesh, PartitionSpec as P

LOW = jnp.bfloat16
F32 = jnp.float32
CORES = 2
THRESHOLDS = (12, 16, 23, 32, 46, 64, 91)
EPSILON = 1e-06
MASKED = -1e30
SKEW = 128


def bucket_of(rel_offset):
    distance = jnp.abs(rel_offset)
    far_bucket = 8 + sum(((distance >= threshold).astype(jnp.int32) for threshold in THRESHOLDS))
    bucket_abs = jnp.where(distance < 8, distance, far_bucket)
    return bucket_abs + jnp.where(rel_offset > 0, 16, 0)


def bucket_onehot(buckets, seq_len):
    offset = lax.broadcasted_iota(jnp.int32, (buckets, 2 * seq_len), 1) - seq_len
    bucket = lax.broadcasted_iota(jnp.int32, (buckets, 2 * seq_len), 0)
    return bucket_of(offset) == bucket


def head_lanes(rows, width, head_width, head):
    lane = lax.broadcasted_iota(jnp.int32, (rows, width), 1)
    return (lane >= head * head_width) & (lane < (head + 1) * head_width)


def only(mask, values):
    return jnp.where(mask, values, jnp.zeros_like(values))


def block_place(block, core, near_count):
    return lax.rem(block, near_count) * CORES + lax.bitwise_xor(lax.div(block, near_count), core)


def bias_places(place_ref, step, blocks, rows, seq_len):
    core, near_count = place_ref[1], blocks // CORES
    query = block_place(step, core, near_count) * rows
    return [
        [
            pl.multiple_of(
                block_place(block, core, near_count) * rows - query - part * SKEW + seq_len - SKEW,
                SKEW,
            )
            for block in range(blocks)
        ]
        for part in range(rows // SKEW)
    ]


def forward_kernel(heads, shard, near_count, count, place_ref, *refs):
    own_ref, moved_ref, core_ref, core_moved_ref, got_ref, table_ref = refs[:6]
    qkv_ref, o_ref, p_ref = refs[6:9]
    other_refs, mine_refs = refs[9 : 9 + count], refs[9 + count : 9 + 2 * count]
    skew_ref, held_ref = refs[9 + 2 * count :]
    step = pl.program_id(0)
    seq_len = qkv_ref.shape[0]
    rows, width = o_ref.shape
    model = held_ref.shape[1]
    head_width = width // heads
    span = 2 * seq_len
    blocks = seq_len // rows
    block = row_block(step, near_count)

    @pl.when(step == 0)
    def _():
        weight = got_ref[:, :shard, : 3 * width].reshape(model, 3 * width)
        near = place_ref[4]
        for at, ref in enumerate((own_ref, moved_ref, core_ref, core_moved_ref)):
            first = (at // 2) * near_count + lax.bitwise_xor(near, at % 2)
            qkv_ref[pl.ds(pl.multiple_of(first * rows, rows), rows), :] = rows_dot(
                ref[...], weight
            ).astype(LOW)
        one_hot = bucket_onehot(table_ref.shape[0], seq_len)
        table = table_ref[...].astype(F32)
        column = lax.broadcasted_iota(jnp.int32, table.shape, 1)
        for head in range(heads):
            here = column == place_ref[2] * heads + head
            levels = jnp.sum(jnp.where(here, table, 0.0), axis=1, keepdims=True)
            line = jnp.sum(jnp.where(one_hot, levels, 0.0), axis=0, keepdims=True)
            line = jnp.broadcast_to(line, (SKEW, span))
            skew_ref[head] = pltpu.roll(line, span - SKEW, 1, stride=1, stride_axis=0)

    row = lax.broadcasted_iota(jnp.int32, (1, rows), 1)
    allowed = jnp.concatenate(
        [
            block_place(at, place_ref[1], near_count) * rows + row < place_ref[0]
            for at in range(blocks)
        ],
        1,
    )
    queries = qkv_ref[pl.ds(pl.multiple_of(block * rows, rows), rows), :width]
    keys = qkv_ref[:, width : 2 * width]
    values = qkv_ref[:, 2 * width :]
    total = jnp.zeros((rows, width), F32)
    places = bias_places(place_ref, block, blocks, rows, seq_len)
    for head in range(heads):
        scores = lax.dot_general(
            only(head_lanes(rows, width, head_width, head), queries),
            keys,
            (((1,), (1,)), ((), ())),
            preferred_element_type=F32,
        )
        bias = jnp.concatenate(
            [
                jnp.concatenate([skew_ref[head, :, pl.ds(place, rows)] for place in part], 1)
                for part in places
            ],
            0,
        )
        scores = jnp.where(allowed, scores + bias, MASKED)
        grown = jnp.exp(scores - jnp.max(scores, axis=1, keepdims=True))
        prob = (grown * (1.0 / jnp.sum(grown, axis=1, keepdims=True))).astype(LOW)
        p_ref[head] = prob
        total = total + jnp.dot(
            prob,
            only(head_lanes(seq_len, width, head_width, head), values),
            preferred_element_type=F32,
        )
    attended = total.astype(LOW)
    o_ref[...] = attended
    weight = got_ref[:, :shard, 3 * width :].reshape(model, width)
    held_ref[...] = contract_cols(attended, weight).astype(LOW)
    send_rows(step, near_count, place_ref[3], held_ref, other_refs, mine_refs)


def attention_forward(parts, got, table, place, heads, shard, count):
    rows, model = parts[0].shape
    blocks = len(parts)
    near_count = blocks // CORES
    seq_len, width = rows * blocks, got.shape[2] // 4
    out_specs, out_shape = sent_specs(near_count, count, rows // count, model)

    def fixed(shape):
        return pl.BlockSpec(shape, lambda i: (0,) * len(shape))

    outs = pl.pallas_call(
        functools.partial(forward_kernel, heads, shard, near_count, count),
        grid=(blocks,),
        in_specs=[pl.BlockSpec(memory_space=pltpu.SMEM)]
        + [fixed(part.shape) for part in parts]
        + [fixed(got.shape), fixed(table.shape)],
        out_specs=[
            fixed((seq_len, 3 * width)),
            pl.BlockSpec((rows, width), lambda i: (row_block(i, near_count), 0)),
            pl.BlockSpec((heads, rows, seq_len), lambda i: (0, row_block(i, near_count), 0)),
        ]
        + out_specs,
        out_shape=[
            jax.ShapeDtypeStruct((seq_len, 3 * width), LOW),
            jax.ShapeDtypeStruct((seq_len, width), LOW),
            jax.ShapeDtypeStruct((heads, seq_len, seq_len), LOW),
        ]
        + out_shape,
        scratch_shapes=[
            pltpu.VMEM((heads, SKEW, 2 * seq_len), F32),
            pltpu.VMEM((rows, model), LOW),
        ],
        compiler_params=pltpu.CompilerParams(vmem_limit_bytes=34 * 2**20),
        cost_estimate=pl.CostEstimate(
            flops=4 * seq_len * seq_len * width,
            bytes_accessed=2 * heads * seq_len * seq_len,
            transcendentals=0,
        ),
        name="attention_forward",
    )(place, *parts, got, table)
    return (*outs[:3], outs[3 + count :], outs[3 : 3 + count])


def backward_kernel(heads, shard, near_count, count, place_ref, *refs):
    came, refs = refs[: 2 * count], refs[2 * count :]
    p_ref, got_ref, qkv_ref, d_ref, dt_ref, rows_ref, dk_sum, dv_sum, skew_ref = refs
    step = pl.program_id(0)
    block = row_block(step, near_count)
    take_rows(step, near_count, place_ref[3], came[:count], came[count:], rows_ref)
    rows, model = rows_ref.shape
    seq_len = qkv_ref.shape[0]
    width = qkv_ref.shape[1] // 3
    head_width = width // heads
    span = 2 * seq_len
    blocks = seq_len // rows

    @pl.when(step == 0)
    def _():
        dk_sum[...] = jnp.zeros_like(dk_sum)
        dv_sum[...] = jnp.zeros_like(dv_sum)
        skew_ref[...] = jnp.zeros_like(skew_ref)

    here = pl.ds(pl.multiple_of(block * rows, rows), rows)
    queries = qkv_ref[here, :width]
    keys = qkv_ref[:, width : 2 * width]
    values = qkv_ref[:, 2 * width :]
    weight = got_ref[:, :shard, 3 * width :].reshape(model, width)
    grads = rows_dot(rows_ref[...], weight).astype(LOW)
    total = jnp.zeros((rows, width), F32)
    places = bias_places(place_ref, block, blocks, rows, seq_len)
    for head in range(heads):
        own = head_lanes(rows, width, head_width, head)
        own_grads = only(own, grads)
        d_prob = lax.dot_general(
            own_grads, values, (((1,), (1,)), ((), ())), preferred_element_type=F32
        )
        prob_low = p_ref[head]
        prob = prob_low.astype(F32)
        weighed = prob * d_prob
        d_scores = (weighed - prob * jnp.sum(weighed, axis=1, keepdims=True)).astype(LOW)
        total = total + jnp.dot(
            d_scores,
            only(head_lanes(seq_len, width, head_width, head), keys),
            preferred_element_type=F32,
        )
        dk_sum[...] += lax.dot_general(
            d_scores, only(own, queries), (((0,), (0,)), ((), ())), preferred_element_type=F32
        )
        dv_sum[...] += lax.dot_general(
            prob_low, own_grads, (((0,), (0,)), ((), ())), preferred_element_type=F32
        )
        for part in range(rows // SKEW):
            for at in range(blocks):
                skew_ref[head, :, pl.ds(places[part][at], rows)] += d_scores[
                    part * SKEW : (part + 1) * SKEW, at * rows : (at + 1) * rows
                ].astype(F32)
    d_ref[here, :width] = total.astype(LOW)

    @pl.when(step == pl.num_programs(0) - 1)
    def _():
        d_ref[:, width : 2 * width] = dk_sum[...].astype(LOW)
        d_ref[:, 2 * width :] = dv_sum[...].astype(LOW)
        one_hot = bucket_onehot(dt_ref.shape[0], seq_len)
        row = lax.broadcasted_iota(jnp.int32, (SKEW, span), 0)
        column = lax.broadcasted_iota(jnp.int32, dt_ref.shape, 1)
        result = jnp.zeros(dt_ref.shape, F32)
        for head in range(heads):
            level = pltpu.roll(skew_ref[head], SKEW, 1)
            bit = 1
            while bit < SKEW:
                level = jnp.where((row & bit) != 0, pltpu.roll(level, span - bit, 1), level)
                bit *= 2
            line = jnp.sum(level, axis=0, keepdims=True)
            summed = jnp.sum(jnp.where(one_hot, line, 0.0), axis=1, keepdims=True)
            result = jnp.where(column == head, summed, result)
        dt_ref[...] = result


def attention_backward(prob, mine, other, got, qkv, place, heads, shard, buckets):
    seq_len, width = qkv.shape[0], qkv.shape[1] // 3
    near_count, own_rows, model = mine[0].shape
    count = len(mine)
    rows = count * own_rows
    came_specs, _ = sent_specs(near_count, count, own_rows, model)
    return pl.pallas_call(
        functools.partial(backward_kernel, heads, shard, near_count, count),
        grid=(seq_len // rows,),
        in_specs=[
            pl.BlockSpec(memory_space=pltpu.SMEM),
            *came_specs,
            pl.BlockSpec((heads, rows, seq_len), lambda i: (0, row_block(i, near_count), 0)),
            pl.BlockSpec(got.shape, lambda i: (0, 0, 0)),
            pl.BlockSpec(qkv.shape, lambda i: (0, 0)),
        ],
        out_specs=[
            pl.BlockSpec(qkv.shape, lambda i: (0, 0)),
            pl.BlockSpec((buckets, 128), lambda i: (0, 0)),
            pl.BlockSpec((rows, model), lambda i: (row_block(i, near_count), 0)),
        ],
        out_shape=[
            jax.ShapeDtypeStruct(qkv.shape, LOW),
            jax.ShapeDtypeStruct((buckets, 128), F32),
            jax.ShapeDtypeStruct((seq_len, model), LOW),
        ],
        scratch_shapes=[
            pltpu.VMEM((seq_len, width), F32),
            pltpu.VMEM((seq_len, width), F32),
            pltpu.VMEM((heads, SKEW, 2 * seq_len), F32),
        ],
        compiler_params=pltpu.CompilerParams(vmem_limit_bytes=34 * 2**20),
        cost_estimate=pl.CostEstimate(
            flops=8 * seq_len * seq_len * width * 4,
            bytes_accessed=2 * heads * seq_len * seq_len,
            transcendentals=0,
        ),
        name="attention_backward",
    )(place, *other, *mine, prob, got, qkv)


EXTRA = 8
OWNER_ROWS = 64


def as_column(row, first, count):
    size = row.shape[1]
    here = lax.broadcasted_iota(jnp.int32, (count, size), 1) == first + lax.broadcasted_iota(
        jnp.int32, (count, size), 0
    )
    return jnp.sum(jnp.where(here, row, 0.0), axis=1, keepdims=True)


def blocks_kernel(seqs, members, q_ref, k_ref, v_ref, o_ref, gain_ref, table_ref, sent_ref):
    shard = q_ref.shape[0]
    width = q_ref.shape[1] // members
    gain = as_column(gain_ref[...].astype(LOW).astype(F32), 0, shard)
    parts = [
        (ref[...].astype(LOW).astype(F32) * gain).astype(LOW) for ref in (q_ref, k_ref, v_ref)
    ]
    parts.append(o_ref[...].T.astype(LOW))
    rest = jnp.zeros((EXTRA, sent_ref.shape[2]), LOW)
    table_rows, heads = table_ref.shape
    for seq in range(seqs):
        for member in range(members):
            at = seq * members + member
            for i, part in enumerate(parts):
                sent_ref[at, :shard, i * width : (i + 1) * width] = part[
                    :, member * width : (member + 1) * width
                ]
            sent_ref[at, shard:, :] = rest
            sent_ref[at, shard : shard + table_rows, :heads] = table_ref[...].astype(LOW)


def attention_blocks(weights, w_out, gain, table, seqs, members):
    shard, columns = weights[0].shape
    return pl.pallas_call(
        functools.partial(blocks_kernel, seqs, members),
        out_shape=jax.ShapeDtypeStruct(
            (seqs * members, shard + EXTRA, 4 * columns // members), LOW
        ),
        compiler_params=pltpu.CompilerParams(vmem_limit_bytes=60 * 2**20),
        cost_estimate=pl.CostEstimate(
            flops=0, bytes_accessed=16 * shard * columns, transcendentals=0
        ),
        name="attention_blocks",
    )(*weights, w_out, gain, table)


def owner_kernel(count, members, table_shape, *refs):
    got_ref, extra_ref = refs[:2]
    weight_refs = refs[2 : 2 + count]
    gain_ref = refs[2 + count]
    grad_refs = refs[3 + count : 3 + 2 * count]
    sum_ref = refs[3 + 2 * count]
    step = pl.program_id(0)
    rows = got_ref.shape[1]
    seqs = got_ref.shape[0] // members
    width = got_ref.shape[2] // count
    size = sum_ref.shape[1]
    gain = as_column(gain_ref[...].astype(LOW).astype(F32), step * rows, rows)
    total = jnp.zeros((rows, 1), F32)
    for member in range(members):
        product = sum(got_ref[seq * members + member].astype(F32) for seq in range(seqs))
        for i in range(count):
            part = product[:, i * width : (i + 1) * width]
            here = pl.ds(member * width, width)
            grad_refs[i][:, here] = part * gain
            weight = weight_refs[i][:, here].astype(LOW).astype(F32)
            total = total + jnp.sum(weight * part, axis=1, keepdims=True)

    @pl.when(step == 0)
    def _():
        sum_ref[...] = jnp.zeros_like(sum_ref)

    diagonal = lax.broadcasted_iota(jnp.int32, (rows, size), 1) == step * rows + (
        lax.broadcasted_iota(jnp.int32, (rows, size), 0)
    )
    sum_ref[...] += jnp.sum(jnp.where(diagonal, total, 0.0), axis=0, keepdims=True)
    if table_shape is not None:
        table_rows, heads = table_shape
        each = heads // members
        for member in range(members):
            piece = sum(extra_ref[seq * members + member].astype(F32) for seq in range(seqs))
            refs[-1][:, member * each : (member + 1) * each] = piece[:table_rows, :each]


def owner_grads(got, weights, gain, members, table_shape):
    sources, height, columns = got.shape
    shard, wide = weights[0].shape
    count = len(weights)
    rows = min(OWNER_ROWS, shard)
    step_rows = pl.BlockSpec((rows, wide), lambda i: (i, 0))
    row = pl.BlockSpec((1, shard), lambda i: (0, 0))
    last = height // EXTRA - 1
    out_specs = [step_rows] * count + [row]
    out_shape = [jax.ShapeDtypeStruct((shard, wide), F32)] * count
    out_shape.append(jax.ShapeDtypeStruct((1, shard), F32))
    if table_shape is not None:
        out_specs.append(pl.BlockSpec(table_shape, lambda i: (0, 0)))
        out_shape.append(jax.ShapeDtypeStruct(table_shape, F32))
    outs = pl.pallas_call(
        functools.partial(owner_kernel, count, members, table_shape),
        grid=(shard // rows,),
        in_specs=[
            pl.BlockSpec((sources, rows, columns), lambda i: (0, i, 0)),
            pl.BlockSpec((sources, EXTRA, columns), lambda i: (0, last, 0)),
        ]
        + [step_rows] * count
        + [row],
        out_specs=out_specs,
        out_shape=out_shape,
        compiler_params=pltpu.CompilerParams(vmem_limit_bytes=32 * 2**20),
        cost_estimate=pl.CostEstimate(
            flops=0, bytes_accessed=10 * count * shard * wide, transcendentals=0
        ),
        name="owner_grads",
    )(got, got, *weights, gain)
    return outs[:count], outs[count], outs[-1] if table_shape is not None else None


def rows_dot(left, right):
    return jnp.dot(left, right, preferred_element_type=F32)


def contract_cols(left, right):
    return lax.dot_general(left, right, (((1,), (1,)), ((), ())), preferred_element_type=F32)


def contract_rows(left, right):
    return lax.dot_general(left, right, (((0,), (0,)), ((), ())), preferred_element_type=F32)

def row_block(step, near_count):
    return lax.rem(step + near_count, CORES * near_count)


def send_rows(step, near_count, mp_at, held_ref, other_refs, mine_refs):
    count = len(other_refs)
    own_rows = held_ref.shape[0] // count

    def write(refs):
        for away, ref in enumerate(refs):
            first = pl.multiple_of(lax.bitwise_xor(mp_at, away) * own_rows, own_rows)
            ref[0] = held_ref[pl.ds(first, own_rows), :]

    @pl.when(step < near_count)
    def _():
        write(other_refs)

    @pl.when(step >= near_count)
    def _():
        write(mine_refs)


def take_rows(step, near_count, mp_at, other_refs, mine_refs, rows_ref):
    own_rows = other_refs[0].shape[1]

    def read(refs):
        for away, ref in enumerate(refs):
            first = pl.multiple_of(lax.bitwise_xor(mp_at, away) * own_rows, own_rows)
            rows_ref[pl.ds(first, own_rows), :] = ref[0]

    @pl.when(step < near_count)
    def _():
        read(other_refs)

    @pl.when(step >= near_count)
    def _():
        read(mine_refs)


def sent_specs(near_count, count, own_rows, model):
    other = pl.BlockSpec((1, own_rows, model), lambda i: (jnp.minimum(i, near_count - 1), 0, 0))
    mine = pl.BlockSpec((1, own_rows, model), lambda i: (jnp.maximum(i - near_count, 0), 0, 0))
    shape = jax.ShapeDtypeStruct((near_count, own_rows, model), LOW)
    return [other] * count + [mine] * count, [shape] * (2 * count)


def partial_kernel(near_count, count, product, place_ref, left_ref, weight_ref, *refs):
    held_ref = refs[-1]
    product(left_ref, weight_ref, held_ref)
    send_rows(
        pl.program_id(0), near_count, place_ref[3], held_ref, refs[:count], refs[count : 2 * count]
    )


def partial_rows(left, weight, model, place, near_count, count, product, name):
    seq_len, depth = left.shape
    rows = seq_len // (CORES * near_count)
    out_specs, out_shape = sent_specs(near_count, count, rows // count, model)
    outs = pl.pallas_call(
        functools.partial(partial_kernel, near_count, count, product),
        grid=(CORES * near_count,),
        in_specs=[
            pl.BlockSpec(memory_space=pltpu.SMEM),
            pl.BlockSpec((rows, depth), lambda i: (row_block(i, near_count), 0)),
            pl.BlockSpec(weight.shape, lambda i: (0, 0, 0)),
        ],
        out_specs=out_specs,
        out_shape=out_shape,
        scratch_shapes=[pltpu.VMEM((rows, model), LOW)],
        compiler_params=pltpu.CompilerParams(vmem_limit_bytes=40 * 2**20),
        cost_estimate=pl.CostEstimate(
            flops=2 * seq_len * depth * model, bytes_accessed=2 * seq_len * model, transcendentals=0
        ),
        name=name,
    )(place, left, weight)
    return outs[count:], outs[:count]


def column_product(shard, first, last, left_ref, weight_ref, held_ref):
    weight = weight_ref[:, :shard, first:last]
    weight = weight.reshape(weight.shape[0] * shard, last - first)
    held_ref[...] = contract_cols(left_ref[...], weight).astype(LOW)


def row_product(height, left_ref, weight_ref, held_ref):
    left = left_ref[...]
    width = weight_ref.shape[2]
    for at in range(weight_ref.shape[0]):
        held_ref[:, at * width : (at + 1) * width] = rows_dot(
            left, weight_ref[at, :height, :]
        ).astype(LOW)


def ffn_blocks_kernel(seqs, members, gate_ref, up_ref, down_ref, gain_ref, first_ref, second_ref):
    shard = gate_ref.shape[0]
    width = gate_ref.shape[1] // members
    gain = as_column(gain_ref[...].astype(LOW).astype(F32), 0, shard)
    for member in range(members):
        here = slice(member * width, (member + 1) * width)
        parts = [
            (ref[:, here].astype(LOW).astype(F32) * gain).astype(LOW) for ref in (gate_ref, up_ref)
        ]
        both = jnp.concatenate(parts, 1)
        down = down_ref[here, :].astype(LOW)
        for seq in range(seqs):
            at = seq * members + member
            first_ref[at, :width, :] = down
            first_ref[at, width:, :] = both[:, :shard]
            second_ref[at] = both[:, shard:]


def ffn_blocks(w_gate, w_up, w_down, gain, seqs, members):
    shard, columns = w_gate.shape
    width = columns // members
    return pl.pallas_call(
        functools.partial(ffn_blocks_kernel, seqs, members),
        out_shape=[
            jax.ShapeDtypeStruct((seqs * members, width + shard, shard), LOW),
            jax.ShapeDtypeStruct((seqs * members, shard, 2 * width - shard), LOW),
        ],
        compiler_params=pltpu.CompilerParams(vmem_limit_bytes=40 * 2**20),
        cost_estimate=pl.CostEstimate(
            flops=0, bytes_accessed=18 * shard * columns, transcendentals=0
        ),
        name="ffn_blocks",
    )(w_gate, w_up, w_down, gain)


def ffn_kernel(near_count, count, place_ref, *refs):
    came, refs = refs[: 2 * count], refs[2 * count :]
    grad_ref, first_ref, second_ref = refs[:3]
    other_refs, mine_refs = refs[3 : 3 + count], refs[3 + count : 3 + 2 * count]
    rows_ref, act_ref, d_ref, down_ref, held_ref, sum_ref = refs[3 + 2 * count :]
    step = pl.program_id(0)
    take_rows(step, near_count, place_ref[3], came[:count], came[count:], rows_ref)
    sources, height, shard = first_ref.shape
    width = height - shard
    rows = rows_ref[...]
    block = row_block(step, near_count)
    first = block_place(block, place_ref[1], near_count) * rows.shape[0]
    valid = first + lax.broadcasted_iota(jnp.int32, (rows.shape[0], 1), 0) < place_ref[0]
    grads = only(valid, grad_ref[...])
    early = first_ref[:, width:, :].reshape(sources * shard, shard)
    late = second_ref[...].reshape(sources * shard, 2 * width - shard)
    both = jnp.concatenate([rows_dot(rows, early), rows_dot(rows, late)], 1)
    gate, up = both[:, :width], both[:, width:]
    scale, cubic = 0.7978845608028654, 0.044715
    square = gate * gate
    bent = jnp.tanh(scale * (gate + cubic * square * gate))
    half = 0.5 * (1.0 + bent)
    value = gate * half
    slope = half + 0.5 * gate * (1.0 - bent * bent) * (scale * (1.0 + 3.0 * cubic * square))
    act = (value * up).astype(LOW)
    act_ref[...] = act
    d_hidden = jnp.zeros((rows.shape[0], width), F32)
    for at in range(sources):
        d_hidden = d_hidden + contract_cols(
            grads[:, at * shard : (at + 1) * shard], first_ref[at, :width, :]
        )
    d_both = jnp.concatenate(
        [(d_hidden * up * slope).astype(LOW), (d_hidden * value).astype(LOW)], 1
    )
    d_ref[...] = d_both
    held_ref[...] = (
        contract_cols(d_both[:, :shard], early) + contract_cols(d_both[:, shard:], late)
    ).astype(LOW)
    send_rows(step, near_count, place_ref[3], held_ref, other_refs, mine_refs)
    product = contract_rows(act, grads)

    @pl.when(step == 0)
    def _():
        sum_ref[...] = product

    @pl.when(step > 0)
    def _():
        sum_ref[...] += product

    @pl.when(step == pl.num_programs(0) - 1)
    def _():
        for at in range(sources):
            down_ref[at] = sum_ref[:, at * shard : (at + 1) * shard].astype(LOW)


def feed_forward(mine, other, grads, first, second, place):
    seq_len, model = grads.shape
    near_count, count = mine[0].shape[0], len(mine)
    sources, height, shard = first.shape
    width = height - shard
    rows = seq_len // (CORES * near_count)
    out_specs, out_shape = sent_specs(near_count, count, rows // count, model)

    def blocks(columns):
        return pl.BlockSpec((rows, columns), lambda i: (row_block(i, near_count), 0))

    outs = pl.pallas_call(
        functools.partial(ffn_kernel, near_count, count),
        grid=(CORES * near_count,),
        in_specs=[
            pl.BlockSpec(memory_space=pltpu.SMEM),
            *out_specs,
            blocks(model),
            pl.BlockSpec(first.shape, lambda i: (0, 0, 0)),
            pl.BlockSpec(second.shape, lambda i: (0, 0, 0)),
        ],
        out_specs=out_specs
        + [
            blocks(model),
            blocks(width),
            blocks(2 * width),
            pl.BlockSpec((sources, width, shard), lambda i: (0, 0, 0)),
        ],
        out_shape=out_shape
        + [
            jax.ShapeDtypeStruct((seq_len, model), LOW),
            jax.ShapeDtypeStruct((seq_len, width), LOW),
            jax.ShapeDtypeStruct((seq_len, 2 * width), LOW),
            jax.ShapeDtypeStruct((sources, width, shard), LOW),
        ],
        scratch_shapes=[pltpu.VMEM((rows, model), LOW), pltpu.VMEM((width, model), F32)],
        compiler_params=pltpu.CompilerParams(vmem_limit_bytes=56 * 2**20),
        cost_estimate=pl.CostEstimate(
            flops=12 * seq_len * model * width, bytes_accessed=12 * seq_len * model, transcendentals=0
        ),
        name="feed_forward",
    )(place, *other, *mine, grads, first, second)
    return outs[count : 2 * count], outs[:count], *outs[2 * count :]


COLUMN = ("seq", "near", "core")


def exchange(blocks, axes):
    return lax.all_to_all(blocks, axes, split_axis=0, concat_axis=0, tiled=True)


def swap(block, axis):
    return lax.ppermute(block, axis, [(0, 1), (1, 0)])


def after(value, *done):
    return lax.optimization_barrier((value,) + done)[0]


def rms(values):
    return lax.rsqrt(jnp.mean(values * values, axis=-1, keepdims=True) + EPSILON)


def norm_grad(inner, normed, inverse):
    return inverse * (inner - normed * jnp.mean(inner * normed, axis=-1, keepdims=True))


def local(
    inputs,
    cotangent,
    lengths,
    attn_scale,
    w_query,
    w_key,
    w_value,
    w_out,
    rel_table,
    ffn_scale,
    w_gate,
    w_up,
    w_down,
):
    seqs = lax.axis_size("seq")
    near_count = lax.axis_size("near")
    mp_count = lax.axis_size("mp")
    members = near_count * CORES
    sources = seqs * members
    tok_rows, model = inputs.shape
    seq_len = tok_rows * members
    own_rows = tok_rows // mp_count
    half_rows = seq_len // CORES
    shard = attn_scale.shape[0]
    table_rows, heads_mp = rel_table.shape
    buckets = table_rows * sources
    heads = heads_mp // members
    width = w_query.shape[1] // members
    hidden_width = w_gate.shape[1] // members

    near_at = lax.axis_index("near")
    core_at = lax.axis_index("core")
    mp_at = lax.axis_index("mp")
    member_at = near_at * CORES + core_at
    length = lax.dynamic_slice_in_dim(lengths, lax.axis_index("seq"), 1, 0)
    place = jnp.stack(
        [length[0]] + [at.astype(jnp.int32) for at in (core_at, member_at, mp_at, near_at)]
    )

    def over_mp(own, axis):
        shape = own.shape[:axis] + (mp_count,) + own.shape[axis:]
        blocks = lax.dynamic_update_index_in_dim(jnp.zeros(shape, own.dtype), own, mp_at, axis)
        moved = [(away, shifted(own, away)) for away in reversed(range(1, mp_count))]
        for away, block in moved:
            blocks = lax.dynamic_update_index_in_dim(blocks, block, mp_at ^ away, axis)
        return blocks

    def shifted(block, away):
        return lax.ppermute(block, "mp", [(i, i ^ away) for i in range(mp_count)])

    def in_near_order(own, moved):
        return jnp.stack(
            [jnp.where(near_at == 0, own, moved), jnp.where(near_at == 0, moved, own)], 0
        )

    def near_rows(blocks):
        own = [lax.dynamic_slice_in_dim(block, mp_at * own_rows, own_rows, 0) for block in blocks]
        near = swap(jnp.stack(own), "near")
        came = [(0, near)] + [(away, shifted(near, away)) for away in range(1, mp_count)]
        halves = []
        for half in (came, [(away, swap(block, "core")) for away, block in came]):
            rows = jnp.zeros((len(blocks), mp_count, own_rows, model), near.dtype)
            for away, block in half:
                rows = lax.dynamic_update_index_in_dim(rows, block, mp_at ^ away, 1)
            halves.append([rows[i].reshape(tok_rows, model) for i in range(len(blocks))])
        return halves

    def in_order(own, moved, core, core_moved):
        rows = jnp.zeros((CORES, near_count, tok_rows, model), own.dtype)
        for at, block in enumerate((own, moved, core, core_moved)):
            rows = lax.dynamic_update_slice(
                rows, block[None, None], (at // 2, near_at ^ (at % 2), 0, 0)
            )
        return rows.reshape(seq_len, model)

    def gather_rows(near):
        mine = [near] + [shifted(near, away) for away in range(1, mp_count)]
        return mine, [swap(block, "core") for block in mine]

    def sum_cores(mine, other):
        return [
            kept.astype(F32) + swap(sent, "core").astype(F32) for kept, sent in zip(mine, other)
        ]

    def send_mp(sums):
        return [shifted(sums[away].astype(LOW), away) for away in reversed(range(1, mp_count))]

    def sum_mp(sums, *meanwhile):
        moved = send_mp(sums)
        if meanwhile:
            moved = [after(piece, *meanwhile) for piece in moved]
        return sum((piece.astype(F32) for piece in moved), sums[0])

    def split_near(pair):
        sent = jnp.where(near_at == 0, pair[1], pair[0]).astype(LOW)
        return sent, jnp.where(near_at == 0, pair[0], pair[1])

    def sum_near_both(pair):
        low = pair.astype(LOW)
        moved = swap(low, "near")
        return low.astype(F32) + moved.astype(F32), moved

    def near_pair(own, moved):
        pair = [
            lax.dynamic_slice_in_dim(block, mp_at * own_rows, own_rows, 0)
            for block in (own, moved)
        ]
        return in_near_order(*pair)

    def here(pair):
        return lax.dynamic_index_in_dim(pair, near_at, 0, keepdims=False)

    attn_sent = attention_blocks(
        (w_query, w_key, w_value), w_out, attn_scale.reshape(1, shard), rel_table, seqs, members
    )
    attn_got = exchange(attn_sent, COLUMN)
    def partial(left, weight, product, name):
        return partial_rows(left, weight, model, place, near_count, mp_count, product, name)

    table = attn_got[:, shard : shard + table_rows, :heads_mp].reshape(buckets, heads_mp)

    def normed(rows):
        values = rows.astype(F32)
        return (values * rms(values)).astype(LOW)

    (moved_inputs, moved_cotangent), core_moved = near_rows([inputs, cotangent])
    input_parts = [inputs, moved_inputs, swap(after(inputs, moved_inputs), "core"), core_moved[0]]
    core_cotangent = swap(after(cotangent, moved_inputs), "core")
    grad_parts = [cotangent, moved_cotangent, core_cotangent, core_moved[1]]
    ffn_first, ffn_second = ffn_blocks(
        w_gate, w_up, w_down, after(ffn_scale.reshape(1, shard), moved_inputs), seqs, members
    )
    parts = [normed(part) for part in input_parts]
    parts = lax.optimization_barrier((*parts, ffn_first, ffn_second))[:4]
    first_got = exchange(after(ffn_first, attn_got), COLUMN)

    qkv, attended, prob, out_mine, out_other = attention_forward(
        parts, attn_got, table, place, heads, shard, mp_count
    )
    normed_rows = in_order(*parts)
    grad_two = in_order(*grad_parts)
    mixed, mixed_moved = sum_near_both(
        after(sum_mp(sum_cores(out_mine, out_other)), first_got, grad_two, normed_rows)
    )
    second_got = exchange(after(ffn_second, mixed_moved), COLUMN)

    pair_inputs = near_pair(inputs, moved_inputs).astype(F32)
    after_attn = pair_inputs + mixed
    inv_two = rms(after_attn)
    normed_two = after_attn * inv_two
    mine_two, other_two = gather_rows(normed_two.astype(LOW))

    d_mine, d_other, hidden_two, acts, d_both, d_down_w = feed_forward(
        mine_two, other_two, grad_two, first_got, second_got, place
    )
    inner_cores = sum_cores(d_mine, d_other)
    down_product = functools.partial(row_product, hidden_width)
    ffn_partial = partial(after(acts, *inner_cores), first_got, down_product, "ffn_out")

    def to_owners(grad):
        return exchange(grad, COLUMN)

    def by_rows(got):
        parts = got.reshape((seqs, members) + got.shape[1:]).astype(F32)
        return jnp.sum(parts, axis=0).reshape(-1, shard)

    d_down = to_owners(after(d_down_w, inner_cores[mp_count - 1].astype(LOW)))
    d_gate_up_w = contract_rows(hidden_two, after(d_both, *inner_cores)).astype(LOW)
    inner_two, inner_moved = sum_near_both(
        after(sum_mp(inner_cores, d_gate_up_w, *ffn_partial[0], *ffn_partial[1]), d_down)
    )

    pair_first = (
        lax.broadcasted_iota(jnp.int32, (near_count, own_rows, 1), 0) * (CORES * tok_rows)
        + lax.broadcasted_iota(jnp.int32, (near_count, own_rows, 1), 1)
        + (core_at * tok_rows + mp_at * own_rows)
    )
    pair_valid = pair_first < length
    pair_grad = near_pair(cotangent, moved_cotangent).astype(F32)
    grad_one = jnp.where(pair_valid, pair_grad, 0.0) + norm_grad(inner_two, normed_two, inv_two)
    grad_one_low = grad_one.astype(LOW)
    mine_one, other_one = gather_rows(grad_one_low)
    d_gate_up = to_owners(
        after(d_gate_up_w, inner_moved, grad_one_low).reshape(sources, shard, -1)
    )
    ffn_cores = sum_cores(*ffn_partial)
    d_qkv, d_table, rows_one = attention_backward(
        prob, mine_one, other_one, attn_got, qkv, place, heads, shard, buckets
    )
    qkv_product = functools.partial(column_product, shard, 0, 3 * width)
    ffn_moved = send_mp([after(rows, *mine_one[1:]) for rows in ffn_cores])
    inner_cores = sum_cores(
        *partial(after(d_qkv, *ffn_moved), attn_got, qkv_product, "attention_in")
    )
    inner_pair = sum_mp(inner_cores)
    table_sent = d_table[:, :heads].astype(LOW).reshape(sources, table_rows, heads)
    table_sent = jnp.pad(
        table_sent, ((0, 0), (0, EXTRA - table_rows), (0, 3 * width - heads))
    )
    d_qkv_w = contract_rows(normed_rows, d_qkv).astype(LOW).reshape(sources, shard, -1)
    d_qkv_sent = jnp.concatenate([d_qkv_w, table_sent], 1)
    d_qkv_got = to_owners(after(d_qkv_sent, d_gate_up))
    d_out = contract_rows(after(attended, inner_cores[0]), rows_one)
    d_out = jnp.moveaxis(d_out.astype(LOW).reshape(width, sources, shard), 1, 0)

    (d_w_gate, d_w_up), ffn_gain, _ = owner_grads(
        after(d_gate_up, inner_cores[0]), (w_gate, w_up), ffn_scale.reshape(1, shard), members, None
    )
    d_w_down = by_rows(after(d_down, d_qkv))

    ffn_sent, ffn_kept = split_near(
        sum((piece.astype(F32) for piece in ffn_moved), ffn_cores[0])
    )
    inner_sent, inner_kept = split_near(inner_pair)
    came = swap(
        after(jnp.stack([ffn_sent, inner_sent]), d_qkv_got, ffn_gain, d_w_down), "near"
    )
    own_inputs = here(pair_inputs)
    inv_one = rms(own_inputs)
    grad_input = here(grad_one) + norm_grad(inner_kept + came[1].astype(F32), own_inputs * inv_one, inv_one)
    own_out = jnp.where(here(pair_valid), here(after_attn) + ffn_kept + came[0].astype(F32), 0.0)
    owned = jnp.stack([own_out.astype(LOW), grad_input.astype(LOW)])
    rows_out = [jnp.zeros((mp_count, own_rows, model), LOW)] * 2
    blocks_out = [owned] + [shifted(owned, away) for away in range(1, mp_count)]
    d_out = to_owners(after(d_out, came))
    for away, block in enumerate(blocks_out):
        rows_out = [
            lax.dynamic_update_index_in_dim(rows, block[i], mp_at ^ away, 0)
            for i, rows in enumerate(rows_out)
        ]
    layer_out, d_inputs = (rows.reshape(tok_rows, model) for rows in rows_out)

    (d_w_query, d_w_key, d_w_value), attn_gain, d_rel_table = owner_grads(
        after(d_qkv_got, blocks_out[1]),
        (w_query, w_key, w_value),
        attn_scale.reshape(1, shard),
        members,
        (table_rows, heads_mp),
    )
    gains = jnp.concatenate([attn_gain, ffn_gain], 0)
    gains = sum((shifted(gains, away) for away in range(1, mp_count)), gains)
    return (
        layer_out,
        d_inputs,
        gains[0],
        d_w_query,
        d_w_key,
        d_w_value,
        by_rows(d_out),
        d_rel_table,
        gains[1],
        d_w_gate,
        d_w_up,
        d_w_down,
    )


def solution(mesh):
    fsdp, mp = mesh.shape["fsdp"], mesh.shape["mp"]

    def run(*args):
        seqs = args[2].shape[0]
        members = fsdp // seqs
        inner = Mesh(
            mesh.devices.reshape(seqs, members // CORES, CORES, mp), ("seq", "near", "core", "mp")
        )
        rows, columns, first = P(COLUMN, None), P("mp", COLUMN), P(COLUMN)
        both = P(COLUMN, "mp")
        in_specs = (
            rows, rows, P(), first, both, both, both, columns, both, first, both, both, columns,
        )
        out_specs = (
            rows, rows, first, both, both, both, columns, both, first, both, both, columns,
        )
        return jax.shard_map(
            local, mesh=inner, in_specs=in_specs, out_specs=out_specs, check_vma=False
        )(*args)

    return run
```

```python
import functools

import jax
import jax.numpy as jnp
from jax import lax
from jax.experimental import pallas as pl
from jax.experimental.pallas import tpu as pltpu
from jax.sharding import Mesh, PartitionSpec as P

LOW = jnp.bfloat16
F32 = jnp.float32
CORES = 2
THRESHOLDS = (12, 16, 23, 32, 46, 64, 91)
EPSILON = 1e-06
MASKED = -1e30
SKEW = 128


def bucket_of(rel_offset):
    distance = jnp.abs(rel_offset)
    far_bucket = 8 + sum(((distance >= threshold).astype(jnp.int32) for threshold in THRESHOLDS))
    bucket_abs = jnp.where(distance < 8, distance, far_bucket)
    return bucket_abs + jnp.where(rel_offset > 0, 16, 0)


def bucket_onehot(buckets, seq_len):
    offset = lax.broadcasted_iota(jnp.int32, (buckets, 2 * seq_len), 1) - seq_len
    bucket = lax.broadcasted_iota(jnp.int32, (buckets, 2 * seq_len), 0)
    return bucket_of(offset) == bucket


def head_lanes(rows, width, head_width, head):
    lane = lax.broadcasted_iota(jnp.int32, (rows, width), 1)
    return (lane >= head * head_width) & (lane < (head + 1) * head_width)


def only(mask, values):
    return jnp.where(mask, values, jnp.zeros_like(values))


def block_place(block, core, near_count):
    return lax.rem(block, near_count) * CORES + lax.bitwise_xor(lax.div(block, near_count), core)


def bias_places(place_ref, step, blocks, rows, seq_len):
    core, near_count = place_ref[1], blocks // CORES
    query = block_place(step, core, near_count) * rows
    return [
        [
            pl.multiple_of(
                block_place(block, core, near_count) * rows - query - part * SKEW + seq_len - SKEW,
                SKEW,
            )
            for block in range(blocks)
        ]
        for part in range(rows // SKEW)
    ]


def forward_kernel(heads, shard, near_count, count, place_ref, *refs):
    own_ref, moved_ref, core_ref, core_moved_ref, got_ref, table_ref = refs[:6]
    qkv_ref, o_ref, p_ref = refs[6:9]
    other_refs, mine_refs = refs[9 : 9 + count], refs[9 + count : 9 + 2 * count]
    skew_ref, held_ref = refs[9 + 2 * count :]
    step = pl.program_id(0)
    seq_len = qkv_ref.shape[0]
    rows, width = o_ref.shape
    model = held_ref.shape[1]
    head_width = width // heads
    span = 2 * seq_len
    blocks = seq_len // rows
    block = row_block(step, near_count)

    @pl.when(step == 0)
    def _():
        weight = got_ref[:, :shard, : 3 * width].reshape(model, 3 * width)
        near = place_ref[4]
        for at, ref in enumerate((own_ref, moved_ref, core_ref, core_moved_ref)):
            first = (at // 2) * near_count + lax.bitwise_xor(near, at % 2)
            qkv_ref[pl.ds(pl.multiple_of(first * rows, rows), rows), :] = rows_dot(
                ref[...], weight
            ).astype(LOW)
        one_hot = bucket_onehot(table_ref.shape[0], seq_len)
        table = table_ref[...].astype(F32)
        column = lax.broadcasted_iota(jnp.int32, table.shape, 1)
        for head in range(heads):
            here = column == place_ref[2] * heads + head
            levels = jnp.sum(jnp.where(here, table, 0.0), axis=1, keepdims=True)
            line = jnp.sum(jnp.where(one_hot, levels, 0.0), axis=0, keepdims=True)
            line = jnp.broadcast_to(line, (SKEW, span))
            skew_ref[head] = pltpu.roll(line, span - SKEW, 1, stride=1, stride_axis=0)

    row = lax.broadcasted_iota(jnp.int32, (1, rows), 1)
    allowed = jnp.concatenate(
        [
            block_place(at, place_ref[1], near_count) * rows + row < place_ref[0]
            for at in range(blocks)
        ],
        1,
    )
    queries = qkv_ref[pl.ds(pl.multiple_of(block * rows, rows), rows), :width]
    keys = qkv_ref[:, width : 2 * width]
    values = qkv_ref[:, 2 * width :]
    total = jnp.zeros((rows, width), F32)
    places = bias_places(place_ref, block, blocks, rows, seq_len)
    for head in range(heads):
        scores = lax.dot_general(
            only(head_lanes(rows, width, head_width, head), queries),
            keys,
            (((1,), (1,)), ((), ())),
            preferred_element_type=F32,
        )
        bias = jnp.concatenate(
            [
                jnp.concatenate([skew_ref[head, :, pl.ds(place, rows)] for place in part], 1)
                for part in places
            ],
            0,
        )
        scores = jnp.where(allowed, scores + bias, MASKED)
        grown = jnp.exp(scores - jnp.max(scores, axis=1, keepdims=True))
        prob = (grown * (1.0 / jnp.sum(grown, axis=1, keepdims=True))).astype(LOW)
        p_ref[head] = prob
        total = total + jnp.dot(
            prob,
            only(head_lanes(seq_len, width, head_width, head), values),
            preferred_element_type=F32,
        )
    attended = total.astype(LOW)
    o_ref[...] = attended
    weight = got_ref[:, :shard, 3 * width :].reshape(model, width)
    held_ref[...] = contract_cols(attended, weight).astype(LOW)
    send_rows(step, near_count, place_ref[3], held_ref, other_refs, mine_refs)


def attention_forward(parts, got, table, place, heads, shard, count):
    rows, model = parts[0].shape
    blocks = len(parts)
    near_count = blocks // CORES
    seq_len, width = rows * blocks, got.shape[2] // 4
    out_specs, out_shape = sent_specs(near_count, count, rows // count, model)

    def fixed(shape):
        return pl.BlockSpec(shape, lambda i: (0,) * len(shape))

    outs = pl.pallas_call(
        functools.partial(forward_kernel, heads, shard, near_count, count),
        grid=(blocks,),
        in_specs=[pl.BlockSpec(memory_space=pltpu.SMEM)]
        + [fixed(part.shape) for part in parts]
        + [fixed(got.shape), fixed(table.shape)],
        out_specs=[
            fixed((seq_len, 3 * width)),
            pl.BlockSpec((rows, width), lambda i: (row_block(i, near_count), 0)),
            pl.BlockSpec((heads, rows, seq_len), lambda i: (0, row_block(i, near_count), 0)),
        ]
        + out_specs,
        out_shape=[
            jax.ShapeDtypeStruct((seq_len, 3 * width), LOW),
            jax.ShapeDtypeStruct((seq_len, width), LOW),
            jax.ShapeDtypeStruct((heads, seq_len, seq_len), LOW),
        ]
        + out_shape,
        scratch_shapes=[
            pltpu.VMEM((heads, SKEW, 2 * seq_len), F32),
            pltpu.VMEM((rows, model), LOW),
        ],
        compiler_params=pltpu.CompilerParams(vmem_limit_bytes=34 * 2**20),
        cost_estimate=pl.CostEstimate(
            flops=4 * seq_len * seq_len * width,
            bytes_accessed=2 * heads * seq_len * seq_len,
            transcendentals=0,
        ),
        name="attention_forward",
    )(place, *parts, got, table)
    return (*outs[:3], outs[3 + count :], outs[3 : 3 + count])


def backward_kernel(heads, shard, near_count, count, place_ref, *refs):
    came, refs = refs[: 2 * count], refs[2 * count :]
    p_ref, got_ref, qkv_ref, d_ref, dt_ref, rows_ref, dk_sum, dv_sum, skew_ref = refs
    step = pl.program_id(0)
    block = row_block(step, near_count)
    take_rows(step, near_count, place_ref[3], came[:count], came[count:], rows_ref)
    rows, model = rows_ref.shape
    seq_len = qkv_ref.shape[0]
    width = qkv_ref.shape[1] // 3
    head_width = width // heads
    span = 2 * seq_len
    blocks = seq_len // rows

    @pl.when(step == 0)
    def _():
        dk_sum[...] = jnp.zeros_like(dk_sum)
        dv_sum[...] = jnp.zeros_like(dv_sum)
        skew_ref[...] = jnp.zeros_like(skew_ref)

    here = pl.ds(pl.multiple_of(block * rows, rows), rows)
    queries = qkv_ref[here, :width]
    keys = qkv_ref[:, width : 2 * width]
    values = qkv_ref[:, 2 * width :]
    weight = got_ref[:, :shard, 3 * width :].reshape(model, width)
    grads = rows_dot(rows_ref[...], weight).astype(LOW)
    total = jnp.zeros((rows, width), F32)
    places = bias_places(place_ref, block, blocks, rows, seq_len)
    for head in range(heads):
        own = head_lanes(rows, width, head_width, head)
        own_grads = only(own, grads)
        d_prob = lax.dot_general(
            own_grads, values, (((1,), (1,)), ((), ())), preferred_element_type=F32
        )
        prob_low = p_ref[head]
        prob = prob_low.astype(F32)
        weighed = prob * d_prob
        d_scores = (weighed - prob * jnp.sum(weighed, axis=1, keepdims=True)).astype(LOW)
        total = total + jnp.dot(
            d_scores,
            only(head_lanes(seq_len, width, head_width, head), keys),
            preferred_element_type=F32,
        )
        dk_sum[...] += lax.dot_general(
            d_scores, only(own, queries), (((0,), (0,)), ((), ())), preferred_element_type=F32
        )
        dv_sum[...] += lax.dot_general(
            prob_low, own_grads, (((0,), (0,)), ((), ())), preferred_element_type=F32
        )
        for part in range(rows // SKEW):
            for at in range(blocks):
                skew_ref[head, :, pl.ds(places[part][at], rows)] += d_scores[
                    part * SKEW : (part + 1) * SKEW, at * rows : (at + 1) * rows
                ].astype(F32)
    d_ref[here, :width] = total.astype(LOW)

    @pl.when(step == pl.num_programs(0) - 1)
    def _():
        d_ref[:, width : 2 * width] = dk_sum[...].astype(LOW)
        d_ref[:, 2 * width :] = dv_sum[...].astype(LOW)
        one_hot = bucket_onehot(dt_ref.shape[0], seq_len)
        row = lax.broadcasted_iota(jnp.int32, (SKEW, span), 0)
        column = lax.broadcasted_iota(jnp.int32, dt_ref.shape, 1)
        result = jnp.zeros(dt_ref.shape, F32)
        for head in range(heads):
            level = pltpu.roll(skew_ref[head], SKEW, 1)
            bit = 1
            while bit < SKEW:
                level = jnp.where((row & bit) != 0, pltpu.roll(level, span - bit, 1), level)
                bit *= 2
            line = jnp.sum(level, axis=0, keepdims=True)
            summed = jnp.sum(jnp.where(one_hot, line, 0.0), axis=1, keepdims=True)
            result = jnp.where(column == head, summed, result)
        dt_ref[...] = result


def attention_backward(prob, mine, other, got, qkv, place, heads, shard, buckets):
    seq_len, width = qkv.shape[0], qkv.shape[1] // 3
    near_count, own_rows, model = mine[0].shape
    count = len(mine)
    rows = count * own_rows
    came_specs, _ = sent_specs(near_count, count, own_rows, model)
    return pl.pallas_call(
        functools.partial(backward_kernel, heads, shard, near_count, count),
        grid=(seq_len // rows,),
        in_specs=[
            pl.BlockSpec(memory_space=pltpu.SMEM),
            *came_specs,
            pl.BlockSpec((heads, rows, seq_len), lambda i: (0, row_block(i, near_count), 0)),
            pl.BlockSpec(got.shape, lambda i: (0, 0, 0)),
            pl.BlockSpec(qkv.shape, lambda i: (0, 0)),
        ],
        out_specs=[
            pl.BlockSpec(qkv.shape, lambda i: (0, 0)),
            pl.BlockSpec((buckets, 128), lambda i: (0, 0)),
            pl.BlockSpec((rows, model), lambda i: (row_block(i, near_count), 0)),
        ],
        out_shape=[
            jax.ShapeDtypeStruct(qkv.shape, LOW),
            jax.ShapeDtypeStruct((buckets, 128), F32),
            jax.ShapeDtypeStruct((seq_len, model), LOW),
        ],
        scratch_shapes=[
            pltpu.VMEM((seq_len, width), F32),
            pltpu.VMEM((seq_len, width), F32),
            pltpu.VMEM((heads, SKEW, 2 * seq_len), F32),
        ],
        compiler_params=pltpu.CompilerParams(vmem_limit_bytes=34 * 2**20),
        cost_estimate=pl.CostEstimate(
            flops=8 * seq_len * seq_len * width * 4,
            bytes_accessed=2 * heads * seq_len * seq_len,
            transcendentals=0,
        ),
        name="attention_backward",
    )(place, *other, *mine, prob, got, qkv)


EXTRA = 8
OWNER_ROWS = 64


def as_column(row, first, count):
    size = row.shape[1]
    here = lax.broadcasted_iota(jnp.int32, (count, size), 1) == first + lax.broadcasted_iota(
        jnp.int32, (count, size), 0
    )
    return jnp.sum(jnp.where(here, row, 0.0), axis=1, keepdims=True)


def blocks_kernel(seqs, members, q_ref, k_ref, v_ref, o_ref, gain_ref, table_ref, sent_ref):
    shard = q_ref.shape[0]
    width = q_ref.shape[1] // members
    gain = as_column(gain_ref[...].astype(LOW).astype(F32), 0, shard)
    parts = [
        (ref[...].astype(LOW).astype(F32) * gain).astype(LOW) for ref in (q_ref, k_ref, v_ref)
    ]
    parts.append(o_ref[...].T.astype(LOW))
    rest = jnp.zeros((EXTRA, sent_ref.shape[2]), LOW)
    table_rows, heads = table_ref.shape
    for seq in range(seqs):
        for member in range(members):
            at = seq * members + member
            for i, part in enumerate(parts):
                sent_ref[at, :shard, i * width : (i + 1) * width] = part[
                    :, member * width : (member + 1) * width
                ]
            sent_ref[at, shard:, :] = rest
            sent_ref[at, shard : shard + table_rows, :heads] = table_ref[...].astype(LOW)


def attention_blocks(weights, w_out, gain, table, seqs, members):
    shard, columns = weights[0].shape
    return pl.pallas_call(
        functools.partial(blocks_kernel, seqs, members),
        out_shape=jax.ShapeDtypeStruct(
            (seqs * members, shard + EXTRA, 4 * columns // members), LOW
        ),
        compiler_params=pltpu.CompilerParams(vmem_limit_bytes=60 * 2**20),
        cost_estimate=pl.CostEstimate(
            flops=0, bytes_accessed=16 * shard * columns, transcendentals=0
        ),
        name="attention_blocks",
    )(*weights, w_out, gain, table)


def owner_kernel(count, members, table_shape, *refs):
    got_ref, extra_ref = refs[:2]
    weight_refs = refs[2 : 2 + count]
    gain_ref = refs[2 + count]
    grad_refs = refs[3 + count : 3 + 2 * count]
    sum_ref = refs[3 + 2 * count]
    step = pl.program_id(0)
    rows = got_ref.shape[1]
    seqs = got_ref.shape[0] // members
    width = got_ref.shape[2] // count
    size = sum_ref.shape[1]
    gain = as_column(gain_ref[...].astype(LOW).astype(F32), step * rows, rows)
    total = jnp.zeros((rows, 1), F32)
    for member in range(members):
        product = sum(got_ref[seq * members + member].astype(F32) for seq in range(seqs))
        for i in range(count):
            part = product[:, i * width : (i + 1) * width]
            here = pl.ds(member * width, width)
            grad_refs[i][:, here] = part * gain
            weight = weight_refs[i][:, here].astype(LOW).astype(F32)
            total = total + jnp.sum(weight * part, axis=1, keepdims=True)

    @pl.when(step == 0)
    def _():
        sum_ref[...] = jnp.zeros_like(sum_ref)

    diagonal = lax.broadcasted_iota(jnp.int32, (rows, size), 1) == step * rows + (
        lax.broadcasted_iota(jnp.int32, (rows, size), 0)
    )
    sum_ref[...] += jnp.sum(jnp.where(diagonal, total, 0.0), axis=0, keepdims=True)
    if table_shape is not None:
        table_rows, heads = table_shape
        each = heads // members
        for member in range(members):
            piece = sum(extra_ref[seq * members + member].astype(F32) for seq in range(seqs))
            refs[-1][:, member * each : (member + 1) * each] = piece[:table_rows, :each]


def owner_grads(got, weights, gain, members, table_shape):
    sources, height, columns = got.shape
    shard, wide = weights[0].shape
    count = len(weights)
    rows = min(OWNER_ROWS, shard)
    step_rows = pl.BlockSpec((rows, wide), lambda i: (i, 0))
    row = pl.BlockSpec((1, shard), lambda i: (0, 0))
    last = height // EXTRA - 1
    out_specs = [step_rows] * count + [row]
    out_shape = [jax.ShapeDtypeStruct((shard, wide), F32)] * count
    out_shape.append(jax.ShapeDtypeStruct((1, shard), F32))
    if table_shape is not None:
        out_specs.append(pl.BlockSpec(table_shape, lambda i: (0, 0)))
        out_shape.append(jax.ShapeDtypeStruct(table_shape, F32))
    outs = pl.pallas_call(
        functools.partial(owner_kernel, count, members, table_shape),
        grid=(shard // rows,),
        in_specs=[
            pl.BlockSpec((sources, rows, columns), lambda i: (0, i, 0)),
            pl.BlockSpec((sources, EXTRA, columns), lambda i: (0, last, 0)),
        ]
        + [step_rows] * count
        + [row],
        out_specs=out_specs,
        out_shape=out_shape,
        compiler_params=pltpu.CompilerParams(vmem_limit_bytes=32 * 2**20),
        cost_estimate=pl.CostEstimate(
            flops=0, bytes_accessed=10 * count * shard * wide, transcendentals=0
        ),
        name="owner_grads",
    )(got, got, *weights, gain)
    return outs[:count], outs[count], outs[-1] if table_shape is not None else None


def rows_dot(left, right):
    return jnp.dot(left, right, preferred_element_type=F32)


def contract_cols(left, right):
    return lax.dot_general(left, right, (((1,), (1,)), ((), ())), preferred_element_type=F32)


def contract_rows(left, right):
    return lax.dot_general(left, right, (((0,), (0,)), ((), ())), preferred_element_type=F32)

def row_block(step, near_count):
    return lax.rem(step + near_count, CORES * near_count)


def send_rows(step, near_count, mp_at, held_ref, other_refs, mine_refs):
    count = len(other_refs)
    own_rows = held_ref.shape[0] // count

    def write(refs):
        for away, ref in enumerate(refs):
            first = pl.multiple_of(lax.bitwise_xor(mp_at, away) * own_rows, own_rows)
            ref[0] = held_ref[pl.ds(first, own_rows), :]

    @pl.when(step < near_count)
    def _():
        write(other_refs)

    @pl.when(step >= near_count)
    def _():
        write(mine_refs)


def take_rows(step, near_count, mp_at, other_refs, mine_refs, rows_ref):
    own_rows = other_refs[0].shape[1]

    def read(refs):
        for away, ref in enumerate(refs):
            first = pl.multiple_of(lax.bitwise_xor(mp_at, away) * own_rows, own_rows)
            rows_ref[pl.ds(first, own_rows), :] = ref[0]

    @pl.when(step < near_count)
    def _():
        read(other_refs)

    @pl.when(step >= near_count)
    def _():
        read(mine_refs)


def sent_specs(near_count, count, own_rows, model):
    other = pl.BlockSpec((1, own_rows, model), lambda i: (jnp.minimum(i, near_count - 1), 0, 0))
    mine = pl.BlockSpec((1, own_rows, model), lambda i: (jnp.maximum(i - near_count, 0), 0, 0))
    shape = jax.ShapeDtypeStruct((near_count, own_rows, model), LOW)
    return [other] * count + [mine] * count, [shape] * (2 * count)


def partial_kernel(near_count, count, product, place_ref, left_ref, weight_ref, *refs):
    held_ref = refs[-1]
    product(left_ref, weight_ref, held_ref)
    send_rows(
        pl.program_id(0), near_count, place_ref[3], held_ref, refs[:count], refs[count : 2 * count]
    )


def partial_rows(left, weight, model, place, near_count, count, product, name):
    seq_len, depth = left.shape
    rows = seq_len // (CORES * near_count)
    out_specs, out_shape = sent_specs(near_count, count, rows // count, model)
    outs = pl.pallas_call(
        functools.partial(partial_kernel, near_count, count, product),
        grid=(CORES * near_count,),
        in_specs=[
            pl.BlockSpec(memory_space=pltpu.SMEM),
            pl.BlockSpec((rows, depth), lambda i: (row_block(i, near_count), 0)),
            pl.BlockSpec(weight.shape, lambda i: (0, 0, 0)),
        ],
        out_specs=out_specs,
        out_shape=out_shape,
        scratch_shapes=[pltpu.VMEM((rows, model), LOW)],
        compiler_params=pltpu.CompilerParams(vmem_limit_bytes=40 * 2**20),
        cost_estimate=pl.CostEstimate(
            flops=2 * seq_len * depth * model, bytes_accessed=2 * seq_len * model, transcendentals=0
        ),
        name=name,
    )(place, left, weight)
    return outs[count:], outs[:count]


def column_product(shard, first, last, left_ref, weight_ref, held_ref):
    weight = weight_ref[:, :shard, first:last]
    weight = weight.reshape(weight.shape[0] * shard, last - first)
    held_ref[...] = contract_cols(left_ref[...], weight).astype(LOW)


def row_product(height, left_ref, weight_ref, held_ref):
    left = left_ref[...]
    width = weight_ref.shape[2]
    for at in range(weight_ref.shape[0]):
        held_ref[:, at * width : (at + 1) * width] = rows_dot(
            left, weight_ref[at, :height, :]
        ).astype(LOW)


def ffn_blocks_kernel(seqs, members, gate_ref, up_ref, down_ref, gain_ref, first_ref, second_ref):
    shard = gate_ref.shape[0]
    width = gate_ref.shape[1] // members
    gain = as_column(gain_ref[...].astype(LOW).astype(F32), 0, shard)
    for member in range(members):
        here = slice(member * width, (member + 1) * width)
        parts = [
            (ref[:, here].astype(LOW).astype(F32) * gain).astype(LOW) for ref in (gate_ref, up_ref)
        ]
        both = jnp.concatenate(parts, 1)
        down = down_ref[here, :].astype(LOW)
        for seq in range(seqs):
            at = seq * members + member
            first_ref[at, :width, :] = down
            first_ref[at, width:, :] = both[:, :shard]
            second_ref[at] = both[:, shard:]


def ffn_blocks(w_gate, w_up, w_down, gain, seqs, members):
    shard, columns = w_gate.shape
    width = columns // members
    return pl.pallas_call(
        functools.partial(ffn_blocks_kernel, seqs, members),
        out_shape=[
            jax.ShapeDtypeStruct((seqs * members, width + shard, shard), LOW),
            jax.ShapeDtypeStruct((seqs * members, shard, 2 * width - shard), LOW),
        ],
        compiler_params=pltpu.CompilerParams(vmem_limit_bytes=40 * 2**20),
        cost_estimate=pl.CostEstimate(
            flops=0, bytes_accessed=18 * shard * columns, transcendentals=0
        ),
        name="ffn_blocks",
    )(w_gate, w_up, w_down, gain)


def ffn_kernel(near_count, count, place_ref, *refs):
    came, refs = refs[: 2 * count], refs[2 * count :]
    grad_ref, first_ref, second_ref = refs[:3]
    other_refs, mine_refs = refs[3 : 3 + count], refs[3 + count : 3 + 2 * count]
    rows_ref, act_ref, d_ref, down_ref, held_ref, sum_ref = refs[3 + 2 * count :]
    step = pl.program_id(0)
    take_rows(step, near_count, place_ref[3], came[:count], came[count:], rows_ref)
    sources, height, shard = first_ref.shape
    width = height - shard
    rows = rows_ref[...]
    block = row_block(step, near_count)
    first = block_place(block, place_ref[1], near_count) * rows.shape[0]
    valid = first + lax.broadcasted_iota(jnp.int32, (rows.shape[0], 1), 0) < place_ref[0]
    grads = only(valid, grad_ref[...])
    early = first_ref[:, width:, :].reshape(sources * shard, shard)
    late = second_ref[...].reshape(sources * shard, 2 * width - shard)
    both = jnp.concatenate([rows_dot(rows, early), rows_dot(rows, late)], 1)
    gate, up = both[:, :width], both[:, width:]
    scale, cubic = 0.7978845608028654, 0.044715
    square = gate * gate
    bent = jnp.tanh(scale * (gate + cubic * square * gate))
    half = 0.5 * (1.0 + bent)
    value = gate * half
    slope = half + 0.5 * gate * (1.0 - bent * bent) * (scale * (1.0 + 3.0 * cubic * square))
    act = (value * up).astype(LOW)
    act_ref[...] = act
    d_hidden = jnp.zeros((rows.shape[0], width), F32)
    for at in range(sources):
        d_hidden = d_hidden + contract_cols(
            grads[:, at * shard : (at + 1) * shard], first_ref[at, :width, :]
        )
    d_both = jnp.concatenate(
        [(d_hidden * up * slope).astype(LOW), (d_hidden * value).astype(LOW)], 1
    )
    d_ref[...] = d_both
    held_ref[...] = (
        contract_cols(d_both[:, :shard], early) + contract_cols(d_both[:, shard:], late)
    ).astype(LOW)
    send_rows(step, near_count, place_ref[3], held_ref, other_refs, mine_refs)
    product = contract_rows(act, grads)

    @pl.when(step == 0)
    def _():
        sum_ref[...] = product

    @pl.when(step > 0)
    def _():
        sum_ref[...] += product

    @pl.when(step == pl.num_programs(0) - 1)
    def _():
        for at in range(sources):
            down_ref[at] = sum_ref[:, at * shard : (at + 1) * shard].astype(LOW)


def feed_forward(mine, other, grads, first, second, place):
    seq_len, model = grads.shape
    near_count, count = mine[0].shape[0], len(mine)
    sources, height, shard = first.shape
    width = height - shard
    rows = seq_len // (CORES * near_count)
    out_specs, out_shape = sent_specs(near_count, count, rows // count, model)

    def blocks(columns):
        return pl.BlockSpec((rows, columns), lambda i: (row_block(i, near_count), 0))

    outs = pl.pallas_call(
        functools.partial(ffn_kernel, near_count, count),
        grid=(CORES * near_count,),
        in_specs=[
            pl.BlockSpec(memory_space=pltpu.SMEM),
            *out_specs,
            blocks(model),
            pl.BlockSpec(first.shape, lambda i: (0, 0, 0)),
            pl.BlockSpec(second.shape, lambda i: (0, 0, 0)),
        ],
        out_specs=out_specs
        + [
            blocks(model),
            blocks(width),
            blocks(2 * width),
            pl.BlockSpec((sources, width, shard), lambda i: (0, 0, 0)),
        ],
        out_shape=out_shape
        + [
            jax.ShapeDtypeStruct((seq_len, model), LOW),
            jax.ShapeDtypeStruct((seq_len, width), LOW),
            jax.ShapeDtypeStruct((seq_len, 2 * width), LOW),
            jax.ShapeDtypeStruct((sources, width, shard), LOW),
        ],
        scratch_shapes=[pltpu.VMEM((rows, model), LOW), pltpu.VMEM((width, model), F32)],
        compiler_params=pltpu.CompilerParams(vmem_limit_bytes=56 * 2**20),
        cost_estimate=pl.CostEstimate(
            flops=12 * seq_len * model * width, bytes_accessed=12 * seq_len * model, transcendentals=0
        ),
        name="feed_forward",
    )(place, *other, *mine, grads, first, second)
    return outs[count : 2 * count], outs[:count], *outs[2 * count :]


COLUMN = ("seq", "near", "core")


def exchange(blocks, axes):
    return lax.all_to_all(blocks, axes, split_axis=0, concat_axis=0, tiled=True)


def swap(block, axis):
    return lax.ppermute(block, axis, [(0, 1), (1, 0)])


def after(value, *done):
    return lax.optimization_barrier((value,) + done)[0]


def rms(values):
    return lax.rsqrt(jnp.mean(values * values, axis=-1, keepdims=True) + EPSILON)


def norm_grad(inner, normed, inverse):
    return inverse * (inner - normed * jnp.mean(inner * normed, axis=-1, keepdims=True))


def local(
    inputs,
    cotangent,
    lengths,
    attn_scale,
    w_query,
    w_key,
    w_value,
    w_out,
    rel_table,
    ffn_scale,
    w_gate,
    w_up,
    w_down,
):
    seqs = lax.axis_size("seq")
    near_count = lax.axis_size("near")
    mp_count = lax.axis_size("mp")
    members = near_count * CORES
    sources = seqs * members
    tok_rows, model = inputs.shape
    seq_len = tok_rows * members
    own_rows = tok_rows // mp_count
    half_rows = seq_len // CORES
    shard = attn_scale.shape[0]
    table_rows, heads_mp = rel_table.shape
    buckets = table_rows * sources
    heads = heads_mp // members
    width = w_query.shape[1] // members
    hidden_width = w_gate.shape[1] // members

    near_at = lax.axis_index("near")
    core_at = lax.axis_index("core")
    mp_at = lax.axis_index("mp")
    member_at = near_at * CORES + core_at
    length = lax.dynamic_slice_in_dim(lengths, lax.axis_index("seq"), 1, 0)
    place = jnp.stack(
        [length[0]] + [at.astype(jnp.int32) for at in (core_at, member_at, mp_at, near_at)]
    )

    def over_mp(own, axis):
        shape = own.shape[:axis] + (mp_count,) + own.shape[axis:]
        blocks = lax.dynamic_update_index_in_dim(jnp.zeros(shape, own.dtype), own, mp_at, axis)
        moved = [(away, shifted(own, away)) for away in reversed(range(1, mp_count))]
        for away, block in moved:
            blocks = lax.dynamic_update_index_in_dim(blocks, block, mp_at ^ away, axis)
        return blocks

    def shifted(block, away):
        return lax.ppermute(block, "mp", [(i, i ^ away) for i in range(mp_count)])

    def in_near_order(own, moved):
        return jnp.stack(
            [jnp.where(near_at == 0, own, moved), jnp.where(near_at == 0, moved, own)], 0
        )

    def over_near(blocks):
        own = [lax.dynamic_slice_in_dim(block, mp_at * own_rows, own_rows, 0) for block in blocks]
        return swap(jnp.stack(own), "near")

    def near_rows(near):
        came = [(0, near)] + [(away, shifted(near, away)) for away in range(1, mp_count)]
        halves = []
        for half in (came, [(away, swap(block, "core")) for away, block in came]):
            rows = jnp.zeros((mp_count, own_rows, model), near.dtype)
            for away, block in half:
                rows = lax.dynamic_update_index_in_dim(rows, block, mp_at ^ away, 0)
            halves.append(rows.reshape(tok_rows, model))
        return halves

    def in_order(own, moved, core, core_moved):
        rows = jnp.zeros((CORES, near_count, tok_rows, model), own.dtype)
        for at, block in enumerate((own, moved, core, core_moved)):
            rows = lax.dynamic_update_slice(
                rows, block[None, None], (at // 2, near_at ^ (at % 2), 0, 0)
            )
        return rows.reshape(seq_len, model)

    def gather_rows(near):
        mine = [near] + [shifted(near, away) for away in range(1, mp_count)]
        return mine, [swap(block, "core") for block in mine]

    def sum_cores(mine, other):
        return [
            kept.astype(F32) + swap(sent, "core").astype(F32) for kept, sent in zip(mine, other)
        ]

    def send_mp(sums):
        return [shifted(sums[away].astype(LOW), away) for away in reversed(range(1, mp_count))]

    def sum_mp(sums, *meanwhile):
        moved = send_mp(sums)
        if meanwhile:
            moved = [after(piece, *meanwhile) for piece in moved]
        return sum((piece.astype(F32) for piece in moved), sums[0])

    def split_near(pair):
        sent = jnp.where(near_at == 0, pair[1], pair[0]).astype(LOW)
        return sent, jnp.where(near_at == 0, pair[0], pair[1])

    def sum_near_both(pair):
        low = pair.astype(LOW)
        moved = swap(low, "near")
        return low.astype(F32) + moved.astype(F32), moved

    def near_pair(own, moved):
        pair = [
            lax.dynamic_slice_in_dim(block, mp_at * own_rows, own_rows, 0)
            for block in (own, moved)
        ]
        return in_near_order(*pair)

    def here(pair):
        return lax.dynamic_index_in_dim(pair, near_at, 0, keepdims=False)

    attn_sent = attention_blocks(
        (w_query, w_key, w_value), w_out, attn_scale.reshape(1, shard), rel_table, seqs, members
    )
    attn_got = exchange(attn_sent, COLUMN)
    def partial(left, weight, product, name):
        return partial_rows(left, weight, model, place, near_count, mp_count, product, name)

    table = attn_got[:, shard : shard + table_rows, :heads_mp].reshape(buckets, heads_mp)

    def normed(rows):
        values = rows.astype(F32)
        return (values * rms(values)).astype(LOW)

    near = over_near([inputs, cotangent])
    moved_inputs, core_moved = near_rows(near[0])
    input_parts = [inputs, moved_inputs, swap(after(inputs, moved_inputs), "core"), core_moved]
    parts = [normed(part) for part in input_parts]
    moved_cotangent, core_moved = near_rows(after(near[1], *parts))
    core_cotangent = swap(after(cotangent, moved_cotangent), "core")
    grad_parts = [cotangent, moved_cotangent, core_cotangent, core_moved]
    ffn_first, ffn_second = ffn_blocks(
        w_gate, w_up, w_down, after(ffn_scale.reshape(1, shard), parts[3]), seqs, members
    )
    parts = lax.optimization_barrier((*parts, ffn_first, ffn_second, moved_cotangent))[:4]
    first_got = exchange(after(ffn_first, attn_got), COLUMN)

    qkv, attended, prob, out_mine, out_other = attention_forward(
        parts, attn_got, table, place, heads, shard, mp_count
    )
    normed_rows = in_order(*parts)
    grad_two = in_order(*grad_parts)
    mixed, mixed_moved = sum_near_both(
        after(sum_mp(sum_cores(out_mine, out_other)), first_got, grad_two, normed_rows)
    )
    second_got = exchange(after(ffn_second, mixed_moved), COLUMN)

    pair_inputs = near_pair(inputs, moved_inputs).astype(F32)
    after_attn = pair_inputs + mixed
    inv_two = rms(after_attn)
    normed_two = after_attn * inv_two
    mine_two, other_two = gather_rows(normed_two.astype(LOW))

    d_mine, d_other, hidden_two, acts, d_both, d_down_w = feed_forward(
        mine_two, other_two, grad_two, first_got, second_got, place
    )
    inner_cores = sum_cores(d_mine, d_other)
    down_product = functools.partial(row_product, hidden_width)
    ffn_partial = partial(after(acts, *inner_cores), first_got, down_product, "ffn_out")

    def to_owners(grad):
        return exchange(grad, COLUMN)

    def by_rows(got):
        parts = got.reshape((seqs, members) + got.shape[1:]).astype(F32)
        return jnp.sum(parts, axis=0).reshape(-1, shard)

    d_down = to_owners(after(d_down_w, *[rows.astype(LOW) for rows in inner_cores[1:]]))
    d_gate_up_w = contract_rows(hidden_two, after(d_both, *inner_cores)).astype(LOW)
    inner_two, inner_moved = sum_near_both(
        after(sum_mp(inner_cores, d_gate_up_w, *ffn_partial[0], *ffn_partial[1]), d_down)
    )

    pair_first = (
        lax.broadcasted_iota(jnp.int32, (near_count, own_rows, 1), 0) * (CORES * tok_rows)
        + lax.broadcasted_iota(jnp.int32, (near_count, own_rows, 1), 1)
        + (core_at * tok_rows + mp_at * own_rows)
    )
    pair_valid = pair_first < length
    pair_grad = near_pair(cotangent, moved_cotangent).astype(F32)
    grad_one = jnp.where(pair_valid, pair_grad, 0.0) + norm_grad(inner_two, normed_two, inv_two)
    grad_one_low = grad_one.astype(LOW)
    mine_one, other_one = gather_rows(grad_one_low)
    d_gate_up = to_owners(
        after(d_gate_up_w, inner_moved, grad_one_low).reshape(sources, shard, -1)
    )
    ffn_cores = sum_cores(*ffn_partial)
    d_qkv, d_table, rows_one = attention_backward(
        prob, mine_one, other_one, attn_got, qkv, place, heads, shard, buckets
    )
    qkv_product = functools.partial(column_product, shard, 0, 3 * width)
    ffn_moved = send_mp([after(rows, *mine_one[1:]) for rows in ffn_cores])
    inner_cores = sum_cores(
        *partial(after(d_qkv, *ffn_moved), attn_got, qkv_product, "attention_in")
    )
    inner_pair = sum_mp(inner_cores)
    table_sent = d_table[:, :heads].astype(LOW).reshape(sources, table_rows, heads)
    table_sent = jnp.pad(
        table_sent, ((0, 0), (0, EXTRA - table_rows), (0, 3 * width - heads))
    )
    d_qkv_w = contract_rows(normed_rows, d_qkv).astype(LOW).reshape(sources, shard, -1)
    d_qkv_sent = jnp.concatenate([d_qkv_w, table_sent], 1)
    d_qkv_got = to_owners(after(d_qkv_sent, d_gate_up))
    d_out = contract_rows(after(attended, inner_cores[0]), rows_one)
    d_out = jnp.moveaxis(d_out.astype(LOW).reshape(width, sources, shard), 1, 0)

    (d_w_gate, d_w_up), ffn_gain, _ = owner_grads(
        after(d_gate_up, inner_cores[0]), (w_gate, w_up), ffn_scale.reshape(1, shard), members, None
    )
    d_w_down = by_rows(after(d_down, d_qkv))

    ffn_sent, ffn_kept = split_near(
        sum((piece.astype(F32) for piece in ffn_moved), ffn_cores[0])
    )
    inner_sent, inner_kept = split_near(inner_pair)
    came = swap(
        after(jnp.stack([ffn_sent, inner_sent]), d_qkv_got, ffn_gain, d_w_down), "near"
    )
    own_inputs = here(pair_inputs)
    inv_one = rms(own_inputs)
    grad_input = here(grad_one) + norm_grad(inner_kept + came[1].astype(F32), own_inputs * inv_one, inv_one)
    own_out = jnp.where(here(pair_valid), here(after_attn) + ffn_kept + came[0].astype(F32), 0.0)
    owned = jnp.stack([own_out.astype(LOW), grad_input.astype(LOW)])
    rows_out = [jnp.zeros((mp_count, own_rows, model), LOW)] * 2
    blocks_out = [owned] + [shifted(owned, away) for away in range(1, mp_count)]
    d_out = to_owners(after(d_out, came))
    for away, block in enumerate(blocks_out):
        rows_out = [
            lax.dynamic_update_index_in_dim(rows, block[i], mp_at ^ away, 0)
            for i, rows in enumerate(rows_out)
        ]
    layer_out, d_inputs = (rows.reshape(tok_rows, model) for rows in rows_out)

    (d_w_query, d_w_key, d_w_value), attn_gain, d_rel_table = owner_grads(
        after(d_qkv_got, blocks_out[1]),
        (w_query, w_key, w_value),
        attn_scale.reshape(1, shard),
        members,
        (table_rows, heads_mp),
    )
    gains = jnp.concatenate([attn_gain, ffn_gain], 0)
    gains = sum((shifted(gains, away) for away in range(1, mp_count)), gains)
    return (
        layer_out,
        d_inputs,
        gains[0],
        d_w_query,
        d_w_key,
        d_w_value,
        by_rows(d_out),
        d_rel_table,
        gains[1],
        d_w_gate,
        d_w_up,
        d_w_down,
    )


def solution(mesh):
    fsdp, mp = mesh.shape["fsdp"], mesh.shape["mp"]

    def run(*args):
        seqs = args[2].shape[0]
        members = fsdp // seqs
        inner = Mesh(
            mesh.devices.reshape(seqs, members // CORES, CORES, mp), ("seq", "near", "core", "mp")
        )
        rows, columns, first = P(COLUMN, None), P("mp", COLUMN), P(COLUMN)
        both = P(COLUMN, "mp")
        in_specs = (
            rows, rows, P(), first, both, both, both, columns, both, first, both, both, columns,
        )
        out_specs = (
            rows, rows, first, both, both, both, columns, both, first, both, both, columns,
        )
        return jax.shard_map(
            local, mesh=inner, in_specs=in_specs, out_specs=out_specs, check_vma=False
        )(*args)

    return run
```

```python
import functools

import jax
import jax.numpy as jnp
from jax import lax
from jax.experimental import pallas as pl
from jax.experimental.pallas import tpu as pltpu
from jax.sharding import Mesh, PartitionSpec as P

LOW = jnp.bfloat16
F32 = jnp.float32
CORES = 2
THRESHOLDS = (12, 16, 23, 32, 46, 64, 91)
EPSILON = 1e-06
MASKED = -1e30
SKEW = 128


def bucket_of(rel_offset):
    distance = jnp.abs(rel_offset)
    far_bucket = 8 + sum(((distance >= threshold).astype(jnp.int32) for threshold in THRESHOLDS))
    bucket_abs = jnp.where(distance < 8, distance, far_bucket)
    return bucket_abs + jnp.where(rel_offset > 0, 16, 0)


def bucket_onehot(buckets, seq_len):
    offset = lax.broadcasted_iota(jnp.int32, (buckets, 2 * seq_len), 1) - seq_len
    bucket = lax.broadcasted_iota(jnp.int32, (buckets, 2 * seq_len), 0)
    return bucket_of(offset) == bucket


def head_lanes(rows, width, head_width, head):
    lane = lax.broadcasted_iota(jnp.int32, (rows, width), 1)
    return (lane >= head * head_width) & (lane < (head + 1) * head_width)


def only(mask, values):
    return jnp.where(mask, values, jnp.zeros_like(values))


def block_place(block, core, near_count):
    return lax.rem(block, near_count) * CORES + lax.bitwise_xor(lax.div(block, near_count), core)


def bias_places(place_ref, step, blocks, rows, seq_len):
    core, near_count = place_ref[1], blocks // CORES
    query = block_place(step, core, near_count) * rows
    return [
        [
            pl.multiple_of(
                block_place(block, core, near_count) * rows - query - part * SKEW + seq_len - SKEW,
                SKEW,
            )
            for block in range(blocks)
        ]
        for part in range(rows // SKEW)
    ]


def forward_kernel(heads, shard, near_count, count, place_ref, *refs):
    own_ref, moved_ref, core_ref, core_moved_ref, got_ref, table_ref = refs[:6]
    qkv_ref, o_ref, p_ref = refs[6:9]
    other_refs, mine_refs = refs[9 : 9 + count], refs[9 + count : 9 + 2 * count]
    skew_ref, held_ref = refs[9 + 2 * count :]
    step = pl.program_id(0)
    seq_len = qkv_ref.shape[0]
    rows, width = o_ref.shape
    model = held_ref.shape[1]
    head_width = width // heads
    span = 2 * seq_len
    blocks = seq_len // rows
    block = row_block(step, near_count)

    @pl.when(step == 0)
    def _():
        weight = got_ref[:, :shard, : 3 * width].reshape(model, 3 * width)
        near = place_ref[4]
        for at, ref in enumerate((own_ref, moved_ref, core_ref, core_moved_ref)):
            first = (at // 2) * near_count + lax.bitwise_xor(near, at % 2)
            qkv_ref[pl.ds(pl.multiple_of(first * rows, rows), rows), :] = rows_dot(
                ref[...], weight
            ).astype(LOW)
        one_hot = bucket_onehot(table_ref.shape[0], seq_len)
        table = table_ref[...].astype(F32)
        column = lax.broadcasted_iota(jnp.int32, table.shape, 1)
        for head in range(heads):
            here = column == place_ref[2] * heads + head
            levels = jnp.sum(jnp.where(here, table, 0.0), axis=1, keepdims=True)
            line = jnp.sum(jnp.where(one_hot, levels, 0.0), axis=0, keepdims=True)
            line = jnp.broadcast_to(line, (SKEW, span))
            skew_ref[head] = pltpu.roll(line, span - SKEW, 1, stride=1, stride_axis=0)

    row = lax.broadcasted_iota(jnp.int32, (1, rows), 1)
    allowed = jnp.concatenate(
        [
            block_place(at, place_ref[1], near_count) * rows + row < place_ref[0]
            for at in range(blocks)
        ],
        1,
    )
    queries = qkv_ref[pl.ds(pl.multiple_of(block * rows, rows), rows), :width]
    keys = qkv_ref[:, width : 2 * width]
    values = qkv_ref[:, 2 * width :]
    total = jnp.zeros((rows, width), F32)
    places = bias_places(place_ref, block, blocks, rows, seq_len)
    for head in range(heads):
        scores = lax.dot_general(
            only(head_lanes(rows, width, head_width, head), queries),
            keys,
            (((1,), (1,)), ((), ())),
            preferred_element_type=F32,
        )
        bias = jnp.concatenate(
            [
                jnp.concatenate([skew_ref[head, :, pl.ds(place, rows)] for place in part], 1)
                for part in places
            ],
            0,
        )
        scores = jnp.where(allowed, scores + bias, MASKED)
        grown = jnp.exp(scores - jnp.max(scores, axis=1, keepdims=True))
        prob = (grown * (1.0 / jnp.sum(grown, axis=1, keepdims=True))).astype(LOW)
        p_ref[head] = prob
        total = total + jnp.dot(
            prob,
            only(head_lanes(seq_len, width, head_width, head), values),
            preferred_element_type=F32,
        )
    attended = total.astype(LOW)
    o_ref[...] = attended
    weight = got_ref[:, :shard, 3 * width :].reshape(model, width)
    held_ref[...] = contract_cols(attended, weight).astype(LOW)
    send_rows(step, near_count, place_ref[3], held_ref, other_refs, mine_refs)


def attention_forward(parts, got, table, place, heads, shard, count):
    rows, model = parts[0].shape
    blocks = len(parts)
    near_count = blocks // CORES
    seq_len, width = rows * blocks, got.shape[2] // 4
    out_specs, out_shape = sent_specs(near_count, count, rows // count, model)

    def fixed(shape):
        return pl.BlockSpec(shape, lambda i: (0,) * len(shape))

    outs = pl.pallas_call(
        functools.partial(forward_kernel, heads, shard, near_count, count),
        grid=(blocks,),
        in_specs=[pl.BlockSpec(memory_space=pltpu.SMEM)]
        + [fixed(part.shape) for part in parts]
        + [fixed(got.shape), fixed(table.shape)],
        out_specs=[
            fixed((seq_len, 3 * width)),
            pl.BlockSpec((rows, width), lambda i: (row_block(i, near_count), 0)),
            pl.BlockSpec((heads, rows, seq_len), lambda i: (0, row_block(i, near_count), 0)),
        ]
        + out_specs,
        out_shape=[
            jax.ShapeDtypeStruct((seq_len, 3 * width), LOW),
            jax.ShapeDtypeStruct((seq_len, width), LOW),
            jax.ShapeDtypeStruct((heads, seq_len, seq_len), LOW),
        ]
        + out_shape,
        scratch_shapes=[
            pltpu.VMEM((heads, SKEW, 2 * seq_len), F32),
            pltpu.VMEM((rows, model), LOW),
        ],
        compiler_params=pltpu.CompilerParams(vmem_limit_bytes=34 * 2**20),
        cost_estimate=pl.CostEstimate(flops=0, bytes_accessed=0, transcendentals=0),
        name="attention_forward",
    )(place, *parts, got, table)
    return (*outs[:3], outs[3 + count :], outs[3 : 3 + count])


def backward_kernel(heads, shard, near_count, count, place_ref, *refs):
    came, refs = refs[: 2 * count], refs[2 * count :]
    p_ref, got_ref, qkv_ref, d_ref, dt_ref, rows_ref, dk_sum, dv_sum, skew_ref = refs
    step = pl.program_id(0)
    block = row_block(step, near_count)
    take_rows(step, near_count, place_ref[3], came[:count], came[count:], rows_ref)
    rows, model = rows_ref.shape
    seq_len = qkv_ref.shape[0]
    width = qkv_ref.shape[1] // 3
    head_width = width // heads
    span = 2 * seq_len
    blocks = seq_len // rows

    @pl.when(step == 0)
    def _():
        dk_sum[...] = jnp.zeros_like(dk_sum)
        dv_sum[...] = jnp.zeros_like(dv_sum)
        skew_ref[...] = jnp.zeros_like(skew_ref)

    here = pl.ds(pl.multiple_of(block * rows, rows), rows)
    queries = qkv_ref[here, :width]
    keys = qkv_ref[:, width : 2 * width]
    values = qkv_ref[:, 2 * width :]
    weight = got_ref[:, :shard, 3 * width :].reshape(model, width)
    grads = rows_dot(rows_ref[...], weight).astype(LOW)
    total = jnp.zeros((rows, width), F32)
    places = bias_places(place_ref, block, blocks, rows, seq_len)
    for head in range(heads):
        own = head_lanes(rows, width, head_width, head)
        own_grads = only(own, grads)
        d_prob = lax.dot_general(
            own_grads, values, (((1,), (1,)), ((), ())), preferred_element_type=F32
        )
        prob_low = p_ref[head]
        prob = prob_low.astype(F32)
        weighed = prob * d_prob
        d_scores = (weighed - prob * jnp.sum(weighed, axis=1, keepdims=True)).astype(LOW)
        total = total + jnp.dot(
            d_scores,
            only(head_lanes(seq_len, width, head_width, head), keys),
            preferred_element_type=F32,
        )
        dk_sum[...] += lax.dot_general(
            d_scores, only(own, queries), (((0,), (0,)), ((), ())), preferred_element_type=F32
        )
        dv_sum[...] += lax.dot_general(
            prob_low, own_grads, (((0,), (0,)), ((), ())), preferred_element_type=F32
        )
        for part in range(rows // SKEW):
            for at in range(blocks):
                skew_ref[head, :, pl.ds(places[part][at], rows)] += d_scores[
                    part * SKEW : (part + 1) * SKEW, at * rows : (at + 1) * rows
                ].astype(F32)
    d_ref[here, :width] = total.astype(LOW)

    @pl.when(step == pl.num_programs(0) - 1)
    def _():
        d_ref[:, width : 2 * width] = dk_sum[...].astype(LOW)
        d_ref[:, 2 * width :] = dv_sum[...].astype(LOW)
        one_hot = bucket_onehot(dt_ref.shape[0], seq_len)
        row = lax.broadcasted_iota(jnp.int32, (SKEW, span), 0)
        column = lax.broadcasted_iota(jnp.int32, dt_ref.shape, 1)
        result = jnp.zeros(dt_ref.shape, F32)
        for head in range(heads):
            level = pltpu.roll(skew_ref[head], SKEW, 1)
            bit = 1
            while bit < SKEW:
                level = jnp.where((row & bit) != 0, pltpu.roll(level, span - bit, 1), level)
                bit *= 2
            line = jnp.sum(level, axis=0, keepdims=True)
            summed = jnp.sum(jnp.where(one_hot, line, 0.0), axis=1, keepdims=True)
            result = jnp.where(column == head, summed, result)
        dt_ref[...] = result


def attention_backward(prob, mine, other, got, qkv, place, heads, shard, buckets):
    seq_len, width = qkv.shape[0], qkv.shape[1] // 3
    near_count, own_rows, model = mine[0].shape
    count = len(mine)
    rows = count * own_rows
    came_specs, _ = sent_specs(near_count, count, own_rows, model)
    return pl.pallas_call(
        functools.partial(backward_kernel, heads, shard, near_count, count),
        grid=(seq_len // rows,),
        in_specs=[
            pl.BlockSpec(memory_space=pltpu.SMEM),
            *came_specs,
            pl.BlockSpec((heads, rows, seq_len), lambda i: (0, row_block(i, near_count), 0)),
            pl.BlockSpec(got.shape, lambda i: (0, 0, 0)),
            pl.BlockSpec(qkv.shape, lambda i: (0, 0)),
        ],
        out_specs=[
            pl.BlockSpec(qkv.shape, lambda i: (0, 0)),
            pl.BlockSpec((buckets, 128), lambda i: (0, 0)),
            pl.BlockSpec((rows, model), lambda i: (row_block(i, near_count), 0)),
        ],
        out_shape=[
            jax.ShapeDtypeStruct(qkv.shape, LOW),
            jax.ShapeDtypeStruct((buckets, 128), F32),
            jax.ShapeDtypeStruct((seq_len, model), LOW),
        ],
        scratch_shapes=[
            pltpu.VMEM((seq_len, width), F32),
            pltpu.VMEM((seq_len, width), F32),
            pltpu.VMEM((heads, SKEW, 2 * seq_len), F32),
        ],
        compiler_params=pltpu.CompilerParams(vmem_limit_bytes=34 * 2**20),
        cost_estimate=pl.CostEstimate(
            flops=8 * seq_len * seq_len * width * 4,
            bytes_accessed=2 * heads * seq_len * seq_len,
            transcendentals=0,
        ),
        name="attention_backward",
    )(place, *other, *mine, prob, got, qkv)


EXTRA = 8
OWNER_ROWS = 64


def as_column(row, first, count):
    size = row.shape[1]
    here = lax.broadcasted_iota(jnp.int32, (count, size), 1) == first + lax.broadcasted_iota(
        jnp.int32, (count, size), 0
    )
    return jnp.sum(jnp.where(here, row, 0.0), axis=1, keepdims=True)


def blocks_kernel(seqs, members, q_ref, k_ref, v_ref, o_ref, gain_ref, table_ref, sent_ref):
    shard = q_ref.shape[0]
    width = q_ref.shape[1] // members
    gain = as_column(gain_ref[...].astype(LOW).astype(F32), 0, shard)
    parts = [
        (ref[...].astype(LOW).astype(F32) * gain).astype(LOW) for ref in (q_ref, k_ref, v_ref)
    ]
    parts.append(o_ref[...].T.astype(LOW))
    rest = jnp.zeros((EXTRA, sent_ref.shape[2]), LOW)
    table_rows, heads = table_ref.shape
    for seq in range(seqs):
        for member in range(members):
            at = seq * members + member
            for i, part in enumerate(parts):
                sent_ref[at, :shard, i * width : (i + 1) * width] = part[
                    :, member * width : (member + 1) * width
                ]
            sent_ref[at, shard:, :] = rest
            sent_ref[at, shard : shard + table_rows, :heads] = table_ref[...].astype(LOW)


def attention_blocks(weights, w_out, gain, table, seqs, members):
    shard, columns = weights[0].shape
    return pl.pallas_call(
        functools.partial(blocks_kernel, seqs, members),
        out_shape=jax.ShapeDtypeStruct(
            (seqs * members, shard + EXTRA, 4 * columns // members), LOW
        ),
        compiler_params=pltpu.CompilerParams(vmem_limit_bytes=60 * 2**20),
        cost_estimate=pl.CostEstimate(
            flops=0, bytes_accessed=16 * shard * columns, transcendentals=0
        ),
        name="attention_blocks",
    )(*weights, w_out, gain, table)


def owner_kernel(count, members, table_shape, *refs):
    got_ref, extra_ref = refs[:2]
    weight_refs = refs[2 : 2 + count]
    gain_ref = refs[2 + count]
    grad_refs = refs[3 + count : 3 + 2 * count]
    sum_ref = refs[3 + 2 * count]
    step = pl.program_id(0)
    rows = got_ref.shape[1]
    seqs = got_ref.shape[0] // members
    width = got_ref.shape[2] // count
    size = sum_ref.shape[1]
    gain = as_column(gain_ref[...].astype(LOW).astype(F32), step * rows, rows)
    total = jnp.zeros((rows, 1), F32)
    for member in range(members):
        product = sum(got_ref[seq * members + member].astype(F32) for seq in range(seqs))
        for i in range(count):
            part = product[:, i * width : (i + 1) * width]
            here = pl.ds(member * width, width)
            grad_refs[i][:, here] = part * gain
            weight = weight_refs[i][:, here].astype(LOW).astype(F32)
            total = total + jnp.sum(weight * part, axis=1, keepdims=True)

    @pl.when(step == 0)
    def _():
        sum_ref[...] = jnp.zeros_like(sum_ref)

    diagonal = lax.broadcasted_iota(jnp.int32, (rows, size), 1) == step * rows + (
        lax.broadcasted_iota(jnp.int32, (rows, size), 0)
    )
    sum_ref[...] += jnp.sum(jnp.where(diagonal, total, 0.0), axis=0, keepdims=True)
    if table_shape is not None:
        table_rows, heads = table_shape
        each = heads // members
        for member in range(members):
            piece = sum(extra_ref[seq * members + member].astype(F32) for seq in range(seqs))
            refs[-1][:, member * each : (member + 1) * each] = piece[:table_rows, :each]


def owner_grads(got, weights, gain, members, table_shape):
    sources, height, columns = got.shape
    shard, wide = weights[0].shape
    count = len(weights)
    rows = min(OWNER_ROWS, shard)
    step_rows = pl.BlockSpec((rows, wide), lambda i: (i, 0))
    row = pl.BlockSpec((1, shard), lambda i: (0, 0))
    last = height // EXTRA - 1
    out_specs = [step_rows] * count + [row]
    out_shape = [jax.ShapeDtypeStruct((shard, wide), F32)] * count
    out_shape.append(jax.ShapeDtypeStruct((1, shard), F32))
    if table_shape is not None:
        out_specs.append(pl.BlockSpec(table_shape, lambda i: (0, 0)))
        out_shape.append(jax.ShapeDtypeStruct(table_shape, F32))
    outs = pl.pallas_call(
        functools.partial(owner_kernel, count, members, table_shape),
        grid=(shard // rows,),
        in_specs=[
            pl.BlockSpec((sources, rows, columns), lambda i: (0, i, 0)),
            pl.BlockSpec((sources, EXTRA, columns), lambda i: (0, last, 0)),
        ]
        + [step_rows] * count
        + [row],
        out_specs=out_specs,
        out_shape=out_shape,
        compiler_params=pltpu.CompilerParams(vmem_limit_bytes=32 * 2**20),
        cost_estimate=pl.CostEstimate(
            flops=0, bytes_accessed=10 * count * shard * wide, transcendentals=0
        ),
        name="owner_grads",
    )(got, got, *weights, gain)
    return outs[:count], outs[count], outs[-1] if table_shape is not None else None


def rows_dot(left, right):
    return jnp.dot(left, right, preferred_element_type=F32)


def contract_cols(left, right):
    return lax.dot_general(left, right, (((1,), (1,)), ((), ())), preferred_element_type=F32)


def contract_rows(left, right):
    return lax.dot_general(left, right, (((0,), (0,)), ((), ())), preferred_element_type=F32)

def row_block(step, near_count):
    return lax.rem(step + near_count, CORES * near_count)


def send_rows(step, near_count, mp_at, held_ref, other_refs, mine_refs):
    count = len(other_refs)
    own_rows = held_ref.shape[0] // count

    def write(refs):
        for away, ref in enumerate(refs):
            first = pl.multiple_of(lax.bitwise_xor(mp_at, away) * own_rows, own_rows)
            ref[0] = held_ref[pl.ds(first, own_rows), :]

    @pl.when(step < near_count)
    def _():
        write(other_refs)

    @pl.when(step >= near_count)
    def _():
        write(mine_refs)


def take_rows(step, near_count, mp_at, other_refs, mine_refs, rows_ref):
    own_rows = other_refs[0].shape[1]

    def read(refs):
        for away, ref in enumerate(refs):
            first = pl.multiple_of(lax.bitwise_xor(mp_at, away) * own_rows, own_rows)
            rows_ref[pl.ds(first, own_rows), :] = ref[0]

    @pl.when(step < near_count)
    def _():
        read(other_refs)

    @pl.when(step >= near_count)
    def _():
        read(mine_refs)


def sent_specs(near_count, count, own_rows, model):
    other = pl.BlockSpec((1, own_rows, model), lambda i: (jnp.minimum(i, near_count - 1), 0, 0))
    mine = pl.BlockSpec((1, own_rows, model), lambda i: (jnp.maximum(i - near_count, 0), 0, 0))
    shape = jax.ShapeDtypeStruct((near_count, own_rows, model), LOW)
    return [other] * count + [mine] * count, [shape] * (2 * count)


def partial_kernel(near_count, count, product, place_ref, left_ref, weight_ref, *refs):
    held_ref = refs[-1]
    product(left_ref, weight_ref, held_ref)
    send_rows(
        pl.program_id(0), near_count, place_ref[3], held_ref, refs[:count], refs[count : 2 * count]
    )


def partial_rows(left, weight, model, place, near_count, count, product, name):
    seq_len, depth = left.shape
    rows = seq_len // (CORES * near_count)
    out_specs, out_shape = sent_specs(near_count, count, rows // count, model)
    outs = pl.pallas_call(
        functools.partial(partial_kernel, near_count, count, product),
        grid=(CORES * near_count,),
        in_specs=[
            pl.BlockSpec(memory_space=pltpu.SMEM),
            pl.BlockSpec((rows, depth), lambda i: (row_block(i, near_count), 0)),
            pl.BlockSpec(weight.shape, lambda i: (0, 0, 0)),
        ],
        out_specs=out_specs,
        out_shape=out_shape,
        scratch_shapes=[pltpu.VMEM((rows, model), LOW)],
        compiler_params=pltpu.CompilerParams(vmem_limit_bytes=40 * 2**20),
        cost_estimate=pl.CostEstimate(
            flops=2 * seq_len * depth * model, bytes_accessed=2 * seq_len * model, transcendentals=0
        ),
        name=name,
    )(place, left, weight)
    return outs[count:], outs[:count]


def column_product(shard, first, last, left_ref, weight_ref, held_ref):
    weight = weight_ref[:, :shard, first:last]
    weight = weight.reshape(weight.shape[0] * shard, last - first)
    held_ref[...] = contract_cols(left_ref[...], weight).astype(LOW)


def row_product(height, left_ref, weight_ref, held_ref):
    left = left_ref[...]
    width = weight_ref.shape[2]
    for at in range(weight_ref.shape[0]):
        held_ref[:, at * width : (at + 1) * width] = rows_dot(
            left, weight_ref[at, :height, :]
        ).astype(LOW)


def ffn_blocks_kernel(seqs, members, gate_ref, up_ref, down_ref, gain_ref, first_ref, second_ref):
    shard = gate_ref.shape[0]
    width = gate_ref.shape[1] // members
    gain = as_column(gain_ref[...].astype(LOW).astype(F32), 0, shard)
    for member in range(members):
        here = slice(member * width, (member + 1) * width)
        parts = [
            (ref[:, here].astype(LOW).astype(F32) * gain).astype(LOW) for ref in (gate_ref, up_ref)
        ]
        both = jnp.concatenate(parts, 1)
        down = down_ref[here, :].astype(LOW)
        for seq in range(seqs):
            at = seq * members + member
            first_ref[at, :width, :] = down
            first_ref[at, width:, :] = both[:, :shard]
            second_ref[at] = both[:, shard:]


def ffn_blocks(w_gate, w_up, w_down, gain, seqs, members):
    shard, columns = w_gate.shape
    width = columns // members
    return pl.pallas_call(
        functools.partial(ffn_blocks_kernel, seqs, members),
        out_shape=[
            jax.ShapeDtypeStruct((seqs * members, width + shard, shard), LOW),
            jax.ShapeDtypeStruct((seqs * members, shard, 2 * width - shard), LOW),
        ],
        compiler_params=pltpu.CompilerParams(vmem_limit_bytes=40 * 2**20),
        cost_estimate=pl.CostEstimate(
            flops=0, bytes_accessed=18 * shard * columns, transcendentals=0
        ),
        name="ffn_blocks",
    )(w_gate, w_up, w_down, gain)


def ffn_kernel(near_count, count, place_ref, *refs):
    came, refs = refs[: 2 * count], refs[2 * count :]
    grad_ref, first_ref, second_ref = refs[:3]
    other_refs, mine_refs = refs[3 : 3 + count], refs[3 + count : 3 + 2 * count]
    rows_ref, act_ref, d_ref, down_ref, held_ref, sum_ref = refs[3 + 2 * count :]
    step = pl.program_id(0)
    take_rows(step, near_count, place_ref[3], came[:count], came[count:], rows_ref)
    sources, height, shard = first_ref.shape
    width = height - shard
    rows = rows_ref[...]
    block = row_block(step, near_count)
    first = block_place(block, place_ref[1], near_count) * rows.shape[0]
    valid = first + lax.broadcasted_iota(jnp.int32, (rows.shape[0], 1), 0) < place_ref[0]
    grads = only(valid, grad_ref[...])
    early = first_ref[:, width:, :].reshape(sources * shard, shard)
    late = second_ref[...].reshape(sources * shard, 2 * width - shard)
    both = jnp.concatenate([rows_dot(rows, early), rows_dot(rows, late)], 1)
    gate, up = both[:, :width], both[:, width:]
    scale, cubic = 0.7978845608028654, 0.044715
    square = gate * gate
    bent = jnp.tanh(scale * (gate + cubic * square * gate))
    half = 0.5 * (1.0 + bent)
    value = gate * half
    slope = half + 0.5 * gate * (1.0 - bent * bent) * (scale * (1.0 + 3.0 * cubic * square))
    act = (value * up).astype(LOW)
    act_ref[...] = act
    d_hidden = jnp.zeros((rows.shape[0], width), F32)
    for at in range(sources):
        d_hidden = d_hidden + contract_cols(
            grads[:, at * shard : (at + 1) * shard], first_ref[at, :width, :]
        )
    d_both = jnp.concatenate(
        [(d_hidden * up * slope).astype(LOW), (d_hidden * value).astype(LOW)], 1
    )
    d_ref[...] = d_both
    held_ref[...] = (
        contract_cols(d_both[:, :shard], early) + contract_cols(d_both[:, shard:], late)
    ).astype(LOW)
    send_rows(step, near_count, place_ref[3], held_ref, other_refs, mine_refs)
    product = contract_rows(act, grads)

    @pl.when(step == 0)
    def _():
        sum_ref[...] = product

    @pl.when(step > 0)
    def _():
        sum_ref[...] += product

    @pl.when(step == pl.num_programs(0) - 1)
    def _():
        for at in range(sources):
            down_ref[at] = sum_ref[:, at * shard : (at + 1) * shard].astype(LOW)


def feed_forward(mine, other, grads, first, second, place):
    seq_len, model = grads.shape
    near_count, count = mine[0].shape[0], len(mine)
    sources, height, shard = first.shape
    width = height - shard
    rows = seq_len // (CORES * near_count)
    out_specs, out_shape = sent_specs(near_count, count, rows // count, model)

    def blocks(columns):
        return pl.BlockSpec((rows, columns), lambda i: (row_block(i, near_count), 0))

    outs = pl.pallas_call(
        functools.partial(ffn_kernel, near_count, count),
        grid=(CORES * near_count,),
        in_specs=[
            pl.BlockSpec(memory_space=pltpu.SMEM),
            *out_specs,
            blocks(model),
            pl.BlockSpec(first.shape, lambda i: (0, 0, 0)),
            pl.BlockSpec(second.shape, lambda i: (0, 0, 0)),
        ],
        out_specs=out_specs
        + [
            blocks(model),
            blocks(width),
            blocks(2 * width),
            pl.BlockSpec((sources, width, shard), lambda i: (0, 0, 0)),
        ],
        out_shape=out_shape
        + [
            jax.ShapeDtypeStruct((seq_len, model), LOW),
            jax.ShapeDtypeStruct((seq_len, width), LOW),
            jax.ShapeDtypeStruct((seq_len, 2 * width), LOW),
            jax.ShapeDtypeStruct((sources, width, shard), LOW),
        ],
        scratch_shapes=[pltpu.VMEM((rows, model), LOW), pltpu.VMEM((width, model), F32)],
        compiler_params=pltpu.CompilerParams(vmem_limit_bytes=56 * 2**20),
        cost_estimate=pl.CostEstimate(
            flops=12 * seq_len * model * width, bytes_accessed=12 * seq_len * model, transcendentals=0
        ),
        name="feed_forward",
    )(place, *other, *mine, grads, first, second)
    return outs[count : 2 * count], outs[:count], *outs[2 * count :]


COLUMN = ("seq", "near", "core")


def exchange(blocks, axes):
    return lax.all_to_all(blocks, axes, split_axis=0, concat_axis=0, tiled=True)


def swap(block, axis):
    return lax.ppermute(block, axis, [(0, 1), (1, 0)])


def after(value, *done):
    return lax.optimization_barrier((value,) + done)[0]


def rms(values):
    return lax.rsqrt(jnp.mean(values * values, axis=-1, keepdims=True) + EPSILON)


def norm_grad(inner, normed, inverse):
    return inverse * (inner - normed * jnp.mean(inner * normed, axis=-1, keepdims=True))


def local(
    inputs,
    cotangent,
    lengths,
    attn_scale,
    w_query,
    w_key,
    w_value,
    w_out,
    rel_table,
    ffn_scale,
    w_gate,
    w_up,
    w_down,
):
    seqs = lax.axis_size("seq")
    near_count = lax.axis_size("near")
    mp_count = lax.axis_size("mp")
    members = near_count * CORES
    sources = seqs * members
    tok_rows, model = inputs.shape
    seq_len = tok_rows * members
    own_rows = tok_rows // mp_count
    half_rows = seq_len // CORES
    shard = attn_scale.shape[0]
    table_rows, heads_mp = rel_table.shape
    buckets = table_rows * sources
    heads = heads_mp // members
    width = w_query.shape[1] // members
    hidden_width = w_gate.shape[1] // members

    near_at = lax.axis_index("near")
    core_at = lax.axis_index("core")
    mp_at = lax.axis_index("mp")
    member_at = near_at * CORES + core_at
    length = lax.dynamic_slice_in_dim(lengths, lax.axis_index("seq"), 1, 0)
    place = jnp.stack(
        [length[0]] + [at.astype(jnp.int32) for at in (core_at, member_at, mp_at, near_at)]
    )

    def over_mp(own, axis):
        shape = own.shape[:axis] + (mp_count,) + own.shape[axis:]
        blocks = lax.dynamic_update_index_in_dim(jnp.zeros(shape, own.dtype), own, mp_at, axis)
        moved = [(away, shifted(own, away)) for away in reversed(range(1, mp_count))]
        for away, block in moved:
            blocks = lax.dynamic_update_index_in_dim(blocks, block, mp_at ^ away, axis)
        return blocks

    def shifted(block, away):
        return lax.ppermute(block, "mp", [(i, i ^ away) for i in range(mp_count)])

    def in_near_order(own, moved):
        return jnp.stack(
            [jnp.where(near_at == 0, own, moved), jnp.where(near_at == 0, moved, own)], 0
        )

    def near_rows(blocks):
        own = [lax.dynamic_slice_in_dim(block, mp_at * own_rows, own_rows, 0) for block in blocks]
        near = swap(jnp.stack(own), "near")
        came = [(0, near)] + [(away, shifted(near, away)) for away in range(1, mp_count)]
        halves = []
        for half in (came, [(away, swap(block, "core")) for away, block in came]):
            rows = jnp.zeros((len(blocks), mp_count, own_rows, model), near.dtype)
            for away, block in half:
                rows = lax.dynamic_update_index_in_dim(rows, block, mp_at ^ away, 1)
            halves.append([rows[i].reshape(tok_rows, model) for i in range(len(blocks))])
        return *halves, came[1][1]

    def in_order(own, moved, core, core_moved):
        rows = jnp.zeros((CORES, near_count, tok_rows, model), own.dtype)
        for at, block in enumerate((own, moved, core, core_moved)):
            rows = lax.dynamic_update_slice(
                rows, block[None, None], (at // 2, near_at ^ (at % 2), 0, 0)
            )
        return rows.reshape(seq_len, model)

    def gather_rows(near):
        mine = [near] + [shifted(near, away) for away in range(1, mp_count)]
        return mine, [swap(block, "core") for block in mine]

    def sum_cores(mine, other):
        return [
            kept.astype(F32) + swap(sent, "core").astype(F32) for kept, sent in zip(mine, other)
        ]

    def send_mp(sums):
        return [shifted(sums[away].astype(LOW), away) for away in reversed(range(1, mp_count))]

    def sum_mp(sums, *meanwhile):
        moved = send_mp(sums)
        if meanwhile:
            moved = [after(piece, *meanwhile) for piece in moved]
        return sum((piece.astype(F32) for piece in moved), sums[0])

    def split_near(pair):
        sent = jnp.where(near_at == 0, pair[1], pair[0]).astype(LOW)
        return sent, jnp.where(near_at == 0, pair[0], pair[1])

    def sum_near_both(pair):
        low = pair.astype(LOW)
        moved = swap(low, "near")
        return low.astype(F32) + moved.astype(F32), moved

    def near_pair(own, moved):
        pair = [
            lax.dynamic_slice_in_dim(block, mp_at * own_rows, own_rows, 0)
            for block in (own, moved)
        ]
        return in_near_order(*pair)

    def here(pair):
        return lax.dynamic_index_in_dim(pair, near_at, 0, keepdims=False)

    attn_sent = attention_blocks(
        (w_query, w_key, w_value), w_out, attn_scale.reshape(1, shard), rel_table, seqs, members
    )
    attn_got = exchange(attn_sent, COLUMN)
    def partial(left, weight, product, name):
        return partial_rows(left, weight, model, place, near_count, mp_count, product, name)

    table = attn_got[:, shard : shard + table_rows, :heads_mp].reshape(buckets, heads_mp)

    def normed(rows):
        values = rows.astype(F32)
        return (values * rms(values)).astype(LOW)

    (moved_inputs, moved_cotangent), core_moved, first_came = near_rows([inputs, cotangent])
    input_parts = [inputs, moved_inputs, swap(inputs, "core"), core_moved[0]]
    core_cotangent = swap(after(cotangent, moved_inputs), "core")
    grad_parts = [cotangent, moved_cotangent, core_cotangent, core_moved[1]]
    ffn_first, ffn_second = ffn_blocks(
        w_gate, w_up, w_down, after(ffn_scale.reshape(1, shard), first_came), seqs, members
    )
    parts = [normed(part) for part in input_parts]
    parts = lax.optimization_barrier((*parts, ffn_first, ffn_second))[:4]
    first_got = exchange(after(ffn_first, attn_got), COLUMN)

    qkv, attended, prob, out_mine, out_other = attention_forward(
        parts, attn_got, table, place, heads, shard, mp_count
    )
    normed_rows, grad_two = in_order(*parts), in_order(*grad_parts)
    mixed, mixed_moved = sum_near_both(
        after(sum_mp(sum_cores(out_mine, out_other)), first_got, grad_two, normed_rows)
    )
    second_got = exchange(after(ffn_second, mixed_moved), COLUMN)

    pair_inputs = near_pair(inputs, moved_inputs).astype(F32)
    after_attn = pair_inputs + mixed
    inv_two = rms(after_attn)
    normed_two = after_attn * inv_two
    mine_two, other_two = gather_rows(normed_two.astype(LOW))

    d_mine, d_other, hidden_two, acts, d_both, d_down_w = feed_forward(
        mine_two, other_two, grad_two, first_got, second_got, place
    )
    inner_cores = sum_cores(d_mine, d_other)
    down_product = functools.partial(row_product, hidden_width)
    ffn_partial = partial(after(acts, *inner_cores), first_got, down_product, "ffn_out")

    def to_owners(grad):
        return exchange(grad, COLUMN)

    def by_rows(got):
        parts = got.reshape((seqs, members) + got.shape[1:]).astype(F32)
        return jnp.sum(parts, axis=0).reshape(-1, shard)

    d_gate_up_w = contract_rows(hidden_two, after(d_both, *inner_cores)).astype(LOW)
    inner_two, inner_moved = sum_near_both(
        sum_mp(inner_cores, d_gate_up_w, *ffn_partial[0], *ffn_partial[1])
    )

    pair_first = (
        lax.broadcasted_iota(jnp.int32, (near_count, own_rows, 1), 0) * (CORES * tok_rows)
        + lax.broadcasted_iota(jnp.int32, (near_count, own_rows, 1), 1)
        + (core_at * tok_rows + mp_at * own_rows)
    )
    pair_valid = pair_first < length
    pair_grad = near_pair(cotangent, moved_cotangent).astype(F32)
    grad_one = jnp.where(pair_valid, pair_grad, 0.0) + norm_grad(inner_two, normed_two, inv_two)
    grad_one_low = grad_one.astype(LOW)
    mine_one, other_one = gather_rows(grad_one_low)
    d_gate_up = to_owners(
        after(d_gate_up_w, inner_moved, grad_one_low).reshape(sources, shard, -1)
    )
    ffn_cores = sum_cores(*ffn_partial)
    d_qkv, d_table, rows_one = attention_backward(
        prob, mine_one, other_one, attn_got, qkv, place, heads, shard, buckets
    )
    qkv_product = functools.partial(column_product, shard, 0, 3 * width)
    ffn_moved = send_mp([after(rows, *mine_one[1:]) for rows in ffn_cores])
    inner_cores = sum_cores(
        *partial(after(d_qkv, *ffn_moved), attn_got, qkv_product, "attention_in")
    )
    inner_pair = sum_mp(inner_cores)
    table_sent = d_table[:, :heads].astype(LOW).reshape(sources, table_rows, heads)
    table_sent = jnp.pad(
        table_sent, ((0, 0), (0, EXTRA - table_rows), (0, 3 * width - heads))
    )
    d_qkv_w = contract_rows(normed_rows, d_qkv).astype(LOW).reshape(sources, shard, -1)
    d_qkv_sent = jnp.concatenate([d_qkv_w, table_sent], 1)
    d_qkv_got = to_owners(after(d_qkv_sent, d_gate_up))
    d_out = contract_rows(after(attended, inner_cores[0]), rows_one)
    d_out = jnp.moveaxis(d_out.astype(LOW).reshape(width, sources, shard), 1, 0)

    (d_w_gate, d_w_up), ffn_gain, _ = owner_grads(
        after(d_gate_up, inner_cores[0]), (w_gate, w_up), ffn_scale.reshape(1, shard), members, None
    )
    ffn_sent, ffn_kept = split_near(
        sum((piece.astype(F32) for piece in ffn_moved), ffn_cores[0])
    )
    inner_sent, inner_kept = split_near(inner_pair)
    came = swap(
        after(jnp.stack([ffn_sent, inner_sent]), d_qkv_got, ffn_gain), "near"
    )
    own_inputs = here(pair_inputs)
    inv_one = rms(own_inputs)
    grad_input = here(grad_one) + norm_grad(inner_kept + came[1].astype(F32), own_inputs * inv_one, inv_one)
    own_out = jnp.where(here(pair_valid), here(after_attn) + ffn_kept + came[0].astype(F32), 0.0)
    owned = jnp.stack([own_out.astype(LOW), grad_input.astype(LOW)])
    rows_out = [jnp.zeros((mp_count, own_rows, model), LOW)] * 2
    blocks_out = [owned] + [shifted(owned, away) for away in range(1, mp_count)]
    d_rows = to_owners(after(jnp.concatenate([d_down_w, d_out], 1), d_qkv_got))
    for away, block in enumerate(blocks_out):
        rows_out = [
            lax.dynamic_update_index_in_dim(rows, block[i], mp_at ^ away, 0)
            for i, rows in enumerate(rows_out)
        ]
    layer_out, d_inputs = (rows.reshape(tok_rows, model) for rows in rows_out)

    (d_w_query, d_w_key, d_w_value), attn_gain, d_rel_table = owner_grads(
        after(d_qkv_got, blocks_out[1]),
        (w_query, w_key, w_value),
        attn_scale.reshape(1, shard),
        members,
        (table_rows, heads_mp),
    )
    gains = jnp.concatenate([attn_gain, ffn_gain], 0)
    gains = sum((shifted(gains, away) for away in range(1, mp_count)), gains)
    return (
        layer_out,
        d_inputs,
        gains[0],
        d_w_query,
        d_w_key,
        d_w_value,
        by_rows(d_rows[:, hidden_width:]),
        d_rel_table,
        gains[1],
        d_w_gate,
        d_w_up,
        by_rows(d_rows[:, :hidden_width]),
    )


def solution(mesh):
    fsdp, mp = mesh.shape["fsdp"], mesh.shape["mp"]

    def run(*args):
        seqs = args[2].shape[0]
        members = fsdp // seqs
        inner = Mesh(
            mesh.devices.reshape(seqs, members // CORES, CORES, mp), ("seq", "near", "core", "mp")
        )
        rows, columns, first = P(COLUMN, None), P("mp", COLUMN), P(COLUMN)
        both = P(COLUMN, "mp")
        in_specs = (
            rows, rows, P(), first, both, both, both, columns, both, first, both, both, columns,
        )
        out_specs = (
            rows, rows, first, both, both, both, columns, both, first, both, both, columns,
        )
        return jax.shard_map(
            local, mesh=inner, in_specs=in_specs, out_specs=out_specs, check_vma=False
        )(*args)

    return run
```

```python
import functools

import jax
import jax.numpy as jnp
from jax import lax
from jax.experimental import pallas as pl
from jax.experimental.pallas import tpu as pltpu
from jax.sharding import Mesh, PartitionSpec as P

LOW = jnp.bfloat16
F32 = jnp.float32
CORES = 2
THRESHOLDS = (12, 16, 23, 32, 46, 64, 91)
EPSILON = 1e-06
MASKED = -1e30
SKEW = 128


def bucket_of(rel_offset):
    distance = jnp.abs(rel_offset)
    far_bucket = 8 + sum(((distance >= threshold).astype(jnp.int32) for threshold in THRESHOLDS))
    bucket_abs = jnp.where(distance < 8, distance, far_bucket)
    return bucket_abs + jnp.where(rel_offset > 0, 16, 0)


def bucket_onehot(buckets, seq_len):
    offset = lax.broadcasted_iota(jnp.int32, (buckets, 2 * seq_len), 1) - seq_len
    bucket = lax.broadcasted_iota(jnp.int32, (buckets, 2 * seq_len), 0)
    return bucket_of(offset) == bucket


def head_lanes(rows, width, head_width, head):
    lane = lax.broadcasted_iota(jnp.int32, (rows, width), 1)
    return (lane >= head * head_width) & (lane < (head + 1) * head_width)


def only(mask, values):
    return jnp.where(mask, values, jnp.zeros_like(values))


def block_place(block, core, near_count):
    return lax.rem(block, near_count) * CORES + lax.bitwise_xor(lax.div(block, near_count), core)


def bias_places(place_ref, step, blocks, rows, seq_len):
    core, near_count = place_ref[1], blocks // CORES
    query = block_place(step, core, near_count) * rows
    return [
        [
            pl.multiple_of(
                block_place(block, core, near_count) * rows - query - part * SKEW + seq_len - SKEW,
                SKEW,
            )
            for block in range(blocks)
        ]
        for part in range(rows // SKEW)
    ]


def forward_kernel(heads, shard, near_count, count, place_ref, *refs):
    own_ref, moved_ref, core_ref, core_moved_ref, got_ref, table_ref = refs[:6]
    qkv_ref, o_ref, p_ref = refs[6:9]
    other_refs, mine_refs = refs[9 : 9 + count], refs[9 + count : 9 + 2 * count]
    skew_ref, held_ref = refs[9 + 2 * count :]
    step = pl.program_id(0)
    seq_len = qkv_ref.shape[0]
    rows, width = o_ref.shape
    model = held_ref.shape[1]
    head_width = width // heads
    span = 2 * seq_len
    blocks = seq_len // rows
    block = row_block(step, near_count)

    @pl.when(step == 0)
    def _():
        weight = got_ref[:, :shard, : 3 * width].reshape(model, 3 * width)
        near = place_ref[4]
        for at, ref in enumerate((own_ref, moved_ref, core_ref, core_moved_ref)):
            first = (at // 2) * near_count + lax.bitwise_xor(near, at % 2)
            qkv_ref[pl.ds(pl.multiple_of(first * rows, rows), rows), :] = rows_dot(
                ref[...], weight
            ).astype(LOW)
        one_hot = bucket_onehot(table_ref.shape[0], seq_len)
        table = table_ref[...].astype(F32)
        column = lax.broadcasted_iota(jnp.int32, table.shape, 1)
        for head in range(heads):
            here = column == place_ref[2] * heads + head
            levels = jnp.sum(jnp.where(here, table, 0.0), axis=1, keepdims=True)
            line = jnp.sum(jnp.where(one_hot, levels, 0.0), axis=0, keepdims=True)
            line = jnp.broadcast_to(line, (SKEW, span))
            skew_ref[head] = pltpu.roll(line, span - SKEW, 1, stride=1, stride_axis=0)

    row = lax.broadcasted_iota(jnp.int32, (1, rows), 1)
    allowed = jnp.concatenate(
        [
            block_place(at, place_ref[1], near_count) * rows + row < place_ref[0]
            for at in range(blocks)
        ],
        1,
    )
    queries = qkv_ref[pl.ds(pl.multiple_of(block * rows, rows), rows), :width]
    keys = qkv_ref[:, width : 2 * width]
    values = qkv_ref[:, 2 * width :]
    total = jnp.zeros((rows, width), F32)
    places = bias_places(place_ref, block, blocks, rows, seq_len)
    for head in range(heads):
        scores = lax.dot_general(
            only(head_lanes(rows, width, head_width, head), queries),
            keys,
            (((1,), (1,)), ((), ())),
            preferred_element_type=F32,
        )
        bias = jnp.concatenate(
            [
                jnp.concatenate([skew_ref[head, :, pl.ds(place, rows)] for place in part], 1)
                for part in places
            ],
            0,
        )
        scores = jnp.where(allowed, scores + bias, MASKED)
        grown = jnp.exp(scores - jnp.max(scores, axis=1, keepdims=True))
        prob = (grown * (1.0 / jnp.sum(grown, axis=1, keepdims=True))).astype(LOW)
        p_ref[head] = prob
        total = total + jnp.dot(
            prob,
            only(head_lanes(seq_len, width, head_width, head), values),
            preferred_element_type=F32,
        )
    attended = total.astype(LOW)
    o_ref[...] = attended
    weight = got_ref[:, :shard, 3 * width :].reshape(model, width)
    held_ref[...] = contract_cols(attended, weight).astype(LOW)
    send_rows(step, near_count, place_ref[3], held_ref, other_refs, mine_refs)


def attention_forward(parts, got, table, place, heads, shard, count):
    rows, model = parts[0].shape
    blocks = len(parts)
    near_count = blocks // CORES
    seq_len, width = rows * blocks, got.shape[2] // 4
    out_specs, out_shape = sent_specs(near_count, count, rows // count, model)

    def fixed(shape):
        return pl.BlockSpec(shape, lambda i: (0,) * len(shape))

    outs = pl.pallas_call(
        functools.partial(forward_kernel, heads, shard, near_count, count),
        grid=(blocks,),
        in_specs=[pl.BlockSpec(memory_space=pltpu.SMEM)]
        + [fixed(part.shape) for part in parts]
        + [fixed(got.shape), fixed(table.shape)],
        out_specs=[
            fixed((seq_len, 3 * width)),
            pl.BlockSpec((rows, width), lambda i: (row_block(i, near_count), 0)),
            pl.BlockSpec((heads, rows, seq_len), lambda i: (0, row_block(i, near_count), 0)),
        ]
        + out_specs,
        out_shape=[
            jax.ShapeDtypeStruct((seq_len, 3 * width), LOW),
            jax.ShapeDtypeStruct((seq_len, width), LOW),
            jax.ShapeDtypeStruct((heads, seq_len, seq_len), LOW),
        ]
        + out_shape,
        scratch_shapes=[
            pltpu.VMEM((heads, SKEW, 2 * seq_len), F32),
            pltpu.VMEM((rows, model), LOW),
        ],
        compiler_params=pltpu.CompilerParams(vmem_limit_bytes=34 * 2**20),
        cost_estimate=pl.CostEstimate(flops=0, bytes_accessed=0, transcendentals=0),
        name="attention_forward",
    )(place, *parts, got, table)
    return (*outs[:3], outs[3 + count :], outs[3 : 3 + count])


def backward_kernel(heads, shard, near_count, count, place_ref, *refs):
    came, refs = refs[: 2 * count], refs[2 * count :]
    p_ref, got_ref, qkv_ref, d_ref, dt_ref, rows_ref, dk_sum, dv_sum, skew_ref = refs
    step = pl.program_id(0)
    block = row_block(step, near_count)
    take_rows(step, near_count, place_ref[3], came[:count], came[count:], rows_ref)
    rows, model = rows_ref.shape
    seq_len = qkv_ref.shape[0]
    width = qkv_ref.shape[1] // 3
    head_width = width // heads
    span = 2 * seq_len
    blocks = seq_len // rows

    @pl.when(step == 0)
    def _():
        dk_sum[...] = jnp.zeros_like(dk_sum)
        dv_sum[...] = jnp.zeros_like(dv_sum)
        skew_ref[...] = jnp.zeros_like(skew_ref)

    here = pl.ds(pl.multiple_of(block * rows, rows), rows)
    queries = qkv_ref[here, :width]
    keys = qkv_ref[:, width : 2 * width]
    values = qkv_ref[:, 2 * width :]
    weight = got_ref[:, :shard, 3 * width :].reshape(model, width)
    grads = rows_dot(rows_ref[...], weight).astype(LOW)
    total = jnp.zeros((rows, width), F32)
    places = bias_places(place_ref, block, blocks, rows, seq_len)
    for head in range(heads):
        own = head_lanes(rows, width, head_width, head)
        own_grads = only(own, grads)
        d_prob = lax.dot_general(
            own_grads, values, (((1,), (1,)), ((), ())), preferred_element_type=F32
        )
        prob_low = p_ref[head]
        prob = prob_low.astype(F32)
        weighed = prob * d_prob
        d_scores = (weighed - prob * jnp.sum(weighed, axis=1, keepdims=True)).astype(LOW)
        total = total + jnp.dot(
            d_scores,
            only(head_lanes(seq_len, width, head_width, head), keys),
            preferred_element_type=F32,
        )
        dk_sum[...] += lax.dot_general(
            d_scores, only(own, queries), (((0,), (0,)), ((), ())), preferred_element_type=F32
        )
        dv_sum[...] += lax.dot_general(
            prob_low, own_grads, (((0,), (0,)), ((), ())), preferred_element_type=F32
        )
        for part in range(rows // SKEW):
            for at in range(blocks):
                skew_ref[head, :, pl.ds(places[part][at], rows)] += d_scores[
                    part * SKEW : (part + 1) * SKEW, at * rows : (at + 1) * rows
                ].astype(F32)
    d_ref[here, :width] = total.astype(LOW)

    @pl.when(step == pl.num_programs(0) - 1)
    def _():
        d_ref[:, width : 2 * width] = dk_sum[...].astype(LOW)
        d_ref[:, 2 * width :] = dv_sum[...].astype(LOW)
        one_hot = bucket_onehot(dt_ref.shape[0], seq_len)
        row = lax.broadcasted_iota(jnp.int32, (SKEW, span), 0)
        column = lax.broadcasted_iota(jnp.int32, dt_ref.shape, 1)
        result = jnp.zeros(dt_ref.shape, F32)
        for head in range(heads):
            level = pltpu.roll(skew_ref[head], SKEW, 1)
            bit = 1
            while bit < SKEW:
                level = jnp.where((row & bit) != 0, pltpu.roll(level, span - bit, 1), level)
                bit *= 2
            line = jnp.sum(level, axis=0, keepdims=True)
            summed = jnp.sum(jnp.where(one_hot, line, 0.0), axis=1, keepdims=True)
            result = jnp.where(column == head, summed, result)
        dt_ref[...] = result


def attention_backward(prob, mine, other, got, qkv, place, heads, shard, buckets):
    seq_len, width = qkv.shape[0], qkv.shape[1] // 3
    near_count, own_rows, model = mine[0].shape
    count = len(mine)
    rows = count * own_rows
    came_specs, _ = sent_specs(near_count, count, own_rows, model)
    return pl.pallas_call(
        functools.partial(backward_kernel, heads, shard, near_count, count),
        grid=(seq_len // rows,),
        in_specs=[
            pl.BlockSpec(memory_space=pltpu.SMEM),
            *came_specs,
            pl.BlockSpec((heads, rows, seq_len), lambda i: (0, row_block(i, near_count), 0)),
            pl.BlockSpec(got.shape, lambda i: (0, 0, 0)),
            pl.BlockSpec(qkv.shape, lambda i: (0, 0)),
        ],
        out_specs=[
            pl.BlockSpec(qkv.shape, lambda i: (0, 0)),
            pl.BlockSpec((buckets, 128), lambda i: (0, 0)),
            pl.BlockSpec((rows, model), lambda i: (row_block(i, near_count), 0)),
        ],
        out_shape=[
            jax.ShapeDtypeStruct(qkv.shape, LOW),
            jax.ShapeDtypeStruct((buckets, 128), F32),
            jax.ShapeDtypeStruct((seq_len, model), LOW),
        ],
        scratch_shapes=[
            pltpu.VMEM((seq_len, width), F32),
            pltpu.VMEM((seq_len, width), F32),
            pltpu.VMEM((heads, SKEW, 2 * seq_len), F32),
        ],
        compiler_params=pltpu.CompilerParams(vmem_limit_bytes=34 * 2**20),
        cost_estimate=pl.CostEstimate(
            flops=8 * seq_len * seq_len * width * 4,
            bytes_accessed=2 * heads * seq_len * seq_len,
            transcendentals=0,
        ),
        name="attention_backward",
    )(place, *other, *mine, prob, got, qkv)


EXTRA = 8
OWNER_ROWS = 64


def as_column(row, first, count):
    size = row.shape[1]
    here = lax.broadcasted_iota(jnp.int32, (count, size), 1) == first + lax.broadcasted_iota(
        jnp.int32, (count, size), 0
    )
    return jnp.sum(jnp.where(here, row, 0.0), axis=1, keepdims=True)


def blocks_kernel(seqs, members, q_ref, k_ref, v_ref, o_ref, gain_ref, table_ref, sent_ref):
    shard = q_ref.shape[0]
    width = q_ref.shape[1] // members
    gain = as_column(gain_ref[...].astype(LOW).astype(F32), 0, shard)
    parts = [
        (ref[...].astype(LOW).astype(F32) * gain).astype(LOW) for ref in (q_ref, k_ref, v_ref)
    ]
    parts.append(o_ref[...].T.astype(LOW))
    rest = jnp.zeros((EXTRA, sent_ref.shape[2]), LOW)
    table_rows, heads = table_ref.shape
    for seq in range(seqs):
        for member in range(members):
            at = seq * members + member
            for i, part in enumerate(parts):
                sent_ref[at, :shard, i * width : (i + 1) * width] = part[
                    :, member * width : (member + 1) * width
                ]
            sent_ref[at, shard:, :] = rest
            sent_ref[at, shard : shard + table_rows, :heads] = table_ref[...].astype(LOW)


def attention_blocks(weights, w_out, gain, table, seqs, members):
    shard, columns = weights[0].shape
    return pl.pallas_call(
        functools.partial(blocks_kernel, seqs, members),
        out_shape=jax.ShapeDtypeStruct(
            (seqs * members, shard + EXTRA, 4 * columns // members), LOW
        ),
        compiler_params=pltpu.CompilerParams(vmem_limit_bytes=60 * 2**20),
        cost_estimate=pl.CostEstimate(
            flops=0, bytes_accessed=16 * shard * columns, transcendentals=0
        ),
        name="attention_blocks",
    )(*weights, w_out, gain, table)


def owner_kernel(count, members, table_shape, *refs):
    got_ref, extra_ref = refs[:2]
    weight_refs = refs[2 : 2 + count]
    gain_ref = refs[2 + count]
    grad_refs = refs[3 + count : 3 + 2 * count]
    sum_ref = refs[3 + 2 * count]
    step = pl.program_id(0)
    rows = got_ref.shape[1]
    seqs = got_ref.shape[0] // members
    width = got_ref.shape[2] // count
    size = sum_ref.shape[1]
    gain = as_column(gain_ref[...].astype(LOW).astype(F32), step * rows, rows)
    total = jnp.zeros((rows, 1), F32)
    for member in range(members):
        product = sum(got_ref[seq * members + member].astype(F32) for seq in range(seqs))
        for i in range(count):
            part = product[:, i * width : (i + 1) * width]
            here = pl.ds(member * width, width)
            grad_refs[i][:, here] = part * gain
            weight = weight_refs[i][:, here].astype(LOW).astype(F32)
            total = total + jnp.sum(weight * part, axis=1, keepdims=True)

    @pl.when(step == 0)
    def _():
        sum_ref[...] = jnp.zeros_like(sum_ref)

    diagonal = lax.broadcasted_iota(jnp.int32, (rows, size), 1) == step * rows + (
        lax.broadcasted_iota(jnp.int32, (rows, size), 0)
    )
    sum_ref[...] += jnp.sum(jnp.where(diagonal, total, 0.0), axis=0, keepdims=True)
    if table_shape is not None:
        table_rows, heads = table_shape
        each = heads // members
        for member in range(members):
            piece = sum(extra_ref[seq * members + member].astype(F32) for seq in range(seqs))
            refs[-1][:, member * each : (member + 1) * each] = piece[:table_rows, :each]


def owner_grads(got, weights, gain, members, table_shape):
    sources, height, columns = got.shape
    shard, wide = weights[0].shape
    count = len(weights)
    rows = min(OWNER_ROWS, shard)
    step_rows = pl.BlockSpec((rows, wide), lambda i: (i, 0))
    row = pl.BlockSpec((1, shard), lambda i: (0, 0))
    last = height // EXTRA - 1
    out_specs = [step_rows] * count + [row]
    out_shape = [jax.ShapeDtypeStruct((shard, wide), F32)] * count
    out_shape.append(jax.ShapeDtypeStruct((1, shard), F32))
    if table_shape is not None:
        out_specs.append(pl.BlockSpec(table_shape, lambda i: (0, 0)))
        out_shape.append(jax.ShapeDtypeStruct(table_shape, F32))
    outs = pl.pallas_call(
        functools.partial(owner_kernel, count, members, table_shape),
        grid=(shard // rows,),
        in_specs=[
            pl.BlockSpec((sources, rows, columns), lambda i: (0, i, 0)),
            pl.BlockSpec((sources, EXTRA, columns), lambda i: (0, last, 0)),
        ]
        + [step_rows] * count
        + [row],
        out_specs=out_specs,
        out_shape=out_shape,
        compiler_params=pltpu.CompilerParams(vmem_limit_bytes=32 * 2**20),
        cost_estimate=pl.CostEstimate(
            flops=0, bytes_accessed=10 * count * shard * wide, transcendentals=0
        ),
        name="owner_grads",
    )(got, got, *weights, gain)
    return outs[:count], outs[count], outs[-1] if table_shape is not None else None


def rows_dot(left, right):
    return jnp.dot(left, right, preferred_element_type=F32)


def contract_cols(left, right):
    return lax.dot_general(left, right, (((1,), (1,)), ((), ())), preferred_element_type=F32)


def contract_rows(left, right):
    return lax.dot_general(left, right, (((0,), (0,)), ((), ())), preferred_element_type=F32)

def row_block(step, near_count):
    return lax.rem(step + near_count, CORES * near_count)


def send_rows(step, near_count, mp_at, held_ref, other_refs, mine_refs):
    count = len(other_refs)
    own_rows = held_ref.shape[0] // count

    def write(refs):
        for away, ref in enumerate(refs):
            first = pl.multiple_of(lax.bitwise_xor(mp_at, away) * own_rows, own_rows)
            ref[0] = held_ref[pl.ds(first, own_rows), :]

    @pl.when(step < near_count)
    def _():
        write(other_refs)

    @pl.when(step >= near_count)
    def _():
        write(mine_refs)


def take_rows(step, near_count, mp_at, other_refs, mine_refs, rows_ref):
    own_rows = other_refs[0].shape[1]

    def read(refs):
        for away, ref in enumerate(refs):
            first = pl.multiple_of(lax.bitwise_xor(mp_at, away) * own_rows, own_rows)
            rows_ref[pl.ds(first, own_rows), :] = ref[0]

    @pl.when(step < near_count)
    def _():
        read(other_refs)

    @pl.when(step >= near_count)
    def _():
        read(mine_refs)


def sent_specs(near_count, count, own_rows, model):
    other = pl.BlockSpec((1, own_rows, model), lambda i: (jnp.minimum(i, near_count - 1), 0, 0))
    mine = pl.BlockSpec((1, own_rows, model), lambda i: (jnp.maximum(i - near_count, 0), 0, 0))
    shape = jax.ShapeDtypeStruct((near_count, own_rows, model), LOW)
    return [other] * count + [mine] * count, [shape] * (2 * count)


def partial_kernel(near_count, count, product, place_ref, left_ref, weight_ref, *refs):
    held_ref = refs[-1]
    product(left_ref, weight_ref, held_ref)
    send_rows(
        pl.program_id(0), near_count, place_ref[3], held_ref, refs[:count], refs[count : 2 * count]
    )


def partial_rows(left, weight, model, place, near_count, count, product, name):
    seq_len, depth = left.shape
    rows = seq_len // (CORES * near_count)
    out_specs, out_shape = sent_specs(near_count, count, rows // count, model)
    outs = pl.pallas_call(
        functools.partial(partial_kernel, near_count, count, product),
        grid=(CORES * near_count,),
        in_specs=[
            pl.BlockSpec(memory_space=pltpu.SMEM),
            pl.BlockSpec((rows, depth), lambda i: (row_block(i, near_count), 0)),
            pl.BlockSpec(weight.shape, lambda i: (0, 0, 0)),
        ],
        out_specs=out_specs,
        out_shape=out_shape,
        scratch_shapes=[pltpu.VMEM((rows, model), LOW)],
        compiler_params=pltpu.CompilerParams(vmem_limit_bytes=40 * 2**20),
        cost_estimate=pl.CostEstimate(
            flops=2 * seq_len * depth * model, bytes_accessed=2 * seq_len * model, transcendentals=0
        ),
        name=name,
    )(place, left, weight)
    return outs[count:], outs[:count]


def column_product(shard, first, last, left_ref, weight_ref, held_ref):
    weight = weight_ref[:, :shard, first:last]
    weight = weight.reshape(weight.shape[0] * shard, last - first)
    held_ref[...] = contract_cols(left_ref[...], weight).astype(LOW)


def row_product(height, left_ref, weight_ref, held_ref):
    left = left_ref[...]
    width = weight_ref.shape[2]
    for at in range(weight_ref.shape[0]):
        held_ref[:, at * width : (at + 1) * width] = rows_dot(
            left, weight_ref[at, :height, :]
        ).astype(LOW)


def ffn_blocks_kernel(seqs, members, gate_ref, up_ref, down_ref, gain_ref, first_ref, second_ref):
    shard = gate_ref.shape[0]
    width = gate_ref.shape[1] // members
    gain = as_column(gain_ref[...].astype(LOW).astype(F32), 0, shard)
    for member in range(members):
        here = slice(member * width, (member + 1) * width)
        parts = [
            (ref[:, here].astype(LOW).astype(F32) * gain).astype(LOW) for ref in (gate_ref, up_ref)
        ]
        both = jnp.concatenate(parts, 1)
        down = down_ref[here, :].astype(LOW)
        for seq in range(seqs):
            at = seq * members + member
            first_ref[at, :width, :] = down
            first_ref[at, width:, :] = both[:, :shard]
            second_ref[at] = both[:, shard:]


def ffn_blocks(w_gate, w_up, w_down, gain, seqs, members):
    shard, columns = w_gate.shape
    width = columns // members
    return pl.pallas_call(
        functools.partial(ffn_blocks_kernel, seqs, members),
        out_shape=[
            jax.ShapeDtypeStruct((seqs * members, width + shard, shard), LOW),
            jax.ShapeDtypeStruct((seqs * members, shard, 2 * width - shard), LOW),
        ],
        compiler_params=pltpu.CompilerParams(vmem_limit_bytes=40 * 2**20),
        cost_estimate=pl.CostEstimate(
            flops=0, bytes_accessed=18 * shard * columns, transcendentals=0
        ),
        name="ffn_blocks",
    )(w_gate, w_up, w_down, gain)


def ffn_kernel(near_count, count, place_ref, *refs):
    came, refs = refs[: 2 * count], refs[2 * count :]
    grad_ref, first_ref, second_ref = refs[:3]
    other_refs, mine_refs = refs[3 : 3 + count], refs[3 + count : 3 + 2 * count]
    rows_ref, act_ref, d_ref, down_ref, held_ref, sum_ref = refs[3 + 2 * count :]
    step = pl.program_id(0)
    take_rows(step, near_count, place_ref[3], came[:count], came[count:], rows_ref)
    sources, height, shard = first_ref.shape
    width = height - shard
    rows = rows_ref[...]
    block = row_block(step, near_count)
    first = block_place(block, place_ref[1], near_count) * rows.shape[0]
    valid = first + lax.broadcasted_iota(jnp.int32, (rows.shape[0], 1), 0) < place_ref[0]
    grads = only(valid, grad_ref[...])
    early = first_ref[:, width:, :].reshape(sources * shard, shard)
    late = second_ref[...].reshape(sources * shard, 2 * width - shard)
    both = jnp.concatenate([rows_dot(rows, early), rows_dot(rows, late)], 1)
    gate, up = both[:, :width], both[:, width:]
    scale, cubic = 0.7978845608028654, 0.044715
    square = gate * gate
    bent = jnp.tanh(scale * (gate + cubic * square * gate))
    half = 0.5 * (1.0 + bent)
    value = gate * half
    slope = half + 0.5 * gate * (1.0 - bent * bent) * (scale * (1.0 + 3.0 * cubic * square))
    act = (value * up).astype(LOW)
    act_ref[...] = act
    d_hidden = jnp.zeros((rows.shape[0], width), F32)
    for at in range(sources):
        d_hidden = d_hidden + contract_cols(
            grads[:, at * shard : (at + 1) * shard], first_ref[at, :width, :]
        )
    d_both = jnp.concatenate(
        [(d_hidden * up * slope).astype(LOW), (d_hidden * value).astype(LOW)], 1
    )
    d_ref[...] = d_both
    held_ref[...] = (
        contract_cols(d_both[:, :shard], early) + contract_cols(d_both[:, shard:], late)
    ).astype(LOW)
    send_rows(step, near_count, place_ref[3], held_ref, other_refs, mine_refs)
    product = contract_rows(act, grads)

    @pl.when(step == 0)
    def _():
        sum_ref[...] = product

    @pl.when(step > 0)
    def _():
        sum_ref[...] += product

    @pl.when(step == pl.num_programs(0) - 1)
    def _():
        for at in range(sources):
            down_ref[at] = sum_ref[:, at * shard : (at + 1) * shard].astype(LOW)


def feed_forward(mine, other, grads, first, second, place):
    seq_len, model = grads.shape
    near_count, count = mine[0].shape[0], len(mine)
    sources, height, shard = first.shape
    width = height - shard
    rows = seq_len // (CORES * near_count)
    out_specs, out_shape = sent_specs(near_count, count, rows // count, model)

    def blocks(columns):
        return pl.BlockSpec((rows, columns), lambda i: (row_block(i, near_count), 0))

    outs = pl.pallas_call(
        functools.partial(ffn_kernel, near_count, count),
        grid=(CORES * near_count,),
        in_specs=[
            pl.BlockSpec(memory_space=pltpu.SMEM),
            *out_specs,
            blocks(model),
            pl.BlockSpec(first.shape, lambda i: (0, 0, 0)),
            pl.BlockSpec(second.shape, lambda i: (0, 0, 0)),
        ],
        out_specs=out_specs
        + [
            blocks(model),
            blocks(width),
            blocks(2 * width),
            pl.BlockSpec((sources, width, shard), lambda i: (0, 0, 0)),
        ],
        out_shape=out_shape
        + [
            jax.ShapeDtypeStruct((seq_len, model), LOW),
            jax.ShapeDtypeStruct((seq_len, width), LOW),
            jax.ShapeDtypeStruct((seq_len, 2 * width), LOW),
            jax.ShapeDtypeStruct((sources, width, shard), LOW),
        ],
        scratch_shapes=[pltpu.VMEM((rows, model), LOW), pltpu.VMEM((width, model), F32)],
        compiler_params=pltpu.CompilerParams(vmem_limit_bytes=56 * 2**20),
        cost_estimate=pl.CostEstimate(
            flops=12 * seq_len * model * width, bytes_accessed=12 * seq_len * model, transcendentals=0
        ),
        name="feed_forward",
    )(place, *other, *mine, grads, first, second)
    return outs[count : 2 * count], outs[:count], *outs[2 * count :]


COLUMN = ("seq", "near", "core")


def exchange(blocks, axes):
    return lax.all_to_all(blocks, axes, split_axis=0, concat_axis=0, tiled=True)


def swap(block, axis):
    return lax.ppermute(block, axis, [(0, 1), (1, 0)])


def after(value, *done):
    return lax.optimization_barrier((value,) + done)[0]


def rms(values):
    return lax.rsqrt(jnp.mean(values * values, axis=-1, keepdims=True) + EPSILON)


def norm_grad(inner, normed, inverse):
    return inverse * (inner - normed * jnp.mean(inner * normed, axis=-1, keepdims=True))


def local(
    inputs,
    cotangent,
    lengths,
    attn_scale,
    w_query,
    w_key,
    w_value,
    w_out,
    rel_table,
    ffn_scale,
    w_gate,
    w_up,
    w_down,
):
    seqs = lax.axis_size("seq")
    near_count = lax.axis_size("near")
    mp_count = lax.axis_size("mp")
    members = near_count * CORES
    sources = seqs * members
    tok_rows, model = inputs.shape
    seq_len = tok_rows * members
    own_rows = tok_rows // mp_count
    half_rows = seq_len // CORES
    shard = attn_scale.shape[0]
    table_rows, heads_mp = rel_table.shape
    buckets = table_rows * sources
    heads = heads_mp // members
    width = w_query.shape[1] // members
    hidden_width = w_gate.shape[1] // members

    near_at = lax.axis_index("near")
    core_at = lax.axis_index("core")
    mp_at = lax.axis_index("mp")
    member_at = near_at * CORES + core_at
    length = lax.dynamic_slice_in_dim(lengths, lax.axis_index("seq"), 1, 0)
    place = jnp.stack(
        [length[0]] + [at.astype(jnp.int32) for at in (core_at, member_at, mp_at, near_at)]
    )

    def over_mp(own, axis):
        shape = own.shape[:axis] + (mp_count,) + own.shape[axis:]
        blocks = lax.dynamic_update_index_in_dim(jnp.zeros(shape, own.dtype), own, mp_at, axis)
        moved = [(away, shifted(own, away)) for away in reversed(range(1, mp_count))]
        for away, block in moved:
            blocks = lax.dynamic_update_index_in_dim(blocks, block, mp_at ^ away, axis)
        return blocks

    def shifted(block, away):
        return lax.ppermute(block, "mp", [(i, i ^ away) for i in range(mp_count)])

    def in_near_order(own, moved):
        return jnp.stack(
            [jnp.where(near_at == 0, own, moved), jnp.where(near_at == 0, moved, own)], 0
        )

    def near_rows(blocks, meanwhile):
        own = [lax.dynamic_slice_in_dim(block, mp_at * own_rows, own_rows, 0) for block in blocks]
        near = swap(jnp.stack(own), "near")
        came = [(0, near)] + [(away, shifted(near, away)) for away in range(1, mp_count)]
        made = meanwhile(came[1][1])
        came = came[:2] + [(away, after(block, *made)) for away, block in came[2:]]
        halves = []
        for half in (came, [(away, swap(block, "core")) for away, block in came]):
            rows = jnp.zeros((len(blocks), mp_count, own_rows, model), near.dtype)
            for away, block in half:
                rows = lax.dynamic_update_index_in_dim(rows, block, mp_at ^ away, 1)
            halves.append([rows[i].reshape(tok_rows, model) for i in range(len(blocks))])
        return *halves, made

    def in_order(own, moved, core, core_moved):
        rows = jnp.zeros((CORES, near_count, tok_rows, model), own.dtype)
        for at, block in enumerate((own, moved, core, core_moved)):
            rows = lax.dynamic_update_slice(
                rows, block[None, None], (at // 2, near_at ^ (at % 2), 0, 0)
            )
        return rows.reshape(seq_len, model)

    def gather_rows(near):
        mine = [near] + [shifted(near, away) for away in range(1, mp_count)]
        return mine, [swap(block, "core") for block in mine]

    def sum_cores(mine, other):
        return [
            kept.astype(F32) + swap(sent, "core").astype(F32) for kept, sent in zip(mine, other)
        ]

    def send_mp(sums):
        return [shifted(sums[away].astype(LOW), away) for away in reversed(range(1, mp_count))]

    def sum_mp(sums, *meanwhile):
        moved = send_mp(sums)
        if meanwhile:
            moved = [after(piece, *meanwhile) for piece in moved]
        return sum((piece.astype(F32) for piece in moved), sums[0])

    def split_near(pair):
        sent = jnp.where(near_at == 0, pair[1], pair[0]).astype(LOW)
        return sent, jnp.where(near_at == 0, pair[0], pair[1])

    def sum_near_both(pair):
        low = pair.astype(LOW)
        moved = swap(low, "near")
        return low.astype(F32) + moved.astype(F32), moved

    def near_pair(own, moved):
        pair = [
            lax.dynamic_slice_in_dim(block, mp_at * own_rows, own_rows, 0)
            for block in (own, moved)
        ]
        return in_near_order(*pair)

    def here(pair):
        return lax.dynamic_index_in_dim(pair, near_at, 0, keepdims=False)

    attn_sent = attention_blocks(
        (w_query, w_key, w_value), w_out, attn_scale.reshape(1, shard), rel_table, seqs, members
    )
    attn_got = exchange(attn_sent, COLUMN)
    def partial(left, weight, product, name):
        return partial_rows(left, weight, model, place, near_count, mp_count, product, name)

    table = attn_got[:, shard : shard + table_rows, :heads_mp].reshape(buckets, heads_mp)

    def normed(rows):
        values = rows.astype(F32)
        return (values * rms(values)).astype(LOW)

    def make_blocks(first_came):
        return ffn_blocks(
            w_gate, w_up, w_down, after(ffn_scale.reshape(1, shard), first_came), seqs, members
        )

    (moved_inputs, moved_cotangent), core_moved, (ffn_first, ffn_second) = near_rows(
        [inputs, cotangent], make_blocks
    )
    input_parts = [inputs, moved_inputs, swap(inputs, "core"), core_moved[0]]
    core_cotangent = swap(after(cotangent, moved_inputs), "core")
    grad_parts = [cotangent, moved_cotangent, core_cotangent, core_moved[1]]
    parts = [normed(part) for part in input_parts]
    parts = lax.optimization_barrier((*parts, ffn_first, ffn_second))[:4]
    first_got = exchange(after(ffn_first, attn_got), COLUMN)

    qkv, attended, prob, out_mine, out_other = attention_forward(
        parts, attn_got, table, place, heads, shard, mp_count
    )
    normed_rows, grad_two = in_order(*parts), in_order(*grad_parts)
    mixed, mixed_moved = sum_near_both(
        after(sum_mp(sum_cores(out_mine, out_other)), first_got, grad_two, normed_rows)
    )
    second_got = exchange(after(ffn_second, mixed_moved), COLUMN)

    pair_inputs = near_pair(inputs, moved_inputs).astype(F32)
    after_attn = pair_inputs + mixed
    inv_two = rms(after_attn)
    normed_two = after_attn * inv_two
    mine_two, other_two = gather_rows(normed_two.astype(LOW))

    d_mine, d_other, hidden_two, acts, d_both, d_down_w = feed_forward(
        mine_two, other_two, grad_two, first_got, second_got, place
    )
    inner_cores = sum_cores(d_mine, d_other)
    down_product = functools.partial(row_product, hidden_width)
    ffn_partial = partial(after(acts, *inner_cores), first_got, down_product, "ffn_out")

    def to_owners(grad):
        return exchange(grad, COLUMN)

    def by_rows(got):
        parts = got.reshape((seqs, members) + got.shape[1:]).astype(F32)
        return jnp.sum(parts, axis=0).reshape(-1, shard)

    d_gate_up_w = contract_rows(hidden_two, after(d_both, *inner_cores)).astype(LOW)
    inner_two, inner_moved = sum_near_both(
        sum_mp(inner_cores, d_gate_up_w, *ffn_partial[0], *ffn_partial[1])
    )

    pair_first = (
        lax.broadcasted_iota(jnp.int32, (near_count, own_rows, 1), 0) * (CORES * tok_rows)
        + lax.broadcasted_iota(jnp.int32, (near_count, own_rows, 1), 1)
        + (core_at * tok_rows + mp_at * own_rows)
    )
    pair_valid = pair_first < length
    pair_grad = near_pair(cotangent, moved_cotangent).astype(F32)
    grad_one = jnp.where(pair_valid, pair_grad, 0.0) + norm_grad(inner_two, normed_two, inv_two)
    grad_one_low = grad_one.astype(LOW)
    mine_one, other_one = gather_rows(grad_one_low)
    d_gate_up = to_owners(
        after(d_gate_up_w, inner_moved, grad_one_low).reshape(sources, shard, -1)
    )
    ffn_cores = sum_cores(*ffn_partial)
    d_qkv, d_table, rows_one = attention_backward(
        prob, mine_one, other_one, attn_got, qkv, place, heads, shard, buckets
    )
    qkv_product = functools.partial(column_product, shard, 0, 3 * width)
    ffn_moved = send_mp([after(rows, *mine_one[1:]) for rows in ffn_cores])
    table_sent = d_table[:, :heads].astype(LOW).reshape(sources, table_rows, heads)
    table_sent = jnp.pad(
        table_sent, ((0, 0), (0, EXTRA - table_rows), (0, 3 * width - heads))
    )
    d_qkv_w = contract_rows(normed_rows, d_qkv).astype(LOW).reshape(sources, shard, -1)
    d_qkv_sent = jnp.concatenate([d_qkv_w, table_sent], 1)
    inner_cores = sum_cores(
        *partial(after(d_qkv, d_qkv_sent, *ffn_moved), attn_got, qkv_product, "attention_in")
    )
    inner_pair = sum_mp(inner_cores)
    d_qkv_got = to_owners(after(d_qkv_sent, d_gate_up))
    d_out = contract_rows(after(attended, inner_cores[0]), rows_one)
    d_out = jnp.moveaxis(d_out.astype(LOW).reshape(width, sources, shard), 1, 0)
    d_rows_sent = jnp.concatenate([d_down_w, d_out], 1)

    (d_w_gate, d_w_up), ffn_gain, _ = owner_grads(
        after(d_gate_up, inner_cores[0]), (w_gate, w_up), ffn_scale.reshape(1, shard), members, None
    )
    ffn_sent, ffn_kept = split_near(
        sum((piece.astype(F32) for piece in ffn_moved), ffn_cores[0])
    )
    inner_sent, inner_kept = split_near(inner_pair)
    came = swap(
        after(jnp.stack([ffn_sent, inner_sent]), d_qkv_got, ffn_gain, d_rows_sent), "near"
    )
    own_inputs = here(pair_inputs)
    inv_one = rms(own_inputs)
    grad_input = here(grad_one) + norm_grad(inner_kept + came[1].astype(F32), own_inputs * inv_one, inv_one)
    own_out = jnp.where(here(pair_valid), here(after_attn) + ffn_kept + came[0].astype(F32), 0.0)
    owned = jnp.stack([own_out.astype(LOW), grad_input.astype(LOW)])
    rows_out = [jnp.zeros((mp_count, own_rows, model), LOW)] * 2
    blocks_out = [owned] + [shifted(owned, away) for away in range(1, mp_count)]
    d_rows = to_owners(after(d_rows_sent, d_qkv_got))
    for away, block in enumerate(blocks_out):
        rows_out = [
            lax.dynamic_update_index_in_dim(rows, block[i], mp_at ^ away, 0)
            for i, rows in enumerate(rows_out)
        ]
    layer_out, d_inputs = (rows.reshape(tok_rows, model) for rows in rows_out)

    (d_w_query, d_w_key, d_w_value), attn_gain, d_rel_table = owner_grads(
        after(d_qkv_got, blocks_out[1]),
        (w_query, w_key, w_value),
        attn_scale.reshape(1, shard),
        members,
        (table_rows, heads_mp),
    )
    gains = jnp.concatenate([attn_gain, ffn_gain], 0)
    gains = sum((shifted(gains, away) for away in range(1, mp_count)), gains)
    return (
        layer_out,
        d_inputs,
        gains[0],
        d_w_query,
        d_w_key,
        d_w_value,
        by_rows(d_rows[:, hidden_width:]),
        d_rel_table,
        gains[1],
        d_w_gate,
        d_w_up,
        by_rows(d_rows[:, :hidden_width]),
    )


def solution(mesh):
    fsdp, mp = mesh.shape["fsdp"], mesh.shape["mp"]

    def run(*args):
        seqs = args[2].shape[0]
        members = fsdp // seqs
        inner = Mesh(
            mesh.devices.reshape(seqs, members // CORES, CORES, mp), ("seq", "near", "core", "mp")
        )
        rows, columns, first = P(COLUMN, None), P("mp", COLUMN), P(COLUMN)
        both = P(COLUMN, "mp")
        in_specs = (
            rows, rows, P(), first, both, both, both, columns, both, first, both, both, columns,
        )
        out_specs = (
            rows, rows, first, both, both, both, columns, both, first, both, both, columns,
        )
        return jax.shard_map(
            local, mesh=inner, in_specs=in_specs, out_specs=out_specs, check_vma=False
        )(*args)

    return run
```

```python
import functools

import jax
import jax.numpy as jnp
from jax import lax
from jax.experimental import pallas as pl
from jax.experimental.pallas import tpu as pltpu
from jax.sharding import Mesh, PartitionSpec as P

LOW = jnp.bfloat16
F32 = jnp.float32
CORES = 2
THRESHOLDS = (12, 16, 23, 32, 46, 64, 91)
EPSILON = 1e-06
MASKED = -1e30
SKEW = 128


def bucket_of(rel_offset):
    distance = jnp.abs(rel_offset)
    far_bucket = 8 + sum(((distance >= threshold).astype(jnp.int32) for threshold in THRESHOLDS))
    bucket_abs = jnp.where(distance < 8, distance, far_bucket)
    return bucket_abs + jnp.where(rel_offset > 0, 16, 0)


def bucket_onehot(buckets, seq_len):
    offset = lax.broadcasted_iota(jnp.int32, (buckets, 2 * seq_len), 1) - seq_len
    bucket = lax.broadcasted_iota(jnp.int32, (buckets, 2 * seq_len), 0)
    return bucket_of(offset) == bucket


def head_lanes(rows, width, head_width, head):
    lane = lax.broadcasted_iota(jnp.int32, (rows, width), 1)
    return (lane >= head * head_width) & (lane < (head + 1) * head_width)


def only(mask, values):
    return jnp.where(mask, values, jnp.zeros_like(values))


def block_place(block, core, near_count):
    return lax.rem(block, near_count) * CORES + lax.bitwise_xor(lax.div(block, near_count), core)


def bias_places(place_ref, step, blocks, rows, seq_len):
    core, near_count = place_ref[1], blocks // CORES
    query = block_place(step, core, near_count) * rows
    return [
        [
            pl.multiple_of(
                block_place(block, core, near_count) * rows - query - part * SKEW + seq_len - SKEW,
                SKEW,
            )
            for block in range(blocks)
        ]
        for part in range(rows // SKEW)
    ]


def forward_kernel(heads, shard, near_count, count, place_ref, *refs):
    own_ref, moved_ref, core_ref, core_moved_ref, got_ref, table_ref = refs[:6]
    qkv_ref, o_ref, p_ref = refs[6:9]
    other_refs, mine_refs = refs[9 : 9 + count], refs[9 + count : 9 + 2 * count]
    skew_ref, held_ref = refs[9 + 2 * count :]
    step = pl.program_id(0)
    seq_len = qkv_ref.shape[0]
    rows, width = o_ref.shape
    model = held_ref.shape[1]
    head_width = width // heads
    span = 2 * seq_len
    blocks = seq_len // rows
    block = row_block(step, near_count)

    @pl.when(step == 0)
    def _():
        weight = got_ref[:, :shard, : 3 * width].reshape(model, 3 * width)
        near = place_ref[4]
        for at, ref in enumerate((own_ref, moved_ref, core_ref, core_moved_ref)):
            first = (at // 2) * near_count + lax.bitwise_xor(near, at % 2)
            qkv_ref[pl.ds(pl.multiple_of(first * rows, rows), rows), :] = rows_dot(
                ref[...], weight
            ).astype(LOW)
        one_hot = bucket_onehot(table_ref.shape[0], seq_len)
        table = table_ref[...].astype(F32)
        column = lax.broadcasted_iota(jnp.int32, table.shape, 1)
        for head in range(heads):
            here = column == place_ref[2] * heads + head
            levels = jnp.sum(jnp.where(here, table, 0.0), axis=1, keepdims=True)
            line = jnp.sum(jnp.where(one_hot, levels, 0.0), axis=0, keepdims=True)
            line = jnp.broadcast_to(line, (SKEW, span))
            skew_ref[head] = pltpu.roll(line, span - SKEW, 1, stride=1, stride_axis=0)

    row = lax.broadcasted_iota(jnp.int32, (1, rows), 1)
    allowed = jnp.concatenate(
        [
            block_place(at, place_ref[1], near_count) * rows + row < place_ref[0]
            for at in range(blocks)
        ],
        1,
    )
    queries = qkv_ref[pl.ds(pl.multiple_of(block * rows, rows), rows), :width]
    keys = qkv_ref[:, width : 2 * width]
    values = qkv_ref[:, 2 * width :]
    total = jnp.zeros((rows, width), F32)
    places = bias_places(place_ref, block, blocks, rows, seq_len)
    for head in range(heads):
        scores = lax.dot_general(
            only(head_lanes(rows, width, head_width, head), queries),
            keys,
            (((1,), (1,)), ((), ())),
            preferred_element_type=F32,
        )
        bias = jnp.concatenate(
            [
                jnp.concatenate([skew_ref[head, :, pl.ds(place, rows)] for place in part], 1)
                for part in places
            ],
            0,
        )
        scores = jnp.where(allowed, scores + bias, MASKED)
        grown = jnp.exp(scores - jnp.max(scores, axis=1, keepdims=True))
        prob = (grown * (1.0 / jnp.sum(grown, axis=1, keepdims=True))).astype(LOW)
        p_ref[head] = prob
        total = total + jnp.dot(
            prob,
            only(head_lanes(seq_len, width, head_width, head), values),
            preferred_element_type=F32,
        )
    attended = total.astype(LOW)
    o_ref[...] = attended
    weight = got_ref[:, :shard, 3 * width :].reshape(model, width)
    held_ref[...] = contract_cols(attended, weight).astype(LOW)
    send_rows(step, near_count, place_ref[3], held_ref, other_refs, mine_refs)


def attention_forward(parts, got, table, place, heads, shard, count):
    rows, model = parts[0].shape
    blocks = len(parts)
    near_count = blocks // CORES
    seq_len, width = rows * blocks, got.shape[2] // 4
    out_specs, out_shape = sent_specs(near_count, count, rows // count, model)

    def fixed(shape):
        return pl.BlockSpec(shape, lambda i: (0,) * len(shape))

    outs = pl.pallas_call(
        functools.partial(forward_kernel, heads, shard, near_count, count),
        grid=(blocks,),
        in_specs=[pl.BlockSpec(memory_space=pltpu.SMEM)]
        + [fixed(part.shape) for part in parts]
        + [fixed(got.shape), fixed(table.shape)],
        out_specs=[
            fixed((seq_len, 3 * width)),
            pl.BlockSpec((rows, width), lambda i: (row_block(i, near_count), 0)),
            pl.BlockSpec((heads, rows, seq_len), lambda i: (0, row_block(i, near_count), 0)),
        ]
        + out_specs,
        out_shape=[
            jax.ShapeDtypeStruct((seq_len, 3 * width), LOW),
            jax.ShapeDtypeStruct((seq_len, width), LOW),
            jax.ShapeDtypeStruct((heads, seq_len, seq_len), LOW),
        ]
        + out_shape,
        scratch_shapes=[
            pltpu.VMEM((heads, SKEW, 2 * seq_len), F32),
            pltpu.VMEM((rows, model), LOW),
        ],
        compiler_params=pltpu.CompilerParams(vmem_limit_bytes=34 * 2**20),
        cost_estimate=pl.CostEstimate(flops=0, bytes_accessed=0, transcendentals=0),
        name="attention_forward",
    )(place, *parts, got, table)
    return (*outs[:3], outs[3 + count :], outs[3 : 3 + count])


def backward_kernel(heads, shard, near_count, count, place_ref, *refs):
    came, refs = refs[: 2 * count], refs[2 * count :]
    p_ref, got_ref, qkv_ref, d_ref, dt_ref, rows_ref, dk_sum, dv_sum, skew_ref = refs
    step = pl.program_id(0)
    block = row_block(step, near_count)
    take_rows(step, near_count, place_ref[3], came[:count], came[count:], rows_ref)
    rows, model = rows_ref.shape
    seq_len = qkv_ref.shape[0]
    width = qkv_ref.shape[1] // 3
    head_width = width // heads
    span = 2 * seq_len
    blocks = seq_len // rows

    @pl.when(step == 0)
    def _():
        dk_sum[...] = jnp.zeros_like(dk_sum)
        dv_sum[...] = jnp.zeros_like(dv_sum)
        skew_ref[...] = jnp.zeros_like(skew_ref)

    here = pl.ds(pl.multiple_of(block * rows, rows), rows)
    queries = qkv_ref[here, :width]
    keys = qkv_ref[:, width : 2 * width]
    values = qkv_ref[:, 2 * width :]
    weight = got_ref[:, :shard, 3 * width :].reshape(model, width)
    grads = rows_dot(rows_ref[...], weight).astype(LOW)
    total = jnp.zeros((rows, width), F32)
    places = bias_places(place_ref, block, blocks, rows, seq_len)
    for head in range(heads):
        own = head_lanes(rows, width, head_width, head)
        own_grads = only(own, grads)
        d_prob = lax.dot_general(
            own_grads, values, (((1,), (1,)), ((), ())), preferred_element_type=F32
        )
        prob_low = p_ref[head]
        prob = prob_low.astype(F32)
        weighed = prob * d_prob
        d_scores = (weighed - prob * jnp.sum(weighed, axis=1, keepdims=True)).astype(LOW)
        total = total + jnp.dot(
            d_scores,
            only(head_lanes(seq_len, width, head_width, head), keys),
            preferred_element_type=F32,
        )
        dk_sum[...] += lax.dot_general(
            d_scores, only(own, queries), (((0,), (0,)), ((), ())), preferred_element_type=F32
        )
        dv_sum[...] += lax.dot_general(
            prob_low, own_grads, (((0,), (0,)), ((), ())), preferred_element_type=F32
        )
        for part in range(rows // SKEW):
            for at in range(blocks):
                skew_ref[head, :, pl.ds(places[part][at], rows)] += d_scores[
                    part * SKEW : (part + 1) * SKEW, at * rows : (at + 1) * rows
                ].astype(F32)
    d_ref[here, :width] = total.astype(LOW)

    @pl.when(step == pl.num_programs(0) - 1)
    def _():
        d_ref[:, width : 2 * width] = dk_sum[...].astype(LOW)
        d_ref[:, 2 * width :] = dv_sum[...].astype(LOW)
        one_hot = bucket_onehot(dt_ref.shape[0], seq_len)
        row = lax.broadcasted_iota(jnp.int32, (SKEW, span), 0)
        column = lax.broadcasted_iota(jnp.int32, dt_ref.shape, 1)
        result = jnp.zeros(dt_ref.shape, F32)
        for head in range(heads):
            level = pltpu.roll(skew_ref[head], SKEW, 1)
            bit = 1
            while bit < SKEW:
                level = jnp.where((row & bit) != 0, pltpu.roll(level, span - bit, 1), level)
                bit *= 2
            line = jnp.sum(level, axis=0, keepdims=True)
            summed = jnp.sum(jnp.where(one_hot, line, 0.0), axis=1, keepdims=True)
            result = jnp.where(column == head, summed, result)
        dt_ref[...] = result


def attention_backward(prob, mine, other, got, qkv, place, heads, shard, buckets):
    seq_len, width = qkv.shape[0], qkv.shape[1] // 3
    near_count, own_rows, model = mine[0].shape
    count = len(mine)
    rows = count * own_rows
    came_specs, _ = sent_specs(near_count, count, own_rows, model)
    return pl.pallas_call(
        functools.partial(backward_kernel, heads, shard, near_count, count),
        grid=(seq_len // rows,),
        in_specs=[
            pl.BlockSpec(memory_space=pltpu.SMEM),
            *came_specs,
            pl.BlockSpec((heads, rows, seq_len), lambda i: (0, row_block(i, near_count), 0)),
            pl.BlockSpec(got.shape, lambda i: (0, 0, 0)),
            pl.BlockSpec(qkv.shape, lambda i: (0, 0)),
        ],
        out_specs=[
            pl.BlockSpec(qkv.shape, lambda i: (0, 0)),
            pl.BlockSpec((buckets, 128), lambda i: (0, 0)),
            pl.BlockSpec((rows, model), lambda i: (row_block(i, near_count), 0)),
        ],
        out_shape=[
            jax.ShapeDtypeStruct(qkv.shape, LOW),
            jax.ShapeDtypeStruct((buckets, 128), F32),
            jax.ShapeDtypeStruct((seq_len, model), LOW),
        ],
        scratch_shapes=[
            pltpu.VMEM((seq_len, width), F32),
            pltpu.VMEM((seq_len, width), F32),
            pltpu.VMEM((heads, SKEW, 2 * seq_len), F32),
        ],
        compiler_params=pltpu.CompilerParams(vmem_limit_bytes=34 * 2**20),
        cost_estimate=pl.CostEstimate(flops=0, bytes_accessed=0, transcendentals=0),
        name="attention_backward",
    )(place, *other, *mine, prob, got, qkv)


EXTRA = 8
OWNER_ROWS = 64


def as_column(row, first, count):
    size = row.shape[1]
    here = lax.broadcasted_iota(jnp.int32, (count, size), 1) == first + lax.broadcasted_iota(
        jnp.int32, (count, size), 0
    )
    return jnp.sum(jnp.where(here, row, 0.0), axis=1, keepdims=True)


def blocks_kernel(seqs, members, q_ref, k_ref, v_ref, o_ref, gain_ref, table_ref, sent_ref):
    shard = q_ref.shape[0]
    width = q_ref.shape[1] // members
    gain = as_column(gain_ref[...].astype(LOW).astype(F32), 0, shard)
    parts = [
        (ref[...].astype(LOW).astype(F32) * gain).astype(LOW) for ref in (q_ref, k_ref, v_ref)
    ]
    parts.append(o_ref[...].T.astype(LOW))
    rest = jnp.zeros((EXTRA, sent_ref.shape[2]), LOW)
    table_rows, heads = table_ref.shape
    for seq in range(seqs):
        for member in range(members):
            at = seq * members + member
            for i, part in enumerate(parts):
                sent_ref[at, :shard, i * width : (i + 1) * width] = part[
                    :, member * width : (member + 1) * width
                ]
            sent_ref[at, shard:, :] = rest
            sent_ref[at, shard : shard + table_rows, :heads] = table_ref[...].astype(LOW)


def attention_blocks(weights, w_out, gain, table, seqs, members):
    shard, columns = weights[0].shape
    return pl.pallas_call(
        functools.partial(blocks_kernel, seqs, members),
        out_shape=jax.ShapeDtypeStruct(
            (seqs * members, shard + EXTRA, 4 * columns // members), LOW
        ),
        compiler_params=pltpu.CompilerParams(vmem_limit_bytes=60 * 2**20),
        cost_estimate=pl.CostEstimate(
            flops=0, bytes_accessed=16 * shard * columns, transcendentals=0
        ),
        name="attention_blocks",
    )(*weights, w_out, gain, table)


def owner_kernel(count, members, table_shape, *refs):
    got_ref, extra_ref = refs[:2]
    weight_refs = refs[2 : 2 + count]
    gain_ref = refs[2 + count]
    grad_refs = refs[3 + count : 3 + 2 * count]
    sum_ref = refs[3 + 2 * count]
    step = pl.program_id(0)
    rows = got_ref.shape[1]
    seqs = got_ref.shape[0] // members
    width = got_ref.shape[2] // count
    size = sum_ref.shape[1]
    gain = as_column(gain_ref[...].astype(LOW).astype(F32), step * rows, rows)
    total = jnp.zeros((rows, 1), F32)
    for member in range(members):
        product = sum(got_ref[seq * members + member].astype(F32) for seq in range(seqs))
        for i in range(count):
            part = product[:, i * width : (i + 1) * width]
            here = pl.ds(member * width, width)
            grad_refs[i][:, here] = part * gain
            weight = weight_refs[i][:, here].astype(LOW).astype(F32)
            total = total + jnp.sum(weight * part, axis=1, keepdims=True)

    @pl.when(step == 0)
    def _():
        sum_ref[...] = jnp.zeros_like(sum_ref)

    diagonal = lax.broadcasted_iota(jnp.int32, (rows, size), 1) == step * rows + (
        lax.broadcasted_iota(jnp.int32, (rows, size), 0)
    )
    sum_ref[...] += jnp.sum(jnp.where(diagonal, total, 0.0), axis=0, keepdims=True)
    if table_shape is not None:
        table_rows, heads = table_shape
        each = heads // members
        for member in range(members):
            piece = sum(extra_ref[seq * members + member].astype(F32) for seq in range(seqs))
            refs[-1][:, member * each : (member + 1) * each] = piece[:table_rows, :each]


def owner_grads(got, weights, gain, members, table_shape):
    sources, height, columns = got.shape
    shard, wide = weights[0].shape
    count = len(weights)
    rows = min(OWNER_ROWS, shard)
    step_rows = pl.BlockSpec((rows, wide), lambda i: (i, 0))
    row = pl.BlockSpec((1, shard), lambda i: (0, 0))
    last = height // EXTRA - 1
    out_specs = [step_rows] * count + [row]
    out_shape = [jax.ShapeDtypeStruct((shard, wide), F32)] * count
    out_shape.append(jax.ShapeDtypeStruct((1, shard), F32))
    if table_shape is not None:
        out_specs.append(pl.BlockSpec(table_shape, lambda i: (0, 0)))
        out_shape.append(jax.ShapeDtypeStruct(table_shape, F32))
    outs = pl.pallas_call(
        functools.partial(owner_kernel, count, members, table_shape),
        grid=(shard // rows,),
        in_specs=[
            pl.BlockSpec((sources, rows, columns), lambda i: (0, i, 0)),
            pl.BlockSpec((sources, EXTRA, columns), lambda i: (0, last, 0)),
        ]
        + [step_rows] * count
        + [row],
        out_specs=out_specs,
        out_shape=out_shape,
        compiler_params=pltpu.CompilerParams(vmem_limit_bytes=32 * 2**20),
        cost_estimate=pl.CostEstimate(
            flops=0, bytes_accessed=10 * count * shard * wide, transcendentals=0
        ),
        name="owner_grads",
    )(got, got, *weights, gain)
    return outs[:count], outs[count], outs[-1] if table_shape is not None else None


def rows_kernel(members, split, got_ref, first_ref, second_ref):
    seqs = got_ref.shape[0] // members
    rest = got_ref.shape[1] - split
    for member in range(members):
        total = sum(got_ref[seq * members + member].astype(F32) for seq in range(seqs))
        first_ref[pl.ds(member * split, split), :] = total[:split]
        second_ref[pl.ds(member * rest, rest), :] = total[split:]


def owner_rows(got, members, split):
    height, columns = got.shape[1:]
    return pl.pallas_call(
        functools.partial(rows_kernel, members, split),
        out_shape=[
            jax.ShapeDtypeStruct((members * split, columns), F32),
            jax.ShapeDtypeStruct((members * (height - split), columns), F32),
        ],
        compiler_params=pltpu.CompilerParams(vmem_limit_bytes=32 * 2**20),
        cost_estimate=pl.CostEstimate(
            flops=0, bytes_accessed=4 * got.size, transcendentals=0
        ),
        name="owner_rows",
    )(got)


def rows_dot(left, right):
    return jnp.dot(left, right, preferred_element_type=F32)


def contract_cols(left, right):
    return lax.dot_general(left, right, (((1,), (1,)), ((), ())), preferred_element_type=F32)


def contract_rows(left, right):
    return lax.dot_general(left, right, (((0,), (0,)), ((), ())), preferred_element_type=F32)

def row_block(step, near_count):
    return lax.rem(step + near_count, CORES * near_count)


def send_rows(step, near_count, mp_at, held_ref, other_refs, mine_refs):
    count = len(other_refs)
    own_rows = held_ref.shape[0] // count

    def write(refs):
        for away, ref in enumerate(refs):
            first = pl.multiple_of(lax.bitwise_xor(mp_at, away) * own_rows, own_rows)
            ref[0] = held_ref[pl.ds(first, own_rows), :]

    @pl.when(step < near_count)
    def _():
        write(other_refs)

    @pl.when(step >= near_count)
    def _():
        write(mine_refs)


def take_rows(step, near_count, mp_at, other_refs, mine_refs, rows_ref):
    own_rows = other_refs[0].shape[1]

    def read(refs):
        for away, ref in enumerate(refs):
            first = pl.multiple_of(lax.bitwise_xor(mp_at, away) * own_rows, own_rows)
            rows_ref[pl.ds(first, own_rows), :] = ref[0]

    @pl.when(step < near_count)
    def _():
        read(other_refs)

    @pl.when(step >= near_count)
    def _():
        read(mine_refs)


def sent_specs(near_count, count, own_rows, model):
    other = pl.BlockSpec((1, own_rows, model), lambda i: (jnp.minimum(i, near_count - 1), 0, 0))
    mine = pl.BlockSpec((1, own_rows, model), lambda i: (jnp.maximum(i - near_count, 0), 0, 0))
    shape = jax.ShapeDtypeStruct((near_count, own_rows, model), LOW)
    return [other] * count + [mine] * count, [shape] * (2 * count)


def partial_kernel(near_count, count, product, place_ref, left_ref, weight_ref, *refs):
    held_ref = refs[-1]
    product(left_ref, weight_ref, held_ref)
    send_rows(
        pl.program_id(0), near_count, place_ref[3], held_ref, refs[:count], refs[count : 2 * count]
    )


def partial_rows(left, weight, model, place, near_count, count, product, name):
    seq_len, depth = left.shape
    rows = seq_len // (CORES * near_count)
    out_specs, out_shape = sent_specs(near_count, count, rows // count, model)
    outs = pl.pallas_call(
        functools.partial(partial_kernel, near_count, count, product),
        grid=(CORES * near_count,),
        in_specs=[
            pl.BlockSpec(memory_space=pltpu.SMEM),
            pl.BlockSpec((rows, depth), lambda i: (row_block(i, near_count), 0)),
            pl.BlockSpec(weight.shape, lambda i: (0, 0, 0)),
        ],
        out_specs=out_specs,
        out_shape=out_shape,
        scratch_shapes=[pltpu.VMEM((rows, model), LOW)],
        compiler_params=pltpu.CompilerParams(vmem_limit_bytes=40 * 2**20),
        cost_estimate=pl.CostEstimate(
            flops=0, bytes_accessed=0, transcendentals=0
        ),
        name=name,
    )(place, left, weight)
    return outs[count:], outs[:count]


def column_product(shard, first, last, left_ref, weight_ref, held_ref):
    weight = weight_ref[:, :shard, first:last]
    weight = weight.reshape(weight.shape[0] * shard, last - first)
    held_ref[...] = contract_cols(left_ref[...], weight).astype(LOW)


def row_product(height, left_ref, weight_ref, held_ref):
    left = left_ref[...]
    width = weight_ref.shape[2]
    for at in range(weight_ref.shape[0]):
        held_ref[:, at * width : (at + 1) * width] = rows_dot(
            left, weight_ref[at, :height, :]
        ).astype(LOW)


def ffn_blocks_kernel(seqs, members, gate_ref, up_ref, down_ref, gain_ref, first_ref, second_ref):
    shard = gate_ref.shape[0]
    width = gate_ref.shape[1] // members
    gain = as_column(gain_ref[...].astype(LOW).astype(F32), 0, shard)
    for member in range(members):
        here = slice(member * width, (member + 1) * width)
        parts = [
            (ref[:, here].astype(LOW).astype(F32) * gain).astype(LOW) for ref in (gate_ref, up_ref)
        ]
        both = jnp.concatenate(parts, 1)
        down = down_ref[here, :].astype(LOW)
        for seq in range(seqs):
            at = seq * members + member
            first_ref[at, :width, :] = down
            first_ref[at, width:, :] = both[:, :shard]
            second_ref[at] = both[:, shard:]


def ffn_blocks(w_gate, w_up, w_down, gain, seqs, members):
    shard, columns = w_gate.shape
    width = columns // members
    return pl.pallas_call(
        functools.partial(ffn_blocks_kernel, seqs, members),
        out_shape=[
            jax.ShapeDtypeStruct((seqs * members, width + shard, shard), LOW),
            jax.ShapeDtypeStruct((seqs * members, shard, 2 * width - shard), LOW),
        ],
        compiler_params=pltpu.CompilerParams(vmem_limit_bytes=40 * 2**20),
        cost_estimate=pl.CostEstimate(
            flops=0, bytes_accessed=18 * shard * columns, transcendentals=0
        ),
        name="ffn_blocks",
    )(w_gate, w_up, w_down, gain)


def ffn_kernel(near_count, count, place_ref, *refs):
    came, refs = refs[: 2 * count], refs[2 * count :]
    grad_ref, first_ref, second_ref = refs[:3]
    other_refs, mine_refs = refs[3 : 3 + count], refs[3 + count : 3 + 2 * count]
    rows_ref, act_ref, d_ref, down_ref, held_ref, sum_ref = refs[3 + 2 * count :]
    step = pl.program_id(0)
    take_rows(step, near_count, place_ref[3], came[:count], came[count:], rows_ref)
    sources, height, shard = first_ref.shape
    width = height - shard
    rows = rows_ref[...]
    block = row_block(step, near_count)
    first = block_place(block, place_ref[1], near_count) * rows.shape[0]
    valid = first + lax.broadcasted_iota(jnp.int32, (rows.shape[0], 1), 0) < place_ref[0]
    grads = only(valid, grad_ref[...])
    early = first_ref[:, width:, :].reshape(sources * shard, shard)
    late = second_ref[...].reshape(sources * shard, 2 * width - shard)
    both = jnp.concatenate([rows_dot(rows, early), rows_dot(rows, late)], 1)
    gate, up = both[:, :width], both[:, width:]
    scale, cubic = 0.7978845608028654, 0.044715
    square = gate * gate
    bent = jnp.tanh(scale * (gate + cubic * square * gate))
    half = 0.5 * (1.0 + bent)
    value = gate * half
    slope = half + 0.5 * gate * (1.0 - bent * bent) * (scale * (1.0 + 3.0 * cubic * square))
    act = (value * up).astype(LOW)
    act_ref[...] = act
    d_hidden = jnp.zeros((rows.shape[0], width), F32)
    for at in range(sources):
        d_hidden = d_hidden + contract_cols(
            grads[:, at * shard : (at + 1) * shard], first_ref[at, :width, :]
        )
    d_both = jnp.concatenate(
        [(d_hidden * up * slope).astype(LOW), (d_hidden * value).astype(LOW)], 1
    )
    d_ref[...] = d_both
    held_ref[...] = (
        contract_cols(d_both[:, :shard], early) + contract_cols(d_both[:, shard:], late)
    ).astype(LOW)
    send_rows(step, near_count, place_ref[3], held_ref, other_refs, mine_refs)
    product = contract_rows(act, grads)

    @pl.when(step == 0)
    def _():
        sum_ref[...] = product

    @pl.when(step > 0)
    def _():
        sum_ref[...] += product

    @pl.when(step == pl.num_programs(0) - 1)
    def _():
        for at in range(sources):
            down_ref[at] = sum_ref[:, at * shard : (at + 1) * shard].astype(LOW)


def feed_forward(mine, other, grads, first, second, place):
    seq_len, model = grads.shape
    near_count, count = mine[0].shape[0], len(mine)
    sources, height, shard = first.shape
    width = height - shard
    rows = seq_len // (CORES * near_count)
    out_specs, out_shape = sent_specs(near_count, count, rows // count, model)

    def blocks(columns):
        return pl.BlockSpec((rows, columns), lambda i: (row_block(i, near_count), 0))

    outs = pl.pallas_call(
        functools.partial(ffn_kernel, near_count, count),
        grid=(CORES * near_count,),
        in_specs=[
            pl.BlockSpec(memory_space=pltpu.SMEM),
            *out_specs,
            blocks(model),
            pl.BlockSpec(first.shape, lambda i: (0, 0, 0)),
            pl.BlockSpec(second.shape, lambda i: (0, 0, 0)),
        ],
        out_specs=out_specs
        + [
            blocks(model),
            blocks(width),
            blocks(2 * width),
            pl.BlockSpec((sources, width, shard), lambda i: (0, 0, 0)),
        ],
        out_shape=out_shape
        + [
            jax.ShapeDtypeStruct((seq_len, model), LOW),
            jax.ShapeDtypeStruct((seq_len, width), LOW),
            jax.ShapeDtypeStruct((seq_len, 2 * width), LOW),
            jax.ShapeDtypeStruct((sources, width, shard), LOW),
        ],
        scratch_shapes=[pltpu.VMEM((rows, model), LOW), pltpu.VMEM((width, model), F32)],
        compiler_params=pltpu.CompilerParams(vmem_limit_bytes=56 * 2**20),
        cost_estimate=pl.CostEstimate(
            flops=12 * seq_len * model * width, bytes_accessed=12 * seq_len * model, transcendentals=0
        ),
        name="feed_forward",
    )(place, *other, *mine, grads, first, second)
    return outs[count : 2 * count], outs[:count], *outs[2 * count :]


COLUMN = ("seq", "near", "core")


def exchange(blocks, axes):
    return lax.all_to_all(blocks, axes, split_axis=0, concat_axis=0, tiled=True)


def swap(block, axis):
    return lax.ppermute(block, axis, [(0, 1), (1, 0)])


def after(value, *done):
    return lax.optimization_barrier((value,) + done)[0]


def rms(values):
    return lax.rsqrt(jnp.mean(values * values, axis=-1, keepdims=True) + EPSILON)


def norm_grad(inner, normed, inverse):
    return inverse * (inner - normed * jnp.mean(inner * normed, axis=-1, keepdims=True))


def local(
    inputs,
    cotangent,
    lengths,
    attn_scale,
    w_query,
    w_key,
    w_value,
    w_out,
    rel_table,
    ffn_scale,
    w_gate,
    w_up,
    w_down,
):
    seqs = lax.axis_size("seq")
    near_count = lax.axis_size("near")
    mp_count = lax.axis_size("mp")
    members = near_count * CORES
    sources = seqs * members
    tok_rows, model = inputs.shape
    seq_len = tok_rows * members
    own_rows = tok_rows // mp_count
    half_rows = seq_len // CORES
    shard = attn_scale.shape[0]
    table_rows, heads_mp = rel_table.shape
    buckets = table_rows * sources
    heads = heads_mp // members
    width = w_query.shape[1] // members
    hidden_width = w_gate.shape[1] // members

    near_at = lax.axis_index("near")
    core_at = lax.axis_index("core")
    mp_at = lax.axis_index("mp")
    member_at = near_at * CORES + core_at
    length = lax.dynamic_slice_in_dim(lengths, lax.axis_index("seq"), 1, 0)
    place = jnp.stack(
        [length[0]] + [at.astype(jnp.int32) for at in (core_at, member_at, mp_at, near_at)]
    )

    def over_mp(own, axis):
        shape = own.shape[:axis] + (mp_count,) + own.shape[axis:]
        blocks = lax.dynamic_update_index_in_dim(jnp.zeros(shape, own.dtype), own, mp_at, axis)
        moved = [(away, shifted(own, away)) for away in reversed(range(1, mp_count))]
        for away, block in moved:
            blocks = lax.dynamic_update_index_in_dim(blocks, block, mp_at ^ away, axis)
        return blocks

    def shifted(block, away):
        return lax.ppermute(block, "mp", [(i, i ^ away) for i in range(mp_count)])

    def in_near_order(own, moved):
        return jnp.stack(
            [jnp.where(near_at == 0, own, moved), jnp.where(near_at == 0, moved, own)], 0
        )

    def near_rows(blocks, meanwhile):
        own = [lax.dynamic_slice_in_dim(block, mp_at * own_rows, own_rows, 0) for block in blocks]
        near = swap(jnp.stack(own), "near")
        came = [(0, near)] + [(away, shifted(near, away)) for away in range(1, mp_count)]
        made = meanwhile(came[1][1])
        came = came[:2] + [(away, after(block, *made)) for away, block in came[2:]]
        halves = []
        for half in (came, [(away, swap(block, "core")) for away, block in came]):
            rows = jnp.zeros((len(blocks), mp_count, own_rows, model), near.dtype)
            for away, block in half:
                rows = lax.dynamic_update_index_in_dim(rows, block, mp_at ^ away, 1)
            halves.append([rows[i].reshape(tok_rows, model) for i in range(len(blocks))])
        return *halves, made

    def in_order(own, moved, core, core_moved):
        rows = jnp.zeros((CORES, near_count, tok_rows, model), own.dtype)
        for at, block in enumerate((own, moved, core, core_moved)):
            rows = lax.dynamic_update_slice(
                rows, block[None, None], (at // 2, near_at ^ (at % 2), 0, 0)
            )
        return rows.reshape(seq_len, model)

    def gather_rows(near):
        mine = [near] + [shifted(near, away) for away in range(1, mp_count)]
        return mine, [swap(block, "core") for block in mine]

    def sum_cores(mine, other):
        return [
            kept.astype(F32) + swap(sent, "core").astype(F32) for kept, sent in zip(mine, other)
        ]

    def send_mp(sums):
        return [shifted(sums[away].astype(LOW), away) for away in reversed(range(1, mp_count))]

    def sum_mp(sums, *meanwhile):
        moved = send_mp(sums)
        if meanwhile:
            moved = [after(piece, *meanwhile) for piece in moved]
        return sum((piece.astype(F32) for piece in moved), sums[0])

    def split_near(pair):
        sent = jnp.where(near_at == 0, pair[1], pair[0]).astype(LOW)
        return sent, jnp.where(near_at == 0, pair[0], pair[1])

    def sum_near_both(pair):
        low = pair.astype(LOW)
        moved = swap(low, "near")
        return low.astype(F32) + moved.astype(F32), moved

    def near_pair(own, moved):
        pair = [
            lax.dynamic_slice_in_dim(block, mp_at * own_rows, own_rows, 0)
            for block in (own, moved)
        ]
        return in_near_order(*pair)

    def here(pair):
        return lax.dynamic_index_in_dim(pair, near_at, 0, keepdims=False)

    attn_sent = attention_blocks(
        (w_query, w_key, w_value), w_out, attn_scale.reshape(1, shard), rel_table, seqs, members
    )
    attn_got = exchange(attn_sent, COLUMN)
    def partial(left, weight, product, name):
        return partial_rows(left, weight, model, place, near_count, mp_count, product, name)

    table = attn_got[:, shard : shard + table_rows, :heads_mp].reshape(buckets, heads_mp)

    def normed(rows):
        values = rows.astype(F32)
        return (values * rms(values)).astype(LOW)

    def make_blocks(first_came):
        return ffn_blocks(
            w_gate, w_up, w_down, after(ffn_scale.reshape(1, shard), first_came), seqs, members
        )

    (moved_inputs, moved_cotangent), core_moved, (ffn_first, ffn_second) = near_rows(
        [inputs, cotangent], make_blocks
    )
    input_parts = [inputs, moved_inputs, swap(inputs, "core"), core_moved[0]]
    core_cotangent = swap(after(cotangent, moved_inputs), "core")
    grad_parts = [cotangent, moved_cotangent, core_cotangent, core_moved[1]]
    parts = [normed(part) for part in input_parts]
    parts = lax.optimization_barrier((*parts, ffn_first, ffn_second))[:4]
    first_got = exchange(after(ffn_first, attn_got), COLUMN)

    qkv, attended, prob, out_mine, out_other = attention_forward(
        parts, attn_got, table, place, heads, shard, mp_count
    )
    normed_rows, grad_two = in_order(*parts), in_order(*grad_parts)
    mixed, mixed_moved = sum_near_both(
        after(sum_mp(sum_cores(out_mine, out_other)), first_got, grad_two, normed_rows)
    )
    second_got = exchange(after(ffn_second, mixed_moved), COLUMN)

    pair_inputs = near_pair(inputs, moved_inputs).astype(F32)
    after_attn = pair_inputs + mixed
    inv_two = rms(after_attn)
    normed_two = after_attn * inv_two
    mine_two, other_two = gather_rows(normed_two.astype(LOW))

    d_mine, d_other, hidden_two, acts, d_both, d_down_w = feed_forward(
        mine_two, other_two, grad_two, first_got, second_got, place
    )
    inner_cores = sum_cores(d_mine, d_other)
    down_product = functools.partial(row_product, hidden_width)
    ffn_partial = partial(after(acts, *inner_cores), first_got, down_product, "ffn_out")

    def to_owners(grad):
        return exchange(grad, COLUMN)

    d_gate_up_w = contract_rows(hidden_two, after(d_both, *inner_cores)).astype(LOW)
    inner_two, inner_moved = sum_near_both(
        sum_mp(inner_cores, d_gate_up_w, *ffn_partial[0], *ffn_partial[1])
    )

    pair_first = (
        lax.broadcasted_iota(jnp.int32, (near_count, own_rows, 1), 0) * (CORES * tok_rows)
        + lax.broadcasted_iota(jnp.int32, (near_count, own_rows, 1), 1)
        + (core_at * tok_rows + mp_at * own_rows)
    )
    pair_valid = pair_first < length
    pair_grad = near_pair(cotangent, moved_cotangent).astype(F32)
    grad_one = jnp.where(pair_valid, pair_grad, 0.0) + norm_grad(inner_two, normed_two, inv_two)
    grad_one_low = grad_one.astype(LOW)
    mine_one, other_one = gather_rows(grad_one_low)
    d_gate_up = to_owners(
        after(d_gate_up_w, inner_moved, grad_one_low).reshape(sources, shard, -1)
    )
    ffn_cores = sum_cores(*ffn_partial)
    d_qkv, d_table, rows_one = attention_backward(
        prob, mine_one, other_one, attn_got, qkv, place, heads, shard, buckets
    )
    qkv_product = functools.partial(column_product, shard, 0, 3 * width)
    ffn_moved = send_mp([after(rows, *mine_one[1:]) for rows in ffn_cores])
    table_sent = d_table[:, :heads].astype(LOW).reshape(sources, table_rows, heads)
    table_sent = jnp.pad(
        table_sent, ((0, 0), (0, EXTRA - table_rows), (0, 3 * width - heads))
    )
    d_qkv_w = contract_rows(normed_rows, d_qkv).astype(LOW).reshape(sources, shard, -1)
    d_qkv_sent = jnp.concatenate([d_qkv_w, table_sent], 1)
    inner_cores = sum_cores(
        *partial(after(d_qkv, d_qkv_sent, *ffn_moved), attn_got, qkv_product, "attention_in")
    )
    inner_pair = sum_mp(inner_cores)
    d_qkv_got = to_owners(after(d_qkv_sent, d_gate_up))
    d_out = contract_rows(after(attended, inner_cores[0]), rows_one)
    d_out = jnp.moveaxis(d_out.astype(LOW).reshape(width, sources, shard), 1, 0)
    d_rows_sent = jnp.concatenate([d_down_w, d_out], 1)

    (d_w_gate, d_w_up), ffn_gain, _ = owner_grads(
        after(d_gate_up, inner_cores[0]), (w_gate, w_up), ffn_scale.reshape(1, shard), members, None
    )
    ffn_sent, ffn_kept = split_near(
        sum((piece.astype(F32) for piece in ffn_moved), ffn_cores[0])
    )
    inner_sent, inner_kept = split_near(inner_pair)
    came = swap(
        after(jnp.stack([ffn_sent, inner_sent]), here(pair_valid), d_rows_sent, ffn_gain), "near"
    )
    own_inputs = here(pair_inputs)
    inv_one = rms(own_inputs)
    grad_input = here(grad_one) + norm_grad(inner_kept + came[1].astype(F32), own_inputs * inv_one, inv_one)
    own_out = jnp.where(here(pair_valid), here(after_attn) + ffn_kept + came[0].astype(F32), 0.0)
    owned = after(
        jnp.stack([own_out.astype(LOW), grad_input.astype(LOW)]), d_qkv_got
    )
    rows_out = [jnp.zeros((mp_count, own_rows, model), LOW)] * 2
    blocks_out = [owned] + [shifted(owned, away) for away in range(1, mp_count)]
    d_rows = to_owners(after(d_rows_sent, d_qkv_got))
    for away, block in enumerate(blocks_out):
        rows_out = [
            lax.dynamic_update_index_in_dim(rows, block[i], mp_at ^ away, 0)
            for i, rows in enumerate(rows_out)
        ]
    layer_out, d_inputs = (rows.reshape(tok_rows, model) for rows in rows_out)

    (d_w_query, d_w_key, d_w_value), attn_gain, d_rel_table = owner_grads(
        after(d_qkv_got, blocks_out[1]),
        (w_query, w_key, w_value),
        attn_scale.reshape(1, shard),
        members,
        (table_rows, heads_mp),
    )
    gains = jnp.concatenate([attn_gain, ffn_gain], 0)
    d_w_down, d_w_out = owner_rows(d_rows, members, hidden_width)
    gains = sum((shifted(gains, away) for away in range(1, mp_count)), gains)
    return (
        layer_out,
        d_inputs,
        gains[0],
        d_w_query,
        d_w_key,
        d_w_value,
        d_w_out,
        d_rel_table,
        gains[1],
        d_w_gate,
        d_w_up,
        d_w_down,
    )


def solution(mesh):
    fsdp, mp = mesh.shape["fsdp"], mesh.shape["mp"]

    def run(*args):
        seqs = args[2].shape[0]
        members = fsdp // seqs
        inner = Mesh(
            mesh.devices.reshape(seqs, members // CORES, CORES, mp), ("seq", "near", "core", "mp")
        )
        rows, columns, first = P(COLUMN, None), P("mp", COLUMN), P(COLUMN)
        both = P(COLUMN, "mp")
        in_specs = (
            rows, rows, P(), first, both, both, both, columns, both, first, both, both, columns,
        )
        out_specs = (
            rows, rows, first, both, both, both, columns, both, first, both, both, columns,
        )
        return jax.shard_map(
            local, mesh=inner, in_specs=in_specs, out_specs=out_specs, check_vma=False
        )(*args)

    return run
```

```python
import functools

import jax
import jax.numpy as jnp
from jax import lax
from jax.experimental import pallas as pl
from jax.experimental.pallas import tpu as pltpu
from jax.sharding import Mesh, PartitionSpec as P

LOW = jnp.bfloat16
F32 = jnp.float32
CORES = 2
THRESHOLDS = (12, 16, 23, 32, 46, 64, 91)
EPSILON = 1e-06
MASKED = -1e30
SKEW = 128


def bucket_of(rel_offset):
    distance = jnp.abs(rel_offset)
    far_bucket = 8 + sum(((distance >= threshold).astype(jnp.int32) for threshold in THRESHOLDS))
    bucket_abs = jnp.where(distance < 8, distance, far_bucket)
    return bucket_abs + jnp.where(rel_offset > 0, 16, 0)


def bucket_onehot(buckets, seq_len):
    offset = lax.broadcasted_iota(jnp.int32, (buckets, 2 * seq_len), 1) - seq_len
    bucket = lax.broadcasted_iota(jnp.int32, (buckets, 2 * seq_len), 0)
    return bucket_of(offset) == bucket


def head_lanes(rows, width, head_width, head):
    lane = lax.broadcasted_iota(jnp.int32, (rows, width), 1)
    return (lane >= head * head_width) & (lane < (head + 1) * head_width)


def only(mask, values):
    return jnp.where(mask, values, jnp.zeros_like(values))


def block_place(block, core, near_count):
    return lax.rem(block, near_count) * CORES + lax.bitwise_xor(lax.div(block, near_count), core)


def bias_places(place_ref, step, blocks, rows, seq_len):
    core, near_count = place_ref[1], blocks // CORES
    query = block_place(step, core, near_count) * rows
    return [
        [
            pl.multiple_of(
                block_place(block, core, near_count) * rows - query - part * SKEW + seq_len - SKEW,
                SKEW,
            )
            for block in range(blocks)
        ]
        for part in range(rows // SKEW)
    ]


def forward_kernel(heads, shard, near_count, count, place_ref, *refs):
    own_ref, moved_ref, core_ref, core_moved_ref, got_ref, table_ref = refs[:6]
    qkv_ref, o_ref, p_ref = refs[6:9]
    other_refs, mine_refs = refs[9 : 9 + count], refs[9 + count : 9 + 2 * count]
    skew_ref, held_ref = refs[9 + 2 * count :]
    step = pl.program_id(0)
    seq_len = qkv_ref.shape[0]
    rows, width = o_ref.shape
    model = held_ref.shape[1]
    head_width = width // heads
    span = 2 * seq_len
    blocks = seq_len // rows
    block = row_block(step, near_count)

    @pl.when(step == 0)
    def _():
        weight = got_ref[:, :shard, : 3 * width].reshape(model, 3 * width)
        near = place_ref[4]
        for at, ref in enumerate((own_ref, moved_ref, core_ref, core_moved_ref)):
            first = (at // 2) * near_count + lax.bitwise_xor(near, at % 2)
            qkv_ref[pl.ds(pl.multiple_of(first * rows, rows), rows), :] = rows_dot(
                ref[...], weight
            ).astype(LOW)
        one_hot = bucket_onehot(table_ref.shape[0], seq_len)
        table = table_ref[...].astype(F32)
        column = lax.broadcasted_iota(jnp.int32, table.shape, 1)
        for head in range(heads):
            here = column == place_ref[2] * heads + head
            levels = jnp.sum(jnp.where(here, table, 0.0), axis=1, keepdims=True)
            line = jnp.sum(jnp.where(one_hot, levels, 0.0), axis=0, keepdims=True)
            line = jnp.broadcast_to(line, (SKEW, span))
            skew_ref[head] = pltpu.roll(line, span - SKEW, 1, stride=1, stride_axis=0)

    row = lax.broadcasted_iota(jnp.int32, (1, rows), 1)
    allowed = jnp.concatenate(
        [
            block_place(at, place_ref[1], near_count) * rows + row < place_ref[0]
            for at in range(blocks)
        ],
        1,
    )
    queries = qkv_ref[pl.ds(pl.multiple_of(block * rows, rows), rows), :width]
    keys = qkv_ref[:, width : 2 * width]
    values = qkv_ref[:, 2 * width :]
    total = jnp.zeros((rows, width), F32)
    places = bias_places(place_ref, block, blocks, rows, seq_len)
    for head in range(heads):
        scores = lax.dot_general(
            only(head_lanes(rows, width, head_width, head), queries),
            keys,
            (((1,), (1,)), ((), ())),
            preferred_element_type=F32,
        )
        bias = jnp.concatenate(
            [
                jnp.concatenate([skew_ref[head, :, pl.ds(place, rows)] for place in part], 1)
                for part in places
            ],
            0,
        )
        scores = jnp.where(allowed, scores + bias, MASKED)
        grown = jnp.exp(scores - jnp.max(scores, axis=1, keepdims=True))
        prob = (grown * (1.0 / jnp.sum(grown, axis=1, keepdims=True))).astype(LOW)
        p_ref[head] = prob
        total = total + jnp.dot(
            prob,
            only(head_lanes(seq_len, width, head_width, head), values),
            preferred_element_type=F32,
        )
    attended = total.astype(LOW)
    o_ref[...] = attended
    weight = got_ref[:, :shard, 3 * width :].reshape(model, width)
    held_ref[...] = contract_cols(attended, weight).astype(LOW)
    send_rows(step, near_count, place_ref[3], held_ref, other_refs, mine_refs)


def attention_forward(parts, got, table, place, heads, shard, count):
    rows, model = parts[0].shape
    blocks = len(parts)
    near_count = blocks // CORES
    seq_len, width = rows * blocks, got.shape[2] // 4
    out_specs, out_shape = sent_specs(near_count, count, rows // count, model)

    def fixed(shape):
        return pl.BlockSpec(shape, lambda i: (0,) * len(shape))

    outs = pl.pallas_call(
        functools.partial(forward_kernel, heads, shard, near_count, count),
        grid=(blocks,),
        in_specs=[pl.BlockSpec(memory_space=pltpu.SMEM)]
        + [fixed(part.shape) for part in parts]
        + [fixed(got.shape), fixed(table.shape)],
        out_specs=[
            fixed((seq_len, 3 * width)),
            pl.BlockSpec((rows, width), lambda i: (row_block(i, near_count), 0)),
            pl.BlockSpec((heads, rows, seq_len), lambda i: (0, row_block(i, near_count), 0)),
        ]
        + out_specs,
        out_shape=[
            jax.ShapeDtypeStruct((seq_len, 3 * width), LOW),
            jax.ShapeDtypeStruct((seq_len, width), LOW),
            jax.ShapeDtypeStruct((heads, seq_len, seq_len), LOW),
        ]
        + out_shape,
        scratch_shapes=[
            pltpu.VMEM((heads, SKEW, 2 * seq_len), F32),
            pltpu.VMEM((rows, model), LOW),
        ],
        compiler_params=pltpu.CompilerParams(vmem_limit_bytes=34 * 2**20),
        cost_estimate=pl.CostEstimate(flops=0, bytes_accessed=0, transcendentals=0),
        name="attention_forward",
    )(place, *parts, got, table)
    return (*outs[:3], outs[3 + count :], outs[3 : 3 + count])


def backward_kernel(heads, shard, near_count, count, place_ref, *refs):
    came, refs = refs[: 2 * count], refs[2 * count :]
    p_ref, got_ref, qkv_ref, d_ref, dt_ref, rows_ref, dk_sum, dv_sum, skew_ref = refs
    step = pl.program_id(0)
    block = row_block(step, near_count)
    take_rows(step, near_count, place_ref[3], came[:count], came[count:], rows_ref)
    rows, model = rows_ref.shape
    seq_len = qkv_ref.shape[0]
    width = qkv_ref.shape[1] // 3
    head_width = width // heads
    span = 2 * seq_len
    blocks = seq_len // rows

    @pl.when(step == 0)
    def _():
        dk_sum[...] = jnp.zeros_like(dk_sum)
        dv_sum[...] = jnp.zeros_like(dv_sum)
        skew_ref[...] = jnp.zeros_like(skew_ref)

    here = pl.ds(pl.multiple_of(block * rows, rows), rows)
    queries = qkv_ref[here, :width]
    keys = qkv_ref[:, width : 2 * width]
    values = qkv_ref[:, 2 * width :]
    weight = got_ref[:, :shard, 3 * width :].reshape(model, width)
    grads = rows_dot(rows_ref[...], weight).astype(LOW)
    total = jnp.zeros((rows, width), F32)
    places = bias_places(place_ref, block, blocks, rows, seq_len)
    for head in range(heads):
        own = head_lanes(rows, width, head_width, head)
        own_grads = only(own, grads)
        d_prob = lax.dot_general(
            own_grads, values, (((1,), (1,)), ((), ())), preferred_element_type=F32
        )
        prob_low = p_ref[head]
        prob = prob_low.astype(F32)
        weighed = prob * d_prob
        d_scores = (weighed - prob * jnp.sum(weighed, axis=1, keepdims=True)).astype(LOW)
        total = total + jnp.dot(
            d_scores,
            only(head_lanes(seq_len, width, head_width, head), keys),
            preferred_element_type=F32,
        )
        dk_sum[...] += lax.dot_general(
            d_scores, only(own, queries), (((0,), (0,)), ((), ())), preferred_element_type=F32
        )
        dv_sum[...] += lax.dot_general(
            prob_low, own_grads, (((0,), (0,)), ((), ())), preferred_element_type=F32
        )
        for part in range(rows // SKEW):
            for at in range(blocks):
                skew_ref[head, :, pl.ds(places[part][at], rows)] += d_scores[
                    part * SKEW : (part + 1) * SKEW, at * rows : (at + 1) * rows
                ].astype(F32)
    d_ref[here, :width] = total.astype(LOW)

    @pl.when(step == pl.num_programs(0) - 1)
    def _():
        d_ref[:, width : 2 * width] = dk_sum[...].astype(LOW)
        d_ref[:, 2 * width :] = dv_sum[...].astype(LOW)
        one_hot = bucket_onehot(dt_ref.shape[0], seq_len)
        row = lax.broadcasted_iota(jnp.int32, (SKEW, span), 0)
        column = lax.broadcasted_iota(jnp.int32, dt_ref.shape, 1)
        result = jnp.zeros(dt_ref.shape, F32)
        for head in range(heads):
            level = pltpu.roll(skew_ref[head], SKEW, 1)
            bit = 1
            while bit < SKEW:
                level = jnp.where((row & bit) != 0, pltpu.roll(level, span - bit, 1), level)
                bit *= 2
            line = jnp.sum(level, axis=0, keepdims=True)
            summed = jnp.sum(jnp.where(one_hot, line, 0.0), axis=1, keepdims=True)
            result = jnp.where(column == head, summed, result)
        dt_ref[...] = result


def attention_backward(prob, mine, other, got, qkv, place, heads, shard, buckets):
    seq_len, width = qkv.shape[0], qkv.shape[1] // 3
    near_count, own_rows, model = mine[0].shape
    count = len(mine)
    rows = count * own_rows
    came_specs, _ = sent_specs(near_count, count, own_rows, model)
    return pl.pallas_call(
        functools.partial(backward_kernel, heads, shard, near_count, count),
        grid=(seq_len // rows,),
        in_specs=[
            pl.BlockSpec(memory_space=pltpu.SMEM),
            *came_specs,
            pl.BlockSpec((heads, rows, seq_len), lambda i: (0, row_block(i, near_count), 0)),
            pl.BlockSpec(got.shape, lambda i: (0, 0, 0)),
            pl.BlockSpec(qkv.shape, lambda i: (0, 0)),
        ],
        out_specs=[
            pl.BlockSpec(qkv.shape, lambda i: (0, 0)),
            pl.BlockSpec((buckets, 128), lambda i: (0, 0)),
            pl.BlockSpec((rows, model), lambda i: (row_block(i, near_count), 0)),
        ],
        out_shape=[
            jax.ShapeDtypeStruct(qkv.shape, LOW),
            jax.ShapeDtypeStruct((buckets, 128), F32),
            jax.ShapeDtypeStruct((seq_len, model), LOW),
        ],
        scratch_shapes=[
            pltpu.VMEM((seq_len, width), F32),
            pltpu.VMEM((seq_len, width), F32),
            pltpu.VMEM((heads, SKEW, 2 * seq_len), F32),
        ],
        compiler_params=pltpu.CompilerParams(vmem_limit_bytes=34 * 2**20),
        cost_estimate=pl.CostEstimate(flops=0, bytes_accessed=0, transcendentals=0),
        name="attention_backward",
    )(place, *other, *mine, prob, got, qkv)


EXTRA = 8
OWNER_ROWS = 64


def as_column(row, first, count):
    size = row.shape[1]
    here = lax.broadcasted_iota(jnp.int32, (count, size), 1) == first + lax.broadcasted_iota(
        jnp.int32, (count, size), 0
    )
    return jnp.sum(jnp.where(here, row, 0.0), axis=1, keepdims=True)


def blocks_kernel(seqs, members, q_ref, k_ref, v_ref, o_ref, gain_ref, table_ref, sent_ref):
    shard = q_ref.shape[0]
    width = q_ref.shape[1] // members
    gain = as_column(gain_ref[...].astype(LOW).astype(F32), 0, shard)
    parts = [
        (ref[...].astype(LOW).astype(F32) * gain).astype(LOW) for ref in (q_ref, k_ref, v_ref)
    ]
    parts.append(o_ref[...].T.astype(LOW))
    rest = jnp.zeros((EXTRA, sent_ref.shape[2]), LOW)
    table_rows, heads = table_ref.shape
    for seq in range(seqs):
        for member in range(members):
            at = seq * members + member
            for i, part in enumerate(parts):
                sent_ref[at, :shard, i * width : (i + 1) * width] = part[
                    :, member * width : (member + 1) * width
                ]
            sent_ref[at, shard:, :] = rest
            sent_ref[at, shard : shard + table_rows, :heads] = table_ref[...].astype(LOW)


def attention_blocks(weights, w_out, gain, table, seqs, members):
    shard, columns = weights[0].shape
    return pl.pallas_call(
        functools.partial(blocks_kernel, seqs, members),
        out_shape=jax.ShapeDtypeStruct(
            (seqs * members, shard + EXTRA, 4 * columns // members), LOW
        ),
        compiler_params=pltpu.CompilerParams(vmem_limit_bytes=60 * 2**20),
        cost_estimate=pl.CostEstimate(
            flops=0, bytes_accessed=16 * shard * columns, transcendentals=0
        ),
        name="attention_blocks",
    )(*weights, w_out, gain, table)


def owner_kernel(count, members, table_shape, *refs):
    got_ref, extra_ref = refs[:2]
    weight_refs = refs[2 : 2 + count]
    gain_ref = refs[2 + count]
    grad_refs = refs[3 + count : 3 + 2 * count]
    sum_ref = refs[3 + 2 * count]
    step = pl.program_id(0)
    rows = got_ref.shape[1]
    seqs = got_ref.shape[0] // members
    width = got_ref.shape[2] // count
    size = sum_ref.shape[1]
    gain = as_column(gain_ref[...].astype(LOW).astype(F32), step * rows, rows)
    total = jnp.zeros((rows, 1), F32)
    for member in range(members):
        product = sum(got_ref[seq * members + member].astype(F32) for seq in range(seqs))
        for i in range(count):
            part = product[:, i * width : (i + 1) * width]
            here = pl.ds(member * width, width)
            grad_refs[i][:, here] = part * gain
            weight = weight_refs[i][:, here].astype(LOW).astype(F32)
            total = total + jnp.sum(weight * part, axis=1, keepdims=True)

    @pl.when(step == 0)
    def _():
        sum_ref[...] = jnp.zeros_like(sum_ref)

    diagonal = lax.broadcasted_iota(jnp.int32, (rows, size), 1) == step * rows + (
        lax.broadcasted_iota(jnp.int32, (rows, size), 0)
    )
    sum_ref[...] += jnp.sum(jnp.where(diagonal, total, 0.0), axis=0, keepdims=True)
    if table_shape is not None:
        table_rows, heads = table_shape
        each = heads // members
        for member in range(members):
            piece = sum(extra_ref[seq * members + member].astype(F32) for seq in range(seqs))
            refs[-1][:, member * each : (member + 1) * each] = piece[:table_rows, :each]


def owner_grads(got, weights, gain, members, table_shape):
    sources, height, columns = got.shape
    shard, wide = weights[0].shape
    count = len(weights)
    rows = min(OWNER_ROWS, shard)
    step_rows = pl.BlockSpec((rows, wide), lambda i: (i, 0))
    row = pl.BlockSpec((1, shard), lambda i: (0, 0))
    last = height // EXTRA - 1
    out_specs = [step_rows] * count + [row]
    out_shape = [jax.ShapeDtypeStruct((shard, wide), F32)] * count
    out_shape.append(jax.ShapeDtypeStruct((1, shard), F32))
    if table_shape is not None:
        out_specs.append(pl.BlockSpec(table_shape, lambda i: (0, 0)))
        out_shape.append(jax.ShapeDtypeStruct(table_shape, F32))
    outs = pl.pallas_call(
        functools.partial(owner_kernel, count, members, table_shape),
        grid=(shard // rows,),
        in_specs=[
            pl.BlockSpec((sources, rows, columns), lambda i: (0, i, 0)),
            pl.BlockSpec((sources, EXTRA, columns), lambda i: (0, last, 0)),
        ]
        + [step_rows] * count
        + [row],
        out_specs=out_specs,
        out_shape=out_shape,
        compiler_params=pltpu.CompilerParams(vmem_limit_bytes=32 * 2**20),
        cost_estimate=pl.CostEstimate(
            flops=0, bytes_accessed=10 * count * shard * wide, transcendentals=0
        ),
        name="owner_grads",
    )(got, got, *weights, gain)
    return outs[:count], outs[count], outs[-1] if table_shape is not None else None


def rows_kernel(members, split, got_ref, first_ref, second_ref):
    seqs = got_ref.shape[0] // members
    rest = got_ref.shape[1] - split
    for member in range(members):
        total = sum(got_ref[seq * members + member].astype(F32) for seq in range(seqs))
        first_ref[pl.ds(member * split, split), :] = total[:split]
        second_ref[pl.ds(member * rest, rest), :] = total[split:]


def owner_rows(got, members, split):
    height, columns = got.shape[1:]
    return pl.pallas_call(
        functools.partial(rows_kernel, members, split),
        out_shape=[
            jax.ShapeDtypeStruct((members * split, columns), F32),
            jax.ShapeDtypeStruct((members * (height - split), columns), F32),
        ],
        compiler_params=pltpu.CompilerParams(vmem_limit_bytes=32 * 2**20),
        cost_estimate=pl.CostEstimate(
            flops=0, bytes_accessed=4 * got.size, transcendentals=0
        ),
        name="owner_rows",
    )(got)


def rows_dot(left, right):
    return jnp.dot(left, right, preferred_element_type=F32)


def contract_cols(left, right):
    return lax.dot_general(left, right, (((1,), (1,)), ((), ())), preferred_element_type=F32)


def contract_rows(left, right):
    return lax.dot_general(left, right, (((0,), (0,)), ((), ())), preferred_element_type=F32)

def row_block(step, near_count):
    return lax.rem(step + near_count, CORES * near_count)


def send_rows(step, near_count, mp_at, held_ref, other_refs, mine_refs):
    count = len(other_refs)
    own_rows = held_ref.shape[0] // count

    def write(refs):
        for away, ref in enumerate(refs):
            first = pl.multiple_of(lax.bitwise_xor(mp_at, away) * own_rows, own_rows)
            ref[0] = held_ref[pl.ds(first, own_rows), :]

    @pl.when(step < near_count)
    def _():
        write(other_refs)

    @pl.when(step >= near_count)
    def _():
        write(mine_refs)


def place_kernel(near_count, place_ref, *refs):
    parts, outs, copied = refs[:-3], refs[-3:-1], refs[-1]
    each = len(parts) // 2
    rows = parts[0].shape[0]
    copies = []
    for i, ref in enumerate(parts):
        at = i % each
        first = (at // 2) * near_count + lax.bitwise_xor(place_ref[4], at % 2)
        place = outs[i // each].at[pl.ds(pl.multiple_of(first * rows, rows), rows), :]
        copies.append(pltpu.make_async_copy(ref, place, copied.at[i]))
    for copy in copies:
        copy.start()
    for copy in copies:
        copy.wait()


def place_rows(first, second, place, near_count):
    rows, model = first[0].shape
    shape = jax.ShapeDtypeStruct((rows * len(first), model), LOW)
    somewhere = pl.BlockSpec(memory_space=pl.ANY)
    return pl.pallas_call(
        functools.partial(place_kernel, near_count),
        in_specs=[pl.BlockSpec(memory_space=pltpu.SMEM)] + [somewhere] * (2 * len(first)),
        out_specs=[somewhere] * 2,
        out_shape=[shape] * 2,
        scratch_shapes=[pltpu.SemaphoreType.DMA((2 * len(first),))],
        cost_estimate=pl.CostEstimate(flops=0, bytes_accessed=0, transcendentals=0),
        name="place_rows",
    )(place, *first, *second)


def take_rows(step, near_count, mp_at, other_refs, mine_refs, rows_ref):
    own_rows = other_refs[0].shape[1]

    def read(refs):
        for away, ref in enumerate(refs):
            first = pl.multiple_of(lax.bitwise_xor(mp_at, away) * own_rows, own_rows)
            rows_ref[pl.ds(first, own_rows), :] = ref[0]

    @pl.when(step < near_count)
    def _():
        read(other_refs)

    @pl.when(step >= near_count)
    def _():
        read(mine_refs)


def sent_specs(near_count, count, own_rows, model):
    other = pl.BlockSpec((1, own_rows, model), lambda i: (jnp.minimum(i, near_count - 1), 0, 0))
    mine = pl.BlockSpec((1, own_rows, model), lambda i: (jnp.maximum(i - near_count, 0), 0, 0))
    shape = jax.ShapeDtypeStruct((near_count, own_rows, model), LOW)
    return [other] * count + [mine] * count, [shape] * (2 * count)


def partial_kernel(near_count, count, product, place_ref, left_ref, weight_ref, *refs):
    held_ref = refs[-1]
    product(left_ref, weight_ref, held_ref)
    send_rows(
        pl.program_id(0), near_count, place_ref[3], held_ref, refs[:count], refs[count : 2 * count]
    )


def partial_rows(left, weight, model, place, near_count, count, product, name):
    seq_len, depth = left.shape
    rows = seq_len // (CORES * near_count)
    out_specs, out_shape = sent_specs(near_count, count, rows // count, model)
    outs = pl.pallas_call(
        functools.partial(partial_kernel, near_count, count, product),
        grid=(CORES * near_count,),
        in_specs=[
            pl.BlockSpec(memory_space=pltpu.SMEM),
            pl.BlockSpec((rows, depth), lambda i: (row_block(i, near_count), 0)),
            pl.BlockSpec(weight.shape, lambda i: (0, 0, 0)),
        ],
        out_specs=out_specs,
        out_shape=out_shape,
        scratch_shapes=[pltpu.VMEM((rows, model), LOW)],
        compiler_params=pltpu.CompilerParams(vmem_limit_bytes=40 * 2**20),
        cost_estimate=pl.CostEstimate(
            flops=0, bytes_accessed=0, transcendentals=0
        ),
        name=name,
    )(place, left, weight)
    return outs[count:], outs[:count]


def column_product(shard, first, last, left_ref, weight_ref, held_ref):
    weight = weight_ref[:, :shard, first:last]
    weight = weight.reshape(weight.shape[0] * shard, last - first)
    held_ref[...] = contract_cols(left_ref[...], weight).astype(LOW)


def row_product(height, left_ref, weight_ref, held_ref):
    left = left_ref[...]
    width = weight_ref.shape[2]
    for at in range(weight_ref.shape[0]):
        held_ref[:, at * width : (at + 1) * width] = rows_dot(
            left, weight_ref[at, :height, :]
        ).astype(LOW)


def ffn_blocks_kernel(seqs, members, gate_ref, up_ref, down_ref, gain_ref, first_ref, second_ref):
    shard = gate_ref.shape[0]
    width = gate_ref.shape[1] // members
    gain = as_column(gain_ref[...].astype(LOW).astype(F32), 0, shard)
    for member in range(members):
        here = slice(member * width, (member + 1) * width)
        parts = [
            (ref[:, here].astype(LOW).astype(F32) * gain).astype(LOW) for ref in (gate_ref, up_ref)
        ]
        both = jnp.concatenate(parts, 1)
        down = down_ref[here, :].astype(LOW)
        for seq in range(seqs):
            at = seq * members + member
            first_ref[at, :width, :] = down
            first_ref[at, width:, :] = both[:, :shard]
            second_ref[at] = both[:, shard:]


def ffn_blocks(w_gate, w_up, w_down, gain, seqs, members):
    shard, columns = w_gate.shape
    width = columns // members
    return pl.pallas_call(
        functools.partial(ffn_blocks_kernel, seqs, members),
        out_shape=[
            jax.ShapeDtypeStruct((seqs * members, width + shard, shard), LOW),
            jax.ShapeDtypeStruct((seqs * members, shard, 2 * width - shard), LOW),
        ],
        compiler_params=pltpu.CompilerParams(vmem_limit_bytes=40 * 2**20),
        cost_estimate=pl.CostEstimate(
            flops=0, bytes_accessed=18 * shard * columns, transcendentals=0
        ),
        name="ffn_blocks",
    )(w_gate, w_up, w_down, gain)


def ffn_kernel(near_count, count, place_ref, *refs):
    came, refs = refs[: 2 * count], refs[2 * count :]
    grad_ref, first_ref, second_ref = refs[:3]
    other_refs, mine_refs = refs[3 : 3 + count], refs[3 + count : 3 + 2 * count]
    rows_ref, act_ref, d_ref, down_ref, held_ref, sum_ref = refs[3 + 2 * count :]
    step = pl.program_id(0)
    take_rows(step, near_count, place_ref[3], came[:count], came[count:], rows_ref)
    sources, height, shard = first_ref.shape
    width = height - shard
    rows = rows_ref[...]
    block = row_block(step, near_count)
    first = block_place(block, place_ref[1], near_count) * rows.shape[0]
    valid = first + lax.broadcasted_iota(jnp.int32, (rows.shape[0], 1), 0) < place_ref[0]
    grads = only(valid, grad_ref[...])
    early = first_ref[:, width:, :].reshape(sources * shard, shard)
    late = second_ref[...].reshape(sources * shard, 2 * width - shard)
    both = jnp.concatenate([rows_dot(rows, early), rows_dot(rows, late)], 1)
    gate, up = both[:, :width], both[:, width:]
    scale, cubic = 0.7978845608028654, 0.044715
    square = gate * gate
    bent = jnp.tanh(scale * (gate + cubic * square * gate))
    half = 0.5 * (1.0 + bent)
    value = gate * half
    slope = half + 0.5 * gate * (1.0 - bent * bent) * (scale * (1.0 + 3.0 * cubic * square))
    act = (value * up).astype(LOW)
    act_ref[...] = act
    d_hidden = jnp.zeros((rows.shape[0], width), F32)
    for at in range(sources):
        d_hidden = d_hidden + contract_cols(
            grads[:, at * shard : (at + 1) * shard], first_ref[at, :width, :]
        )
    d_both = jnp.concatenate(
        [(d_hidden * up * slope).astype(LOW), (d_hidden * value).astype(LOW)], 1
    )
    d_ref[...] = d_both
    held_ref[...] = (
        contract_cols(d_both[:, :shard], early) + contract_cols(d_both[:, shard:], late)
    ).astype(LOW)
    send_rows(step, near_count, place_ref[3], held_ref, other_refs, mine_refs)
    product = contract_rows(act, grads)

    @pl.when(step == 0)
    def _():
        sum_ref[...] = product

    @pl.when(step > 0)
    def _():
        sum_ref[...] += product

    @pl.when(step == pl.num_programs(0) - 1)
    def _():
        for at in range(sources):
            down_ref[at] = sum_ref[:, at * shard : (at + 1) * shard].astype(LOW)


def feed_forward(mine, other, grads, first, second, place):
    seq_len, model = grads.shape
    near_count, count = mine[0].shape[0], len(mine)
    sources, height, shard = first.shape
    width = height - shard
    rows = seq_len // (CORES * near_count)
    out_specs, out_shape = sent_specs(near_count, count, rows // count, model)

    def blocks(columns):
        return pl.BlockSpec((rows, columns), lambda i: (row_block(i, near_count), 0))

    outs = pl.pallas_call(
        functools.partial(ffn_kernel, near_count, count),
        grid=(CORES * near_count,),
        in_specs=[
            pl.BlockSpec(memory_space=pltpu.SMEM),
            *out_specs,
            blocks(model),
            pl.BlockSpec(first.shape, lambda i: (0, 0, 0)),
            pl.BlockSpec(second.shape, lambda i: (0, 0, 0)),
        ],
        out_specs=out_specs
        + [
            blocks(model),
            blocks(width),
            blocks(2 * width),
            pl.BlockSpec((sources, width, shard), lambda i: (0, 0, 0)),
        ],
        out_shape=out_shape
        + [
            jax.ShapeDtypeStruct((seq_len, model), LOW),
            jax.ShapeDtypeStruct((seq_len, width), LOW),
            jax.ShapeDtypeStruct((seq_len, 2 * width), LOW),
            jax.ShapeDtypeStruct((sources, width, shard), LOW),
        ],
        scratch_shapes=[pltpu.VMEM((rows, model), LOW), pltpu.VMEM((width, model), F32)],
        compiler_params=pltpu.CompilerParams(vmem_limit_bytes=56 * 2**20),
        cost_estimate=pl.CostEstimate(
            flops=12 * seq_len * model * width, bytes_accessed=12 * seq_len * model, transcendentals=0
        ),
        name="feed_forward",
    )(place, *other, *mine, grads, first, second)
    return outs[count : 2 * count], outs[:count], *outs[2 * count :]


COLUMN = ("seq", "near", "core")


def exchange(blocks, axes):
    return lax.all_to_all(blocks, axes, split_axis=0, concat_axis=0, tiled=True)


def swap(block, axis):
    return lax.ppermute(block, axis, [(0, 1), (1, 0)])


def after(value, *done):
    return lax.optimization_barrier((value,) + done)[0]


def rms(values):
    return lax.rsqrt(jnp.mean(values * values, axis=-1, keepdims=True) + EPSILON)


def norm_grad(inner, normed, inverse):
    return inverse * (inner - normed * jnp.mean(inner * normed, axis=-1, keepdims=True))


def local(
    inputs,
    cotangent,
    lengths,
    attn_scale,
    w_query,
    w_key,
    w_value,
    w_out,
    rel_table,
    ffn_scale,
    w_gate,
    w_up,
    w_down,
):
    seqs = lax.axis_size("seq")
    near_count = lax.axis_size("near")
    mp_count = lax.axis_size("mp")
    members = near_count * CORES
    sources = seqs * members
    tok_rows, model = inputs.shape
    seq_len = tok_rows * members
    own_rows = tok_rows // mp_count
    half_rows = seq_len // CORES
    shard = attn_scale.shape[0]
    table_rows, heads_mp = rel_table.shape
    buckets = table_rows * sources
    heads = heads_mp // members
    width = w_query.shape[1] // members
    hidden_width = w_gate.shape[1] // members

    near_at = lax.axis_index("near")
    core_at = lax.axis_index("core")
    mp_at = lax.axis_index("mp")
    member_at = near_at * CORES + core_at
    length = lax.dynamic_slice_in_dim(lengths, lax.axis_index("seq"), 1, 0)
    place = jnp.stack(
        [length[0]] + [at.astype(jnp.int32) for at in (core_at, member_at, mp_at, near_at)]
    )

    def over_mp(own, axis):
        shape = own.shape[:axis] + (mp_count,) + own.shape[axis:]
        blocks = lax.dynamic_update_index_in_dim(jnp.zeros(shape, own.dtype), own, mp_at, axis)
        moved = [(away, shifted(own, away)) for away in reversed(range(1, mp_count))]
        for away, block in moved:
            blocks = lax.dynamic_update_index_in_dim(blocks, block, mp_at ^ away, axis)
        return blocks

    def shifted(block, away):
        return lax.ppermute(block, "mp", [(i, i ^ away) for i in range(mp_count)])

    def in_near_order(own, moved):
        return jnp.stack(
            [jnp.where(near_at == 0, own, moved), jnp.where(near_at == 0, moved, own)], 0
        )

    def near_rows(blocks, meanwhile):
        own = [lax.dynamic_slice_in_dim(block, mp_at * own_rows, own_rows, 0) for block in blocks]
        near = swap(jnp.stack(own), "near")
        came = [(0, near)] + [(away, shifted(near, away)) for away in range(1, mp_count)]
        made = meanwhile(came[1][1])
        came = came[:2] + [(away, after(block, *made)) for away, block in came[2:]]
        halves = []
        for half in (came, [(away, swap(block, "core")) for away, block in came]):
            rows = jnp.zeros((len(blocks), mp_count, own_rows, model), near.dtype)
            for away, block in half:
                rows = lax.dynamic_update_index_in_dim(rows, block, mp_at ^ away, 1)
            halves.append([rows[i].reshape(tok_rows, model) for i in range(len(blocks))])
        return *halves, made

    def gather_rows(near):
        mine = [near] + [shifted(near, away) for away in range(1, mp_count)]
        return mine, [swap(block, "core") for block in mine]

    def sum_cores(mine, other):
        return [
            kept.astype(F32) + swap(sent, "core").astype(F32) for kept, sent in zip(mine, other)
        ]

    def send_mp(sums):
        return [shifted(sums[away].astype(LOW), away) for away in reversed(range(1, mp_count))]

    def sum_mp(sums, *meanwhile):
        moved = send_mp(sums)
        if meanwhile:
            moved = [after(piece, *meanwhile) for piece in moved]
        return sum((piece.astype(F32) for piece in moved), sums[0])

    def split_near(pair):
        sent = jnp.where(near_at == 0, pair[1], pair[0]).astype(LOW)
        return sent, jnp.where(near_at == 0, pair[0], pair[1])

    def sum_near_both(pair):
        low = pair.astype(LOW)
        moved = swap(low, "near")
        return low.astype(F32) + moved.astype(F32), moved

    def near_pair(own, moved):
        pair = [
            lax.dynamic_slice_in_dim(block, mp_at * own_rows, own_rows, 0)
            for block in (own, moved)
        ]
        return in_near_order(*pair)

    def here(pair):
        return lax.dynamic_index_in_dim(pair, near_at, 0, keepdims=False)

    attn_sent = attention_blocks(
        (w_query, w_key, w_value), w_out, attn_scale.reshape(1, shard), rel_table, seqs, members
    )
    attn_got = exchange(attn_sent, COLUMN)
    def partial(left, weight, product, name):
        return partial_rows(left, weight, model, place, near_count, mp_count, product, name)

    table = attn_got[:, shard : shard + table_rows, :heads_mp].reshape(buckets, heads_mp)

    def normed(rows):
        values = rows.astype(F32)
        return (values * rms(values)).astype(LOW)

    def make_blocks(first_came):
        return ffn_blocks(
            w_gate, w_up, w_down, after(ffn_scale.reshape(1, shard), first_came), seqs, members
        )

    (moved_inputs, moved_cotangent), core_moved, (ffn_first, ffn_second) = near_rows(
        [inputs, cotangent], make_blocks
    )
    input_parts = [inputs, moved_inputs, swap(inputs, "core"), core_moved[0]]
    core_cotangent = swap(after(cotangent, moved_inputs), "core")
    grad_parts = [cotangent, moved_cotangent, core_cotangent, core_moved[1]]
    parts = [normed(part) for part in input_parts]
    parts = lax.optimization_barrier((*parts, ffn_first, ffn_second))[:4]
    first_got = exchange(after(ffn_first, attn_got), COLUMN)

    qkv, attended, prob, out_mine, out_other = attention_forward(
        parts, attn_got, table, place, heads, shard, mp_count
    )
    normed_rows, grad_two = place_rows(parts, grad_parts, after(place, attended), near_count)
    mixed, mixed_moved = sum_near_both(
        after(sum_mp(sum_cores(out_mine, out_other), grad_two, normed_rows), first_got)
    )
    second_got = exchange(after(ffn_second, mixed_moved), COLUMN)

    pair_inputs = near_pair(inputs, moved_inputs).astype(F32)
    after_attn = pair_inputs + mixed
    inv_two = rms(after_attn)
    normed_two = after_attn * inv_two
    mine_two, other_two = gather_rows(normed_two.astype(LOW))

    d_mine, d_other, hidden_two, acts, d_both, d_down_w = feed_forward(
        mine_two, other_two, grad_two, first_got, second_got, place
    )
    inner_cores = sum_cores(d_mine, d_other)
    down_product = functools.partial(row_product, hidden_width)
    ffn_partial = partial(after(acts, *inner_cores), first_got, down_product, "ffn_out")

    def to_owners(grad):
        return exchange(grad, COLUMN)

    d_gate_up_w = contract_rows(hidden_two, after(d_both, *inner_cores)).astype(LOW)
    inner_two, inner_moved = sum_near_both(
        sum_mp(inner_cores, d_gate_up_w, *ffn_partial[0], *ffn_partial[1])
    )

    pair_first = (
        lax.broadcasted_iota(jnp.int32, (near_count, own_rows, 1), 0) * (CORES * tok_rows)
        + lax.broadcasted_iota(jnp.int32, (near_count, own_rows, 1), 1)
        + (core_at * tok_rows + mp_at * own_rows)
    )
    pair_valid = pair_first < length
    pair_grad = near_pair(cotangent, moved_cotangent).astype(F32)
    grad_one = jnp.where(pair_valid, pair_grad, 0.0) + norm_grad(inner_two, normed_two, inv_two)
    grad_one_low = grad_one.astype(LOW)
    mine_one, other_one = gather_rows(grad_one_low)
    d_gate_up = to_owners(
        after(d_gate_up_w, inner_moved, grad_one_low).reshape(sources, shard, -1)
    )
    ffn_cores = sum_cores(*ffn_partial)
    d_qkv, d_table, rows_one = attention_backward(
        prob, mine_one, other_one, attn_got, qkv, place, heads, shard, buckets
    )
    qkv_product = functools.partial(column_product, shard, 0, 3 * width)
    ffn_moved = send_mp([after(rows, *mine_one[1:]) for rows in ffn_cores])
    table_sent = d_table[:, :heads].astype(LOW).reshape(sources, table_rows, heads)
    table_sent = jnp.pad(
        table_sent, ((0, 0), (0, EXTRA - table_rows), (0, 3 * width - heads))
    )
    d_qkv_w = contract_rows(normed_rows, d_qkv).astype(LOW).reshape(sources, shard, -1)
    d_qkv_sent = jnp.concatenate([d_qkv_w, table_sent], 1)
    inner_cores = sum_cores(
        *partial(after(d_qkv, d_qkv_sent, *ffn_moved), attn_got, qkv_product, "attention_in")
    )
    inner_pair = sum_mp(inner_cores)
    d_qkv_got = to_owners(after(d_qkv_sent, d_gate_up))
    d_out = contract_rows(after(attended, inner_cores[0]), rows_one)
    d_out = jnp.moveaxis(d_out.astype(LOW).reshape(width, sources, shard), 1, 0)
    d_rows_sent = jnp.concatenate([d_down_w, d_out], 1)

    (d_w_gate, d_w_up), ffn_gain, _ = owner_grads(
        after(d_gate_up, inner_cores[0]), (w_gate, w_up), ffn_scale.reshape(1, shard), members, None
    )
    ffn_sent, ffn_kept = split_near(
        sum((piece.astype(F32) for piece in ffn_moved), ffn_cores[0])
    )
    inner_sent, inner_kept = split_near(inner_pair)
    came = swap(
        after(jnp.stack([ffn_sent, inner_sent]), here(pair_valid), d_rows_sent, ffn_gain), "near"
    )
    own_inputs = here(pair_inputs)
    inv_one = rms(own_inputs)
    grad_input = here(grad_one) + norm_grad(inner_kept + came[1].astype(F32), own_inputs * inv_one, inv_one)
    own_out = jnp.where(here(pair_valid), here(after_attn) + ffn_kept + came[0].astype(F32), 0.0)
    owned = after(
        jnp.stack([own_out.astype(LOW), grad_input.astype(LOW)]), d_qkv_got
    )
    rows_out = [jnp.zeros((mp_count, own_rows, model), LOW)] * 2
    blocks_out = [owned] + [shifted(owned, away) for away in range(1, mp_count)]
    d_rows = to_owners(after(d_rows_sent, d_qkv_got))
    for away, block in enumerate(blocks_out):
        rows_out = [
            lax.dynamic_update_index_in_dim(rows, block[i], mp_at ^ away, 0)
            for i, rows in enumerate(rows_out)
        ]
    layer_out, d_inputs = (rows.reshape(tok_rows, model) for rows in rows_out)

    (d_w_query, d_w_key, d_w_value), attn_gain, d_rel_table = owner_grads(
        after(d_qkv_got, blocks_out[1]),
        (w_query, w_key, w_value),
        attn_scale.reshape(1, shard),
        members,
        (table_rows, heads_mp),
    )
    gains = jnp.concatenate([attn_gain, ffn_gain], 0)
    d_w_down, d_w_out = owner_rows(d_rows, members, hidden_width)
    gains = sum((shifted(gains, away) for away in range(1, mp_count)), gains)
    return (
        layer_out,
        d_inputs,
        gains[0],
        d_w_query,
        d_w_key,
        d_w_value,
        d_w_out,
        d_rel_table,
        gains[1],
        d_w_gate,
        d_w_up,
        d_w_down,
    )


def solution(mesh):
    fsdp, mp = mesh.shape["fsdp"], mesh.shape["mp"]

    def run(*args):
        seqs = args[2].shape[0]
        members = fsdp // seqs
        inner = Mesh(
            mesh.devices.reshape(seqs, members // CORES, CORES, mp), ("seq", "near", "core", "mp")
        )
        rows, columns, first = P(COLUMN, None), P("mp", COLUMN), P(COLUMN)
        both = P(COLUMN, "mp")
        in_specs = (
            rows, rows, P(), first, both, both, both, columns, both, first, both, both, columns,
        )
        out_specs = (
            rows, rows, first, both, both, both, columns, both, first, both, both, columns,
        )
        return jax.shard_map(
            local, mesh=inner, in_specs=in_specs, out_specs=out_specs, check_vma=False
        )(*args)

    return run
```

```python
import functools

import jax
import jax.numpy as jnp
from jax import lax
from jax.experimental import pallas as pl
from jax.experimental.pallas import tpu as pltpu
from jax.sharding import Mesh, PartitionSpec as P

LOW = jnp.bfloat16
F32 = jnp.float32
CORES = 2
THRESHOLDS = (12, 16, 23, 32, 46, 64, 91)
EPSILON = 1e-06
MASKED = -1e30
SKEW = 128


def bucket_of(rel_offset):
    distance = jnp.abs(rel_offset)
    far_bucket = 8 + sum(((distance >= threshold).astype(jnp.int32) for threshold in THRESHOLDS))
    bucket_abs = jnp.where(distance < 8, distance, far_bucket)
    return bucket_abs + jnp.where(rel_offset > 0, 16, 0)


def bucket_onehot(buckets, seq_len):
    offset = lax.broadcasted_iota(jnp.int32, (buckets, 2 * seq_len), 1) - seq_len
    bucket = lax.broadcasted_iota(jnp.int32, (buckets, 2 * seq_len), 0)
    return bucket_of(offset) == bucket


def head_lanes(rows, width, head_width, head):
    lane = lax.broadcasted_iota(jnp.int32, (rows, width), 1)
    return (lane >= head * head_width) & (lane < (head + 1) * head_width)


def only(mask, values):
    return jnp.where(mask, values, jnp.zeros_like(values))


def block_place(block, core, near_count):
    return lax.rem(block, near_count) * CORES + lax.bitwise_xor(lax.div(block, near_count), core)


def bias_places(place_ref, step, blocks, rows, seq_len):
    core, near_count = place_ref[1], blocks // CORES
    query = block_place(step, core, near_count) * rows
    return [
        [
            pl.multiple_of(
                block_place(block, core, near_count) * rows - query - part * SKEW + seq_len - SKEW,
                SKEW,
            )
            for block in range(blocks)
        ]
        for part in range(rows // SKEW)
    ]


def forward_kernel(heads, shard, near_count, count, place_ref, *refs):
    own_ref, moved_ref, core_ref, core_moved_ref, got_ref, table_ref = refs[:6]
    qkv_ref, o_ref, p_ref = refs[6:9]
    other_refs, mine_refs = refs[9 : 9 + count], refs[9 + count : 9 + 2 * count]
    skew_ref, held_ref = refs[9 + 2 * count :]
    step = pl.program_id(0)
    seq_len = qkv_ref.shape[0]
    rows, width = o_ref.shape
    model = held_ref.shape[1]
    head_width = width // heads
    span = 2 * seq_len
    blocks = seq_len // rows
    block = row_block(step, near_count)

    @pl.when(step == 0)
    def _():
        weight = got_ref[:, :shard, : 3 * width].reshape(model, 3 * width)
        near = place_ref[4]
        for at, ref in enumerate((own_ref, moved_ref, core_ref, core_moved_ref)):
            first = (at // 2) * near_count + lax.bitwise_xor(near, at % 2)
            qkv_ref[pl.ds(pl.multiple_of(first * rows, rows), rows), :] = rows_dot(
                ref[...], weight
            ).astype(LOW)
        one_hot = bucket_onehot(table_ref.shape[0], seq_len)
        table = table_ref[...].astype(F32)
        column = lax.broadcasted_iota(jnp.int32, table.shape, 1)
        for head in range(heads):
            here = column == place_ref[2] * heads + head
            levels = jnp.sum(jnp.where(here, table, 0.0), axis=1, keepdims=True)
            line = jnp.sum(jnp.where(one_hot, levels, 0.0), axis=0, keepdims=True)
            line = jnp.broadcast_to(line, (SKEW, span))
            skew_ref[head] = pltpu.roll(line, span - SKEW, 1, stride=1, stride_axis=0)

    row = lax.broadcasted_iota(jnp.int32, (1, rows), 1)
    allowed = jnp.concatenate(
        [
            block_place(at, place_ref[1], near_count) * rows + row < place_ref[0]
            for at in range(blocks)
        ],
        1,
    )
    queries = qkv_ref[pl.ds(pl.multiple_of(block * rows, rows), rows), :width]
    keys = qkv_ref[:, width : 2 * width]
    values = qkv_ref[:, 2 * width :]
    total = jnp.zeros((rows, width), F32)
    places = bias_places(place_ref, block, blocks, rows, seq_len)
    for head in range(heads):
        scores = lax.dot_general(
            only(head_lanes(rows, width, head_width, head), queries),
            keys,
            (((1,), (1,)), ((), ())),
            preferred_element_type=F32,
        )
        bias = jnp.concatenate(
            [
                jnp.concatenate([skew_ref[head, :, pl.ds(place, rows)] for place in part], 1)
                for part in places
            ],
            0,
        )
        scores = jnp.where(allowed, scores + bias, MASKED)
        grown = jnp.exp(scores - jnp.max(scores, axis=1, keepdims=True))
        prob = (grown * (1.0 / jnp.sum(grown, axis=1, keepdims=True))).astype(LOW)
        p_ref[head] = prob
        total = total + jnp.dot(
            prob,
            only(head_lanes(seq_len, width, head_width, head), values),
            preferred_element_type=F32,
        )
    attended = total.astype(LOW)
    o_ref[...] = attended
    weight = got_ref[:, :shard, 3 * width :].reshape(model, width)
    held_ref[...] = contract_cols(attended, weight).astype(LOW)
    send_rows(step, near_count, place_ref[3], held_ref, other_refs, mine_refs)


def attention_forward(parts, got, table, place, heads, shard, count):
    rows, model = parts[0].shape
    blocks = len(parts)
    near_count = blocks // CORES
    seq_len, width = rows * blocks, got.shape[2] // 4
    out_specs, out_shape = sent_specs(near_count, count, rows // count, model)

    def fixed(shape):
        return pl.BlockSpec(shape, lambda i: (0,) * len(shape))

    outs = pl.pallas_call(
        functools.partial(forward_kernel, heads, shard, near_count, count),
        grid=(blocks,),
        in_specs=[pl.BlockSpec(memory_space=pltpu.SMEM)]
        + [fixed(part.shape) for part in parts]
        + [fixed(got.shape), fixed(table.shape)],
        out_specs=[
            fixed((seq_len, 3 * width)),
            pl.BlockSpec((rows, width), lambda i: (row_block(i, near_count), 0)),
            pl.BlockSpec((heads, rows, seq_len), lambda i: (0, row_block(i, near_count), 0)),
        ]
        + out_specs,
        out_shape=[
            jax.ShapeDtypeStruct((seq_len, 3 * width), LOW),
            jax.ShapeDtypeStruct((seq_len, width), LOW),
            jax.ShapeDtypeStruct((heads, seq_len, seq_len), LOW),
        ]
        + out_shape,
        scratch_shapes=[
            pltpu.VMEM((heads, SKEW, 2 * seq_len), F32),
            pltpu.VMEM((rows, model), LOW),
        ],
        compiler_params=pltpu.CompilerParams(vmem_limit_bytes=34 * 2**20),
        cost_estimate=pl.CostEstimate(flops=0, bytes_accessed=0, transcendentals=0),
        name="attention_forward",
    )(place, *parts, got, table)
    return (*outs[:3], outs[3 + count :], outs[3 : 3 + count])


def backward_kernel(heads, shard, near_count, count, place_ref, *refs):
    came, refs = refs[: 2 * count], refs[2 * count :]
    p_ref, got_ref, qkv_ref, d_ref, dt_ref, rows_ref, dk_sum, dv_sum, skew_ref = refs
    step = pl.program_id(0)
    block = row_block(step, near_count)
    take_rows(step, near_count, place_ref[3], came[:count], came[count:], rows_ref)
    rows, model = rows_ref.shape
    seq_len = qkv_ref.shape[0]
    width = qkv_ref.shape[1] // 3
    head_width = width // heads
    span = 2 * seq_len
    blocks = seq_len // rows

    @pl.when(step == 0)
    def _():
        dk_sum[...] = jnp.zeros_like(dk_sum)
        dv_sum[...] = jnp.zeros_like(dv_sum)
        skew_ref[...] = jnp.zeros_like(skew_ref)

    here = pl.ds(pl.multiple_of(block * rows, rows), rows)
    queries = qkv_ref[here, :width]
    keys = qkv_ref[:, width : 2 * width]
    values = qkv_ref[:, 2 * width :]
    weight = got_ref[:, :shard, 3 * width :].reshape(model, width)
    grads = rows_dot(rows_ref[...], weight).astype(LOW)
    total = jnp.zeros((rows, width), F32)
    places = bias_places(place_ref, block, blocks, rows, seq_len)
    for head in range(heads):
        own = head_lanes(rows, width, head_width, head)
        own_grads = only(own, grads)
        d_prob = lax.dot_general(
            own_grads, values, (((1,), (1,)), ((), ())), preferred_element_type=F32
        )
        prob_low = p_ref[head]
        prob = prob_low.astype(F32)
        weighed = prob * d_prob
        d_scores = (weighed - prob * jnp.sum(weighed, axis=1, keepdims=True)).astype(LOW)
        total = total + jnp.dot(
            d_scores,
            only(head_lanes(seq_len, width, head_width, head), keys),
            preferred_element_type=F32,
        )
        dk_sum[...] += lax.dot_general(
            d_scores, only(own, queries), (((0,), (0,)), ((), ())), preferred_element_type=F32
        )
        dv_sum[...] += lax.dot_general(
            prob_low, own_grads, (((0,), (0,)), ((), ())), preferred_element_type=F32
        )
        for part in range(rows // SKEW):
            for at in range(blocks):
                skew_ref[head, :, pl.ds(places[part][at], rows)] += d_scores[
                    part * SKEW : (part + 1) * SKEW, at * rows : (at + 1) * rows
                ].astype(F32)
    d_ref[here, :width] = total.astype(LOW)

    @pl.when(step == pl.num_programs(0) - 1)
    def _():
        d_ref[:, width : 2 * width] = dk_sum[...].astype(LOW)
        d_ref[:, 2 * width :] = dv_sum[...].astype(LOW)
        one_hot = bucket_onehot(dt_ref.shape[0], seq_len)
        row = lax.broadcasted_iota(jnp.int32, (SKEW, span), 0)
        column = lax.broadcasted_iota(jnp.int32, dt_ref.shape, 1)
        result = jnp.zeros(dt_ref.shape, F32)
        for head in range(heads):
            level = pltpu.roll(skew_ref[head], SKEW, 1)
            bit = 1
            while bit < SKEW:
                level = jnp.where((row & bit) != 0, pltpu.roll(level, span - bit, 1), level)
                bit *= 2
            line = jnp.sum(level, axis=0, keepdims=True)
            summed = jnp.sum(jnp.where(one_hot, line, 0.0), axis=1, keepdims=True)
            result = jnp.where(column == head, summed, result)
        dt_ref[...] = result


def attention_backward(prob, mine, other, got, qkv, place, heads, shard, buckets):
    seq_len, width = qkv.shape[0], qkv.shape[1] // 3
    near_count, own_rows, model = mine[0].shape
    count = len(mine)
    rows = count * own_rows
    came_specs, _ = sent_specs(near_count, count, own_rows, model)
    return pl.pallas_call(
        functools.partial(backward_kernel, heads, shard, near_count, count),
        grid=(seq_len // rows,),
        in_specs=[
            pl.BlockSpec(memory_space=pltpu.SMEM),
            *came_specs,
            pl.BlockSpec((heads, rows, seq_len), lambda i: (0, row_block(i, near_count), 0)),
            pl.BlockSpec(got.shape, lambda i: (0, 0, 0)),
            pl.BlockSpec(qkv.shape, lambda i: (0, 0)),
        ],
        out_specs=[
            pl.BlockSpec(qkv.shape, lambda i: (0, 0)),
            pl.BlockSpec((buckets, 128), lambda i: (0, 0)),
            pl.BlockSpec((rows, model), lambda i: (row_block(i, near_count), 0)),
        ],
        out_shape=[
            jax.ShapeDtypeStruct(qkv.shape, LOW),
            jax.ShapeDtypeStruct((buckets, 128), F32),
            jax.ShapeDtypeStruct((seq_len, model), LOW),
        ],
        scratch_shapes=[
            pltpu.VMEM((seq_len, width), F32),
            pltpu.VMEM((seq_len, width), F32),
            pltpu.VMEM((heads, SKEW, 2 * seq_len), F32),
        ],
        compiler_params=pltpu.CompilerParams(vmem_limit_bytes=34 * 2**20),
        cost_estimate=pl.CostEstimate(flops=0, bytes_accessed=0, transcendentals=0),
        name="attention_backward",
    )(place, *other, *mine, prob, got, qkv)


EXTRA = 8
OWNER_ROWS = 64


def as_column(row, first, count):
    size = row.shape[1]
    here = lax.broadcasted_iota(jnp.int32, (count, size), 1) == first + lax.broadcasted_iota(
        jnp.int32, (count, size), 0
    )
    return jnp.sum(jnp.where(here, row, 0.0), axis=1, keepdims=True)


def blocks_kernel(seqs, members, q_ref, k_ref, v_ref, o_ref, gain_ref, table_ref, sent_ref):
    shard = q_ref.shape[0]
    width = q_ref.shape[1] // members
    gain = as_column(gain_ref[...].astype(LOW).astype(F32), 0, shard)
    parts = [
        (ref[...].astype(LOW).astype(F32) * gain).astype(LOW) for ref in (q_ref, k_ref, v_ref)
    ]
    parts.append(o_ref[...].T.astype(LOW))
    rest = jnp.zeros((EXTRA, sent_ref.shape[2]), LOW)
    table_rows, heads = table_ref.shape
    for seq in range(seqs):
        for member in range(members):
            at = seq * members + member
            for i, part in enumerate(parts):
                sent_ref[at, :shard, i * width : (i + 1) * width] = part[
                    :, member * width : (member + 1) * width
                ]
            sent_ref[at, shard:, :] = rest
            sent_ref[at, shard : shard + table_rows, :heads] = table_ref[...].astype(LOW)


def attention_blocks(weights, w_out, gain, table, seqs, members):
    shard, columns = weights[0].shape
    return pl.pallas_call(
        functools.partial(blocks_kernel, seqs, members),
        out_shape=jax.ShapeDtypeStruct(
            (seqs * members, shard + EXTRA, 4 * columns // members), LOW
        ),
        compiler_params=pltpu.CompilerParams(vmem_limit_bytes=60 * 2**20),
        cost_estimate=pl.CostEstimate(
            flops=0, bytes_accessed=16 * shard * columns, transcendentals=0
        ),
        name="attention_blocks",
    )(*weights, w_out, gain, table)


def owner_kernel(count, members, table_shape, *refs):
    got_ref, extra_ref = refs[:2]
    weight_refs = refs[2 : 2 + count]
    gain_ref = refs[2 + count]
    grad_refs = refs[3 + count : 3 + 2 * count]
    sum_ref = refs[3 + 2 * count]
    step = pl.program_id(0)
    rows = got_ref.shape[1]
    seqs = got_ref.shape[0] // members
    width = got_ref.shape[2] // count
    size = sum_ref.shape[1]
    gain = as_column(gain_ref[...].astype(LOW).astype(F32), step * rows, rows)
    total = jnp.zeros((rows, 1), F32)
    for member in range(members):
        product = sum(got_ref[seq * members + member].astype(F32) for seq in range(seqs))
        for i in range(count):
            part = product[:, i * width : (i + 1) * width]
            here = pl.ds(member * width, width)
            grad_refs[i][:, here] = part * gain
            weight = weight_refs[i][:, here].astype(LOW).astype(F32)
            total = total + jnp.sum(weight * part, axis=1, keepdims=True)

    @pl.when(step == 0)
    def _():
        sum_ref[...] = jnp.zeros_like(sum_ref)

    diagonal = lax.broadcasted_iota(jnp.int32, (rows, size), 1) == step * rows + (
        lax.broadcasted_iota(jnp.int32, (rows, size), 0)
    )
    sum_ref[...] += jnp.sum(jnp.where(diagonal, total, 0.0), axis=0, keepdims=True)
    if table_shape is not None:
        table_rows, heads = table_shape
        each = heads // members
        for member in range(members):
            piece = sum(extra_ref[seq * members + member].astype(F32) for seq in range(seqs))
            refs[-1][:, member * each : (member + 1) * each] = piece[:table_rows, :each]


def owner_grads(got, weights, gain, members, table_shape):
    sources, height, columns = got.shape
    shard, wide = weights[0].shape
    count = len(weights)
    rows = min(OWNER_ROWS, shard)
    step_rows = pl.BlockSpec((rows, wide), lambda i: (i, 0))
    row = pl.BlockSpec((1, shard), lambda i: (0, 0))
    last = height // EXTRA - 1
    out_specs = [step_rows] * count + [row]
    out_shape = [jax.ShapeDtypeStruct((shard, wide), F32)] * count
    out_shape.append(jax.ShapeDtypeStruct((1, shard), F32))
    if table_shape is not None:
        out_specs.append(pl.BlockSpec(table_shape, lambda i: (0, 0)))
        out_shape.append(jax.ShapeDtypeStruct(table_shape, F32))
    outs = pl.pallas_call(
        functools.partial(owner_kernel, count, members, table_shape),
        grid=(shard // rows,),
        in_specs=[
            pl.BlockSpec((sources, rows, columns), lambda i: (0, i, 0)),
            pl.BlockSpec((sources, EXTRA, columns), lambda i: (0, last, 0)),
        ]
        + [step_rows] * count
        + [row],
        out_specs=out_specs,
        out_shape=out_shape,
        compiler_params=pltpu.CompilerParams(vmem_limit_bytes=32 * 2**20),
        cost_estimate=pl.CostEstimate(
            flops=0, bytes_accessed=10 * count * shard * wide, transcendentals=0
        ),
        name="owner_grads",
    )(got, got, *weights, gain)
    return outs[:count], outs[count], outs[-1] if table_shape is not None else None


def rows_kernel(members, split, got_ref, first_ref, second_ref):
    seqs = got_ref.shape[0] // members
    rest = got_ref.shape[1] - split
    for member in range(members):
        total = sum(got_ref[seq * members + member].astype(F32) for seq in range(seqs))
        first_ref[pl.ds(member * split, split), :] = total[:split]
        second_ref[pl.ds(member * rest, rest), :] = total[split:]


def owner_rows(got, members, split):
    height, columns = got.shape[1:]
    return pl.pallas_call(
        functools.partial(rows_kernel, members, split),
        out_shape=[
            jax.ShapeDtypeStruct((members * split, columns), F32),
            jax.ShapeDtypeStruct((members * (height - split), columns), F32),
        ],
        compiler_params=pltpu.CompilerParams(vmem_limit_bytes=32 * 2**20),
        cost_estimate=pl.CostEstimate(
            flops=0, bytes_accessed=4 * got.size, transcendentals=0
        ),
        name="owner_rows",
    )(got)


def rows_dot(left, right):
    return jnp.dot(left, right, preferred_element_type=F32)


def contract_cols(left, right):
    return lax.dot_general(left, right, (((1,), (1,)), ((), ())), preferred_element_type=F32)


def contract_rows(left, right):
    return lax.dot_general(left, right, (((0,), (0,)), ((), ())), preferred_element_type=F32)

def row_block(step, near_count):
    return lax.rem(step + near_count, CORES * near_count)


def send_rows(step, near_count, mp_at, held_ref, other_refs, mine_refs):
    count = len(other_refs)
    own_rows = held_ref.shape[0] // count

    def write(refs):
        for away, ref in enumerate(refs):
            first = pl.multiple_of(lax.bitwise_xor(mp_at, away) * own_rows, own_rows)
            ref[0] = held_ref[pl.ds(first, own_rows), :]

    @pl.when(step < near_count)
    def _():
        write(other_refs)

    @pl.when(step >= near_count)
    def _():
        write(mine_refs)


def place_kernel(place_ref, *refs):
    parts, outs = refs[:-2], refs[-2:]
    each = len(parts) // 2
    for at in range(each):

        @pl.when(pl.program_id(0) == at)
        def _():
            for i, out_ref in enumerate(outs):
                out_ref[...] = parts[i * each + at][...]


def place_rows(first, second, place, near_count):
    rows, model = first[0].shape
    shape = jax.ShapeDtypeStruct((rows * len(first), model), LOW)

    def place_of(i, place_ref):
        return (i // 2) * near_count + lax.bitwise_xor(place_ref[4], lax.rem(i, 2)), 0

    part = pl.BlockSpec((rows, model), lambda i, place_ref: (0, 0))
    return pl.pallas_call(
        place_kernel,
        grid_spec=pltpu.PrefetchScalarGridSpec(
            num_scalar_prefetch=1,
            grid=(len(first),),
            in_specs=[part] * (2 * len(first)),
            out_specs=[pl.BlockSpec((rows, model), place_of)] * 2,
        ),
        out_shape=[shape] * 2,
        compiler_params=pltpu.CompilerParams(vmem_limit_bytes=32 * 2**20),
        cost_estimate=pl.CostEstimate(flops=0, bytes_accessed=0, transcendentals=0),
        name="place_rows",
    )(place, *first, *second)


def take_rows(step, near_count, mp_at, other_refs, mine_refs, rows_ref):
    own_rows = other_refs[0].shape[1]

    def read(refs):
        for away, ref in enumerate(refs):
            first = pl.multiple_of(lax.bitwise_xor(mp_at, away) * own_rows, own_rows)
            rows_ref[pl.ds(first, own_rows), :] = ref[0]

    @pl.when(step < near_count)
    def _():
        read(other_refs)

    @pl.when(step >= near_count)
    def _():
        read(mine_refs)


def sent_specs(near_count, count, own_rows, model):
    other = pl.BlockSpec((1, own_rows, model), lambda i: (jnp.minimum(i, near_count - 1), 0, 0))
    mine = pl.BlockSpec((1, own_rows, model), lambda i: (jnp.maximum(i - near_count, 0), 0, 0))
    shape = jax.ShapeDtypeStruct((near_count, own_rows, model), LOW)
    return [other] * count + [mine] * count, [shape] * (2 * count)


def partial_kernel(near_count, count, product, place_ref, left_ref, weight_ref, *refs):
    held_ref = refs[-1]
    product(left_ref, weight_ref, held_ref)
    send_rows(
        pl.program_id(0), near_count, place_ref[3], held_ref, refs[:count], refs[count : 2 * count]
    )


def partial_rows(left, weight, model, place, near_count, count, product, name):
    seq_len, depth = left.shape
    rows = seq_len // (CORES * near_count)
    out_specs, out_shape = sent_specs(near_count, count, rows // count, model)
    outs = pl.pallas_call(
        functools.partial(partial_kernel, near_count, count, product),
        grid=(CORES * near_count,),
        in_specs=[
            pl.BlockSpec(memory_space=pltpu.SMEM),
            pl.BlockSpec((rows, depth), lambda i: (row_block(i, near_count), 0)),
            pl.BlockSpec(weight.shape, lambda i: (0, 0, 0)),
        ],
        out_specs=out_specs,
        out_shape=out_shape,
        scratch_shapes=[pltpu.VMEM((rows, model), LOW)],
        compiler_params=pltpu.CompilerParams(vmem_limit_bytes=40 * 2**20),
        cost_estimate=pl.CostEstimate(
            flops=0, bytes_accessed=0, transcendentals=0
        ),
        name=name,
    )(place, left, weight)
    return outs[count:], outs[:count]


def column_product(shard, first, last, left_ref, weight_ref, held_ref):
    weight = weight_ref[:, :shard, first:last]
    weight = weight.reshape(weight.shape[0] * shard, last - first)
    held_ref[...] = contract_cols(left_ref[...], weight).astype(LOW)


def row_product(height, left_ref, weight_ref, held_ref):
    left = left_ref[...]
    width = weight_ref.shape[2]
    for at in range(weight_ref.shape[0]):
        held_ref[:, at * width : (at + 1) * width] = rows_dot(
            left, weight_ref[at, :height, :]
        ).astype(LOW)


def ffn_blocks_kernel(seqs, members, gate_ref, up_ref, down_ref, gain_ref, first_ref, second_ref):
    shard = gate_ref.shape[0]
    width = gate_ref.shape[1] // members
    gain = as_column(gain_ref[...].astype(LOW).astype(F32), 0, shard)
    for member in range(members):
        here = slice(member * width, (member + 1) * width)
        parts = [
            (ref[:, here].astype(LOW).astype(F32) * gain).astype(LOW) for ref in (gate_ref, up_ref)
        ]
        both = jnp.concatenate(parts, 1)
        down = down_ref[here, :].astype(LOW)
        for seq in range(seqs):
            at = seq * members + member
            first_ref[at, :width, :] = down
            first_ref[at, width:, :] = both[:, :shard]
            second_ref[at] = both[:, shard:]


def ffn_blocks(w_gate, w_up, w_down, gain, seqs, members):
    shard, columns = w_gate.shape
    width = columns // members
    return pl.pallas_call(
        functools.partial(ffn_blocks_kernel, seqs, members),
        out_shape=[
            jax.ShapeDtypeStruct((seqs * members, width + shard, shard), LOW),
            jax.ShapeDtypeStruct((seqs * members, shard, 2 * width - shard), LOW),
        ],
        compiler_params=pltpu.CompilerParams(vmem_limit_bytes=40 * 2**20),
        cost_estimate=pl.CostEstimate(
            flops=0, bytes_accessed=18 * shard * columns, transcendentals=0
        ),
        name="ffn_blocks",
    )(w_gate, w_up, w_down, gain)


def ffn_kernel(near_count, count, place_ref, *refs):
    came, refs = refs[: 2 * count], refs[2 * count :]
    grad_ref, first_ref, second_ref = refs[:3]
    other_refs, mine_refs = refs[3 : 3 + count], refs[3 + count : 3 + 2 * count]
    rows_ref, act_ref, d_ref, down_ref, held_ref, sum_ref = refs[3 + 2 * count :]
    step = pl.program_id(0)
    take_rows(step, near_count, place_ref[3], came[:count], came[count:], rows_ref)
    sources, height, shard = first_ref.shape
    width = height - shard
    rows = rows_ref[...]
    block = row_block(step, near_count)
    first = block_place(block, place_ref[1], near_count) * rows.shape[0]
    valid = first + lax.broadcasted_iota(jnp.int32, (rows.shape[0], 1), 0) < place_ref[0]
    grads = only(valid, grad_ref[...])
    early = first_ref[:, width:, :].reshape(sources * shard, shard)
    late = second_ref[...].reshape(sources * shard, 2 * width - shard)
    both = jnp.concatenate([rows_dot(rows, early), rows_dot(rows, late)], 1)
    gate, up = both[:, :width], both[:, width:]
    scale, cubic = 0.7978845608028654, 0.044715
    square = gate * gate
    bent = jnp.tanh(scale * (gate + cubic * square * gate))
    half = 0.5 * (1.0 + bent)
    value = gate * half
    slope = half + 0.5 * gate * (1.0 - bent * bent) * (scale * (1.0 + 3.0 * cubic * square))
    act = (value * up).astype(LOW)
    act_ref[...] = act
    d_hidden = jnp.zeros((rows.shape[0], width), F32)
    for at in range(sources):
        d_hidden = d_hidden + contract_cols(
            grads[:, at * shard : (at + 1) * shard], first_ref[at, :width, :]
        )
    d_both = jnp.concatenate(
        [(d_hidden * up * slope).astype(LOW), (d_hidden * value).astype(LOW)], 1
    )
    d_ref[...] = d_both
    held_ref[...] = (
        contract_cols(d_both[:, :shard], early) + contract_cols(d_both[:, shard:], late)
    ).astype(LOW)
    send_rows(step, near_count, place_ref[3], held_ref, other_refs, mine_refs)
    product = contract_rows(act, grads)

    @pl.when(step == 0)
    def _():
        sum_ref[...] = product

    @pl.when(step > 0)
    def _():
        sum_ref[...] += product

    @pl.when(step == pl.num_programs(0) - 1)
    def _():
        for at in range(sources):
            down_ref[at] = sum_ref[:, at * shard : (at + 1) * shard].astype(LOW)


def feed_forward(mine, other, grads, first, second, place):
    seq_len, model = grads.shape
    near_count, count = mine[0].shape[0], len(mine)
    sources, height, shard = first.shape
    width = height - shard
    rows = seq_len // (CORES * near_count)
    out_specs, out_shape = sent_specs(near_count, count, rows // count, model)

    def blocks(columns):
        return pl.BlockSpec((rows, columns), lambda i: (row_block(i, near_count), 0))

    outs = pl.pallas_call(
        functools.partial(ffn_kernel, near_count, count),
        grid=(CORES * near_count,),
        in_specs=[
            pl.BlockSpec(memory_space=pltpu.SMEM),
            *out_specs,
            blocks(model),
            pl.BlockSpec(first.shape, lambda i: (0, 0, 0)),
            pl.BlockSpec(second.shape, lambda i: (0, 0, 0)),
        ],
        out_specs=out_specs
        + [
            blocks(model),
            blocks(width),
            blocks(2 * width),
            pl.BlockSpec((sources, width, shard), lambda i: (0, 0, 0)),
        ],
        out_shape=out_shape
        + [
            jax.ShapeDtypeStruct((seq_len, model), LOW),
            jax.ShapeDtypeStruct((seq_len, width), LOW),
            jax.ShapeDtypeStruct((seq_len, 2 * width), LOW),
            jax.ShapeDtypeStruct((sources, width, shard), LOW),
        ],
        scratch_shapes=[pltpu.VMEM((rows, model), LOW), pltpu.VMEM((width, model), F32)],
        compiler_params=pltpu.CompilerParams(vmem_limit_bytes=56 * 2**20),
        cost_estimate=pl.CostEstimate(
            flops=12 * seq_len * model * width, bytes_accessed=12 * seq_len * model, transcendentals=0
        ),
        name="feed_forward",
    )(place, *other, *mine, grads, first, second)
    return outs[count : 2 * count], outs[:count], *outs[2 * count :]


COLUMN = ("seq", "near", "core")


def exchange(blocks, axes):
    return lax.all_to_all(blocks, axes, split_axis=0, concat_axis=0, tiled=True)


def swap(block, axis):
    return lax.ppermute(block, axis, [(0, 1), (1, 0)])


def after(value, *done):
    return lax.optimization_barrier((value,) + done)[0]


def rms(values):
    return lax.rsqrt(jnp.mean(values * values, axis=-1, keepdims=True) + EPSILON)


def norm_grad(inner, normed, inverse):
    return inverse * (inner - normed * jnp.mean(inner * normed, axis=-1, keepdims=True))


def local(
    inputs,
    cotangent,
    lengths,
    attn_scale,
    w_query,
    w_key,
    w_value,
    w_out,
    rel_table,
    ffn_scale,
    w_gate,
    w_up,
    w_down,
):
    seqs = lax.axis_size("seq")
    near_count = lax.axis_size("near")
    mp_count = lax.axis_size("mp")
    members = near_count * CORES
    sources = seqs * members
    tok_rows, model = inputs.shape
    seq_len = tok_rows * members
    own_rows = tok_rows // mp_count
    half_rows = seq_len // CORES
    shard = attn_scale.shape[0]
    table_rows, heads_mp = rel_table.shape
    buckets = table_rows * sources
    heads = heads_mp // members
    width = w_query.shape[1] // members
    hidden_width = w_gate.shape[1] // members

    near_at = lax.axis_index("near")
    core_at = lax.axis_index("core")
    mp_at = lax.axis_index("mp")
    member_at = near_at * CORES + core_at
    length = lax.dynamic_slice_in_dim(lengths, lax.axis_index("seq"), 1, 0)
    place = jnp.stack(
        [length[0]] + [at.astype(jnp.int32) for at in (core_at, member_at, mp_at, near_at)]
    )

    def over_mp(own, axis):
        shape = own.shape[:axis] + (mp_count,) + own.shape[axis:]
        blocks = lax.dynamic_update_index_in_dim(jnp.zeros(shape, own.dtype), own, mp_at, axis)
        moved = [(away, shifted(own, away)) for away in reversed(range(1, mp_count))]
        for away, block in moved:
            blocks = lax.dynamic_update_index_in_dim(blocks, block, mp_at ^ away, axis)
        return blocks

    def shifted(block, away):
        return lax.ppermute(block, "mp", [(i, i ^ away) for i in range(mp_count)])

    def in_near_order(own, moved):
        return jnp.stack(
            [jnp.where(near_at == 0, own, moved), jnp.where(near_at == 0, moved, own)], 0
        )

    def near_rows(blocks, meanwhile):
        own = [lax.dynamic_slice_in_dim(block, mp_at * own_rows, own_rows, 0) for block in blocks]
        near = swap(jnp.stack(own), "near")
        came = [(0, near)] + [(away, shifted(near, away)) for away in range(1, mp_count)]
        made = meanwhile(came[1][1])
        came = came[:2] + [(away, after(block, *made)) for away, block in came[2:]]
        halves = []
        for half in (came, [(away, swap(block, "core")) for away, block in came]):
            rows = jnp.zeros((len(blocks), mp_count, own_rows, model), near.dtype)
            for away, block in half:
                rows = lax.dynamic_update_index_in_dim(rows, block, mp_at ^ away, 1)
            halves.append([rows[i].reshape(tok_rows, model) for i in range(len(blocks))])
        return *halves, made

    def gather_rows(near):
        mine = [near] + [shifted(near, away) for away in range(1, mp_count)]
        return mine, [swap(block, "core") for block in mine]

    def sum_cores(mine, other):
        return [
            kept.astype(F32) + swap(sent, "core").astype(F32) for kept, sent in zip(mine, other)
        ]

    def send_mp(sums):
        return [shifted(sums[away].astype(LOW), away) for away in reversed(range(1, mp_count))]

    def sum_mp(sums, *meanwhile):
        moved = send_mp(sums)
        if meanwhile:
            moved = [after(piece, *meanwhile) for piece in moved]
        return sum((piece.astype(F32) for piece in moved), sums[0])

    def split_near(pair):
        sent = jnp.where(near_at == 0, pair[1], pair[0]).astype(LOW)
        return sent, jnp.where(near_at == 0, pair[0], pair[1])

    def sum_near_both(pair):
        low = pair.astype(LOW)
        moved = swap(low, "near")
        return low.astype(F32) + moved.astype(F32), moved

    def near_pair(own, moved):
        pair = [
            lax.dynamic_slice_in_dim(block, mp_at * own_rows, own_rows, 0)
            for block in (own, moved)
        ]
        return in_near_order(*pair)

    def here(pair):
        return lax.dynamic_index_in_dim(pair, near_at, 0, keepdims=False)

    attn_sent = attention_blocks(
        (w_query, w_key, w_value), w_out, attn_scale.reshape(1, shard), rel_table, seqs, members
    )
    attn_got = exchange(attn_sent, COLUMN)
    def partial(left, weight, product, name):
        return partial_rows(left, weight, model, place, near_count, mp_count, product, name)

    table = attn_got[:, shard : shard + table_rows, :heads_mp].reshape(buckets, heads_mp)

    def normed(rows):
        values = rows.astype(F32)
        return (values * rms(values)).astype(LOW)

    def make_blocks(first_came):
        return ffn_blocks(
            w_gate, w_up, w_down, after(ffn_scale.reshape(1, shard), first_came), seqs, members
        )

    (moved_inputs, moved_cotangent), core_moved, (ffn_first, ffn_second) = near_rows(
        [inputs, cotangent], make_blocks
    )
    input_parts = [inputs, moved_inputs, swap(inputs, "core"), core_moved[0]]
    core_cotangent = swap(after(cotangent, moved_inputs), "core")
    grad_parts = [cotangent, moved_cotangent, core_cotangent, core_moved[1]]
    parts = [normed(part) for part in input_parts]
    parts = lax.optimization_barrier((*parts, ffn_first, ffn_second))[:4]
    first_got = exchange(after(ffn_first, attn_got), COLUMN)

    qkv, attended, prob, out_mine, out_other = attention_forward(
        parts, attn_got, table, place, heads, shard, mp_count
    )
    normed_rows, grad_two = place_rows(parts, grad_parts, after(place, attended), near_count)
    mixed, mixed_moved = sum_near_both(
        after(sum_mp(sum_cores(out_mine, out_other), grad_two, normed_rows), first_got)
    )
    second_got = exchange(after(ffn_second, mixed_moved), COLUMN)

    pair_inputs = near_pair(inputs, moved_inputs).astype(F32)
    after_attn = pair_inputs + mixed
    inv_two = rms(after_attn)
    normed_two = after_attn * inv_two
    mine_two, other_two = gather_rows(normed_two.astype(LOW))

    d_mine, d_other, hidden_two, acts, d_both, d_down_w = feed_forward(
        mine_two, other_two, grad_two, first_got, second_got, place
    )
    inner_cores = sum_cores(d_mine, d_other)
    down_product = functools.partial(row_product, hidden_width)
    ffn_partial = partial(after(acts, *inner_cores), first_got, down_product, "ffn_out")

    def to_owners(grad):
        return exchange(grad, COLUMN)

    d_gate_up_w = contract_rows(hidden_two, after(d_both, *inner_cores)).astype(LOW)
    inner_two, inner_moved = sum_near_both(
        sum_mp(inner_cores, d_gate_up_w, *ffn_partial[0], *ffn_partial[1])
    )

    pair_first = (
        lax.broadcasted_iota(jnp.int32, (near_count, own_rows, 1), 0) * (CORES * tok_rows)
        + lax.broadcasted_iota(jnp.int32, (near_count, own_rows, 1), 1)
        + (core_at * tok_rows + mp_at * own_rows)
    )
    pair_valid = pair_first < length
    pair_grad = near_pair(cotangent, moved_cotangent).astype(F32)
    grad_one = jnp.where(pair_valid, pair_grad, 0.0) + norm_grad(inner_two, normed_two, inv_two)
    grad_one_low = grad_one.astype(LOW)
    mine_one, other_one = gather_rows(grad_one_low)
    d_gate_up = to_owners(
        after(d_gate_up_w, inner_moved, grad_one_low).reshape(sources, shard, -1)
    )
    ffn_cores = sum_cores(*ffn_partial)
    d_qkv, d_table, rows_one = attention_backward(
        prob, mine_one, other_one, attn_got, qkv, place, heads, shard, buckets
    )
    qkv_product = functools.partial(column_product, shard, 0, 3 * width)
    ffn_moved = send_mp([after(rows, *mine_one[1:]) for rows in ffn_cores])
    table_sent = d_table[:, :heads].astype(LOW).reshape(sources, table_rows, heads)
    table_sent = jnp.pad(
        table_sent, ((0, 0), (0, EXTRA - table_rows), (0, 3 * width - heads))
    )
    d_qkv_w = contract_rows(normed_rows, d_qkv).astype(LOW).reshape(sources, shard, -1)
    d_qkv_sent = jnp.concatenate([d_qkv_w, table_sent], 1)
    inner_cores = sum_cores(
        *partial(after(d_qkv, d_qkv_sent, *ffn_moved), attn_got, qkv_product, "attention_in")
    )
    inner_pair = sum_mp(inner_cores)
    d_qkv_got = to_owners(after(d_qkv_sent, d_gate_up))
    d_out = contract_rows(after(attended, inner_cores[0]), rows_one)
    d_out = jnp.moveaxis(d_out.astype(LOW).reshape(width, sources, shard), 1, 0)
    d_rows_sent = jnp.concatenate([d_down_w, d_out], 1)

    (d_w_gate, d_w_up), ffn_gain, _ = owner_grads(
        after(d_gate_up, inner_cores[0]), (w_gate, w_up), ffn_scale.reshape(1, shard), members, None
    )
    ffn_sent, ffn_kept = split_near(
        sum((piece.astype(F32) for piece in ffn_moved), ffn_cores[0])
    )
    inner_sent, inner_kept = split_near(inner_pair)
    came = swap(
        after(jnp.stack([ffn_sent, inner_sent]), here(pair_valid), d_rows_sent, ffn_gain), "near"
    )
    own_inputs = here(pair_inputs)
    inv_one = rms(own_inputs)
    grad_input = here(grad_one) + norm_grad(inner_kept + came[1].astype(F32), own_inputs * inv_one, inv_one)
    own_out = jnp.where(here(pair_valid), here(after_attn) + ffn_kept + came[0].astype(F32), 0.0)
    owned = after(
        jnp.stack([own_out.astype(LOW), grad_input.astype(LOW)]), d_qkv_got
    )
    rows_out = [jnp.zeros((mp_count, own_rows, model), LOW)] * 2
    blocks_out = [owned] + [shifted(owned, away) for away in range(1, mp_count)]
    d_rows = to_owners(after(d_rows_sent, d_qkv_got))
    for away, block in enumerate(blocks_out):
        rows_out = [
            lax.dynamic_update_index_in_dim(rows, block[i], mp_at ^ away, 0)
            for i, rows in enumerate(rows_out)
        ]
    layer_out, d_inputs = (rows.reshape(tok_rows, model) for rows in rows_out)

    (d_w_query, d_w_key, d_w_value), attn_gain, d_rel_table = owner_grads(
        after(d_qkv_got, blocks_out[1]),
        (w_query, w_key, w_value),
        attn_scale.reshape(1, shard),
        members,
        (table_rows, heads_mp),
    )
    gains = jnp.concatenate([attn_gain, ffn_gain], 0)
    d_w_down, d_w_out = owner_rows(d_rows, members, hidden_width)
    gains = sum((shifted(gains, away) for away in range(1, mp_count)), gains)
    return (
        layer_out,
        d_inputs,
        gains[0],
        d_w_query,
        d_w_key,
        d_w_value,
        d_w_out,
        d_rel_table,
        gains[1],
        d_w_gate,
        d_w_up,
        d_w_down,
    )


def solution(mesh):
    fsdp, mp = mesh.shape["fsdp"], mesh.shape["mp"]

    def run(*args):
        seqs = args[2].shape[0]
        members = fsdp // seqs
        inner = Mesh(
            mesh.devices.reshape(seqs, members // CORES, CORES, mp), ("seq", "near", "core", "mp")
        )
        rows, columns, first = P(COLUMN, None), P("mp", COLUMN), P(COLUMN)
        both = P(COLUMN, "mp")
        in_specs = (
            rows, rows, P(), first, both, both, both, columns, both, first, both, both, columns,
        )
        out_specs = (
            rows, rows, first, both, both, both, columns, both, first, both, both, columns,
        )
        return jax.shard_map(
            local, mesh=inner, in_specs=in_specs, out_specs=out_specs, check_vma=False
        )(*args)

    return run
```

```python
import functools

import jax
import jax.numpy as jnp
from jax import lax
from jax.experimental import pallas as pl
from jax.experimental.pallas import tpu as pltpu
from jax.sharding import Mesh, PartitionSpec as P

LOW = jnp.bfloat16
F32 = jnp.float32
CORES = 2
THRESHOLDS = (12, 16, 23, 32, 46, 64, 91)
EPSILON = 1e-06
MASKED = -1e30
SKEW = 128


def bucket_of(rel_offset):
    distance = jnp.abs(rel_offset)
    far_bucket = 8 + sum(((distance >= threshold).astype(jnp.int32) for threshold in THRESHOLDS))
    bucket_abs = jnp.where(distance < 8, distance, far_bucket)
    return bucket_abs + jnp.where(rel_offset > 0, 16, 0)


def bucket_onehot(buckets, seq_len):
    offset = lax.broadcasted_iota(jnp.int32, (buckets, 2 * seq_len), 1) - seq_len
    bucket = lax.broadcasted_iota(jnp.int32, (buckets, 2 * seq_len), 0)
    return bucket_of(offset) == bucket


def head_lanes(rows, width, head_width, head):
    lane = lax.broadcasted_iota(jnp.int32, (rows, width), 1)
    return (lane >= head * head_width) & (lane < (head + 1) * head_width)


def only(mask, values):
    return jnp.where(mask, values, jnp.zeros_like(values))


def block_place(block, core, near_count):
    return lax.rem(block, near_count) * CORES + lax.bitwise_xor(lax.div(block, near_count), core)


def bias_places(place_ref, step, blocks, rows, seq_len):
    core, near_count = place_ref[1], blocks // CORES
    query = block_place(step, core, near_count) * rows
    return [
        [
            pl.multiple_of(
                block_place(block, core, near_count) * rows - query - part * SKEW + seq_len - SKEW,
                SKEW,
            )
            for block in range(blocks)
        ]
        for part in range(rows // SKEW)
    ]


def forward_kernel(heads, shard, near_count, count, place_ref, *refs):
    own_ref, moved_ref, core_ref, core_moved_ref, got_ref, table_ref = refs[:6]
    qkv_ref, o_ref, p_ref = refs[6:9]
    other_refs, mine_refs = refs[9 : 9 + count], refs[9 + count : 9 + 2 * count]
    skew_ref, held_ref = refs[9 + 2 * count :]
    step = pl.program_id(0)
    seq_len = qkv_ref.shape[0]
    rows, width = o_ref.shape
    model = held_ref.shape[1]
    head_width = width // heads
    span = 2 * seq_len
    blocks = seq_len // rows
    block = row_block(step, near_count)

    @pl.when(step == 0)
    def _():
        weight = got_ref[:, :shard, : 3 * width].reshape(model, 3 * width)
        near = place_ref[4]
        for at, ref in enumerate((own_ref, moved_ref, core_ref, core_moved_ref)):
            first = (at // 2) * near_count + lax.bitwise_xor(near, at % 2)
            qkv_ref[pl.ds(pl.multiple_of(first * rows, rows), rows), :] = rows_dot(
                ref[...], weight
            ).astype(LOW)
        one_hot = bucket_onehot(table_ref.shape[0], seq_len)
        table = table_ref[...].astype(F32)
        column = lax.broadcasted_iota(jnp.int32, table.shape, 1)
        for head in range(heads):
            here = column == place_ref[2] * heads + head
            levels = jnp.sum(jnp.where(here, table, 0.0), axis=1, keepdims=True)
            line = jnp.sum(jnp.where(one_hot, levels, 0.0), axis=0, keepdims=True)
            line = jnp.broadcast_to(line, (SKEW, span))
            skew_ref[head] = pltpu.roll(line, span - SKEW, 1, stride=1, stride_axis=0)

    row = lax.broadcasted_iota(jnp.int32, (1, rows), 1)
    allowed = jnp.concatenate(
        [
            block_place(at, place_ref[1], near_count) * rows + row < place_ref[0]
            for at in range(blocks)
        ],
        1,
    )
    queries = qkv_ref[pl.ds(pl.multiple_of(block * rows, rows), rows), :width]
    keys = qkv_ref[:, width : 2 * width]
    values = qkv_ref[:, 2 * width :]
    total = jnp.zeros((rows, width), F32)
    places = bias_places(place_ref, block, blocks, rows, seq_len)
    for head in range(heads):
        scores = lax.dot_general(
            only(head_lanes(rows, width, head_width, head), queries),
            keys,
            (((1,), (1,)), ((), ())),
            preferred_element_type=F32,
        )
        bias = jnp.concatenate(
            [
                jnp.concatenate([skew_ref[head, :, pl.ds(place, rows)] for place in part], 1)
                for part in places
            ],
            0,
        )
        scores = jnp.where(allowed, scores + bias, MASKED)
        grown = jnp.exp(scores - jnp.max(scores, axis=1, keepdims=True))
        prob = (grown * (1.0 / jnp.sum(grown, axis=1, keepdims=True))).astype(LOW)
        p_ref[head] = prob
        total = total + jnp.dot(
            prob,
            only(head_lanes(seq_len, width, head_width, head), values),
            preferred_element_type=F32,
        )
    attended = total.astype(LOW)
    o_ref[...] = attended
    weight = got_ref[:, :shard, 3 * width :].reshape(model, width)
    held_ref[...] = contract_cols(attended, weight).astype(LOW)
    send_rows(step, near_count, place_ref[3], held_ref, other_refs, mine_refs)


def attention_forward(parts, got, table, place, heads, shard, count):
    rows, model = parts[0].shape
    blocks = len(parts)
    near_count = blocks // CORES
    seq_len, width = rows * blocks, got.shape[2] // 4
    out_specs, out_shape = sent_specs(near_count, count, rows // count, model)

    def fixed(shape):
        return pl.BlockSpec(shape, lambda i: (0,) * len(shape))

    outs = pl.pallas_call(
        functools.partial(forward_kernel, heads, shard, near_count, count),
        grid=(blocks,),
        in_specs=[pl.BlockSpec(memory_space=pltpu.SMEM)]
        + [fixed(part.shape) for part in parts]
        + [fixed(got.shape), fixed(table.shape)],
        out_specs=[
            fixed((seq_len, 3 * width)),
            pl.BlockSpec((rows, width), lambda i: (row_block(i, near_count), 0)),
            pl.BlockSpec((heads, rows, seq_len), lambda i: (0, row_block(i, near_count), 0)),
        ]
        + out_specs,
        out_shape=[
            jax.ShapeDtypeStruct((seq_len, 3 * width), LOW),
            jax.ShapeDtypeStruct((seq_len, width), LOW),
            jax.ShapeDtypeStruct((heads, seq_len, seq_len), LOW),
        ]
        + out_shape,
        scratch_shapes=[
            pltpu.VMEM((heads, SKEW, 2 * seq_len), F32),
            pltpu.VMEM((rows, model), LOW),
        ],
        compiler_params=pltpu.CompilerParams(vmem_limit_bytes=34 * 2**20),
        cost_estimate=pl.CostEstimate(flops=0, bytes_accessed=0, transcendentals=0),
        name="attention_forward",
    )(place, *parts, got, table)
    return (*outs[:3], outs[3 + count :], outs[3 : 3 + count])


def backward_kernel(heads, shard, near_count, count, place_ref, *refs):
    came, refs = refs[: 2 * count], refs[2 * count :]
    p_ref, got_ref, qkv_ref, d_ref, dt_ref, rows_ref, dk_sum, dv_sum, skew_ref = refs
    step = pl.program_id(0)
    block = row_block(step, near_count)
    take_rows(step, near_count, place_ref[3], came[:count], came[count:], rows_ref)
    rows, model = rows_ref.shape
    seq_len = qkv_ref.shape[0]
    width = qkv_ref.shape[1] // 3
    head_width = width // heads
    span = 2 * seq_len
    blocks = seq_len // rows

    @pl.when(step == 0)
    def _():
        dk_sum[...] = jnp.zeros_like(dk_sum)
        dv_sum[...] = jnp.zeros_like(dv_sum)
        skew_ref[...] = jnp.zeros_like(skew_ref)

    here = pl.ds(pl.multiple_of(block * rows, rows), rows)
    queries = qkv_ref[here, :width]
    keys = qkv_ref[:, width : 2 * width]
    values = qkv_ref[:, 2 * width :]
    weight = got_ref[:, :shard, 3 * width :].reshape(model, width)
    grads = rows_dot(rows_ref[...], weight).astype(LOW)
    total = jnp.zeros((rows, width), F32)
    places = bias_places(place_ref, block, blocks, rows, seq_len)
    for head in range(heads):
        own = head_lanes(rows, width, head_width, head)
        own_grads = only(own, grads)
        d_prob = lax.dot_general(
            own_grads, values, (((1,), (1,)), ((), ())), preferred_element_type=F32
        )
        prob_low = p_ref[head]
        prob = prob_low.astype(F32)
        weighed = prob * d_prob
        d_scores = (weighed - prob * jnp.sum(weighed, axis=1, keepdims=True)).astype(LOW)
        total = total + jnp.dot(
            d_scores,
            only(head_lanes(seq_len, width, head_width, head), keys),
            preferred_element_type=F32,
        )
        dk_sum[...] += lax.dot_general(
            d_scores, only(own, queries), (((0,), (0,)), ((), ())), preferred_element_type=F32
        )
        dv_sum[...] += lax.dot_general(
            prob_low, own_grads, (((0,), (0,)), ((), ())), preferred_element_type=F32
        )
        for part in range(rows // SKEW):
            for at in range(blocks):
                skew_ref[head, :, pl.ds(places[part][at], rows)] += d_scores[
                    part * SKEW : (part + 1) * SKEW, at * rows : (at + 1) * rows
                ].astype(F32)
    d_ref[here, :width] = total.astype(LOW)

    @pl.when(step == pl.num_programs(0) - 1)
    def _():
        d_ref[:, width : 2 * width] = dk_sum[...].astype(LOW)
        d_ref[:, 2 * width :] = dv_sum[...].astype(LOW)
        one_hot = bucket_onehot(dt_ref.shape[0], seq_len)
        row = lax.broadcasted_iota(jnp.int32, (SKEW, span), 0)
        column = lax.broadcasted_iota(jnp.int32, dt_ref.shape, 1)
        result = jnp.zeros(dt_ref.shape, F32)
        for head in range(heads):
            level = pltpu.roll(skew_ref[head], SKEW, 1)
            bit = 1
            while bit < SKEW:
                level = jnp.where((row & bit) != 0, pltpu.roll(level, span - bit, 1), level)
                bit *= 2
            line = jnp.sum(level, axis=0, keepdims=True)
            summed = jnp.sum(jnp.where(one_hot, line, 0.0), axis=1, keepdims=True)
            result = jnp.where(column == head, summed, result)
        dt_ref[...] = result


def attention_backward(prob, mine, other, got, qkv, place, heads, shard, buckets):
    seq_len, width = qkv.shape[0], qkv.shape[1] // 3
    near_count, own_rows, model = mine[0].shape
    count = len(mine)
    rows = count * own_rows
    came_specs, _ = sent_specs(near_count, count, own_rows, model)
    return pl.pallas_call(
        functools.partial(backward_kernel, heads, shard, near_count, count),
        grid=(seq_len // rows,),
        in_specs=[
            pl.BlockSpec(memory_space=pltpu.SMEM),
            *came_specs,
            pl.BlockSpec((heads, rows, seq_len), lambda i: (0, row_block(i, near_count), 0)),
            pl.BlockSpec(got.shape, lambda i: (0, 0, 0)),
            pl.BlockSpec(qkv.shape, lambda i: (0, 0)),
        ],
        out_specs=[
            pl.BlockSpec(qkv.shape, lambda i: (0, 0)),
            pl.BlockSpec((buckets, 128), lambda i: (0, 0)),
            pl.BlockSpec((rows, model), lambda i: (row_block(i, near_count), 0)),
        ],
        out_shape=[
            jax.ShapeDtypeStruct(qkv.shape, LOW),
            jax.ShapeDtypeStruct((buckets, 128), F32),
            jax.ShapeDtypeStruct((seq_len, model), LOW),
        ],
        scratch_shapes=[
            pltpu.VMEM((seq_len, width), F32),
            pltpu.VMEM((seq_len, width), F32),
            pltpu.VMEM((heads, SKEW, 2 * seq_len), F32),
        ],
        compiler_params=pltpu.CompilerParams(vmem_limit_bytes=34 * 2**20),
        cost_estimate=pl.CostEstimate(flops=0, bytes_accessed=0, transcendentals=0),
        name="attention_backward",
    )(place, *other, *mine, prob, got, qkv)


EXTRA = 8
OWNER_ROWS = 64


def as_column(row, first, count):
    size = row.shape[1]
    here = lax.broadcasted_iota(jnp.int32, (count, size), 1) == first + lax.broadcasted_iota(
        jnp.int32, (count, size), 0
    )
    return jnp.sum(jnp.where(here, row, 0.0), axis=1, keepdims=True)


def blocks_kernel(seqs, members, q_ref, k_ref, v_ref, o_ref, gain_ref, table_ref, sent_ref):
    shard = q_ref.shape[0]
    width = q_ref.shape[1] // members
    gain = as_column(gain_ref[...].astype(LOW).astype(F32), 0, shard)
    parts = [
        (ref[...].astype(LOW).astype(F32) * gain).astype(LOW) for ref in (q_ref, k_ref, v_ref)
    ]
    parts.append(o_ref[...].T.astype(LOW))
    rest = jnp.zeros((EXTRA, sent_ref.shape[2]), LOW)
    table_rows, heads = table_ref.shape
    for seq in range(seqs):
        for member in range(members):
            at = seq * members + member
            for i, part in enumerate(parts):
                sent_ref[at, :shard, i * width : (i + 1) * width] = part[
                    :, member * width : (member + 1) * width
                ]
            sent_ref[at, shard:, :] = rest
            sent_ref[at, shard : shard + table_rows, :heads] = table_ref[...].astype(LOW)


def attention_blocks(weights, w_out, gain, table, seqs, members):
    shard, columns = weights[0].shape
    return pl.pallas_call(
        functools.partial(blocks_kernel, seqs, members),
        out_shape=jax.ShapeDtypeStruct(
            (seqs * members, shard + EXTRA, 4 * columns // members), LOW
        ),
        compiler_params=pltpu.CompilerParams(vmem_limit_bytes=60 * 2**20),
        cost_estimate=pl.CostEstimate(
            flops=0, bytes_accessed=16 * shard * columns, transcendentals=0
        ),
        name="attention_blocks",
    )(*weights, w_out, gain, table)


def owner_kernel(count, members, table_shape, *refs):
    got_ref, extra_ref = refs[:2]
    weight_refs = refs[2 : 2 + count]
    gain_ref = refs[2 + count]
    grad_refs = refs[3 + count : 3 + 2 * count]
    sum_ref = refs[3 + 2 * count]
    step = pl.program_id(0)
    rows = got_ref.shape[1]
    seqs = got_ref.shape[0] // members
    width = got_ref.shape[2] // count
    size = sum_ref.shape[1]
    gain = as_column(gain_ref[...].astype(LOW).astype(F32), step * rows, rows)
    total = jnp.zeros((rows, 1), F32)
    for member in range(members):
        product = sum(got_ref[seq * members + member].astype(F32) for seq in range(seqs))
        for i in range(count):
            part = product[:, i * width : (i + 1) * width]
            here = pl.ds(member * width, width)
            grad_refs[i][:, here] = part * gain
            weight = weight_refs[i][:, here].astype(LOW).astype(F32)
            total = total + jnp.sum(weight * part, axis=1, keepdims=True)

    @pl.when(step == 0)
    def _():
        sum_ref[...] = jnp.zeros_like(sum_ref)

    diagonal = lax.broadcasted_iota(jnp.int32, (rows, size), 1) == step * rows + (
        lax.broadcasted_iota(jnp.int32, (rows, size), 0)
    )
    sum_ref[...] += jnp.sum(jnp.where(diagonal, total, 0.0), axis=0, keepdims=True)
    if table_shape is not None:
        table_rows, heads = table_shape
        each = heads // members
        for member in range(members):
            piece = sum(extra_ref[seq * members + member].astype(F32) for seq in range(seqs))
            refs[-1][:, member * each : (member + 1) * each] = piece[:table_rows, :each]


def owner_grads(got, weights, gain, members, table_shape):
    sources, height, columns = got.shape
    shard, wide = weights[0].shape
    count = len(weights)
    rows = min(OWNER_ROWS, shard)
    step_rows = pl.BlockSpec((rows, wide), lambda i: (i, 0))
    row = pl.BlockSpec((1, shard), lambda i: (0, 0))
    last = height // EXTRA - 1
    out_specs = [step_rows] * count + [row]
    out_shape = [jax.ShapeDtypeStruct((shard, wide), F32)] * count
    out_shape.append(jax.ShapeDtypeStruct((1, shard), F32))
    if table_shape is not None:
        out_specs.append(pl.BlockSpec(table_shape, lambda i: (0, 0)))
        out_shape.append(jax.ShapeDtypeStruct(table_shape, F32))
    outs = pl.pallas_call(
        functools.partial(owner_kernel, count, members, table_shape),
        grid=(shard // rows,),
        in_specs=[
            pl.BlockSpec((sources, rows, columns), lambda i: (0, i, 0)),
            pl.BlockSpec((sources, EXTRA, columns), lambda i: (0, last, 0)),
        ]
        + [step_rows] * count
        + [row],
        out_specs=out_specs,
        out_shape=out_shape,
        compiler_params=pltpu.CompilerParams(vmem_limit_bytes=32 * 2**20),
        cost_estimate=pl.CostEstimate(
            flops=0, bytes_accessed=10 * count * shard * wide, transcendentals=0
        ),
        name="owner_grads",
    )(got, got, *weights, gain)
    return outs[:count], outs[count], outs[-1] if table_shape is not None else None


def rows_kernel(members, split, got_ref, first_ref, second_ref):
    seqs = got_ref.shape[0] // members
    rest = got_ref.shape[1] - split
    for member in range(members):
        total = sum(got_ref[seq * members + member].astype(F32) for seq in range(seqs))
        first_ref[pl.ds(member * split, split), :] = total[:split]
        second_ref[pl.ds(member * rest, rest), :] = total[split:]


def owner_rows(got, members, split):
    height, columns = got.shape[1:]
    return pl.pallas_call(
        functools.partial(rows_kernel, members, split),
        out_shape=[
            jax.ShapeDtypeStruct((members * split, columns), F32),
            jax.ShapeDtypeStruct((members * (height - split), columns), F32),
        ],
        compiler_params=pltpu.CompilerParams(vmem_limit_bytes=32 * 2**20),
        cost_estimate=pl.CostEstimate(
            flops=0, bytes_accessed=4 * got.size, transcendentals=0
        ),
        name="owner_rows",
    )(got)


def rows_dot(left, right):
    return jnp.dot(left, right, preferred_element_type=F32)


def contract_cols(left, right):
    return lax.dot_general(left, right, (((1,), (1,)), ((), ())), preferred_element_type=F32)


def contract_rows(left, right):
    return lax.dot_general(left, right, (((0,), (0,)), ((), ())), preferred_element_type=F32)

def row_block(step, near_count):
    return lax.rem(step + near_count, CORES * near_count)


def send_rows(step, near_count, mp_at, held_ref, other_refs, mine_refs):
    count = len(other_refs)
    own_rows = held_ref.shape[0] // count

    def write(refs):
        for away, ref in enumerate(refs):
            first = pl.multiple_of(lax.bitwise_xor(mp_at, away) * own_rows, own_rows)
            ref[0] = held_ref[pl.ds(first, own_rows), :]

    @pl.when(step < near_count)
    def _():
        write(other_refs)

    @pl.when(step >= near_count)
    def _():
        write(mine_refs)


def place_kernel(place_ref, *refs):
    parts, outs = refs[:-2], refs[-2:]
    each = len(parts) // 2
    for at in range(each):

        @pl.when(pl.program_id(0) == at)
        def _():
            for i, out_ref in enumerate(outs):
                out_ref[...] = parts[i * each + at][...]


def place_rows(first, second, place, near_count):
    rows, model = first[0].shape
    shape = jax.ShapeDtypeStruct((rows * len(first), model), LOW)

    def place_of(i, place_ref):
        return (i // 2) * near_count + lax.bitwise_xor(place_ref[4], lax.rem(i, 2)), 0

    part = pl.BlockSpec((rows, model), lambda i, place_ref: (0, 0))
    return pl.pallas_call(
        place_kernel,
        grid_spec=pltpu.PrefetchScalarGridSpec(
            num_scalar_prefetch=1,
            grid=(len(first),),
            in_specs=[part] * (2 * len(first)),
            out_specs=[pl.BlockSpec((rows, model), place_of)] * 2,
        ),
        out_shape=[shape] * 2,
        compiler_params=pltpu.CompilerParams(vmem_limit_bytes=32 * 2**20),
        cost_estimate=pl.CostEstimate(flops=0, bytes_accessed=0, transcendentals=0),
        name="place_rows",
    )(place, *first, *second)


def take_rows(step, near_count, mp_at, other_refs, mine_refs, rows_ref):
    own_rows = other_refs[0].shape[1]

    def read(refs):
        for away, ref in enumerate(refs):
            first = pl.multiple_of(lax.bitwise_xor(mp_at, away) * own_rows, own_rows)
            rows_ref[pl.ds(first, own_rows), :] = ref[0]

    @pl.when(step < near_count)
    def _():
        read(other_refs)

    @pl.when(step >= near_count)
    def _():
        read(mine_refs)


def sent_specs(near_count, count, own_rows, model):
    other = pl.BlockSpec((1, own_rows, model), lambda i: (jnp.minimum(i, near_count - 1), 0, 0))
    mine = pl.BlockSpec((1, own_rows, model), lambda i: (jnp.maximum(i - near_count, 0), 0, 0))
    shape = jax.ShapeDtypeStruct((near_count, own_rows, model), LOW)
    return [other] * count + [mine] * count, [shape] * (2 * count)


def partial_kernel(near_count, count, product, place_ref, left_ref, weight_ref, *refs):
    held_ref = refs[-1]
    product(left_ref, weight_ref, held_ref)
    send_rows(
        pl.program_id(0), near_count, place_ref[3], held_ref, refs[:count], refs[count : 2 * count]
    )


def partial_rows(left, weight, model, place, near_count, count, product, name):
    seq_len, depth = left.shape
    rows = seq_len // (CORES * near_count)
    out_specs, out_shape = sent_specs(near_count, count, rows // count, model)
    outs = pl.pallas_call(
        functools.partial(partial_kernel, near_count, count, product),
        grid=(CORES * near_count,),
        in_specs=[
            pl.BlockSpec(memory_space=pltpu.SMEM),
            pl.BlockSpec((rows, depth), lambda i: (row_block(i, near_count), 0)),
            pl.BlockSpec(weight.shape, lambda i: (0, 0, 0)),
        ],
        out_specs=out_specs,
        out_shape=out_shape,
        scratch_shapes=[pltpu.VMEM((rows, model), LOW)],
        compiler_params=pltpu.CompilerParams(vmem_limit_bytes=40 * 2**20),
        cost_estimate=pl.CostEstimate(
            flops=0, bytes_accessed=0, transcendentals=0
        ),
        name=name,
    )(place, left, weight)
    return outs[count:], outs[:count]


def column_product(shard, first, last, left_ref, weight_ref, held_ref):
    weight = weight_ref[:, :shard, first:last]
    weight = weight.reshape(weight.shape[0] * shard, last - first)
    held_ref[...] = contract_cols(left_ref[...], weight).astype(LOW)


def row_product(height, left_ref, weight_ref, held_ref):
    left = left_ref[...]
    width = weight_ref.shape[2]
    for at in range(weight_ref.shape[0]):
        held_ref[:, at * width : (at + 1) * width] = rows_dot(
            left, weight_ref[at, :height, :]
        ).astype(LOW)


def ffn_blocks_kernel(seqs, members, gate_ref, up_ref, down_ref, gain_ref, first_ref, second_ref):
    shard = gate_ref.shape[0]
    width = gate_ref.shape[1] // members
    gain = as_column(gain_ref[...].astype(LOW).astype(F32), 0, shard)
    for member in range(members):
        here = slice(member * width, (member + 1) * width)
        parts = [
            (ref[:, here].astype(LOW).astype(F32) * gain).astype(LOW) for ref in (gate_ref, up_ref)
        ]
        both = jnp.concatenate(parts, 1)
        down = down_ref[here, :].astype(LOW)
        for seq in range(seqs):
            at = seq * members + member
            first_ref[at, :width, :] = down
            first_ref[at, width:, :] = both[:, :shard]
            second_ref[at] = both[:, shard:]


def ffn_blocks(w_gate, w_up, w_down, gain, seqs, members):
    shard, columns = w_gate.shape
    width = columns // members
    return pl.pallas_call(
        functools.partial(ffn_blocks_kernel, seqs, members),
        out_shape=[
            jax.ShapeDtypeStruct((seqs * members, width + shard, shard), LOW),
            jax.ShapeDtypeStruct((seqs * members, shard, 2 * width - shard), LOW),
        ],
        compiler_params=pltpu.CompilerParams(vmem_limit_bytes=40 * 2**20),
        cost_estimate=pl.CostEstimate(
            flops=0, bytes_accessed=18 * shard * columns, transcendentals=0
        ),
        name="ffn_blocks",
    )(w_gate, w_up, w_down, gain)


def ffn_kernel(near_count, count, place_ref, *refs):
    came, refs = refs[: 2 * count], refs[2 * count :]
    grad_ref, first_ref, second_ref = refs[:3]
    other_refs, mine_refs = refs[3 : 3 + count], refs[3 + count : 3 + 2 * count]
    rows_ref, act_ref, d_ref, down_ref, held_ref, sum_ref = refs[3 + 2 * count :]
    step = pl.program_id(0)
    take_rows(step, near_count, place_ref[3], came[:count], came[count:], rows_ref)
    sources, height, shard = first_ref.shape
    width = height - shard
    rows = rows_ref[...]
    block = row_block(step, near_count)
    first = block_place(block, place_ref[1], near_count) * rows.shape[0]
    valid = first + lax.broadcasted_iota(jnp.int32, (rows.shape[0], 1), 0) < place_ref[0]
    grads = only(valid, grad_ref[...])
    early = first_ref[:, width:, :].reshape(sources * shard, shard)
    late = second_ref[...].reshape(sources * shard, 2 * width - shard)
    both = jnp.concatenate([rows_dot(rows, early), rows_dot(rows, late)], 1)
    gate, up = both[:, :width], both[:, width:]
    scale, cubic = 0.7978845608028654, 0.044715
    square = gate * gate
    bent = jnp.tanh(scale * (gate + cubic * square * gate))
    half = 0.5 * (1.0 + bent)
    value = gate * half
    slope = half + 0.5 * gate * (1.0 - bent * bent) * (scale * (1.0 + 3.0 * cubic * square))
    act = (value * up).astype(LOW)
    act_ref[...] = act
    d_hidden = jnp.zeros((rows.shape[0], width), F32)
    for at in range(sources):
        d_hidden = d_hidden + contract_cols(
            grads[:, at * shard : (at + 1) * shard], first_ref[at, :width, :]
        )
    d_both = jnp.concatenate(
        [(d_hidden * up * slope).astype(LOW), (d_hidden * value).astype(LOW)], 1
    )
    d_ref[...] = d_both
    held_ref[...] = (
        contract_cols(d_both[:, :shard], early) + contract_cols(d_both[:, shard:], late)
    ).astype(LOW)
    send_rows(step, near_count, place_ref[3], held_ref, other_refs, mine_refs)
    product = contract_rows(act, grads)

    @pl.when(step == 0)
    def _():
        sum_ref[...] = product

    @pl.when(step > 0)
    def _():
        sum_ref[...] += product

    @pl.when(step == pl.num_programs(0) - 1)
    def _():
        for at in range(sources):
            down_ref[at] = sum_ref[:, at * shard : (at + 1) * shard].astype(LOW)


def feed_forward(mine, other, grads, first, second, place):
    seq_len, model = grads.shape
    near_count, count = mine[0].shape[0], len(mine)
    sources, height, shard = first.shape
    width = height - shard
    rows = seq_len // (CORES * near_count)
    out_specs, out_shape = sent_specs(near_count, count, rows // count, model)

    def blocks(columns):
        return pl.BlockSpec((rows, columns), lambda i: (row_block(i, near_count), 0))

    outs = pl.pallas_call(
        functools.partial(ffn_kernel, near_count, count),
        grid=(CORES * near_count,),
        in_specs=[
            pl.BlockSpec(memory_space=pltpu.SMEM),
            *out_specs,
            blocks(model),
            pl.BlockSpec(first.shape, lambda i: (0, 0, 0)),
            pl.BlockSpec(second.shape, lambda i: (0, 0, 0)),
        ],
        out_specs=out_specs
        + [
            blocks(model),
            blocks(width),
            blocks(2 * width),
            pl.BlockSpec((sources, width, shard), lambda i: (0, 0, 0)),
        ],
        out_shape=out_shape
        + [
            jax.ShapeDtypeStruct((seq_len, model), LOW),
            jax.ShapeDtypeStruct((seq_len, width), LOW),
            jax.ShapeDtypeStruct((seq_len, 2 * width), LOW),
            jax.ShapeDtypeStruct((sources, width, shard), LOW),
        ],
        scratch_shapes=[pltpu.VMEM((rows, model), LOW), pltpu.VMEM((width, model), F32)],
        compiler_params=pltpu.CompilerParams(vmem_limit_bytes=56 * 2**20),
        cost_estimate=pl.CostEstimate(
            flops=12 * seq_len * model * width, bytes_accessed=12 * seq_len * model, transcendentals=0
        ),
        name="feed_forward",
    )(place, *other, *mine, grads, first, second)
    return outs[count : 2 * count], outs[:count], *outs[2 * count :]


COLUMN = ("seq", "near", "core")


def exchange(blocks, axes):
    return lax.all_to_all(blocks, axes, split_axis=0, concat_axis=0, tiled=True)


def swap(block, axis):
    return lax.ppermute(block, axis, [(0, 1), (1, 0)])


def after(value, *done):
    return lax.optimization_barrier((value,) + done)[0]


def rms(values):
    return lax.rsqrt(jnp.mean(values * values, axis=-1, keepdims=True) + EPSILON)


def norm_grad(inner, normed, inverse):
    return inverse * (inner - normed * jnp.mean(inner * normed, axis=-1, keepdims=True))


def local(
    inputs,
    cotangent,
    lengths,
    attn_scale,
    w_query,
    w_key,
    w_value,
    w_out,
    rel_table,
    ffn_scale,
    w_gate,
    w_up,
    w_down,
):
    seqs = lax.axis_size("seq")
    near_count = lax.axis_size("near")
    mp_count = lax.axis_size("mp")
    members = near_count * CORES
    sources = seqs * members
    tok_rows, model = inputs.shape
    seq_len = tok_rows * members
    own_rows = tok_rows // mp_count
    half_rows = seq_len // CORES
    shard = attn_scale.shape[0]
    table_rows, heads_mp = rel_table.shape
    buckets = table_rows * sources
    heads = heads_mp // members
    width = w_query.shape[1] // members
    hidden_width = w_gate.shape[1] // members

    near_at = lax.axis_index("near")
    core_at = lax.axis_index("core")
    mp_at = lax.axis_index("mp")
    member_at = near_at * CORES + core_at
    length = lax.dynamic_slice_in_dim(lengths, lax.axis_index("seq"), 1, 0)
    place = jnp.stack(
        [length[0]] + [at.astype(jnp.int32) for at in (core_at, member_at, mp_at, near_at)]
    )

    def over_mp(own, axis):
        shape = own.shape[:axis] + (mp_count,) + own.shape[axis:]
        blocks = lax.dynamic_update_index_in_dim(jnp.zeros(shape, own.dtype), own, mp_at, axis)
        moved = [(away, shifted(own, away)) for away in reversed(range(1, mp_count))]
        for away, block in moved:
            blocks = lax.dynamic_update_index_in_dim(blocks, block, mp_at ^ away, axis)
        return blocks

    def shifted(block, away):
        return lax.ppermute(block, "mp", [(i, i ^ away) for i in range(mp_count)])

    def in_near_order(own, moved):
        return jnp.stack(
            [jnp.where(near_at == 0, own, moved), jnp.where(near_at == 0, moved, own)], 0
        )

    def near_rows(blocks, meanwhile):
        own = [lax.dynamic_slice_in_dim(block, mp_at * own_rows, own_rows, 0) for block in blocks]
        near = swap(jnp.stack(own), "near")
        came = [(0, near)] + [(away, shifted(near, away)) for away in range(1, mp_count)]
        made = meanwhile(came[1][1])
        came = came[:2] + [(away, after(block, *made)) for away, block in came[2:]]
        halves = []
        for half in (came, [(away, swap(block, "core")) for away, block in came]):
            rows = jnp.zeros((len(blocks), mp_count, own_rows, model), near.dtype)
            for away, block in half:
                rows = lax.dynamic_update_index_in_dim(rows, block, mp_at ^ away, 1)
            halves.append([rows[i].reshape(tok_rows, model) for i in range(len(blocks))])
        return *halves, made

    def gather_rows(near):
        mine = [near] + [shifted(near, away) for away in range(1, mp_count)]
        return mine, [swap(block, "core") for block in mine]

    def sum_cores(mine, other):
        return [
            kept.astype(F32) + swap(sent, "core").astype(F32) for kept, sent in zip(mine, other)
        ]

    def send_mp(sums):
        return [shifted(sums[away].astype(LOW), away) for away in reversed(range(1, mp_count))]

    def sum_mp(sums, *meanwhile):
        moved = send_mp(sums)
        if meanwhile:
            moved = [after(piece, *meanwhile) for piece in moved]
        return sum((piece.astype(F32) for piece in moved), sums[0])

    def split_near(pair):
        sent = jnp.where(near_at == 0, pair[1], pair[0]).astype(LOW)
        return sent, jnp.where(near_at == 0, pair[0], pair[1])

    def sum_near_both(pair, *last_after):
        low = pair.astype(LOW)
        if not last_after:
            moved = swap(low, "near")
            return low.astype(F32) + moved.astype(F32), moved
        moved = [swap(low[i], "near") for i in range(near_count - 1)]
        moved.append(swap(after(low[near_count - 1], *moved, *last_after), "near"))
        return low.astype(F32) + jnp.stack(moved).astype(F32), moved[-1]

    def near_pair(own, moved):
        pair = [
            lax.dynamic_slice_in_dim(block, mp_at * own_rows, own_rows, 0)
            for block in (own, moved)
        ]
        return in_near_order(*pair)

    def here(pair):
        return lax.dynamic_index_in_dim(pair, near_at, 0, keepdims=False)

    attn_sent = attention_blocks(
        (w_query, w_key, w_value), w_out, attn_scale.reshape(1, shard), rel_table, seqs, members
    )
    attn_got = exchange(attn_sent, COLUMN)
    def partial(left, weight, product, name):
        return partial_rows(left, weight, model, place, near_count, mp_count, product, name)

    table = attn_got[:, shard : shard + table_rows, :heads_mp].reshape(buckets, heads_mp)

    def normed(rows):
        values = rows.astype(F32)
        return (values * rms(values)).astype(LOW)

    def make_blocks(first_came):
        return ffn_blocks(
            w_gate, w_up, w_down, after(ffn_scale.reshape(1, shard), first_came), seqs, members
        )

    (moved_inputs, moved_cotangent), core_moved, (ffn_first, ffn_second) = near_rows(
        [inputs, cotangent], make_blocks
    )
    input_parts = [inputs, moved_inputs, swap(inputs, "core"), core_moved[0]]
    core_cotangent = swap(after(cotangent, moved_inputs), "core")
    grad_parts = [cotangent, moved_cotangent, core_cotangent, core_moved[1]]
    parts = [normed(part) for part in input_parts]
    parts = lax.optimization_barrier((*parts, ffn_first, ffn_second))[:4]
    first_got = exchange(after(ffn_first, attn_got), COLUMN)

    qkv, attended, prob, out_mine, out_other = attention_forward(
        parts, attn_got, table, place, heads, shard, mp_count
    )
    normed_rows, grad_two = place_rows(parts, grad_parts, after(place, attended), near_count)
    mixed, mixed_moved = sum_near_both(
        sum_mp(sum_cores(out_mine, out_other), grad_two, normed_rows), first_got
    )
    second_got = exchange(after(ffn_second, mixed_moved), COLUMN)

    pair_inputs = near_pair(inputs, moved_inputs).astype(F32)
    after_attn = pair_inputs + mixed
    inv_two = rms(after_attn)
    normed_two = after_attn * inv_two
    mine_two, other_two = gather_rows(normed_two.astype(LOW))

    d_mine, d_other, hidden_two, acts, d_both, d_down_w = feed_forward(
        mine_two, other_two, grad_two, first_got, second_got, place
    )
    inner_cores = sum_cores(d_mine, d_other)
    down_product = functools.partial(row_product, hidden_width)
    ffn_partial = partial(after(acts, *inner_cores), first_got, down_product, "ffn_out")

    def to_owners(grad):
        return exchange(grad, COLUMN)

    d_gate_up_w = contract_rows(hidden_two, after(d_both, *inner_cores)).astype(LOW)
    inner_two, inner_moved = sum_near_both(
        sum_mp(inner_cores, d_gate_up_w, *ffn_partial[0], *ffn_partial[1])
    )

    pair_first = (
        lax.broadcasted_iota(jnp.int32, (near_count, own_rows, 1), 0) * (CORES * tok_rows)
        + lax.broadcasted_iota(jnp.int32, (near_count, own_rows, 1), 1)
        + (core_at * tok_rows + mp_at * own_rows)
    )
    pair_valid = pair_first < length
    pair_grad = near_pair(cotangent, moved_cotangent).astype(F32)
    grad_one = jnp.where(pair_valid, pair_grad, 0.0) + norm_grad(inner_two, normed_two, inv_two)
    grad_one_low = grad_one.astype(LOW)
    mine_one, other_one = gather_rows(grad_one_low)
    d_gate_up = to_owners(
        after(d_gate_up_w, inner_moved, grad_one_low).reshape(sources, shard, -1)
    )
    ffn_cores = sum_cores(*ffn_partial)
    d_qkv, d_table, rows_one = attention_backward(
        prob, mine_one, other_one, attn_got, qkv, place, heads, shard, buckets
    )
    qkv_product = functools.partial(column_product, shard, 0, 3 * width)
    ffn_moved = send_mp([after(rows, *mine_one[1:]) for rows in ffn_cores])
    table_sent = d_table[:, :heads].astype(LOW).reshape(sources, table_rows, heads)
    table_sent = jnp.pad(
        table_sent, ((0, 0), (0, EXTRA - table_rows), (0, 3 * width - heads))
    )
    d_qkv_w = contract_rows(normed_rows, d_qkv).astype(LOW).reshape(sources, shard, -1)
    d_qkv_sent = jnp.concatenate([d_qkv_w, table_sent], 1)
    inner_cores = sum_cores(
        *partial(after(d_qkv, d_qkv_sent, *ffn_moved), attn_got, qkv_product, "attention_in")
    )
    inner_pair = sum_mp(inner_cores)
    d_qkv_got = to_owners(after(d_qkv_sent, d_gate_up))
    d_out = contract_rows(after(attended, inner_cores[0]), rows_one)
    d_out = jnp.moveaxis(d_out.astype(LOW).reshape(width, sources, shard), 1, 0)
    d_rows_sent = jnp.concatenate([d_down_w, d_out], 1)

    (d_w_gate, d_w_up), ffn_gain, _ = owner_grads(
        after(d_gate_up, inner_cores[0]), (w_gate, w_up), ffn_scale.reshape(1, shard), members, None
    )
    ffn_sent, ffn_kept = split_near(
        sum((piece.astype(F32) for piece in ffn_moved), ffn_cores[0])
    )
    inner_sent, inner_kept = split_near(inner_pair)
    came = swap(
        after(jnp.stack([ffn_sent, inner_sent]), here(pair_valid), d_rows_sent, ffn_gain), "near"
    )
    came = after(came, d_qkv_got)
    own_inputs = here(pair_inputs)
    inv_one = rms(own_inputs)
    grad_input = here(grad_one) + norm_grad(inner_kept + came[1].astype(F32), own_inputs * inv_one, inv_one)
    own_out = jnp.where(here(pair_valid), here(after_attn) + ffn_kept + came[0].astype(F32), 0.0)
    owned = jnp.stack([own_out.astype(LOW), grad_input.astype(LOW)])
    rows_out = [jnp.zeros((mp_count, own_rows, model), LOW)] * 2
    blocks_out = [owned] + [shifted(owned, away) for away in range(1, mp_count)]
    d_rows = to_owners(after(d_rows_sent, d_qkv_got))
    for away, block in enumerate(blocks_out):
        rows_out = [
            lax.dynamic_update_index_in_dim(rows, block[i], mp_at ^ away, 0)
            for i, rows in enumerate(rows_out)
        ]
    layer_out, d_inputs = (rows.reshape(tok_rows, model) for rows in rows_out)

    (d_w_query, d_w_key, d_w_value), attn_gain, d_rel_table = owner_grads(
        after(d_qkv_got, blocks_out[1]),
        (w_query, w_key, w_value),
        attn_scale.reshape(1, shard),
        members,
        (table_rows, heads_mp),
    )
    gains = jnp.concatenate([attn_gain, ffn_gain], 0)
    d_w_down, d_w_out = owner_rows(d_rows, members, hidden_width)
    gains = sum((shifted(gains, away) for away in range(1, mp_count)), gains)
    return (
        layer_out,
        d_inputs,
        gains[0],
        d_w_query,
        d_w_key,
        d_w_value,
        d_w_out,
        d_rel_table,
        gains[1],
        d_w_gate,
        d_w_up,
        d_w_down,
    )


def solution(mesh):
    fsdp, mp = mesh.shape["fsdp"], mesh.shape["mp"]

    def run(*args):
        seqs = args[2].shape[0]
        members = fsdp // seqs
        inner = Mesh(
            mesh.devices.reshape(seqs, members // CORES, CORES, mp), ("seq", "near", "core", "mp")
        )
        rows, columns, first = P(COLUMN, None), P("mp", COLUMN), P(COLUMN)
        both = P(COLUMN, "mp")
        in_specs = (
            rows, rows, P(), first, both, both, both, columns, both, first, both, both, columns,
        )
        out_specs = (
            rows, rows, first, both, both, both, columns, both, first, both, both, columns,
        )
        return jax.shard_map(
            local, mesh=inner, in_specs=in_specs, out_specs=out_specs, check_vma=False
        )(*args)

    return run
```

```python
import functools

import jax
import jax.numpy as jnp
from jax import lax
from jax.experimental import pallas as pl
from jax.experimental.pallas import tpu as pltpu
from jax.sharding import Mesh, PartitionSpec as P

LOW = jnp.bfloat16
F32 = jnp.float32
CORES = 2
THRESHOLDS = (12, 16, 23, 32, 46, 64, 91)
EPSILON = 1e-06
MASKED = -1e30
SKEW = 128


def bucket_of(rel_offset):
    distance = jnp.abs(rel_offset)
    far_bucket = 8 + sum(((distance >= threshold).astype(jnp.int32) for threshold in THRESHOLDS))
    bucket_abs = jnp.where(distance < 8, distance, far_bucket)
    return bucket_abs + jnp.where(rel_offset > 0, 16, 0)


def bucket_onehot(buckets, seq_len):
    offset = lax.broadcasted_iota(jnp.int32, (buckets, 2 * seq_len), 1) - seq_len
    bucket = lax.broadcasted_iota(jnp.int32, (buckets, 2 * seq_len), 0)
    return bucket_of(offset) == bucket


def head_lanes(rows, width, head_width, head):
    lane = lax.broadcasted_iota(jnp.int32, (rows, width), 1)
    return (lane >= head * head_width) & (lane < (head + 1) * head_width)


def only(mask, values):
    return jnp.where(mask, values, jnp.zeros_like(values))


def block_place(block, core, near_count):
    return lax.rem(block, near_count) * CORES + lax.bitwise_xor(lax.div(block, near_count), core)


def bias_places(place_ref, step, blocks, rows, seq_len):
    core, near_count = place_ref[1], blocks // CORES
    query = block_place(step, core, near_count) * rows
    return [
        [
            pl.multiple_of(
                block_place(block, core, near_count) * rows - query - part * SKEW + seq_len - SKEW,
                SKEW,
            )
            for block in range(blocks)
        ]
        for part in range(rows // SKEW)
    ]


def forward_kernel(heads, shard, near_count, count, place_ref, *refs):
    own_ref, moved_ref, core_ref, core_moved_ref, got_ref, table_ref = refs[:6]
    qkv_ref, o_ref, p_ref = refs[6:9]
    other_refs, mine_refs = refs[9 : 9 + count], refs[9 + count : 9 + 2 * count]
    skew_ref, held_ref = refs[9 + 2 * count :]
    step = pl.program_id(0)
    seq_len = qkv_ref.shape[0]
    rows, width = o_ref.shape
    model = held_ref.shape[1]
    head_width = width // heads
    span = 2 * seq_len
    blocks = seq_len // rows
    block = row_block(step, near_count)

    @pl.when(step == 0)
    def _():
        weight = got_ref[:, :shard, : 3 * width].reshape(model, 3 * width)
        near = place_ref[4]
        for at, ref in enumerate((own_ref, moved_ref, core_ref, core_moved_ref)):
            first = (at // 2) * near_count + lax.bitwise_xor(near, at % 2)
            qkv_ref[pl.ds(pl.multiple_of(first * rows, rows), rows), :] = rows_dot(
                ref[...], weight
            ).astype(LOW)
        one_hot = bucket_onehot(table_ref.shape[0], seq_len)
        table = table_ref[...].astype(F32)
        column = lax.broadcasted_iota(jnp.int32, table.shape, 1)
        for head in range(heads):
            here = column == place_ref[2] * heads + head
            levels = jnp.sum(jnp.where(here, table, 0.0), axis=1, keepdims=True)
            line = jnp.sum(jnp.where(one_hot, levels, 0.0), axis=0, keepdims=True)
            line = jnp.broadcast_to(line, (SKEW, span))
            skew_ref[head] = pltpu.roll(line, span - SKEW, 1, stride=1, stride_axis=0)

    row = lax.broadcasted_iota(jnp.int32, (1, rows), 1)
    allowed = jnp.concatenate(
        [
            block_place(at, place_ref[1], near_count) * rows + row < place_ref[0]
            for at in range(blocks)
        ],
        1,
    )
    queries = qkv_ref[pl.ds(pl.multiple_of(block * rows, rows), rows), :width]
    keys = qkv_ref[:, width : 2 * width]
    values = qkv_ref[:, 2 * width :]
    total = jnp.zeros((rows, width), F32)
    places = bias_places(place_ref, block, blocks, rows, seq_len)
    for head in range(heads):
        scores = lax.dot_general(
            only(head_lanes(rows, width, head_width, head), queries),
            keys,
            (((1,), (1,)), ((), ())),
            preferred_element_type=F32,
        )
        bias = jnp.concatenate(
            [
                jnp.concatenate([skew_ref[head, :, pl.ds(place, rows)] for place in part], 1)
                for part in places
            ],
            0,
        )
        scores = jnp.where(allowed, scores + bias, MASKED)
        grown = jnp.exp(scores - jnp.max(scores, axis=1, keepdims=True))
        prob = (grown * (1.0 / jnp.sum(grown, axis=1, keepdims=True))).astype(LOW)
        p_ref[head] = prob
        total = total + jnp.dot(
            prob,
            only(head_lanes(seq_len, width, head_width, head), values),
            preferred_element_type=F32,
        )
    attended = total.astype(LOW)
    o_ref[...] = attended
    weight = got_ref[:, :shard, 3 * width :].reshape(model, width)
    held_ref[...] = contract_cols(attended, weight).astype(LOW)
    send_rows(step, near_count, place_ref[3], held_ref, other_refs, mine_refs)


def attention_forward(parts, got, table, place, heads, shard, count):
    rows, model = parts[0].shape
    blocks = len(parts)
    near_count = blocks // CORES
    seq_len, width = rows * blocks, got.shape[2] // 4
    out_specs, out_shape = sent_specs(near_count, count, rows // count, model)

    def fixed(shape):
        return pl.BlockSpec(shape, lambda i: (0,) * len(shape))

    outs = pl.pallas_call(
        functools.partial(forward_kernel, heads, shard, near_count, count),
        grid=(blocks,),
        in_specs=[pl.BlockSpec(memory_space=pltpu.SMEM)]
        + [fixed(part.shape) for part in parts]
        + [fixed(got.shape), fixed(table.shape)],
        out_specs=[
            fixed((seq_len, 3 * width)),
            pl.BlockSpec((rows, width), lambda i: (row_block(i, near_count), 0)),
            pl.BlockSpec((heads, rows, seq_len), lambda i: (0, row_block(i, near_count), 0)),
        ]
        + out_specs,
        out_shape=[
            jax.ShapeDtypeStruct((seq_len, 3 * width), LOW),
            jax.ShapeDtypeStruct((seq_len, width), LOW),
            jax.ShapeDtypeStruct((heads, seq_len, seq_len), LOW),
        ]
        + out_shape,
        scratch_shapes=[
            pltpu.VMEM((heads, SKEW, 2 * seq_len), F32),
            pltpu.VMEM((rows, model), LOW),
        ],
        compiler_params=pltpu.CompilerParams(vmem_limit_bytes=34 * 2**20),
        cost_estimate=pl.CostEstimate(flops=0, bytes_accessed=0, transcendentals=0),
        name="attention_forward",
    )(place, *parts, got, table)
    return (*outs[:3], outs[3 + count :], outs[3 : 3 + count])


def backward_kernel(heads, shard, near_count, count, place_ref, *refs):
    came, refs = refs[: 2 * count], refs[2 * count :]
    p_ref, got_ref, qkv_ref, o_ref, d_ref, dt_ref, do_ref = refs[:7]
    rows_ref, dk_sum, dv_sum, do_sum, skew_ref = refs[7:]
    step = pl.program_id(0)
    block = row_block(step, near_count)
    take_rows(step, near_count, place_ref[3], came[:count], came[count:], rows_ref)
    rows, model = rows_ref.shape
    seq_len = qkv_ref.shape[0]
    width = qkv_ref.shape[1] // 3
    head_width = width // heads
    span = 2 * seq_len
    blocks = seq_len // rows

    @pl.when(step == 0)
    def _():
        dk_sum[...] = jnp.zeros_like(dk_sum)
        dv_sum[...] = jnp.zeros_like(dv_sum)
        do_sum[...] = jnp.zeros_like(do_sum)
        skew_ref[...] = jnp.zeros_like(skew_ref)

    here = pl.ds(pl.multiple_of(block * rows, rows), rows)
    queries = qkv_ref[here, :width]
    keys = qkv_ref[:, width : 2 * width]
    values = qkv_ref[:, 2 * width :]
    weight = got_ref[:, :shard, 3 * width :].reshape(model, width)
    grads = rows_dot(rows_ref[...], weight).astype(LOW)
    do_sum[...] += contract_rows(o_ref[...], rows_ref[...])
    total = jnp.zeros((rows, width), F32)
    places = bias_places(place_ref, block, blocks, rows, seq_len)
    for head in range(heads):
        own = head_lanes(rows, width, head_width, head)
        own_grads = only(own, grads)
        d_prob = lax.dot_general(
            own_grads, values, (((1,), (1,)), ((), ())), preferred_element_type=F32
        )
        prob_low = p_ref[head]
        prob = prob_low.astype(F32)
        weighed = prob * d_prob
        d_scores = (weighed - prob * jnp.sum(weighed, axis=1, keepdims=True)).astype(LOW)
        total = total + jnp.dot(
            d_scores,
            only(head_lanes(seq_len, width, head_width, head), keys),
            preferred_element_type=F32,
        )
        dk_sum[...] += lax.dot_general(
            d_scores, only(own, queries), (((0,), (0,)), ((), ())), preferred_element_type=F32
        )
        dv_sum[...] += lax.dot_general(
            prob_low, own_grads, (((0,), (0,)), ((), ())), preferred_element_type=F32
        )
        for part in range(rows // SKEW):
            for at in range(blocks):
                skew_ref[head, :, pl.ds(places[part][at], rows)] += d_scores[
                    part * SKEW : (part + 1) * SKEW, at * rows : (at + 1) * rows
                ].astype(F32)
    d_ref[here, :width] = total.astype(LOW)

    @pl.when(step == pl.num_programs(0) - 1)
    def _():
        d_ref[:, width : 2 * width] = dk_sum[...].astype(LOW)
        d_ref[:, 2 * width :] = dv_sum[...].astype(LOW)
        for at in range(do_ref.shape[0]):
            do_ref[at] = do_sum[:, at * shard : (at + 1) * shard].astype(LOW)
        one_hot = bucket_onehot(dt_ref.shape[0], seq_len)
        row = lax.broadcasted_iota(jnp.int32, (SKEW, span), 0)
        column = lax.broadcasted_iota(jnp.int32, dt_ref.shape, 1)
        result = jnp.zeros(dt_ref.shape, F32)
        for head in range(heads):
            level = pltpu.roll(skew_ref[head], SKEW, 1)
            bit = 1
            while bit < SKEW:
                level = jnp.where((row & bit) != 0, pltpu.roll(level, span - bit, 1), level)
                bit *= 2
            line = jnp.sum(level, axis=0, keepdims=True)
            summed = jnp.sum(jnp.where(one_hot, line, 0.0), axis=1, keepdims=True)
            result = jnp.where(column == head, summed, result)
        dt_ref[...] = result


def attention_backward(prob, mine, other, got, qkv, attended, place, heads, shard, buckets):
    seq_len, width = qkv.shape[0], qkv.shape[1] // 3
    near_count, own_rows, model = mine[0].shape
    count = len(mine)
    rows = count * own_rows
    came_specs, _ = sent_specs(near_count, count, own_rows, model)
    return pl.pallas_call(
        functools.partial(backward_kernel, heads, shard, near_count, count),
        grid=(seq_len // rows,),
        in_specs=[
            pl.BlockSpec(memory_space=pltpu.SMEM),
            *came_specs,
            pl.BlockSpec((heads, rows, seq_len), lambda i: (0, row_block(i, near_count), 0)),
            pl.BlockSpec(got.shape, lambda i: (0, 0, 0)),
            pl.BlockSpec(qkv.shape, lambda i: (0, 0)),
            pl.BlockSpec((rows, width), lambda i: (row_block(i, near_count), 0)),
        ],
        out_specs=[
            pl.BlockSpec(qkv.shape, lambda i: (0, 0)),
            pl.BlockSpec((buckets, 128), lambda i: (0, 0)),
            pl.BlockSpec((model // shard, width, shard), lambda i: (0, 0, 0)),
        ],
        out_shape=[
            jax.ShapeDtypeStruct(qkv.shape, LOW),
            jax.ShapeDtypeStruct((buckets, 128), F32),
            jax.ShapeDtypeStruct((model // shard, width, shard), LOW),
        ],
        scratch_shapes=[
            pltpu.VMEM((rows, model), LOW),
            pltpu.VMEM((seq_len, width), F32),
            pltpu.VMEM((seq_len, width), F32),
            pltpu.VMEM((width, model), F32),
            pltpu.VMEM((heads, SKEW, 2 * seq_len), F32),
        ],
        compiler_params=pltpu.CompilerParams(vmem_limit_bytes=34 * 2**20),
        cost_estimate=pl.CostEstimate(flops=0, bytes_accessed=0, transcendentals=0),
        name="attention_backward",
    )(place, *other, *mine, prob, got, qkv, attended)


EXTRA = 8
OWNER_ROWS = 64


def as_column(row, first, count):
    size = row.shape[1]
    here = lax.broadcasted_iota(jnp.int32, (count, size), 1) == first + lax.broadcasted_iota(
        jnp.int32, (count, size), 0
    )
    return jnp.sum(jnp.where(here, row, 0.0), axis=1, keepdims=True)


def blocks_kernel(seqs, members, q_ref, k_ref, v_ref, o_ref, gain_ref, table_ref, sent_ref):
    shard = q_ref.shape[0]
    width = q_ref.shape[1] // members
    gain = as_column(gain_ref[...].astype(LOW).astype(F32), 0, shard)
    parts = [
        (ref[...].astype(LOW).astype(F32) * gain).astype(LOW) for ref in (q_ref, k_ref, v_ref)
    ]
    parts.append(o_ref[...].T.astype(LOW))
    rest = jnp.zeros((EXTRA, sent_ref.shape[2]), LOW)
    table_rows, heads = table_ref.shape
    for seq in range(seqs):
        for member in range(members):
            at = seq * members + member
            for i, part in enumerate(parts):
                sent_ref[at, :shard, i * width : (i + 1) * width] = part[
                    :, member * width : (member + 1) * width
                ]
            sent_ref[at, shard:, :] = rest
            sent_ref[at, shard : shard + table_rows, :heads] = table_ref[...].astype(LOW)


def attention_blocks(weights, w_out, gain, table, seqs, members):
    shard, columns = weights[0].shape
    return pl.pallas_call(
        functools.partial(blocks_kernel, seqs, members),
        out_shape=jax.ShapeDtypeStruct(
            (seqs * members, shard + EXTRA, 4 * columns // members), LOW
        ),
        compiler_params=pltpu.CompilerParams(vmem_limit_bytes=60 * 2**20),
        cost_estimate=pl.CostEstimate(
            flops=0, bytes_accessed=16 * shard * columns, transcendentals=0
        ),
        name="attention_blocks",
    )(*weights, w_out, gain, table)


def owner_kernel(count, members, table_shape, *refs):
    got_ref, extra_ref = refs[:2]
    weight_refs = refs[2 : 2 + count]
    gain_ref = refs[2 + count]
    grad_refs = refs[3 + count : 3 + 2 * count]
    sum_ref = refs[3 + 2 * count]
    step = pl.program_id(0)
    rows = got_ref.shape[1]
    seqs = got_ref.shape[0] // members
    width = got_ref.shape[2] // count
    size = sum_ref.shape[1]
    gain = as_column(gain_ref[...].astype(LOW).astype(F32), step * rows, rows)
    total = jnp.zeros((rows, 1), F32)
    for member in range(members):
        product = sum(got_ref[seq * members + member].astype(F32) for seq in range(seqs))
        for i in range(count):
            part = product[:, i * width : (i + 1) * width]
            here = pl.ds(member * width, width)
            grad_refs[i][:, here] = part * gain
            weight = weight_refs[i][:, here].astype(LOW).astype(F32)
            total = total + jnp.sum(weight * part, axis=1, keepdims=True)

    @pl.when(step == 0)
    def _():
        sum_ref[...] = jnp.zeros_like(sum_ref)

    diagonal = lax.broadcasted_iota(jnp.int32, (rows, size), 1) == step * rows + (
        lax.broadcasted_iota(jnp.int32, (rows, size), 0)
    )
    sum_ref[...] += jnp.sum(jnp.where(diagonal, total, 0.0), axis=0, keepdims=True)
    if table_shape is not None:
        table_rows, heads = table_shape
        each = heads // members
        for member in range(members):
            piece = sum(extra_ref[seq * members + member].astype(F32) for seq in range(seqs))
            refs[-1][:, member * each : (member + 1) * each] = piece[:table_rows, :each]


def owner_grads(got, weights, gain, members, table_shape):
    sources, height, columns = got.shape
    shard, wide = weights[0].shape
    count = len(weights)
    rows = min(OWNER_ROWS, shard)
    step_rows = pl.BlockSpec((rows, wide), lambda i: (i, 0))
    row = pl.BlockSpec((1, shard), lambda i: (0, 0))
    last = height // EXTRA - 1
    out_specs = [step_rows] * count + [row]
    out_shape = [jax.ShapeDtypeStruct((shard, wide), F32)] * count
    out_shape.append(jax.ShapeDtypeStruct((1, shard), F32))
    if table_shape is not None:
        out_specs.append(pl.BlockSpec(table_shape, lambda i: (0, 0)))
        out_shape.append(jax.ShapeDtypeStruct(table_shape, F32))
    outs = pl.pallas_call(
        functools.partial(owner_kernel, count, members, table_shape),
        grid=(shard // rows,),
        in_specs=[
            pl.BlockSpec((sources, rows, columns), lambda i: (0, i, 0)),
            pl.BlockSpec((sources, EXTRA, columns), lambda i: (0, last, 0)),
        ]
        + [step_rows] * count
        + [row],
        out_specs=out_specs,
        out_shape=out_shape,
        compiler_params=pltpu.CompilerParams(vmem_limit_bytes=32 * 2**20),
        cost_estimate=pl.CostEstimate(
            flops=0, bytes_accessed=10 * count * shard * wide, transcendentals=0
        ),
        name="owner_grads",
    )(got, got, *weights, gain)
    return outs[:count], outs[count], outs[-1] if table_shape is not None else None


def rows_kernel(members, split, got_ref, first_ref, second_ref):
    seqs = got_ref.shape[0] // members
    rest = got_ref.shape[1] - split
    for member in range(members):
        total = sum(got_ref[seq * members + member].astype(F32) for seq in range(seqs))
        first_ref[pl.ds(member * split, split), :] = total[:split]
        second_ref[pl.ds(member * rest, rest), :] = total[split:]


def owner_rows(got, members, split):
    height, columns = got.shape[1:]
    return pl.pallas_call(
        functools.partial(rows_kernel, members, split),
        out_shape=[
            jax.ShapeDtypeStruct((members * split, columns), F32),
            jax.ShapeDtypeStruct((members * (height - split), columns), F32),
        ],
        compiler_params=pltpu.CompilerParams(vmem_limit_bytes=32 * 2**20),
        cost_estimate=pl.CostEstimate(
            flops=0, bytes_accessed=4 * got.size, transcendentals=0
        ),
        name="owner_rows",
    )(got)


def rows_dot(left, right):
    return jnp.dot(left, right, preferred_element_type=F32)


def contract_cols(left, right):
    return lax.dot_general(left, right, (((1,), (1,)), ((), ())), preferred_element_type=F32)


def contract_rows(left, right):
    return lax.dot_general(left, right, (((0,), (0,)), ((), ())), preferred_element_type=F32)

def row_block(step, near_count):
    return lax.rem(step + near_count, CORES * near_count)


def send_rows(step, near_count, mp_at, held_ref, other_refs, mine_refs):
    count = len(other_refs)
    own_rows = held_ref.shape[0] // count

    def write(refs):
        for away, ref in enumerate(refs):
            first = pl.multiple_of(lax.bitwise_xor(mp_at, away) * own_rows, own_rows)
            ref[0] = held_ref[pl.ds(first, own_rows), :]

    @pl.when(step < near_count)
    def _():
        write(other_refs)

    @pl.when(step >= near_count)
    def _():
        write(mine_refs)


def place_kernel(place_ref, *refs):
    parts, outs = refs[:-2], refs[-2:]
    each = len(parts) // 2
    for at in range(each):

        @pl.when(pl.program_id(0) == at)
        def _():
            for i, out_ref in enumerate(outs):
                out_ref[...] = parts[i * each + at][...]


def place_rows(first, second, place, near_count):
    rows, model = first[0].shape
    shape = jax.ShapeDtypeStruct((rows * len(first), model), LOW)

    def place_of(i, place_ref):
        return (i // 2) * near_count + lax.bitwise_xor(place_ref[4], lax.rem(i, 2)), 0

    part = pl.BlockSpec((rows, model), lambda i, place_ref: (0, 0))
    return pl.pallas_call(
        place_kernel,
        grid_spec=pltpu.PrefetchScalarGridSpec(
            num_scalar_prefetch=1,
            grid=(len(first),),
            in_specs=[part] * (2 * len(first)),
            out_specs=[pl.BlockSpec((rows, model), place_of)] * 2,
        ),
        out_shape=[shape] * 2,
        compiler_params=pltpu.CompilerParams(vmem_limit_bytes=32 * 2**20),
        cost_estimate=pl.CostEstimate(flops=0, bytes_accessed=0, transcendentals=0),
        name="place_rows",
    )(place, *first, *second)


def take_rows(step, near_count, mp_at, other_refs, mine_refs, rows_ref):
    own_rows = other_refs[0].shape[1]

    def read(refs):
        for away, ref in enumerate(refs):
            first = pl.multiple_of(lax.bitwise_xor(mp_at, away) * own_rows, own_rows)
            rows_ref[pl.ds(first, own_rows), :] = ref[0]

    @pl.when(step < near_count)
    def _():
        read(other_refs)

    @pl.when(step >= near_count)
    def _():
        read(mine_refs)


def sent_specs(near_count, count, own_rows, model):
    other = pl.BlockSpec((1, own_rows, model), lambda i: (jnp.minimum(i, near_count - 1), 0, 0))
    mine = pl.BlockSpec((1, own_rows, model), lambda i: (jnp.maximum(i - near_count, 0), 0, 0))
    shape = jax.ShapeDtypeStruct((near_count, own_rows, model), LOW)
    return [other] * count + [mine] * count, [shape] * (2 * count)


def partial_kernel(near_count, count, product, place_ref, left_ref, weight_ref, *refs):
    held_ref = refs[-1]
    product(left_ref, weight_ref, held_ref)
    send_rows(
        pl.program_id(0), near_count, place_ref[3], held_ref, refs[:count], refs[count : 2 * count]
    )


def partial_rows(left, weight, model, place, near_count, count, product, name):
    seq_len, depth = left.shape
    rows = seq_len // (CORES * near_count)
    out_specs, out_shape = sent_specs(near_count, count, rows // count, model)
    outs = pl.pallas_call(
        functools.partial(partial_kernel, near_count, count, product),
        grid=(CORES * near_count,),
        in_specs=[
            pl.BlockSpec(memory_space=pltpu.SMEM),
            pl.BlockSpec((rows, depth), lambda i: (row_block(i, near_count), 0)),
            pl.BlockSpec(weight.shape, lambda i: (0, 0, 0)),
        ],
        out_specs=out_specs,
        out_shape=out_shape,
        scratch_shapes=[pltpu.VMEM((rows, model), LOW)],
        compiler_params=pltpu.CompilerParams(vmem_limit_bytes=40 * 2**20),
        cost_estimate=pl.CostEstimate(
            flops=0, bytes_accessed=0, transcendentals=0
        ),
        name=name,
    )(place, left, weight)
    return outs[count:], outs[:count]


def column_product(shard, first, last, left_ref, weight_ref, held_ref):
    weight = weight_ref[:, :shard, first:last]
    weight = weight.reshape(weight.shape[0] * shard, last - first)
    held_ref[...] = contract_cols(left_ref[...], weight).astype(LOW)


def row_product(height, left_ref, weight_ref, held_ref):
    left = left_ref[...]
    width = weight_ref.shape[2]
    for at in range(weight_ref.shape[0]):
        held_ref[:, at * width : (at + 1) * width] = rows_dot(
            left, weight_ref[at, :height, :]
        ).astype(LOW)


def ffn_blocks_kernel(seqs, members, gate_ref, up_ref, down_ref, gain_ref, first_ref, second_ref):
    shard = gate_ref.shape[0]
    width = gate_ref.shape[1] // members
    gain = as_column(gain_ref[...].astype(LOW).astype(F32), 0, shard)
    for member in range(members):
        here = slice(member * width, (member + 1) * width)
        parts = [
            (ref[:, here].astype(LOW).astype(F32) * gain).astype(LOW) for ref in (gate_ref, up_ref)
        ]
        both = jnp.concatenate(parts, 1)
        down = down_ref[here, :].astype(LOW)
        for seq in range(seqs):
            at = seq * members + member
            first_ref[at, :width, :] = down
            first_ref[at, width:, :] = both[:, :shard]
            second_ref[at] = both[:, shard:]


def ffn_blocks(w_gate, w_up, w_down, gain, seqs, members):
    shard, columns = w_gate.shape
    width = columns // members
    return pl.pallas_call(
        functools.partial(ffn_blocks_kernel, seqs, members),
        out_shape=[
            jax.ShapeDtypeStruct((seqs * members, width + shard, shard), LOW),
            jax.ShapeDtypeStruct((seqs * members, shard, 2 * width - shard), LOW),
        ],
        compiler_params=pltpu.CompilerParams(vmem_limit_bytes=40 * 2**20),
        cost_estimate=pl.CostEstimate(
            flops=0, bytes_accessed=18 * shard * columns, transcendentals=0
        ),
        name="ffn_blocks",
    )(w_gate, w_up, w_down, gain)


def ffn_kernel(near_count, count, place_ref, *refs):
    came, refs = refs[: 2 * count], refs[2 * count :]
    grad_ref, first_ref, second_ref = refs[:3]
    other_refs, mine_refs = refs[3 : 3 + count], refs[3 + count : 3 + 2 * count]
    rows_ref, act_ref, d_ref, down_ref, held_ref, sum_ref = refs[3 + 2 * count :]
    step = pl.program_id(0)
    take_rows(step, near_count, place_ref[3], came[:count], came[count:], rows_ref)
    sources, height, shard = first_ref.shape
    width = height - shard
    rows = rows_ref[...]
    block = row_block(step, near_count)
    first = block_place(block, place_ref[1], near_count) * rows.shape[0]
    valid = first + lax.broadcasted_iota(jnp.int32, (rows.shape[0], 1), 0) < place_ref[0]
    grads = only(valid, grad_ref[...])
    early = first_ref[:, width:, :].reshape(sources * shard, shard)
    late = second_ref[...].reshape(sources * shard, 2 * width - shard)
    both = jnp.concatenate([rows_dot(rows, early), rows_dot(rows, late)], 1)
    gate, up = both[:, :width], both[:, width:]
    scale, cubic = 0.7978845608028654, 0.044715
    square = gate * gate
    bent = jnp.tanh(scale * (gate + cubic * square * gate))
    half = 0.5 * (1.0 + bent)
    value = gate * half
    slope = half + 0.5 * gate * (1.0 - bent * bent) * (scale * (1.0 + 3.0 * cubic * square))
    act = (value * up).astype(LOW)
    act_ref[...] = act
    d_hidden = jnp.zeros((rows.shape[0], width), F32)
    for at in range(sources):
        d_hidden = d_hidden + contract_cols(
            grads[:, at * shard : (at + 1) * shard], first_ref[at, :width, :]
        )
    d_both = jnp.concatenate(
        [(d_hidden * up * slope).astype(LOW), (d_hidden * value).astype(LOW)], 1
    )
    d_ref[...] = d_both
    held_ref[...] = (
        contract_cols(d_both[:, :shard], early) + contract_cols(d_both[:, shard:], late)
    ).astype(LOW)
    send_rows(step, near_count, place_ref[3], held_ref, other_refs, mine_refs)
    product = contract_rows(act, grads)

    @pl.when(step == 0)
    def _():
        sum_ref[...] = product

    @pl.when(step > 0)
    def _():
        sum_ref[...] += product

    @pl.when(step == pl.num_programs(0) - 1)
    def _():
        for at in range(sources):
            down_ref[at] = sum_ref[:, at * shard : (at + 1) * shard].astype(LOW)


def feed_forward(mine, other, grads, first, second, place):
    seq_len, model = grads.shape
    near_count, count = mine[0].shape[0], len(mine)
    sources, height, shard = first.shape
    width = height - shard
    rows = seq_len // (CORES * near_count)
    out_specs, out_shape = sent_specs(near_count, count, rows // count, model)

    def blocks(columns):
        return pl.BlockSpec((rows, columns), lambda i: (row_block(i, near_count), 0))

    outs = pl.pallas_call(
        functools.partial(ffn_kernel, near_count, count),
        grid=(CORES * near_count,),
        in_specs=[
            pl.BlockSpec(memory_space=pltpu.SMEM),
            *out_specs,
            blocks(model),
            pl.BlockSpec(first.shape, lambda i: (0, 0, 0)),
            pl.BlockSpec(second.shape, lambda i: (0, 0, 0)),
        ],
        out_specs=out_specs
        + [
            blocks(model),
            blocks(width),
            blocks(2 * width),
            pl.BlockSpec((sources, width, shard), lambda i: (0, 0, 0)),
        ],
        out_shape=out_shape
        + [
            jax.ShapeDtypeStruct((seq_len, model), LOW),
            jax.ShapeDtypeStruct((seq_len, width), LOW),
            jax.ShapeDtypeStruct((seq_len, 2 * width), LOW),
            jax.ShapeDtypeStruct((sources, width, shard), LOW),
        ],
        scratch_shapes=[pltpu.VMEM((rows, model), LOW), pltpu.VMEM((width, model), F32)],
        compiler_params=pltpu.CompilerParams(vmem_limit_bytes=56 * 2**20),
        cost_estimate=pl.CostEstimate(
            flops=12 * seq_len * model * width, bytes_accessed=12 * seq_len * model, transcendentals=0
        ),
        name="feed_forward",
    )(place, *other, *mine, grads, first, second)
    return outs[count : 2 * count], outs[:count], *outs[2 * count :]


COLUMN = ("seq", "near", "core")


def exchange(blocks, axes):
    return lax.all_to_all(blocks, axes, split_axis=0, concat_axis=0, tiled=True)


def swap(block, axis):
    return lax.ppermute(block, axis, [(0, 1), (1, 0)])


def after(value, *done):
    return lax.optimization_barrier((value,) + done)[0]


def rms(values):
    return lax.rsqrt(jnp.mean(values * values, axis=-1, keepdims=True) + EPSILON)


def norm_grad(inner, normed, inverse):
    return inverse * (inner - normed * jnp.mean(inner * normed, axis=-1, keepdims=True))


def local(
    inputs,
    cotangent,
    lengths,
    attn_scale,
    w_query,
    w_key,
    w_value,
    w_out,
    rel_table,
    ffn_scale,
    w_gate,
    w_up,
    w_down,
):
    seqs = lax.axis_size("seq")
    near_count = lax.axis_size("near")
    mp_count = lax.axis_size("mp")
    members = near_count * CORES
    sources = seqs * members
    tok_rows, model = inputs.shape
    seq_len = tok_rows * members
    own_rows = tok_rows // mp_count
    half_rows = seq_len // CORES
    shard = attn_scale.shape[0]
    table_rows, heads_mp = rel_table.shape
    buckets = table_rows * sources
    heads = heads_mp // members
    width = w_query.shape[1] // members
    hidden_width = w_gate.shape[1] // members

    near_at = lax.axis_index("near")
    core_at = lax.axis_index("core")
    mp_at = lax.axis_index("mp")
    member_at = near_at * CORES + core_at
    length = lax.dynamic_slice_in_dim(lengths, lax.axis_index("seq"), 1, 0)
    place = jnp.stack(
        [length[0]] + [at.astype(jnp.int32) for at in (core_at, member_at, mp_at, near_at)]
    )

    def over_mp(own, axis):
        shape = own.shape[:axis] + (mp_count,) + own.shape[axis:]
        blocks = lax.dynamic_update_index_in_dim(jnp.zeros(shape, own.dtype), own, mp_at, axis)
        moved = [(away, shifted(own, away)) for away in reversed(range(1, mp_count))]
        for away, block in moved:
            blocks = lax.dynamic_update_index_in_dim(blocks, block, mp_at ^ away, axis)
        return blocks

    def shifted(block, away):
        return lax.ppermute(block, "mp", [(i, i ^ away) for i in range(mp_count)])

    def in_near_order(own, moved):
        return jnp.stack(
            [jnp.where(near_at == 0, own, moved), jnp.where(near_at == 0, moved, own)], 0
        )

    def near_rows(blocks, meanwhile):
        own = [lax.dynamic_slice_in_dim(block, mp_at * own_rows, own_rows, 0) for block in blocks]
        near = swap(jnp.stack(own), "near")
        came = [(0, near)] + [(away, shifted(near, away)) for away in range(1, mp_count)]
        made = meanwhile(came[1][1])
        came = came[:2] + [(away, after(block, *made)) for away, block in came[2:]]
        halves = []
        for half in (came, [(away, swap(block, "core")) for away, block in came]):
            rows = jnp.zeros((len(blocks), mp_count, own_rows, model), near.dtype)
            for away, block in half:
                rows = lax.dynamic_update_index_in_dim(rows, block, mp_at ^ away, 1)
            halves.append([rows[i].reshape(tok_rows, model) for i in range(len(blocks))])
        return *halves, made

    def gather_rows(near):
        mine = [near] + [shifted(near, away) for away in range(1, mp_count)]
        return mine, [swap(block, "core") for block in mine]

    def sum_cores(mine, other):
        return [
            kept.astype(F32) + swap(sent, "core").astype(F32) for kept, sent in zip(mine, other)
        ]

    def send_mp(sums):
        return [shifted(sums[away].astype(LOW), away) for away in reversed(range(1, mp_count))]

    def sum_mp(sums, *meanwhile):
        moved = send_mp(sums)
        if meanwhile:
            moved = [after(piece, *meanwhile) for piece in moved]
        return sum((piece.astype(F32) for piece in moved), sums[0])

    def split_near(pair):
        sent = jnp.where(near_at == 0, pair[1], pair[0]).astype(LOW)
        return sent, jnp.where(near_at == 0, pair[0], pair[1])

    def sum_near_both(pair):
        low = pair.astype(LOW)
        moved = swap(low, "near")
        return low.astype(F32) + moved.astype(F32), moved

    def near_pair(own, moved):
        pair = [
            lax.dynamic_slice_in_dim(block, mp_at * own_rows, own_rows, 0)
            for block in (own, moved)
        ]
        return in_near_order(*pair)

    def here(pair):
        return lax.dynamic_index_in_dim(pair, near_at, 0, keepdims=False)

    attn_sent = attention_blocks(
        (w_query, w_key, w_value), w_out, attn_scale.reshape(1, shard), rel_table, seqs, members
    )
    attn_got = exchange(attn_sent, COLUMN)
    def partial(left, weight, product, name):
        return partial_rows(left, weight, model, place, near_count, mp_count, product, name)

    table = attn_got[:, shard : shard + table_rows, :heads_mp].reshape(buckets, heads_mp)

    def normed(rows):
        values = rows.astype(F32)
        return (values * rms(values)).astype(LOW)

    def make_blocks(first_came):
        return ffn_blocks(
            w_gate, w_up, w_down, after(ffn_scale.reshape(1, shard), first_came), seqs, members
        )

    (moved_inputs, moved_cotangent), core_moved, (ffn_first, ffn_second) = near_rows(
        [inputs, cotangent], make_blocks
    )
    input_parts = [inputs, moved_inputs, swap(inputs, "core"), core_moved[0]]
    core_cotangent = swap(after(cotangent, moved_inputs), "core")
    grad_parts = [cotangent, moved_cotangent, core_cotangent, core_moved[1]]
    parts = [normed(part) for part in input_parts]
    parts = lax.optimization_barrier((*parts, ffn_first, ffn_second))[:4]
    first_got = exchange(after(ffn_first, attn_got), COLUMN)

    qkv, attended, prob, out_mine, out_other = attention_forward(
        parts, attn_got, table, place, heads, shard, mp_count
    )
    normed_rows, grad_two = place_rows(parts, grad_parts, after(place, attended), near_count)
    mixed, mixed_moved = sum_near_both(
        after(sum_mp(sum_cores(out_mine, out_other), grad_two, normed_rows), first_got)
    )
    second_got = exchange(after(ffn_second, mixed_moved), COLUMN)

    pair_inputs = near_pair(inputs, moved_inputs).astype(F32)
    after_attn = pair_inputs + mixed
    inv_two = rms(after_attn)
    normed_two = after_attn * inv_two
    mine_two, other_two = gather_rows(normed_two.astype(LOW))

    d_mine, d_other, hidden_two, acts, d_both, d_down_w = feed_forward(
        mine_two, other_two, grad_two, first_got, second_got, place
    )
    inner_cores = sum_cores(d_mine, d_other)
    down_product = functools.partial(row_product, hidden_width)
    ffn_partial = partial(after(acts, *inner_cores), first_got, down_product, "ffn_out")

    def to_owners(grad):
        return exchange(grad, COLUMN)

    d_gate_up_w = contract_rows(hidden_two, after(d_both, *inner_cores)).astype(LOW)
    inner_two, inner_moved = sum_near_both(
        sum_mp(inner_cores, d_gate_up_w, *ffn_partial[0], *ffn_partial[1])
    )

    pair_first = (
        lax.broadcasted_iota(jnp.int32, (near_count, own_rows, 1), 0) * (CORES * tok_rows)
        + lax.broadcasted_iota(jnp.int32, (near_count, own_rows, 1), 1)
        + (core_at * tok_rows + mp_at * own_rows)
    )
    pair_valid = pair_first < length
    pair_grad = near_pair(cotangent, moved_cotangent).astype(F32)
    grad_one = jnp.where(pair_valid, pair_grad, 0.0) + norm_grad(inner_two, normed_two, inv_two)
    grad_one_low = grad_one.astype(LOW)
    mine_one, other_one = gather_rows(grad_one_low)
    d_gate_up = to_owners(
        after(d_gate_up_w, inner_moved, grad_one_low).reshape(sources, shard, -1)
    )
    ffn_cores = sum_cores(*ffn_partial)
    d_qkv, d_table, d_out = attention_backward(
        prob, mine_one, other_one, attn_got, qkv, attended, place, heads, shard, buckets
    )
    qkv_product = functools.partial(column_product, shard, 0, 3 * width)
    ffn_moved = send_mp([after(rows, *mine_one[1:]) for rows in ffn_cores])
    table_sent = d_table[:, :heads].astype(LOW).reshape(sources, table_rows, heads)
    table_sent = jnp.pad(
        table_sent, ((0, 0), (0, EXTRA - table_rows), (0, 3 * width - heads))
    )
    d_qkv_w = contract_rows(normed_rows, d_qkv).astype(LOW).reshape(sources, shard, -1)
    d_qkv_sent = jnp.concatenate([d_qkv_w, table_sent], 1)
    inner_cores = sum_cores(
        *partial(after(d_qkv, d_qkv_sent, *ffn_moved), attn_got, qkv_product, "attention_in")
    )
    inner_pair = sum_mp(inner_cores)
    d_qkv_got = to_owners(after(d_qkv_sent, d_gate_up))
    d_rows_sent = jnp.concatenate([d_down_w, after(d_out, inner_cores[0])], 1)

    ffn_sent, ffn_kept = split_near(
        sum((piece.astype(F32) for piece in ffn_moved), ffn_cores[0])
    )
    inner_sent, inner_kept = split_near(inner_pair)
    came = swap(
        after(jnp.stack([ffn_sent, inner_sent]), here(pair_valid), d_rows_sent), "near"
    )
    came = after(came, d_qkv_got)
    own_inputs = here(pair_inputs)
    inv_one = rms(own_inputs)
    grad_input = here(grad_one) + norm_grad(inner_kept + came[1].astype(F32), own_inputs * inv_one, inv_one)
    own_out = jnp.where(here(pair_valid), here(after_attn) + ffn_kept + came[0].astype(F32), 0.0)
    owned = jnp.stack([own_out.astype(LOW), grad_input.astype(LOW)])
    rows_out = [jnp.zeros((mp_count, own_rows, model), LOW)] * 2
    blocks_out = [owned] + [shifted(owned, away) for away in range(1, mp_count)]
    d_rows = to_owners(after(d_rows_sent, d_qkv_got))
    for away, block in enumerate(blocks_out):
        rows_out = [
            lax.dynamic_update_index_in_dim(rows, block[i], mp_at ^ away, 0)
            for i, rows in enumerate(rows_out)
        ]
    layer_out, d_inputs = (rows.reshape(tok_rows, model) for rows in rows_out)

    (d_w_gate, d_w_up), ffn_gain, _ = owner_grads(
        after(d_gate_up, blocks_out[1]), (w_gate, w_up), ffn_scale.reshape(1, shard), members, None
    )
    (d_w_query, d_w_key, d_w_value), attn_gain, d_rel_table = owner_grads(
        after(d_qkv_got, blocks_out[1]),
        (w_query, w_key, w_value),
        attn_scale.reshape(1, shard),
        members,
        (table_rows, heads_mp),
    )
    gains = jnp.concatenate([attn_gain, ffn_gain], 0)
    d_w_down, d_w_out = owner_rows(d_rows, members, hidden_width)
    gains = sum((shifted(gains, away) for away in range(1, mp_count)), gains)
    return (
        layer_out,
        d_inputs,
        gains[0],
        d_w_query,
        d_w_key,
        d_w_value,
        d_w_out,
        d_rel_table,
        gains[1],
        d_w_gate,
        d_w_up,
        d_w_down,
    )


def solution(mesh):
    fsdp, mp = mesh.shape["fsdp"], mesh.shape["mp"]

    def run(*args):
        seqs = args[2].shape[0]
        members = fsdp // seqs
        inner = Mesh(
            mesh.devices.reshape(seqs, members // CORES, CORES, mp), ("seq", "near", "core", "mp")
        )
        rows, columns, first = P(COLUMN, None), P("mp", COLUMN), P(COLUMN)
        both = P(COLUMN, "mp")
        in_specs = (
            rows, rows, P(), first, both, both, both, columns, both, first, both, both, columns,
        )
        out_specs = (
            rows, rows, first, both, both, both, columns, both, first, both, both, columns,
        )
        return jax.shard_map(
            local, mesh=inner, in_specs=in_specs, out_specs=out_specs, check_vma=False
        )(*args)

    return run
```

```python
import functools

import jax
import jax.numpy as jnp
from jax import lax
from jax.experimental import pallas as pl
from jax.experimental.pallas import tpu as pltpu
from jax.sharding import Mesh, PartitionSpec as P

LOW = jnp.bfloat16
F32 = jnp.float32
CORES = 2
THRESHOLDS = (12, 16, 23, 32, 46, 64, 91)
EPSILON = 1e-06
MASKED = -1e30
SKEW = 128


def bucket_of(rel_offset):
    distance = jnp.abs(rel_offset)
    far_bucket = 8 + sum(((distance >= threshold).astype(jnp.int32) for threshold in THRESHOLDS))
    bucket_abs = jnp.where(distance < 8, distance, far_bucket)
    return bucket_abs + jnp.where(rel_offset > 0, 16, 0)


def bucket_onehot(buckets, seq_len):
    offset = lax.broadcasted_iota(jnp.int32, (buckets, 2 * seq_len), 1) - seq_len
    bucket = lax.broadcasted_iota(jnp.int32, (buckets, 2 * seq_len), 0)
    return bucket_of(offset) == bucket


def head_lanes(rows, width, head_width, head):
    lane = lax.broadcasted_iota(jnp.int32, (rows, width), 1)
    return (lane >= head * head_width) & (lane < (head + 1) * head_width)


def only(mask, values):
    return jnp.where(mask, values, jnp.zeros_like(values))


def block_place(block, core, near_count):
    return lax.rem(block, near_count) * CORES + lax.bitwise_xor(lax.div(block, near_count), core)


def bias_places(place_ref, step, blocks, rows, seq_len):
    core, near_count = place_ref[1], blocks // CORES
    query = block_place(step, core, near_count) * rows
    return [
        [
            pl.multiple_of(
                block_place(block, core, near_count) * rows - query - part * SKEW + seq_len - SKEW,
                SKEW,
            )
            for block in range(blocks)
        ]
        for part in range(rows // SKEW)
    ]


def forward_kernel(heads, shard, near_count, count, place_ref, *refs):
    own_ref, moved_ref, core_ref, core_moved_ref, got_ref, table_ref = refs[:6]
    qkv_ref, o_ref, p_ref = refs[6:9]
    other_refs, mine_refs = refs[9 : 9 + count], refs[9 + count : 9 + 2 * count]
    skew_ref, held_ref = refs[9 + 2 * count :]
    step = pl.program_id(0)
    seq_len = qkv_ref.shape[0]
    rows, width = o_ref.shape
    model = held_ref.shape[1]
    head_width = width // heads
    span = 2 * seq_len
    blocks = seq_len // rows
    block = row_block(step, near_count)

    @pl.when(step == 0)
    def _():
        weight = got_ref[:, :shard, : 3 * width].reshape(model, 3 * width)
        near = place_ref[4]
        for at, ref in enumerate((own_ref, moved_ref, core_ref, core_moved_ref)):
            first = (at // 2) * near_count + lax.bitwise_xor(near, at % 2)
            qkv_ref[pl.ds(pl.multiple_of(first * rows, rows), rows), :] = rows_dot(
                ref[...], weight
            ).astype(LOW)
        one_hot = bucket_onehot(table_ref.shape[0], seq_len)
        table = table_ref[...].astype(F32)
        column = lax.broadcasted_iota(jnp.int32, table.shape, 1)
        for head in range(heads):
            here = column == place_ref[2] * heads + head
            levels = jnp.sum(jnp.where(here, table, 0.0), axis=1, keepdims=True)
            line = jnp.sum(jnp.where(one_hot, levels, 0.0), axis=0, keepdims=True)
            line = jnp.broadcast_to(line, (SKEW, span))
            skew_ref[head] = pltpu.roll(line, span - SKEW, 1, stride=1, stride_axis=0)

    row = lax.broadcasted_iota(jnp.int32, (1, rows), 1)
    allowed = jnp.concatenate(
        [
            block_place(at, place_ref[1], near_count) * rows + row < place_ref[0]
            for at in range(blocks)
        ],
        1,
    )
    queries = qkv_ref[pl.ds(pl.multiple_of(block * rows, rows), rows), :width]
    keys = qkv_ref[:, width : 2 * width]
    values = qkv_ref[:, 2 * width :]
    total = jnp.zeros((rows, width), F32)
    places = bias_places(place_ref, block, blocks, rows, seq_len)
    for head in range(heads):
        scores = lax.dot_general(
            only(head_lanes(rows, width, head_width, head), queries),
            keys,
            (((1,), (1,)), ((), ())),
            preferred_element_type=F32,
        )
        bias = jnp.concatenate(
            [
                jnp.concatenate([skew_ref[head, :, pl.ds(place, rows)] for place in part], 1)
                for part in places
            ],
            0,
        )
        scores = jnp.where(allowed, scores + bias, MASKED)
        grown = jnp.exp(scores - jnp.max(scores, axis=1, keepdims=True))
        prob = (grown * (1.0 / jnp.sum(grown, axis=1, keepdims=True))).astype(LOW)
        p_ref[head] = prob
        total = total + jnp.dot(
            prob,
            only(head_lanes(seq_len, width, head_width, head), values),
            preferred_element_type=F32,
        )
    attended = total.astype(LOW)
    o_ref[...] = attended
    weight = got_ref[:, :shard, 3 * width :].reshape(model, width)
    held_ref[...] = contract_cols(attended, weight).astype(LOW)
    send_rows(step, near_count, place_ref[3], held_ref, other_refs, mine_refs)


def attention_forward(parts, got, table, place, heads, shard, count):
    rows, model = parts[0].shape
    blocks = len(parts)
    near_count = blocks // CORES
    seq_len, width = rows * blocks, got.shape[2] // 4
    out_specs, out_shape = sent_specs(near_count, count, rows // count, model)

    def fixed(shape):
        return pl.BlockSpec(shape, lambda i: (0,) * len(shape))

    outs = pl.pallas_call(
        functools.partial(forward_kernel, heads, shard, near_count, count),
        grid=(blocks,),
        in_specs=[pl.BlockSpec(memory_space=pltpu.SMEM)]
        + [fixed(part.shape) for part in parts]
        + [fixed(got.shape), fixed(table.shape)],
        out_specs=[
            fixed((seq_len, 3 * width)),
            pl.BlockSpec((rows, width), lambda i: (row_block(i, near_count), 0)),
            pl.BlockSpec((heads, rows, seq_len), lambda i: (0, row_block(i, near_count), 0)),
        ]
        + out_specs,
        out_shape=[
            jax.ShapeDtypeStruct((seq_len, 3 * width), LOW),
            jax.ShapeDtypeStruct((seq_len, width), LOW),
            jax.ShapeDtypeStruct((heads, seq_len, seq_len), LOW),
        ]
        + out_shape,
        scratch_shapes=[
            pltpu.VMEM((heads, SKEW, 2 * seq_len), F32),
            pltpu.VMEM((rows, model), LOW),
        ],
        compiler_params=pltpu.CompilerParams(vmem_limit_bytes=34 * 2**20),
        cost_estimate=pl.CostEstimate(flops=0, bytes_accessed=0, transcendentals=0),
        name="attention_forward",
    )(place, *parts, got, table)
    return (*outs[:3], outs[3 + count :], outs[3 : 3 + count])


def backward_kernel(heads, shard, near_count, count, place_ref, *refs):
    came, refs = refs[: 2 * count], refs[2 * count :]
    p_ref, got_ref, qkv_ref, o_ref, d_ref, dt_ref, do_ref = refs[:7]
    rows_ref, dk_sum, dv_sum, do_sum, skew_ref = refs[7:]
    step = pl.program_id(0)
    block = row_block(step, near_count)
    take_rows(step, near_count, place_ref[3], came[:count], came[count:], rows_ref)
    rows, model = rows_ref.shape
    seq_len = qkv_ref.shape[0]
    width = qkv_ref.shape[1] // 3
    head_width = width // heads
    span = 2 * seq_len
    blocks = seq_len // rows

    @pl.when(step == 0)
    def _():
        dk_sum[...] = jnp.zeros_like(dk_sum)
        dv_sum[...] = jnp.zeros_like(dv_sum)
        do_sum[...] = jnp.zeros_like(do_sum)
        skew_ref[...] = jnp.zeros_like(skew_ref)

    here = pl.ds(pl.multiple_of(block * rows, rows), rows)
    queries = qkv_ref[here, :width]
    keys = qkv_ref[:, width : 2 * width]
    values = qkv_ref[:, 2 * width :]
    weight = got_ref[:, :shard, 3 * width :].reshape(model, width)
    grads = rows_dot(rows_ref[...], weight).astype(LOW)
    do_sum[...] += contract_rows(o_ref[...], rows_ref[...])
    total = jnp.zeros((rows, width), F32)
    places = bias_places(place_ref, block, blocks, rows, seq_len)
    for head in range(heads):
        own = head_lanes(rows, width, head_width, head)
        own_grads = only(own, grads)
        d_prob = lax.dot_general(
            own_grads, values, (((1,), (1,)), ((), ())), preferred_element_type=F32
        )
        prob_low = p_ref[head]
        prob = prob_low.astype(F32)
        weighed = prob * d_prob
        d_scores = (weighed - prob * jnp.sum(weighed, axis=1, keepdims=True)).astype(LOW)
        total = total + jnp.dot(
            d_scores,
            only(head_lanes(seq_len, width, head_width, head), keys),
            preferred_element_type=F32,
        )
        dk_sum[...] += lax.dot_general(
            d_scores, only(own, queries), (((0,), (0,)), ((), ())), preferred_element_type=F32
        )
        dv_sum[...] += lax.dot_general(
            prob_low, own_grads, (((0,), (0,)), ((), ())), preferred_element_type=F32
        )
        for part in range(rows // SKEW):
            for at in range(blocks):
                skew_ref[head, :, pl.ds(places[part][at], rows)] += d_scores[
                    part * SKEW : (part + 1) * SKEW, at * rows : (at + 1) * rows
                ].astype(F32)
    d_ref[here, :width] = total.astype(LOW)

    @pl.when(step == pl.num_programs(0) - 1)
    def _():
        d_ref[:, width : 2 * width] = dk_sum[...].astype(LOW)
        d_ref[:, 2 * width :] = dv_sum[...].astype(LOW)
        for at in range(do_ref.shape[0]):
            do_ref[at] = do_sum[:, at * shard : (at + 1) * shard].astype(LOW)
        one_hot = bucket_onehot(dt_ref.shape[0], seq_len)
        row = lax.broadcasted_iota(jnp.int32, (SKEW, span), 0)
        column = lax.broadcasted_iota(jnp.int32, dt_ref.shape, 1)
        result = jnp.zeros(dt_ref.shape, F32)
        for head in range(heads):
            level = pltpu.roll(skew_ref[head], SKEW, 1)
            bit = 1
            while bit < SKEW:
                level = jnp.where((row & bit) != 0, pltpu.roll(level, span - bit, 1), level)
                bit *= 2
            line = jnp.sum(level, axis=0, keepdims=True)
            summed = jnp.sum(jnp.where(one_hot, line, 0.0), axis=1, keepdims=True)
            result = jnp.where(column == head, summed, result)
        dt_ref[...] = result


def attention_backward(prob, mine, other, got, qkv, attended, place, heads, shard, buckets):
    seq_len, width = qkv.shape[0], qkv.shape[1] // 3
    near_count, own_rows, model = mine[0].shape
    count = len(mine)
    rows = count * own_rows
    came_specs, _ = sent_specs(near_count, count, own_rows, model)
    return pl.pallas_call(
        functools.partial(backward_kernel, heads, shard, near_count, count),
        grid=(seq_len // rows,),
        in_specs=[
            pl.BlockSpec(memory_space=pltpu.SMEM),
            *came_specs,
            pl.BlockSpec((heads, rows, seq_len), lambda i: (0, row_block(i, near_count), 0)),
            pl.BlockSpec(got.shape, lambda i: (0, 0, 0)),
            pl.BlockSpec(qkv.shape, lambda i: (0, 0)),
            pl.BlockSpec((rows, width), lambda i: (row_block(i, near_count), 0)),
        ],
        out_specs=[
            pl.BlockSpec(qkv.shape, lambda i: (0, 0)),
            pl.BlockSpec((buckets, 128), lambda i: (0, 0)),
            pl.BlockSpec((model // shard, width, shard), lambda i: (0, 0, 0)),
        ],
        out_shape=[
            jax.ShapeDtypeStruct(qkv.shape, LOW),
            jax.ShapeDtypeStruct((buckets, 128), F32),
            jax.ShapeDtypeStruct((model // shard, width, shard), LOW),
        ],
        scratch_shapes=[
            pltpu.VMEM((rows, model), LOW),
            pltpu.VMEM((seq_len, width), F32),
            pltpu.VMEM((seq_len, width), F32),
            pltpu.VMEM((width, model), F32),
            pltpu.VMEM((heads, SKEW, 2 * seq_len), F32),
        ],
        compiler_params=pltpu.CompilerParams(vmem_limit_bytes=34 * 2**20),
        cost_estimate=pl.CostEstimate(flops=0, bytes_accessed=0, transcendentals=0),
        name="attention_backward",
    )(place, *other, *mine, prob, got, qkv, attended)


EXTRA = 8
OWNER_ROWS = 64


def as_column(row, first, count):
    size = row.shape[1]
    here = lax.broadcasted_iota(jnp.int32, (count, size), 1) == first + lax.broadcasted_iota(
        jnp.int32, (count, size), 0
    )
    return jnp.sum(jnp.where(here, row, 0.0), axis=1, keepdims=True)


def blocks_kernel(seqs, members, q_ref, k_ref, v_ref, o_ref, gain_ref, table_ref, sent_ref):
    shard = q_ref.shape[0]
    width = q_ref.shape[1] // members
    gain = as_column(gain_ref[...].astype(LOW).astype(F32), 0, shard)
    parts = [
        (ref[...].astype(LOW).astype(F32) * gain).astype(LOW) for ref in (q_ref, k_ref, v_ref)
    ]
    parts.append(o_ref[...].T.astype(LOW))
    rest = jnp.zeros((EXTRA, sent_ref.shape[2]), LOW)
    table_rows, heads = table_ref.shape
    for seq in range(seqs):
        for member in range(members):
            at = seq * members + member
            for i, part in enumerate(parts):
                sent_ref[at, :shard, i * width : (i + 1) * width] = part[
                    :, member * width : (member + 1) * width
                ]
            sent_ref[at, shard:, :] = rest
            sent_ref[at, shard : shard + table_rows, :heads] = table_ref[...].astype(LOW)


def attention_blocks(weights, w_out, gain, table, seqs, members):
    shard, columns = weights[0].shape
    return pl.pallas_call(
        functools.partial(blocks_kernel, seqs, members),
        out_shape=jax.ShapeDtypeStruct(
            (seqs * members, shard + EXTRA, 4 * columns // members), LOW
        ),
        compiler_params=pltpu.CompilerParams(vmem_limit_bytes=60 * 2**20),
        cost_estimate=pl.CostEstimate(
            flops=0, bytes_accessed=16 * shard * columns, transcendentals=0
        ),
        name="attention_blocks",
    )(*weights, w_out, gain, table)


def owner_kernel(count, members, table_shape, *refs):
    got_ref, extra_ref = refs[:2]
    weight_refs = refs[2 : 2 + count]
    gain_ref = refs[2 + count]
    grad_refs = refs[3 + count : 3 + 2 * count]
    sum_ref = refs[3 + 2 * count]
    step = pl.program_id(0)
    rows = got_ref.shape[1]
    seqs = got_ref.shape[0] // members
    width = got_ref.shape[2] // count
    size = sum_ref.shape[1]
    gain = as_column(gain_ref[...].astype(LOW).astype(F32), step * rows, rows)
    total = jnp.zeros((rows, 1), F32)
    for member in range(members):
        product = sum(got_ref[seq * members + member].astype(F32) for seq in range(seqs))
        for i in range(count):
            part = product[:, i * width : (i + 1) * width]
            here = pl.ds(member * width, width)
            grad_refs[i][:, here] = part * gain
            weight = weight_refs[i][:, here].astype(LOW).astype(F32)
            total = total + jnp.sum(weight * part, axis=1, keepdims=True)

    @pl.when(step == 0)
    def _():
        sum_ref[...] = jnp.zeros_like(sum_ref)

    diagonal = lax.broadcasted_iota(jnp.int32, (rows, size), 1) == step * rows + (
        lax.broadcasted_iota(jnp.int32, (rows, size), 0)
    )
    sum_ref[...] += jnp.sum(jnp.where(diagonal, total, 0.0), axis=0, keepdims=True)
    if table_shape is not None:
        table_rows, heads = table_shape
        each = heads // members
        for member in range(members):
            piece = sum(extra_ref[seq * members + member].astype(F32) for seq in range(seqs))
            refs[-1][:, member * each : (member + 1) * each] = piece[:table_rows, :each]


def owner_grads(got, weights, gain, members, table_shape):
    sources, height, columns = got.shape
    shard, wide = weights[0].shape
    count = len(weights)
    rows = min(OWNER_ROWS, shard)
    step_rows = pl.BlockSpec((rows, wide), lambda i: (i, 0))
    row = pl.BlockSpec((1, shard), lambda i: (0, 0))
    last = height // EXTRA - 1
    out_specs = [step_rows] * count + [row]
    out_shape = [jax.ShapeDtypeStruct((shard, wide), F32)] * count
    out_shape.append(jax.ShapeDtypeStruct((1, shard), F32))
    if table_shape is not None:
        out_specs.append(pl.BlockSpec(table_shape, lambda i: (0, 0)))
        out_shape.append(jax.ShapeDtypeStruct(table_shape, F32))
    outs = pl.pallas_call(
        functools.partial(owner_kernel, count, members, table_shape),
        grid=(shard // rows,),
        in_specs=[
            pl.BlockSpec((sources, rows, columns), lambda i: (0, i, 0)),
            pl.BlockSpec((sources, EXTRA, columns), lambda i: (0, last, 0)),
        ]
        + [step_rows] * count
        + [row],
        out_specs=out_specs,
        out_shape=out_shape,
        compiler_params=pltpu.CompilerParams(vmem_limit_bytes=32 * 2**20),
        cost_estimate=pl.CostEstimate(
            flops=0, bytes_accessed=10 * count * shard * wide, transcendentals=0
        ),
        name="owner_grads",
    )(got, got, *weights, gain)
    return outs[:count], outs[count], outs[-1] if table_shape is not None else None


def rows_kernel(members, split, got_ref, first_ref, second_ref):
    seqs = got_ref.shape[0] // members
    rest = got_ref.shape[1] - split
    for member in range(members):
        total = sum(got_ref[seq * members + member].astype(F32) for seq in range(seqs))
        first_ref[pl.ds(member * split, split), :] = total[:split]
        second_ref[pl.ds(member * rest, rest), :] = total[split:]


def owner_rows(got, members, split):
    height, columns = got.shape[1:]
    return pl.pallas_call(
        functools.partial(rows_kernel, members, split),
        out_shape=[
            jax.ShapeDtypeStruct((members * split, columns), F32),
            jax.ShapeDtypeStruct((members * (height - split), columns), F32),
        ],
        compiler_params=pltpu.CompilerParams(vmem_limit_bytes=32 * 2**20),
        cost_estimate=pl.CostEstimate(
            flops=0, bytes_accessed=4 * got.size, transcendentals=0
        ),
        name="owner_rows",
    )(got)


def rows_dot(left, right):
    return jnp.dot(left, right, preferred_element_type=F32)


def contract_cols(left, right):
    return lax.dot_general(left, right, (((1,), (1,)), ((), ())), preferred_element_type=F32)


def contract_rows(left, right):
    return lax.dot_general(left, right, (((0,), (0,)), ((), ())), preferred_element_type=F32)

def row_block(step, near_count):
    return lax.rem(step + near_count, CORES * near_count)


def send_rows(step, near_count, mp_at, held_ref, other_refs, mine_refs):
    count = len(other_refs)
    own_rows = held_ref.shape[0] // count

    def write(refs):
        for away, ref in enumerate(refs):
            first = pl.multiple_of(lax.bitwise_xor(mp_at, away) * own_rows, own_rows)
            ref[0] = held_ref[pl.ds(first, own_rows), :]

    @pl.when(step < near_count)
    def _():
        write(other_refs)

    @pl.when(step >= near_count)
    def _():
        write(mine_refs)


def place_kernel(place_ref, *refs):
    parts, outs = refs[:-2], refs[-2:]
    each = len(parts) // 2
    for at in range(each):

        @pl.when(pl.program_id(0) == at)
        def _():
            for i, out_ref in enumerate(outs):
                out_ref[...] = parts[i * each + at][...]


def place_rows(first, second, place, near_count):
    rows, model = first[0].shape
    shape = jax.ShapeDtypeStruct((rows * len(first), model), LOW)

    def place_of(i, place_ref):
        return (i // 2) * near_count + lax.bitwise_xor(place_ref[4], lax.rem(i, 2)), 0

    part = pl.BlockSpec((rows, model), lambda i, place_ref: (0, 0))
    return pl.pallas_call(
        place_kernel,
        grid_spec=pltpu.PrefetchScalarGridSpec(
            num_scalar_prefetch=1,
            grid=(len(first),),
            in_specs=[part] * (2 * len(first)),
            out_specs=[pl.BlockSpec((rows, model), place_of)] * 2,
        ),
        out_shape=[shape] * 2,
        compiler_params=pltpu.CompilerParams(vmem_limit_bytes=32 * 2**20),
        cost_estimate=pl.CostEstimate(flops=0, bytes_accessed=0, transcendentals=0),
        name="place_rows",
    )(place, *first, *second)


def take_rows(step, near_count, mp_at, other_refs, mine_refs, rows_ref):
    own_rows = other_refs[0].shape[1]

    def read(refs):
        for away, ref in enumerate(refs):
            first = pl.multiple_of(lax.bitwise_xor(mp_at, away) * own_rows, own_rows)
            rows_ref[pl.ds(first, own_rows), :] = ref[0]

    @pl.when(step < near_count)
    def _():
        read(other_refs)

    @pl.when(step >= near_count)
    def _():
        read(mine_refs)


def sent_specs(near_count, count, own_rows, model):
    other = pl.BlockSpec((1, own_rows, model), lambda i: (jnp.minimum(i, near_count - 1), 0, 0))
    mine = pl.BlockSpec((1, own_rows, model), lambda i: (jnp.maximum(i - near_count, 0), 0, 0))
    shape = jax.ShapeDtypeStruct((near_count, own_rows, model), LOW)
    return [other] * count + [mine] * count, [shape] * (2 * count)


def partial_kernel(near_count, count, product, place_ref, left_ref, weight_ref, *refs):
    held_ref = refs[-1]
    product(left_ref, weight_ref, held_ref)
    send_rows(
        pl.program_id(0), near_count, place_ref[3], held_ref, refs[:count], refs[count : 2 * count]
    )


def partial_rows(left, weight, model, place, near_count, count, product, name):
    seq_len, depth = left.shape
    rows = seq_len // (CORES * near_count)
    out_specs, out_shape = sent_specs(near_count, count, rows // count, model)
    outs = pl.pallas_call(
        functools.partial(partial_kernel, near_count, count, product),
        grid=(CORES * near_count,),
        in_specs=[
            pl.BlockSpec(memory_space=pltpu.SMEM),
            pl.BlockSpec((rows, depth), lambda i: (row_block(i, near_count), 0)),
            pl.BlockSpec(weight.shape, lambda i: (0, 0, 0)),
        ],
        out_specs=out_specs,
        out_shape=out_shape,
        scratch_shapes=[pltpu.VMEM((rows, model), LOW)],
        compiler_params=pltpu.CompilerParams(vmem_limit_bytes=40 * 2**20),
        cost_estimate=pl.CostEstimate(
            flops=0, bytes_accessed=0, transcendentals=0
        ),
        name=name,
    )(place, left, weight)
    return outs[count:], outs[:count]


def column_product(shard, first, last, left_ref, weight_ref, held_ref):
    weight = weight_ref[:, :shard, first:last]
    weight = weight.reshape(weight.shape[0] * shard, last - first)
    held_ref[...] = contract_cols(left_ref[...], weight).astype(LOW)


def row_product(height, left_ref, weight_ref, held_ref):
    left = left_ref[...]
    width = weight_ref.shape[2]
    for at in range(weight_ref.shape[0]):
        held_ref[:, at * width : (at + 1) * width] = rows_dot(
            left, weight_ref[at, :height, :]
        ).astype(LOW)


def ffn_blocks_kernel(seqs, members, gate_ref, up_ref, down_ref, gain_ref, first_ref, second_ref):
    shard = gate_ref.shape[0]
    width = gate_ref.shape[1] // members
    gain = as_column(gain_ref[...].astype(LOW).astype(F32), 0, shard)
    for member in range(members):
        here = slice(member * width, (member + 1) * width)
        parts = [
            (ref[:, here].astype(LOW).astype(F32) * gain).astype(LOW) for ref in (gate_ref, up_ref)
        ]
        both = jnp.concatenate(parts, 1)
        down = down_ref[here, :].astype(LOW)
        for seq in range(seqs):
            at = seq * members + member
            first_ref[at, :width, :] = down
            first_ref[at, width:, :] = both[:, :shard]
            second_ref[at] = both[:, shard:]


def ffn_blocks(w_gate, w_up, w_down, gain, seqs, members):
    shard, columns = w_gate.shape
    width = columns // members
    return pl.pallas_call(
        functools.partial(ffn_blocks_kernel, seqs, members),
        out_shape=[
            jax.ShapeDtypeStruct((seqs * members, width + shard, shard), LOW),
            jax.ShapeDtypeStruct((seqs * members, shard, 2 * width - shard), LOW),
        ],
        compiler_params=pltpu.CompilerParams(vmem_limit_bytes=40 * 2**20),
        cost_estimate=pl.CostEstimate(
            flops=0, bytes_accessed=18 * shard * columns, transcendentals=0
        ),
        name="ffn_blocks",
    )(w_gate, w_up, w_down, gain)


def ffn_kernel(near_count, count, place_ref, *refs):
    came, refs = refs[: 2 * count], refs[2 * count :]
    grad_ref, first_ref, second_ref = refs[:3]
    other_refs, mine_refs = refs[3 : 3 + count], refs[3 + count : 3 + 2 * count]
    rows_ref, act_ref, d_ref, down_ref, held_ref, sum_ref = refs[3 + 2 * count :]
    step = pl.program_id(0)
    take_rows(step, near_count, place_ref[3], came[:count], came[count:], rows_ref)
    sources, height, shard = first_ref.shape
    width = height - shard
    rows = rows_ref[...]
    block = row_block(step, near_count)
    first = block_place(block, place_ref[1], near_count) * rows.shape[0]
    valid = first + lax.broadcasted_iota(jnp.int32, (rows.shape[0], 1), 0) < place_ref[0]
    grads = only(valid, grad_ref[...])
    early = first_ref[:, width:, :].reshape(sources * shard, shard)
    late = second_ref[...].reshape(sources * shard, 2 * width - shard)
    both = jnp.concatenate([rows_dot(rows, early), rows_dot(rows, late)], 1)
    gate, up = both[:, :width], both[:, width:]
    scale, cubic = 0.7978845608028654, 0.044715
    square = gate * gate
    bent = jnp.tanh(scale * (gate + cubic * square * gate))
    half = 0.5 * (1.0 + bent)
    value = gate * half
    slope = half + 0.5 * gate * (1.0 - bent * bent) * (scale * (1.0 + 3.0 * cubic * square))
    act = (value * up).astype(LOW)
    act_ref[...] = act
    d_hidden = jnp.zeros((rows.shape[0], width), F32)
    for at in range(sources):
        d_hidden = d_hidden + contract_cols(
            grads[:, at * shard : (at + 1) * shard], first_ref[at, :width, :]
        )
    d_both = jnp.concatenate(
        [(d_hidden * up * slope).astype(LOW), (d_hidden * value).astype(LOW)], 1
    )
    d_ref[...] = d_both
    held_ref[...] = (
        contract_cols(d_both[:, :shard], early) + contract_cols(d_both[:, shard:], late)
    ).astype(LOW)
    send_rows(step, near_count, place_ref[3], held_ref, other_refs, mine_refs)
    product = contract_rows(act, grads)

    @pl.when(step == 0)
    def _():
        sum_ref[...] = product

    @pl.when(step > 0)
    def _():
        sum_ref[...] += product

    @pl.when(step == pl.num_programs(0) - 1)
    def _():
        for at in range(sources):
            down_ref[at] = sum_ref[:, at * shard : (at + 1) * shard].astype(LOW)


def feed_forward(mine, other, grads, first, second, place):
    seq_len, model = grads.shape
    near_count, count = mine[0].shape[0], len(mine)
    sources, height, shard = first.shape
    width = height - shard
    rows = seq_len // (CORES * near_count)
    out_specs, out_shape = sent_specs(near_count, count, rows // count, model)

    def blocks(columns):
        return pl.BlockSpec((rows, columns), lambda i: (row_block(i, near_count), 0))

    outs = pl.pallas_call(
        functools.partial(ffn_kernel, near_count, count),
        grid=(CORES * near_count,),
        in_specs=[
            pl.BlockSpec(memory_space=pltpu.SMEM),
            *out_specs,
            blocks(model),
            pl.BlockSpec(first.shape, lambda i: (0, 0, 0)),
            pl.BlockSpec(second.shape, lambda i: (0, 0, 0)),
        ],
        out_specs=out_specs
        + [
            blocks(model),
            blocks(width),
            blocks(2 * width),
            pl.BlockSpec((sources, width, shard), lambda i: (0, 0, 0)),
        ],
        out_shape=out_shape
        + [
            jax.ShapeDtypeStruct((seq_len, model), LOW),
            jax.ShapeDtypeStruct((seq_len, width), LOW),
            jax.ShapeDtypeStruct((seq_len, 2 * width), LOW),
            jax.ShapeDtypeStruct((sources, width, shard), LOW),
        ],
        scratch_shapes=[pltpu.VMEM((rows, model), LOW), pltpu.VMEM((width, model), F32)],
        compiler_params=pltpu.CompilerParams(vmem_limit_bytes=56 * 2**20),
        cost_estimate=pl.CostEstimate(
            flops=12 * seq_len * model * width, bytes_accessed=12 * seq_len * model, transcendentals=0
        ),
        name="feed_forward",
    )(place, *other, *mine, grads, first, second)
    return outs[count : 2 * count], outs[:count], *outs[2 * count :]


COLUMN = ("seq", "near", "core")


def exchange(blocks, axes):
    return lax.all_to_all(blocks, axes, split_axis=0, concat_axis=0, tiled=True)


def swap(block, axis):
    return lax.ppermute(block, axis, [(0, 1), (1, 0)])


def after(value, *done):
    return lax.optimization_barrier((value,) + done)[0]


def rms(values):
    return lax.rsqrt(jnp.mean(values * values, axis=-1, keepdims=True) + EPSILON)


def norm_grad(inner, normed, inverse):
    return inverse * (inner - normed * jnp.mean(inner * normed, axis=-1, keepdims=True))


def local(
    inputs,
    cotangent,
    lengths,
    attn_scale,
    w_query,
    w_key,
    w_value,
    w_out,
    rel_table,
    ffn_scale,
    w_gate,
    w_up,
    w_down,
):
    seqs = lax.axis_size("seq")
    near_count = lax.axis_size("near")
    mp_count = lax.axis_size("mp")
    members = near_count * CORES
    sources = seqs * members
    tok_rows, model = inputs.shape
    seq_len = tok_rows * members
    own_rows = tok_rows // mp_count
    half_rows = seq_len // CORES
    shard = attn_scale.shape[0]
    table_rows, heads_mp = rel_table.shape
    buckets = table_rows * sources
    heads = heads_mp // members
    width = w_query.shape[1] // members
    hidden_width = w_gate.shape[1] // members

    near_at = lax.axis_index("near")
    core_at = lax.axis_index("core")
    mp_at = lax.axis_index("mp")
    member_at = near_at * CORES + core_at
    length = lax.dynamic_slice_in_dim(lengths, lax.axis_index("seq"), 1, 0)
    place = jnp.stack(
        [length[0]] + [at.astype(jnp.int32) for at in (core_at, member_at, mp_at, near_at)]
    )

    def over_mp(own, axis):
        shape = own.shape[:axis] + (mp_count,) + own.shape[axis:]
        blocks = lax.dynamic_update_index_in_dim(jnp.zeros(shape, own.dtype), own, mp_at, axis)
        moved = [(away, shifted(own, away)) for away in reversed(range(1, mp_count))]
        for away, block in moved:
            blocks = lax.dynamic_update_index_in_dim(blocks, block, mp_at ^ away, axis)
        return blocks

    def shifted(block, away):
        return lax.ppermute(block, "mp", [(i, i ^ away) for i in range(mp_count)])

    def in_near_order(own, moved):
        return jnp.stack(
            [jnp.where(near_at == 0, own, moved), jnp.where(near_at == 0, moved, own)], 0
        )

    def near_rows(blocks, meanwhile):
        own = [lax.dynamic_slice_in_dim(block, mp_at * own_rows, own_rows, 0) for block in blocks]
        near = swap(jnp.stack(own), "near")
        came = [(0, near)] + [(away, shifted(near, away)) for away in range(1, mp_count)]
        made = meanwhile(came[1][1])
        came = came[:2] + [(away, after(block, *made)) for away, block in came[2:]]
        halves = []
        for half in (came, [(away, swap(block, "core")) for away, block in came]):
            rows = jnp.zeros((len(blocks), mp_count, own_rows, model), near.dtype)
            for away, block in half:
                rows = lax.dynamic_update_index_in_dim(rows, block, mp_at ^ away, 1)
            halves.append([rows[i].reshape(tok_rows, model) for i in range(len(blocks))])
        return *halves, made

    def gather_rows(near):
        mine = [near] + [shifted(near, away) for away in range(1, mp_count)]
        return mine, [swap(block, "core") for block in mine]

    def sum_cores(mine, other):
        return [
            kept.astype(F32) + swap(sent, "core").astype(F32) for kept, sent in zip(mine, other)
        ]

    def send_mp(sums):
        return [shifted(sums[away].astype(LOW), away) for away in reversed(range(1, mp_count))]

    def sum_mp(sums, *meanwhile):
        moved = send_mp(sums)
        if meanwhile:
            moved = [after(piece, *meanwhile) for piece in moved]
        return sum((piece.astype(F32) for piece in moved), sums[0])

    def split_near(pair):
        sent = jnp.where(near_at == 0, pair[1], pair[0]).astype(LOW)
        return sent, jnp.where(near_at == 0, pair[0], pair[1])

    def sum_near_both(pair):
        low = pair.astype(LOW)
        moved = swap(low, "near")
        return low.astype(F32) + moved.astype(F32), moved

    def near_pair(own, moved):
        pair = [
            lax.dynamic_slice_in_dim(block, mp_at * own_rows, own_rows, 0)
            for block in (own, moved)
        ]
        return in_near_order(*pair)

    def here(pair):
        return lax.dynamic_index_in_dim(pair, near_at, 0, keepdims=False)

    attn_sent = attention_blocks(
        (w_query, w_key, w_value), w_out, attn_scale.reshape(1, shard), rel_table, seqs, members
    )
    attn_got = exchange(attn_sent, COLUMN)
    def partial(left, weight, product, name):
        return partial_rows(left, weight, model, place, near_count, mp_count, product, name)

    table = attn_got[:, shard : shard + table_rows, :heads_mp].reshape(buckets, heads_mp)

    def normed(rows):
        values = rows.astype(F32)
        return (values * rms(values)).astype(LOW)

    def make_blocks(first_came):
        return ffn_blocks(
            w_gate, w_up, w_down, after(ffn_scale.reshape(1, shard), first_came), seqs, members
        )

    (moved_inputs, moved_cotangent), core_moved, (ffn_first, ffn_second) = near_rows(
        [inputs, cotangent], make_blocks
    )
    input_parts = [inputs, moved_inputs, swap(inputs, "core"), core_moved[0]]
    core_cotangent = swap(after(cotangent, moved_inputs), "core")
    grad_parts = [cotangent, moved_cotangent, core_cotangent, core_moved[1]]
    parts = [normed(part) for part in input_parts]
    parts = lax.optimization_barrier((*parts, ffn_first, ffn_second))[:4]
    first_got = exchange(after(ffn_first, attn_got), COLUMN)

    qkv, attended, prob, out_mine, out_other = attention_forward(
        parts, attn_got, table, place, heads, shard, mp_count
    )
    normed_rows, grad_two = place_rows(parts, grad_parts, after(place, attended), near_count)
    mixed, mixed_moved = sum_near_both(
        after(sum_mp(sum_cores(out_mine, out_other), grad_two, normed_rows), first_got)
    )
    second_got = exchange(after(ffn_second, mixed_moved), COLUMN)

    pair_inputs = near_pair(inputs, moved_inputs).astype(F32)
    after_attn = pair_inputs + mixed
    inv_two = rms(after_attn)
    normed_two = after_attn * inv_two
    mine_two, other_two = gather_rows(normed_two.astype(LOW))

    d_mine, d_other, hidden_two, acts, d_both, d_down_w = feed_forward(
        mine_two, other_two, grad_two, first_got, second_got, place
    )
    inner_cores = sum_cores(d_mine, d_other)
    down_product = functools.partial(row_product, hidden_width)
    ffn_partial = partial(after(acts, *inner_cores), first_got, down_product, "ffn_out")

    def to_owners(grad):
        return exchange(grad, COLUMN)

    d_gate_up_w = contract_rows(hidden_two, after(d_both, *inner_cores)).astype(LOW)
    inner_two, inner_moved = sum_near_both(
        sum_mp(inner_cores, d_gate_up_w, *ffn_partial[0], *ffn_partial[1])
    )

    pair_first = (
        lax.broadcasted_iota(jnp.int32, (near_count, own_rows, 1), 0) * (CORES * tok_rows)
        + lax.broadcasted_iota(jnp.int32, (near_count, own_rows, 1), 1)
        + (core_at * tok_rows + mp_at * own_rows)
    )
    pair_valid = pair_first < length
    pair_grad = near_pair(cotangent, moved_cotangent).astype(F32)
    grad_one = jnp.where(pair_valid, pair_grad, 0.0) + norm_grad(inner_two, normed_two, inv_two)
    grad_one_low = grad_one.astype(LOW)
    mine_one, other_one = gather_rows(grad_one_low)
    d_gate_up = to_owners(
        after(d_gate_up_w, inner_moved, grad_one_low).reshape(sources, shard, -1)
    )
    ffn_cores = sum_cores(*ffn_partial)
    d_qkv, d_table, d_out = attention_backward(
        prob, mine_one, other_one, attn_got, qkv, attended, place, heads, shard, buckets
    )
    qkv_product = functools.partial(column_product, shard, 0, 3 * width)
    ffn_moved = send_mp([after(rows, *mine_one[1:]) for rows in ffn_cores])
    table_sent = d_table[:, :heads].astype(LOW).reshape(sources, table_rows, heads)
    table_sent = jnp.pad(
        table_sent, ((0, 0), (0, EXTRA - table_rows), (0, 3 * width - heads))
    )
    d_qkv_w = contract_rows(normed_rows, d_qkv).astype(LOW).reshape(sources, shard, -1)
    d_qkv_sent = jnp.concatenate([d_qkv_w, table_sent], 1)
    kept, sent = partial(
        after(d_qkv, d_qkv_sent, *ffn_moved), attn_got, qkv_product, "attention_in"
    )
    inner_cores = sum_cores(kept, [after(rows, d_gate_up) for rows in sent])
    inner_pair = sum_mp(inner_cores)
    d_qkv_got = to_owners(after(d_qkv_sent, d_gate_up))
    d_rows_sent = jnp.concatenate([d_down_w, after(d_out, inner_cores[0])], 1)

    ffn_sent, ffn_kept = split_near(
        sum((piece.astype(F32) for piece in ffn_moved), ffn_cores[0])
    )
    inner_sent, inner_kept = split_near(inner_pair)
    came = swap(
        after(jnp.stack([ffn_sent, inner_sent]), here(pair_valid), d_rows_sent), "near"
    )
    came = after(came, d_qkv_got)
    own_inputs = here(pair_inputs)
    inv_one = rms(own_inputs)
    grad_input = here(grad_one) + norm_grad(inner_kept + came[1].astype(F32), own_inputs * inv_one, inv_one)
    own_out = jnp.where(here(pair_valid), here(after_attn) + ffn_kept + came[0].astype(F32), 0.0)
    owned = jnp.stack([own_out.astype(LOW), grad_input.astype(LOW)])
    rows_out = [jnp.zeros((mp_count, own_rows, model), LOW)] * 2
    blocks_out = [owned] + [shifted(owned, away) for away in range(1, mp_count)]
    d_rows = to_owners(after(d_rows_sent, d_qkv_got))
    for away, block in enumerate(blocks_out):
        rows_out = [
            lax.dynamic_update_index_in_dim(rows, block[i], mp_at ^ away, 0)
            for i, rows in enumerate(rows_out)
        ]
    layer_out, d_inputs = (rows.reshape(tok_rows, model) for rows in rows_out)

    (d_w_gate, d_w_up), ffn_gain, _ = owner_grads(
        after(d_gate_up, blocks_out[1]), (w_gate, w_up), ffn_scale.reshape(1, shard), members, None
    )
    (d_w_query, d_w_key, d_w_value), attn_gain, d_rel_table = owner_grads(
        after(d_qkv_got, blocks_out[1]),
        (w_query, w_key, w_value),
        attn_scale.reshape(1, shard),
        members,
        (table_rows, heads_mp),
    )
    gains = jnp.concatenate([attn_gain, ffn_gain], 0)
    d_w_down, d_w_out = owner_rows(d_rows, members, hidden_width)
    gains = sum((shifted(gains, away) for away in range(1, mp_count)), gains)
    return (
        layer_out,
        d_inputs,
        gains[0],
        d_w_query,
        d_w_key,
        d_w_value,
        d_w_out,
        d_rel_table,
        gains[1],
        d_w_gate,
        d_w_up,
        d_w_down,
    )


def solution(mesh):
    fsdp, mp = mesh.shape["fsdp"], mesh.shape["mp"]

    def run(*args):
        seqs = args[2].shape[0]
        members = fsdp // seqs
        inner = Mesh(
            mesh.devices.reshape(seqs, members // CORES, CORES, mp), ("seq", "near", "core", "mp")
        )
        rows, columns, first = P(COLUMN, None), P("mp", COLUMN), P(COLUMN)
        both = P(COLUMN, "mp")
        in_specs = (
            rows, rows, P(), first, both, both, both, columns, both, first, both, both, columns,
        )
        out_specs = (
            rows, rows, first, both, both, both, columns, both, first, both, both, columns,
        )
        return jax.shard_map(
            local, mesh=inner, in_specs=in_specs, out_specs=out_specs, check_vma=False
        )(*args)

    return run
```

```python
import functools

import jax
import jax.numpy as jnp
from jax import lax
from jax.experimental import pallas as pl
from jax.experimental.pallas import tpu as pltpu
from jax.sharding import Mesh, PartitionSpec as P

LOW = jnp.bfloat16
F32 = jnp.float32
CORES = 2
THRESHOLDS = (12, 16, 23, 32, 46, 64, 91)
EPSILON = 1e-06
MASKED = -1e30
SKEW = 128


def bucket_of(rel_offset):
    distance = jnp.abs(rel_offset)
    far_bucket = 8 + sum(((distance >= threshold).astype(jnp.int32) for threshold in THRESHOLDS))
    bucket_abs = jnp.where(distance < 8, distance, far_bucket)
    return bucket_abs + jnp.where(rel_offset > 0, 16, 0)


def bucket_onehot(buckets, seq_len):
    offset = lax.broadcasted_iota(jnp.int32, (buckets, 2 * seq_len), 1) - seq_len
    bucket = lax.broadcasted_iota(jnp.int32, (buckets, 2 * seq_len), 0)
    return bucket_of(offset) == bucket


def head_lanes(rows, width, head_width, head):
    lane = lax.broadcasted_iota(jnp.int32, (rows, width), 1)
    return (lane >= head * head_width) & (lane < (head + 1) * head_width)


def only(mask, values):
    return jnp.where(mask, values, jnp.zeros_like(values))


def block_place(block, core, near_count):
    return lax.rem(block, near_count) * CORES + lax.bitwise_xor(lax.div(block, near_count), core)


def bias_places(place_ref, step, blocks, rows, seq_len):
    core, near_count = place_ref[1], blocks // CORES
    query = block_place(step, core, near_count) * rows
    return [
        [
            pl.multiple_of(
                block_place(block, core, near_count) * rows - query - part * SKEW + seq_len - SKEW,
                SKEW,
            )
            for block in range(blocks)
        ]
        for part in range(rows // SKEW)
    ]


def forward_kernel(heads, shard, near_count, count, place_ref, *refs):
    own_ref, moved_ref, core_ref, core_moved_ref, got_ref, table_ref = refs[:6]
    qkv_ref, o_ref, p_ref = refs[6:9]
    other_refs, mine_refs = refs[9 : 9 + count], refs[9 + count : 9 + 2 * count]
    skew_ref, held_ref = refs[9 + 2 * count :]
    step = pl.program_id(0)
    seq_len = qkv_ref.shape[0]
    rows, width = o_ref.shape
    model = held_ref.shape[1]
    head_width = width // heads
    span = 2 * seq_len
    blocks = seq_len // rows
    block = row_block(step, near_count)

    @pl.when(step == 0)
    def _():
        weight = got_ref[:, :shard, : 3 * width].reshape(model, 3 * width)
        near = place_ref[4]
        for at, ref in enumerate((own_ref, moved_ref, core_ref, core_moved_ref)):
            first = (at // 2) * near_count + lax.bitwise_xor(near, at % 2)
            qkv_ref[pl.ds(pl.multiple_of(first * rows, rows), rows), :] = rows_dot(
                ref[...], weight
            ).astype(LOW)
        one_hot = bucket_onehot(table_ref.shape[0], seq_len)
        table = table_ref[...].astype(F32)
        column = lax.broadcasted_iota(jnp.int32, table.shape, 1)
        for head in range(heads):
            here = column == place_ref[2] * heads + head
            levels = jnp.sum(jnp.where(here, table, 0.0), axis=1, keepdims=True)
            line = jnp.sum(jnp.where(one_hot, levels, 0.0), axis=0, keepdims=True)
            line = jnp.broadcast_to(line, (SKEW, span))
            skew_ref[head] = pltpu.roll(line, span - SKEW, 1, stride=1, stride_axis=0)

    row = lax.broadcasted_iota(jnp.int32, (1, rows), 1)
    allowed = jnp.concatenate(
        [
            block_place(at, place_ref[1], near_count) * rows + row < place_ref[0]
            for at in range(blocks)
        ],
        1,
    )
    queries = qkv_ref[pl.ds(pl.multiple_of(block * rows, rows), rows), :width]
    keys = qkv_ref[:, width : 2 * width]
    values = qkv_ref[:, 2 * width :]
    total = jnp.zeros((rows, width), F32)
    places = bias_places(place_ref, block, blocks, rows, seq_len)
    for head in range(heads):
        scores = lax.dot_general(
            only(head_lanes(rows, width, head_width, head), queries),
            keys,
            (((1,), (1,)), ((), ())),
            preferred_element_type=F32,
        )
        bias = jnp.concatenate(
            [
                jnp.concatenate([skew_ref[head, :, pl.ds(place, rows)] for place in part], 1)
                for part in places
            ],
            0,
        )
        scores = jnp.where(allowed, scores + bias, MASKED)
        grown = jnp.exp(scores - jnp.max(scores, axis=1, keepdims=True))
        prob = (grown * (1.0 / jnp.sum(grown, axis=1, keepdims=True))).astype(LOW)
        p_ref[head] = prob
        total = total + jnp.dot(
            prob,
            only(head_lanes(seq_len, width, head_width, head), values),
            preferred_element_type=F32,
        )
    attended = total.astype(LOW)
    o_ref[...] = attended
    weight = got_ref[:, :shard, 3 * width :].reshape(model, width)
    held_ref[...] = contract_cols(attended, weight).astype(LOW)
    send_rows(step, near_count, place_ref[3], held_ref, other_refs, mine_refs)


def attention_forward(parts, got, table, place, heads, shard, count):
    rows, model = parts[0].shape
    blocks = len(parts)
    near_count = blocks // CORES
    seq_len, width = rows * blocks, got.shape[2] // 4
    out_specs, out_shape = sent_specs(near_count, count, rows // count, model)

    def fixed(shape):
        return pl.BlockSpec(shape, lambda i: (0,) * len(shape))

    outs = pl.pallas_call(
        functools.partial(forward_kernel, heads, shard, near_count, count),
        grid=(blocks,),
        in_specs=[pl.BlockSpec(memory_space=pltpu.SMEM)]
        + [fixed(part.shape) for part in parts]
        + [fixed(got.shape), fixed(table.shape)],
        out_specs=[
            fixed((seq_len, 3 * width)),
            pl.BlockSpec((rows, width), lambda i: (row_block(i, near_count), 0)),
            pl.BlockSpec((heads, rows, seq_len), lambda i: (0, row_block(i, near_count), 0)),
        ]
        + out_specs,
        out_shape=[
            jax.ShapeDtypeStruct((seq_len, 3 * width), LOW),
            jax.ShapeDtypeStruct((seq_len, width), LOW),
            jax.ShapeDtypeStruct((heads, seq_len, seq_len), LOW),
        ]
        + out_shape,
        scratch_shapes=[
            pltpu.VMEM((heads, SKEW, 2 * seq_len), F32),
            pltpu.VMEM((rows, model), LOW),
        ],
        compiler_params=pltpu.CompilerParams(vmem_limit_bytes=34 * 2**20),
        cost_estimate=pl.CostEstimate(flops=0, bytes_accessed=0, transcendentals=0),
        name="attention_forward",
    )(place, *parts, got, table)
    return (*outs[:3], outs[3 + count :], outs[3 : 3 + count])


def backward_kernel(heads, shard, near_count, count, place_ref, *refs):
    came, refs = refs[: 2 * count], refs[2 * count :]
    p_ref, got_ref, qkv_ref, o_ref, d_ref, dt_ref, do_ref = refs[:7]
    rows_ref, dk_sum, dv_sum, do_sum, skew_ref = refs[7:]
    step = pl.program_id(0)
    block = row_block(step, near_count)
    take_rows(step, near_count, place_ref[3], came[:count], came[count:], rows_ref)
    rows, model = rows_ref.shape
    seq_len = qkv_ref.shape[0]
    width = qkv_ref.shape[1] // 3
    head_width = width // heads
    span = 2 * seq_len
    blocks = seq_len // rows

    @pl.when(step == 0)
    def _():
        dk_sum[...] = jnp.zeros_like(dk_sum)
        dv_sum[...] = jnp.zeros_like(dv_sum)
        do_sum[...] = jnp.zeros_like(do_sum)
        skew_ref[...] = jnp.zeros_like(skew_ref)

    here = pl.ds(pl.multiple_of(block * rows, rows), rows)
    queries = qkv_ref[here, :width]
    keys = qkv_ref[:, width : 2 * width]
    values = qkv_ref[:, 2 * width :]
    weight = got_ref[:, :shard, 3 * width :].reshape(model, width)
    grads = rows_dot(rows_ref[...], weight).astype(LOW)
    do_sum[...] += contract_rows(o_ref[...], rows_ref[...])
    total = jnp.zeros((rows, width), F32)
    places = bias_places(place_ref, block, blocks, rows, seq_len)
    for head in range(heads):
        own = head_lanes(rows, width, head_width, head)
        own_grads = only(own, grads)
        d_prob = lax.dot_general(
            own_grads, values, (((1,), (1,)), ((), ())), preferred_element_type=F32
        )
        prob_low = p_ref[head]
        prob = prob_low.astype(F32)
        weighed = prob * d_prob
        d_scores = (weighed - prob * jnp.sum(weighed, axis=1, keepdims=True)).astype(LOW)
        total = total + jnp.dot(
            d_scores,
            only(head_lanes(seq_len, width, head_width, head), keys),
            preferred_element_type=F32,
        )
        dk_sum[...] += lax.dot_general(
            d_scores, only(own, queries), (((0,), (0,)), ((), ())), preferred_element_type=F32
        )
        dv_sum[...] += lax.dot_general(
            prob_low, own_grads, (((0,), (0,)), ((), ())), preferred_element_type=F32
        )
        for part in range(rows // SKEW):
            for at in range(blocks):
                skew_ref[head, :, pl.ds(places[part][at], rows)] += d_scores[
                    part * SKEW : (part + 1) * SKEW, at * rows : (at + 1) * rows
                ].astype(F32)
    d_ref[here, :width] = total.astype(LOW)

    @pl.when(step == pl.num_programs(0) - 1)
    def _():
        d_ref[:, width : 2 * width] = dk_sum[...].astype(LOW)
        d_ref[:, 2 * width :] = dv_sum[...].astype(LOW)
        for at in range(do_ref.shape[0]):
            do_ref[at] = do_sum[:, at * shard : (at + 1) * shard].astype(LOW)
        one_hot = bucket_onehot(dt_ref.shape[0], seq_len)
        row = lax.broadcasted_iota(jnp.int32, (SKEW, span), 0)
        column = lax.broadcasted_iota(jnp.int32, dt_ref.shape, 1)
        result = jnp.zeros(dt_ref.shape, F32)
        for head in range(heads):
            level = pltpu.roll(skew_ref[head], SKEW, 1)
            bit = 1
            while bit < SKEW:
                level = jnp.where((row & bit) != 0, pltpu.roll(level, span - bit, 1), level)
                bit *= 2
            line = jnp.sum(level, axis=0, keepdims=True)
            summed = jnp.sum(jnp.where(one_hot, line, 0.0), axis=1, keepdims=True)
            result = jnp.where(column == head, summed, result)
        dt_ref[...] = result


def attention_backward(prob, mine, other, got, qkv, attended, place, heads, shard, buckets):
    seq_len, width = qkv.shape[0], qkv.shape[1] // 3
    near_count, own_rows, model = mine[0].shape
    count = len(mine)
    rows = count * own_rows
    came_specs, _ = sent_specs(near_count, count, own_rows, model)
    return pl.pallas_call(
        functools.partial(backward_kernel, heads, shard, near_count, count),
        grid=(seq_len // rows,),
        in_specs=[
            pl.BlockSpec(memory_space=pltpu.SMEM),
            *came_specs,
            pl.BlockSpec((heads, rows, seq_len), lambda i: (0, row_block(i, near_count), 0)),
            pl.BlockSpec(got.shape, lambda i: (0, 0, 0)),
            pl.BlockSpec(qkv.shape, lambda i: (0, 0)),
            pl.BlockSpec((rows, width), lambda i: (row_block(i, near_count), 0)),
        ],
        out_specs=[
            pl.BlockSpec(qkv.shape, lambda i: (0, 0)),
            pl.BlockSpec((buckets, 128), lambda i: (0, 0)),
            pl.BlockSpec((model // shard, width, shard), lambda i: (0, 0, 0)),
        ],
        out_shape=[
            jax.ShapeDtypeStruct(qkv.shape, LOW),
            jax.ShapeDtypeStruct((buckets, 128), F32),
            jax.ShapeDtypeStruct((model // shard, width, shard), LOW),
        ],
        scratch_shapes=[
            pltpu.VMEM((rows, model), LOW),
            pltpu.VMEM((seq_len, width), F32),
            pltpu.VMEM((seq_len, width), F32),
            pltpu.VMEM((width, model), F32),
            pltpu.VMEM((heads, SKEW, 2 * seq_len), F32),
        ],
        compiler_params=pltpu.CompilerParams(vmem_limit_bytes=34 * 2**20),
        cost_estimate=pl.CostEstimate(flops=0, bytes_accessed=0, transcendentals=0),
        name="attention_backward",
    )(place, *other, *mine, prob, got, qkv, attended)


EXTRA = 8
OWNER_ROWS = 64


def as_column(row, first, count):
    size = row.shape[1]
    here = lax.broadcasted_iota(jnp.int32, (count, size), 1) == first + lax.broadcasted_iota(
        jnp.int32, (count, size), 0
    )
    return jnp.sum(jnp.where(here, row, 0.0), axis=1, keepdims=True)


def blocks_kernel(seqs, members, q_ref, k_ref, v_ref, o_ref, gain_ref, table_ref, sent_ref):
    shard = q_ref.shape[0]
    width = q_ref.shape[1] // members
    gain = as_column(gain_ref[...].astype(LOW).astype(F32), 0, shard)
    parts = [
        (ref[...].astype(LOW).astype(F32) * gain).astype(LOW) for ref in (q_ref, k_ref, v_ref)
    ]
    parts.append(o_ref[...].T.astype(LOW))
    rest = jnp.zeros((EXTRA, sent_ref.shape[2]), LOW)
    table_rows, heads = table_ref.shape
    for seq in range(seqs):
        for member in range(members):
            at = seq * members + member
            for i, part in enumerate(parts):
                sent_ref[at, :shard, i * width : (i + 1) * width] = part[
                    :, member * width : (member + 1) * width
                ]
            sent_ref[at, shard:, :] = rest
            sent_ref[at, shard : shard + table_rows, :heads] = table_ref[...].astype(LOW)


def attention_blocks(weights, w_out, gain, table, seqs, members):
    shard, columns = weights[0].shape
    return pl.pallas_call(
        functools.partial(blocks_kernel, seqs, members),
        out_shape=jax.ShapeDtypeStruct(
            (seqs * members, shard + EXTRA, 4 * columns // members), LOW
        ),
        compiler_params=pltpu.CompilerParams(vmem_limit_bytes=60 * 2**20),
        cost_estimate=pl.CostEstimate(
            flops=0, bytes_accessed=16 * shard * columns, transcendentals=0
        ),
        name="attention_blocks",
    )(*weights, w_out, gain, table)


def owner_kernel(count, members, table_shape, *refs):
    got_ref, extra_ref = refs[:2]
    weight_refs = refs[2 : 2 + count]
    gain_ref = refs[2 + count]
    grad_refs = refs[3 + count : 3 + 2 * count]
    sum_ref = refs[3 + 2 * count]
    step = pl.program_id(0)
    rows = got_ref.shape[1]
    seqs = got_ref.shape[0] // members
    width = got_ref.shape[2] // count
    size = sum_ref.shape[1]
    gain = as_column(gain_ref[...].astype(LOW).astype(F32), step * rows, rows)
    total = jnp.zeros((rows, 1), F32)
    for member in range(members):
        product = sum(got_ref[seq * members + member].astype(F32) for seq in range(seqs))
        for i in range(count):
            part = product[:, i * width : (i + 1) * width]
            here = pl.ds(member * width, width)
            grad_refs[i][:, here] = part * gain
            weight = weight_refs[i][:, here].astype(LOW).astype(F32)
            total = total + jnp.sum(weight * part, axis=1, keepdims=True)

    @pl.when(step == 0)
    def _():
        sum_ref[...] = jnp.zeros_like(sum_ref)

    diagonal = lax.broadcasted_iota(jnp.int32, (rows, size), 1) == step * rows + (
        lax.broadcasted_iota(jnp.int32, (rows, size), 0)
    )
    sum_ref[...] += jnp.sum(jnp.where(diagonal, total, 0.0), axis=0, keepdims=True)
    if table_shape is not None:
        table_rows, heads = table_shape
        each = heads // members
        for member in range(members):
            piece = sum(extra_ref[seq * members + member].astype(F32) for seq in range(seqs))
            refs[-1][:, member * each : (member + 1) * each] = piece[:table_rows, :each]


def owner_grads(got, weights, gain, members, table_shape):
    sources, height, columns = got.shape
    shard, wide = weights[0].shape
    count = len(weights)
    rows = min(OWNER_ROWS, shard)
    step_rows = pl.BlockSpec((rows, wide), lambda i: (i, 0))
    row = pl.BlockSpec((1, shard), lambda i: (0, 0))
    last = height // EXTRA - 1
    out_specs = [step_rows] * count + [row]
    out_shape = [jax.ShapeDtypeStruct((shard, wide), F32)] * count
    out_shape.append(jax.ShapeDtypeStruct((1, shard), F32))
    if table_shape is not None:
        out_specs.append(pl.BlockSpec(table_shape, lambda i: (0, 0)))
        out_shape.append(jax.ShapeDtypeStruct(table_shape, F32))
    outs = pl.pallas_call(
        functools.partial(owner_kernel, count, members, table_shape),
        grid=(shard // rows,),
        in_specs=[
            pl.BlockSpec((sources, rows, columns), lambda i: (0, i, 0)),
            pl.BlockSpec((sources, EXTRA, columns), lambda i: (0, last, 0)),
        ]
        + [step_rows] * count
        + [row],
        out_specs=out_specs,
        out_shape=out_shape,
        compiler_params=pltpu.CompilerParams(vmem_limit_bytes=32 * 2**20),
        cost_estimate=pl.CostEstimate(
            flops=0, bytes_accessed=10 * count * shard * wide, transcendentals=0
        ),
        name="owner_grads",
    )(got, got, *weights, gain)
    return outs[:count], outs[count], outs[-1] if table_shape is not None else None


def rows_kernel(members, split, got_ref, first_ref, second_ref):
    seqs = got_ref.shape[0] // members
    rest = got_ref.shape[1] - split
    for member in range(members):
        total = sum(got_ref[seq * members + member].astype(F32) for seq in range(seqs))
        first_ref[pl.ds(member * split, split), :] = total[:split]
        second_ref[pl.ds(member * rest, rest), :] = total[split:]


def owner_rows(got, members, split):
    height, columns = got.shape[1:]
    return pl.pallas_call(
        functools.partial(rows_kernel, members, split),
        out_shape=[
            jax.ShapeDtypeStruct((members * split, columns), F32),
            jax.ShapeDtypeStruct((members * (height - split), columns), F32),
        ],
        compiler_params=pltpu.CompilerParams(vmem_limit_bytes=32 * 2**20),
        cost_estimate=pl.CostEstimate(
            flops=0, bytes_accessed=4 * got.size, transcendentals=0
        ),
        name="owner_rows",
    )(got)


def rows_dot(left, right):
    return jnp.dot(left, right, preferred_element_type=F32)


def contract_cols(left, right):
    return lax.dot_general(left, right, (((1,), (1,)), ((), ())), preferred_element_type=F32)


def contract_rows(left, right):
    return lax.dot_general(left, right, (((0,), (0,)), ((), ())), preferred_element_type=F32)

def row_block(step, near_count):
    return lax.rem(step + near_count, CORES * near_count)


def send_rows(step, near_count, mp_at, held_ref, other_refs, mine_refs):
    count = len(other_refs)
    own_rows = held_ref.shape[0] // count

    def write(refs):
        for away, ref in enumerate(refs):
            first = pl.multiple_of(lax.bitwise_xor(mp_at, away) * own_rows, own_rows)
            ref[0] = held_ref[pl.ds(first, own_rows), :]

    @pl.when(step < near_count)
    def _():
        write(other_refs)

    @pl.when(step >= near_count)
    def _():
        write(mine_refs)


def place_kernel(place_ref, *refs):
    parts, outs = refs[:-2], refs[-2:]
    each = len(parts) // 2
    for at in range(each):

        @pl.when(pl.program_id(0) == at)
        def _():
            for i, out_ref in enumerate(outs):
                out_ref[...] = parts[i * each + at][...]


def place_rows(first, second, place, near_count):
    rows, model = first[0].shape
    shape = jax.ShapeDtypeStruct((rows * len(first), model), LOW)

    def place_of(i, place_ref):
        return (i // 2) * near_count + lax.bitwise_xor(place_ref[4], lax.rem(i, 2)), 0

    part = pl.BlockSpec((rows, model), lambda i, place_ref: (0, 0))
    return pl.pallas_call(
        place_kernel,
        grid_spec=pltpu.PrefetchScalarGridSpec(
            num_scalar_prefetch=1,
            grid=(len(first),),
            in_specs=[part] * (2 * len(first)),
            out_specs=[pl.BlockSpec((rows, model), place_of)] * 2,
        ),
        out_shape=[shape] * 2,
        compiler_params=pltpu.CompilerParams(vmem_limit_bytes=32 * 2**20),
        cost_estimate=pl.CostEstimate(flops=0, bytes_accessed=0, transcendentals=0),
        name="place_rows",
    )(place, *first, *second)


def take_rows(step, near_count, mp_at, other_refs, mine_refs, rows_ref):
    own_rows = other_refs[0].shape[1]

    def read(refs):
        for away, ref in enumerate(refs):
            first = pl.multiple_of(lax.bitwise_xor(mp_at, away) * own_rows, own_rows)
            rows_ref[pl.ds(first, own_rows), :] = ref[0]

    @pl.when(step < near_count)
    def _():
        read(other_refs)

    @pl.when(step >= near_count)
    def _():
        read(mine_refs)


def sent_specs(near_count, count, own_rows, model):
    other = pl.BlockSpec((1, own_rows, model), lambda i: (jnp.minimum(i, near_count - 1), 0, 0))
    mine = pl.BlockSpec((1, own_rows, model), lambda i: (jnp.maximum(i - near_count, 0), 0, 0))
    shape = jax.ShapeDtypeStruct((near_count, own_rows, model), LOW)
    return [other] * count + [mine] * count, [shape] * (2 * count)


def partial_kernel(near_count, count, product, place_ref, left_ref, weight_ref, *refs):
    held_ref = refs[-1]
    product(left_ref, weight_ref, held_ref)
    send_rows(
        pl.program_id(0), near_count, place_ref[3], held_ref, refs[:count], refs[count : 2 * count]
    )


def partial_rows(left, weight, model, place, near_count, count, product, name):
    seq_len, depth = left.shape
    rows = seq_len // (CORES * near_count)
    out_specs, out_shape = sent_specs(near_count, count, rows // count, model)
    outs = pl.pallas_call(
        functools.partial(partial_kernel, near_count, count, product),
        grid=(CORES * near_count,),
        in_specs=[
            pl.BlockSpec(memory_space=pltpu.SMEM),
            pl.BlockSpec((rows, depth), lambda i: (row_block(i, near_count), 0)),
            pl.BlockSpec(weight.shape, lambda i: (0, 0, 0)),
        ],
        out_specs=out_specs,
        out_shape=out_shape,
        scratch_shapes=[pltpu.VMEM((rows, model), LOW)],
        compiler_params=pltpu.CompilerParams(vmem_limit_bytes=40 * 2**20),
        cost_estimate=pl.CostEstimate(
            flops=0, bytes_accessed=0, transcendentals=0
        ),
        name=name,
    )(place, left, weight)
    return outs[count:], outs[:count]


def column_product(shard, first, last, left_ref, weight_ref, held_ref):
    weight = weight_ref[:, :shard, first:last]
    weight = weight.reshape(weight.shape[0] * shard, last - first)
    held_ref[...] = contract_cols(left_ref[...], weight).astype(LOW)


def row_product(height, left_ref, weight_ref, held_ref):
    left = left_ref[...]
    width = weight_ref.shape[2]
    for at in range(weight_ref.shape[0]):
        held_ref[:, at * width : (at + 1) * width] = rows_dot(
            left, weight_ref[at, :height, :]
        ).astype(LOW)


def ffn_blocks_kernel(seqs, members, gate_ref, up_ref, down_ref, gain_ref, first_ref, second_ref):
    shard = gate_ref.shape[0]
    width = gate_ref.shape[1] // members
    gain = as_column(gain_ref[...].astype(LOW).astype(F32), 0, shard)
    for member in range(members):
        here = slice(member * width, (member + 1) * width)
        parts = [
            (ref[:, here].astype(LOW).astype(F32) * gain).astype(LOW) for ref in (gate_ref, up_ref)
        ]
        both = jnp.concatenate(parts, 1)
        down = down_ref[here, :].astype(LOW)
        for seq in range(seqs):
            at = seq * members + member
            first_ref[at, :width, :] = down
            first_ref[at, width:, :] = both[:, :shard]
            second_ref[at] = both[:, shard:]


def ffn_blocks(w_gate, w_up, w_down, gain, seqs, members):
    shard, columns = w_gate.shape
    width = columns // members
    return pl.pallas_call(
        functools.partial(ffn_blocks_kernel, seqs, members),
        out_shape=[
            jax.ShapeDtypeStruct((seqs * members, width + shard, shard), LOW),
            jax.ShapeDtypeStruct((seqs * members, shard, 2 * width - shard), LOW),
        ],
        compiler_params=pltpu.CompilerParams(vmem_limit_bytes=40 * 2**20),
        cost_estimate=pl.CostEstimate(
            flops=0, bytes_accessed=18 * shard * columns, transcendentals=0
        ),
        name="ffn_blocks",
    )(w_gate, w_up, w_down, gain)


def ffn_kernel(near_count, count, place_ref, *refs):
    came, refs = refs[: 2 * count], refs[2 * count :]
    grad_ref, first_ref, second_ref = refs[:3]
    other_refs, mine_refs = refs[3 : 3 + count], refs[3 + count : 3 + 2 * count]
    rows_ref, act_ref, d_ref, down_ref, held_ref, sum_ref = refs[3 + 2 * count :]
    step = pl.program_id(0)
    take_rows(step, near_count, place_ref[3], came[:count], came[count:], rows_ref)
    sources, height, shard = first_ref.shape
    width = height - shard
    rows = rows_ref[...]
    block = row_block(step, near_count)
    first = block_place(block, place_ref[1], near_count) * rows.shape[0]
    valid = first + lax.broadcasted_iota(jnp.int32, (rows.shape[0], 1), 0) < place_ref[0]
    grads = only(valid, grad_ref[...])
    early = first_ref[:, width:, :].reshape(sources * shard, shard)
    late = second_ref[...].reshape(sources * shard, 2 * width - shard)
    both = jnp.concatenate([rows_dot(rows, early), rows_dot(rows, late)], 1)
    gate, up = both[:, :width], both[:, width:]
    scale, cubic = 0.7978845608028654, 0.044715
    square = gate * gate
    bent = jnp.tanh(scale * (gate + cubic * square * gate))
    half = 0.5 * (1.0 + bent)
    value = gate * half
    slope = half + 0.5 * gate * (1.0 - bent * bent) * (scale * (1.0 + 3.0 * cubic * square))
    act = (value * up).astype(LOW)
    act_ref[...] = act
    d_hidden = jnp.zeros((rows.shape[0], width), F32)
    for at in range(sources):
        d_hidden = d_hidden + contract_cols(
            grads[:, at * shard : (at + 1) * shard], first_ref[at, :width, :]
        )
    d_both = jnp.concatenate(
        [(d_hidden * up * slope).astype(LOW), (d_hidden * value).astype(LOW)], 1
    )
    d_ref[...] = d_both
    held_ref[...] = (
        contract_cols(d_both[:, :shard], early) + contract_cols(d_both[:, shard:], late)
    ).astype(LOW)
    send_rows(step, near_count, place_ref[3], held_ref, other_refs, mine_refs)
    product = contract_rows(act, grads)

    @pl.when(step == 0)
    def _():
        sum_ref[...] = product

    @pl.when(step > 0)
    def _():
        sum_ref[...] += product

    @pl.when(step == pl.num_programs(0) - 1)
    def _():
        for at in range(sources):
            down_ref[at] = sum_ref[:, at * shard : (at + 1) * shard].astype(LOW)


def feed_forward(mine, other, grads, first, second, place):
    seq_len, model = grads.shape
    near_count, count = mine[0].shape[0], len(mine)
    sources, height, shard = first.shape
    width = height - shard
    rows = seq_len // (CORES * near_count)
    out_specs, out_shape = sent_specs(near_count, count, rows // count, model)

    def blocks(columns):
        return pl.BlockSpec((rows, columns), lambda i: (row_block(i, near_count), 0))

    outs = pl.pallas_call(
        functools.partial(ffn_kernel, near_count, count),
        grid=(CORES * near_count,),
        in_specs=[
            pl.BlockSpec(memory_space=pltpu.SMEM),
            *out_specs,
            blocks(model),
            pl.BlockSpec(first.shape, lambda i: (0, 0, 0)),
            pl.BlockSpec(second.shape, lambda i: (0, 0, 0)),
        ],
        out_specs=out_specs
        + [
            blocks(model),
            blocks(width),
            blocks(2 * width),
            pl.BlockSpec((sources, width, shard), lambda i: (0, 0, 0)),
        ],
        out_shape=out_shape
        + [
            jax.ShapeDtypeStruct((seq_len, model), LOW),
            jax.ShapeDtypeStruct((seq_len, width), LOW),
            jax.ShapeDtypeStruct((seq_len, 2 * width), LOW),
            jax.ShapeDtypeStruct((sources, width, shard), LOW),
        ],
        scratch_shapes=[pltpu.VMEM((rows, model), LOW), pltpu.VMEM((width, model), F32)],
        compiler_params=pltpu.CompilerParams(vmem_limit_bytes=50 * 2**20),
        cost_estimate=pl.CostEstimate(
            flops=12 * seq_len * model * width, bytes_accessed=12 * seq_len * model, transcendentals=0
        ),
        name="feed_forward",
    )(place, *other, *mine, grads, first, second)
    return outs[count : 2 * count], outs[:count], *outs[2 * count :]


COLUMN = ("seq", "near", "core")


def exchange(blocks, axes):
    return lax.all_to_all(blocks, axes, split_axis=0, concat_axis=0, tiled=True)


def swap(block, axis):
    return lax.ppermute(block, axis, [(0, 1), (1, 0)])


def after(value, *done):
    return lax.optimization_barrier((value,) + done)[0]


def rms(values):
    return lax.rsqrt(jnp.mean(values * values, axis=-1, keepdims=True) + EPSILON)


def norm_grad(inner, normed, inverse):
    return inverse * (inner - normed * jnp.mean(inner * normed, axis=-1, keepdims=True))


def local(
    inputs,
    cotangent,
    lengths,
    attn_scale,
    w_query,
    w_key,
    w_value,
    w_out,
    rel_table,
    ffn_scale,
    w_gate,
    w_up,
    w_down,
):
    seqs = lax.axis_size("seq")
    near_count = lax.axis_size("near")
    mp_count = lax.axis_size("mp")
    members = near_count * CORES
    sources = seqs * members
    tok_rows, model = inputs.shape
    seq_len = tok_rows * members
    own_rows = tok_rows // mp_count
    half_rows = seq_len // CORES
    shard = attn_scale.shape[0]
    table_rows, heads_mp = rel_table.shape
    buckets = table_rows * sources
    heads = heads_mp // members
    width = w_query.shape[1] // members
    hidden_width = w_gate.shape[1] // members

    near_at = lax.axis_index("near")
    core_at = lax.axis_index("core")
    mp_at = lax.axis_index("mp")
    member_at = near_at * CORES + core_at
    length = lax.dynamic_slice_in_dim(lengths, lax.axis_index("seq"), 1, 0)
    place = jnp.stack(
        [length[0]] + [at.astype(jnp.int32) for at in (core_at, member_at, mp_at, near_at)]
    )

    def over_mp(own, axis):
        shape = own.shape[:axis] + (mp_count,) + own.shape[axis:]
        blocks = lax.dynamic_update_index_in_dim(jnp.zeros(shape, own.dtype), own, mp_at, axis)
        moved = [(away, shifted(own, away)) for away in reversed(range(1, mp_count))]
        for away, block in moved:
            blocks = lax.dynamic_update_index_in_dim(blocks, block, mp_at ^ away, axis)
        return blocks

    def shifted(block, away):
        return lax.ppermute(block, "mp", [(i, i ^ away) for i in range(mp_count)])

    def in_near_order(own, moved):
        return jnp.stack(
            [jnp.where(near_at == 0, own, moved), jnp.where(near_at == 0, moved, own)], 0
        )

    def near_rows(blocks, meanwhile):
        own = [lax.dynamic_slice_in_dim(block, mp_at * own_rows, own_rows, 0) for block in blocks]
        near = swap(jnp.stack(own), "near")
        came = [(0, near)] + [(away, shifted(near, away)) for away in range(1, mp_count)]
        made = meanwhile(came[1][1])
        came = came[:2] + [(away, after(block, *made)) for away, block in came[2:]]
        halves = []
        for half in (came, [(away, swap(block, "core")) for away, block in came]):
            rows = jnp.zeros((len(blocks), mp_count, own_rows, model), near.dtype)
            for away, block in half:
                rows = lax.dynamic_update_index_in_dim(rows, block, mp_at ^ away, 1)
            halves.append([rows[i].reshape(tok_rows, model) for i in range(len(blocks))])
        return *halves, made

    def gather_rows(near):
        mine = [near] + [shifted(near, away) for away in range(1, mp_count)]
        return mine, [swap(block, "core") for block in mine]

    def sum_cores(mine, other):
        return [
            kept.astype(F32) + swap(sent, "core").astype(F32) for kept, sent in zip(mine, other)
        ]

    def send_mp(sums):
        return [shifted(sums[away].astype(LOW), away) for away in reversed(range(1, mp_count))]

    def sum_mp(sums, *meanwhile):
        moved = send_mp(sums)
        if meanwhile:
            moved = [after(piece, *meanwhile) for piece in moved]
        return sum((piece.astype(F32) for piece in moved), sums[0])

    def split_near(pair):
        sent = jnp.where(near_at == 0, pair[1], pair[0]).astype(LOW)
        return sent, jnp.where(near_at == 0, pair[0], pair[1])

    def sum_near_both(pair):
        low = pair.astype(LOW)
        moved = swap(low, "near")
        return low.astype(F32) + moved.astype(F32), moved

    def near_pair(own, moved):
        pair = [
            lax.dynamic_slice_in_dim(block, mp_at * own_rows, own_rows, 0)
            for block in (own, moved)
        ]
        return in_near_order(*pair)

    def here(pair):
        return lax.dynamic_index_in_dim(pair, near_at, 0, keepdims=False)

    attn_sent = attention_blocks(
        (w_query, w_key, w_value), w_out, attn_scale.reshape(1, shard), rel_table, seqs, members
    )
    attn_got = exchange(attn_sent, COLUMN)
    def partial(left, weight, product, name):
        return partial_rows(left, weight, model, place, near_count, mp_count, product, name)

    table = attn_got[:, shard : shard + table_rows, :heads_mp].reshape(buckets, heads_mp)

    def normed(rows):
        values = rows.astype(F32)
        return (values * rms(values)).astype(LOW)

    def make_blocks(first_came):
        return ffn_blocks(
            w_gate, w_up, w_down, after(ffn_scale.reshape(1, shard), first_came), seqs, members
        )

    (moved_inputs, moved_cotangent), core_moved, (ffn_first, ffn_second) = near_rows(
        [inputs, cotangent], make_blocks
    )
    input_parts = [inputs, moved_inputs, swap(inputs, "core"), core_moved[0]]
    core_cotangent = swap(after(cotangent, moved_inputs), "core")
    grad_parts = [cotangent, moved_cotangent, core_cotangent, core_moved[1]]
    parts = [normed(part) for part in input_parts]
    parts = lax.optimization_barrier((*parts, ffn_first, ffn_second))[:4]
    first_got = exchange(after(ffn_first, attn_got), COLUMN)

    qkv, attended, prob, out_mine, out_other = attention_forward(
        parts, attn_got, table, place, heads, shard, mp_count
    )
    normed_rows, grad_two = place_rows(parts, grad_parts, after(place, attended), near_count)
    mixed, mixed_moved = sum_near_both(
        after(sum_mp(sum_cores(out_mine, out_other), grad_two, normed_rows), first_got)
    )
    second_got = exchange(after(ffn_second, mixed_moved), COLUMN)

    pair_inputs = near_pair(inputs, moved_inputs).astype(F32)
    after_attn = pair_inputs + mixed
    inv_two = rms(after_attn)
    normed_two = after_attn * inv_two
    mine_two, other_two = gather_rows(normed_two.astype(LOW))

    d_mine, d_other, hidden_two, acts, d_both, d_down_w = feed_forward(
        mine_two, other_two, grad_two, first_got, second_got, place
    )
    inner_cores = sum_cores(d_mine, d_other)
    down_product = functools.partial(row_product, hidden_width)
    ffn_partial = partial(after(acts, *inner_cores), first_got, down_product, "ffn_out")

    def to_owners(grad):
        return exchange(grad, COLUMN)

    d_gate_up_w = contract_rows(hidden_two, after(d_both, *inner_cores)).astype(LOW)
    inner_two, inner_moved = sum_near_both(
        sum_mp(inner_cores, d_gate_up_w, *ffn_partial[0], *ffn_partial[1])
    )

    pair_first = (
        lax.broadcasted_iota(jnp.int32, (near_count, own_rows, 1), 0) * (CORES * tok_rows)
        + lax.broadcasted_iota(jnp.int32, (near_count, own_rows, 1), 1)
        + (core_at * tok_rows + mp_at * own_rows)
    )
    pair_valid = pair_first < length
    pair_grad = near_pair(cotangent, moved_cotangent).astype(F32)
    grad_one = jnp.where(pair_valid, pair_grad, 0.0) + norm_grad(inner_two, normed_two, inv_two)
    grad_one_low = grad_one.astype(LOW)
    mine_one, other_one = gather_rows(grad_one_low)
    d_gate_up = to_owners(
        after(d_gate_up_w, inner_moved, grad_one_low).reshape(sources, shard, -1)
    )
    ffn_cores = sum_cores(*ffn_partial)
    d_qkv, d_table, d_out = attention_backward(
        prob, mine_one, other_one, attn_got, qkv, attended, place, heads, shard, buckets
    )
    qkv_product = functools.partial(column_product, shard, 0, 3 * width)
    ffn_moved = send_mp([after(rows, *mine_one[1:]) for rows in ffn_cores])
    table_sent = d_table[:, :heads].astype(LOW).reshape(sources, table_rows, heads)
    table_sent = jnp.pad(
        table_sent, ((0, 0), (0, EXTRA - table_rows), (0, 3 * width - heads))
    )
    d_qkv_w = contract_rows(normed_rows, d_qkv).astype(LOW).reshape(sources, shard, -1)
    d_qkv_sent = jnp.concatenate([d_qkv_w, table_sent], 1)
    inner_cores = sum_cores(
        *partial(after(d_qkv, d_qkv_sent, *ffn_moved), attn_got, qkv_product, "attention_in")
    )
    inner_pair = sum_mp(inner_cores)
    d_qkv_got = to_owners(after(d_qkv_sent, d_gate_up))
    d_rows_sent = jnp.concatenate([d_down_w, after(d_out, inner_cores[0])], 1)

    ffn_sent, ffn_kept = split_near(
        sum((piece.astype(F32) for piece in ffn_moved), ffn_cores[0])
    )
    inner_sent, inner_kept = split_near(inner_pair)
    came = swap(
        after(jnp.stack([ffn_sent, inner_sent]), here(pair_valid), d_rows_sent), "near"
    )
    came = after(came, d_qkv_got)
    own_inputs = here(pair_inputs)
    inv_one = rms(own_inputs)
    grad_input = here(grad_one) + norm_grad(inner_kept + came[1].astype(F32), own_inputs * inv_one, inv_one)
    own_out = jnp.where(here(pair_valid), here(after_attn) + ffn_kept + came[0].astype(F32), 0.0)
    owned = jnp.stack([own_out.astype(LOW), grad_input.astype(LOW)])
    rows_out = [jnp.zeros((mp_count, own_rows, model), LOW)] * 2
    blocks_out = [owned] + [shifted(owned, away) for away in range(1, mp_count)]
    d_rows = to_owners(after(d_rows_sent, d_qkv_got))
    for away, block in enumerate(blocks_out):
        rows_out = [
            lax.dynamic_update_index_in_dim(rows, block[i], mp_at ^ away, 0)
            for i, rows in enumerate(rows_out)
        ]
    layer_out, d_inputs = (rows.reshape(tok_rows, model) for rows in rows_out)

    (d_w_gate, d_w_up), ffn_gain, _ = owner_grads(
        after(d_gate_up, blocks_out[1]), (w_gate, w_up), ffn_scale.reshape(1, shard), members, None
    )
    (d_w_query, d_w_key, d_w_value), attn_gain, d_rel_table = owner_grads(
        after(d_qkv_got, blocks_out[1]),
        (w_query, w_key, w_value),
        attn_scale.reshape(1, shard),
        members,
        (table_rows, heads_mp),
    )
    gains = jnp.concatenate([attn_gain, ffn_gain], 0)
    d_w_down, d_w_out = owner_rows(d_rows, members, hidden_width)
    gains = sum((shifted(gains, away) for away in range(1, mp_count)), gains)
    return (
        layer_out,
        d_inputs,
        gains[0],
        d_w_query,
        d_w_key,
        d_w_value,
        d_w_out,
        d_rel_table,
        gains[1],
        d_w_gate,
        d_w_up,
        d_w_down,
    )


def solution(mesh):
    fsdp, mp = mesh.shape["fsdp"], mesh.shape["mp"]

    def run(*args):
        seqs = args[2].shape[0]
        members = fsdp // seqs
        inner = Mesh(
            mesh.devices.reshape(seqs, members // CORES, CORES, mp), ("seq", "near", "core", "mp")
        )
        rows, columns, first = P(COLUMN, None), P("mp", COLUMN), P(COLUMN)
        both = P(COLUMN, "mp")
        in_specs = (
            rows, rows, P(), first, both, both, both, columns, both, first, both, both, columns,
        )
        out_specs = (
            rows, rows, first, both, both, both, columns, both, first, both, both, columns,
        )
        return jax.shard_map(
            local, mesh=inner, in_specs=in_specs, out_specs=out_specs, check_vma=False
        )(*args)

    return run
```
